32 devices in a mesh: seq: 4 (over y, x), exp: 8 (over z, core).
Axes of the slice: x: 2, y: 2, z: 4, core: 2. Of those that a mesh axis runs over, the one named last changes fastest.
Arguments:
- query: bfloat16 [512, 1024], P('seq', 'exp'), may hold values from -6 to 6
- key_in: bfloat16 [512, 1024], P('seq', 'exp'), may hold values from -6 to 6
- value: bfloat16 [512, 1024], P('seq', 'exp'), may hold values from -6 to 6
- decay_log: float32 [512, 8], P('seq', 'exp'), may hold values from -1 to 0
- norm_gain: bfloat16 [1024], P('exp'), may hold values from 0.099609375 to 1.8984375
- w_out: bfloat16 [1024, 4096], P('exp'), may hold values from -0.1875 to 0.1875
- router: bfloat16 [4096, 4], replicated, may hold values from -0.09375 to 0.09375
- routes: int32 [512, 2], P('seq'), may hold values from 0 to 3, all different within a row; in each aligned block of 128 rows (0 to 127, 128 to 255, ...) at most 96 rows name the same one
- w_gate: bfloat16 [8, 4096, 288], P('exp'), may hold values from -0.09375 to 0.09375
- w_up: bfloat16 [8, 4096, 288], P('exp'), may hold values from -0.09375 to 0.09375
- w_down: bfloat16 [8, 288, 4096], P('exp'), may hold values from -0.25 to 0.25
Outputs:
- output: bfloat16 [512, 4096], P(('seq', 'exp'))
The draws below stay inside these ranges and needn't reach their ends.
Inputs may be any that keep to these rules, and one draw needn't show every extreme that they name: `routes`: among the positions of one block of 128 positions no expert is named more than 96 times, a bound that some block reaches; a position names 2 different experts.
All inputs are finite; a program needn't handle non-finite values.
Results may differ from the reference program's by a relative error of at most 0.015.
Values may be sent and summed in bfloat16 or wider, within the bound.
No kernel may reach another device: no remote copies, remote signals or barrier semaphores. Data moves between devices by JAX's collectives and lax.ppermute only.
A program may use at most 64 MiB of HBM per device.

```python
import math
import jax
import jax.numpy as jnp
import numpy as np
from jax import lax

HEAD = 128
DM = 4096
FFW = 288
EXPERTS = 4
TOP = 2
TOK_DEV = 128
HEAD_TOTAL = 8
ATT = 1024
SLICES = 2
SLICED = 8
CAP = 96
SEQUENCE_LENGTH = 512
N_SEQ = 4


def draw_decay_log(key, part):
    random_subkeys = jax.random.split(key, 7)
    fast_share = 0.5
    fast_heads = jax.random.bernoulli(random_subkeys[0], fast_share, (HEAD_TOTAL,))
    fast_rate = jax.random.uniform(random_subkeys[1], (HEAD_TOTAL,), jnp.float32, 1.0 / 50.0, 1.0 / 30.0)
    slow_rate = jnp.exp(jax.random.uniform(random_subkeys[2], (HEAD_TOTAL,), jnp.float32, jnp.log(0.1 / SEQUENCE_LENGTH), jnp.log(1.5 / SEQUENCE_LENGTH)))
    baseline_rate = jnp.where(fast_heads, fast_rate, slow_rate)
    jitter_level = jax.random.uniform(random_subkeys[4], (SEQUENCE_LENGTH, HEAD_TOTAL), jnp.float32, 0.5, 1.5)
    spike_mask = jax.random.bernoulli(random_subkeys[5], 3.0 / SEQUENCE_LENGTH, (SEQUENCE_LENGTH, HEAD_TOTAL))
    spike_loss = jax.random.uniform(random_subkeys[6], (SEQUENCE_LENGTH, HEAD_TOTAL), jnp.float32, 0.2, 0.5)
    return -(baseline_rate * jitter_level) + jnp.where(spike_mask, jnp.log(1.0 - spike_loss), 0.0)


def level_of(own_key, dims, pieces, smallest, top_value):
    loudness, own = 1.0, jax.random.fold_in(own_key, 6)
    for position, blocks in pieces:
        heights = jnp.exp(jax.random.uniform(jax.random.fold_in(own, position), (blocks,), jnp.float32, smallest / len(pieces), top_value / len(pieces)))
        loudness = loudness * jnp.repeat(heights, dims[position] // blocks).reshape([-1 if axis == position else 1 for axis in range(len(dims))])
    return loudness


def routed_block(rng, own, number, rows, number_of, top, reach, skew):
    sequence = jax.random.permutation(rng, number_of)
    packed, usual = portions_of(number_of, rows * top, reach, skew, True), portions_of(number_of, rows * top, reach, skew, False)
    places = jnp.arange(number_of)

    def named(sizes, turn):
        used = int((sizes > 0).sum())
        fixed = max(1, used // 4)
        shifted = fixed + (places - fixed + turn * (used - fixed)) % max(1, number_of - fixed)
        return jnp.zeros((number_of,), jnp.int32).at[sequence[jnp.where(places < fixed, places, shifted)]].set(jnp.asarray(sizes, jnp.int32))

    sizes = jnp.where(number % 4 == 0, named(packed, number // 4), named(usual, number - number // 4 - 1))
    mixed = jax.random.permutation(jax.random.fold_in(own, 3), number_of)
    source_of, receiver = mixed[0:number_of // 2 * 2:2], mixed[1:number_of // 2 * 2:2]
    room = jnp.minimum(sizes[source_of] - 1, reach - sizes[receiver]) // 2
    room = jnp.where((source_of == sequence[0]) | (receiver == sequence[0]) | (sizes[receiver] == 0), 0, jnp.maximum(room, 0))
    shifted = jax.random.randint(jax.random.fold_in(own, 4), (number_of // 2,), 0, 1 << 20) % (room + 1)
    sizes = sizes.at[source_of].add(-shifted).at[receiver].add(shifted)
    labels = jnp.searchsorted(jnp.cumsum(sizes), jnp.arange(rows * top), side="right").astype(jnp.int32)
    grid = labels.reshape(top, rows).T
    grid = grid[jax.random.permutation(jax.random.fold_in(own, 1), rows)]
    turn = jax.random.randint(jax.random.fold_in(own, 2), (rows, 1), 0, top)
    return jnp.take_along_axis(grid, (jnp.arange(top)[None, :] + turn) % top, axis=1)


def portions_of(number_of, total, most, skew, full):
    weights = [(1 << 20) // math.isqrt(rank ** skew) + 1 for rank in range(1, number_of + 1)]
    largest = most if full else min(most, max(-(-total // number_of), total * weights[0] // sum(weights)))
    least = 1 if total - largest >= number_of - 1 else 0
    given, rest = [largest] + [least] * (number_of - 1), total - largest - least * (number_of - 1)
    while rest > 0:
        candidates = [i for i in range(1, number_of) if given[i] < largest] or [i for i in range(1, number_of) if given[i] < most]
        pool, budget = sum([weights[i] for i in candidates]), rest
        for i in candidates:
            extra = min(most - given[i], max(1, budget * weights[i] // pool), rest)
            given[i] = given[i] + extra
            rest = rest - extra
    return np.array(given)


def bell_draw(key, extent, scale, limit, cuts=(), kind=jnp.bfloat16):
    array = jax.random.normal(key, extent, jnp.float32) * scale
    if len(cuts) > 0:
        array = level_of(key, extent, cuts, -0.22, 0.18) * array
    return jnp.clip(array, min=-limit, max=limit).astype(kind)


def setup_inputs(seed: int = 0) -> dict:
    streams_of = jax.random.split(jax.random.key(seed), 12)
    query = bell_draw(streams_of[0], (SEQUENCE_LENGTH, ATT), 1.0, 6.0, ((0, 4), (1, 8)))
    key_in = bell_draw(streams_of[1], (SEQUENCE_LENGTH, ATT), 1.0, 6.0, ((0, 4), (1, 8)))
    value = bell_draw(streams_of[2], (SEQUENCE_LENGTH, ATT), 1.0, 6.0, ((0, 4), (1, 8)))
    decay_log = draw_decay_log(jax.random.fold_in(streams_of[11], 71), 0)
    norm_gain = jnp.clip(1.0 + 0.18 * jax.random.normal(streams_of[4], (ATT,), jnp.float32), 0.099609375, 1.8984375).astype(jnp.bfloat16)
    w_out = bell_draw(streams_of[5], (ATT, DM), ATT ** -0.5, 0.1875, ((0, 8),))
    router = bell_draw(streams_of[6], (DM, EXPERTS), DM ** -0.5, 0.09375)
    routes_keys = jax.random.split(jax.random.fold_in(streams_of[7], 1), SEQUENCE_LENGTH // TOK_DEV)
    routes_turns = jax.random.permutation(jax.random.fold_in(streams_of[7], 3), SEQUENCE_LENGTH // TOK_DEV)
    routes = jax.vmap(lambda own, number: routed_block(jax.random.fold_in(streams_of[7], 2), own, number, TOK_DEV, EXPERTS, TOP, CAP, 2))(routes_keys, routes_turns).reshape((SEQUENCE_LENGTH, TOP))
    w_gate = bell_draw(streams_of[8], (SLICED, DM, FFW), DM ** -0.5, 0.09375, ((0, 8),))
    w_up = bell_draw(streams_of[9], (SLICED, DM, FFW), DM ** -0.5, 0.09375, ((0, 8),))
    w_down = bell_draw(streams_of[10], (SLICED, FFW, DM), (FFW * SLICES) ** -0.5, 0.25, ((0, 8),))
    return {"query": query, "key_in": key_in, "value": value, "decay_log": decay_log, "norm_gain": norm_gain, "w_out": w_out, "router": router, "routes": routes, "w_gate": w_gate, "w_up": w_up, "w_down": w_down}


def attend_block(state, block):
    query_blk, key_blk, value_blk, decay_blk = block
    query_f32 = query_blk.astype(jnp.float32)
    key_f32 = key_blk.astype(jnp.float32)
    value_f32 = value_blk.astype(jnp.float32)
    cumulative = jnp.cumsum(decay_blk, axis=0)
    scores = jnp.einsum('thd,shd->hts', query_f32, key_f32)
    spread = cumulative.T[:, :, None] - cumulative.T[:, None, :]
    causal = jnp.arange(TOK_DEV, dtype=jnp.int32)[:, None] >= jnp.arange(TOK_DEV, dtype=jnp.int32)[None, :]
    weights = jnp.where(causal, jnp.exp(jnp.where(causal, spread, 0.0)), 0.0)
    attend = (scores * weights / HEAD).astype(jnp.bfloat16)
    intra_part = jnp.einsum('hts,she->the', attend.astype(jnp.float32), value_f32)
    inter_part = jnp.exp(cumulative)[:, :, None] * jnp.einsum('thd,hde->the', query_f32, state, precision=lax.Precision.HIGHEST) / HEAD
    totals = cumulative[-1]
    tail_decay = jnp.exp(totals[None, :] - cumulative)
    state_delta = jnp.einsum('shd,she->hde', key_f32 * tail_decay[:, :, None], value_f32, precision=lax.Precision.HIGHEST)
    new_state = jnp.exp(totals)[:, None, None] * state + state_delta
    return (new_state, intra_part + inter_part)

def reference(query, key_in, value, decay_log, norm_gain, w_out, router, routes, w_gate, w_up, w_down):
    blocks = (query.reshape(N_SEQ, TOK_DEV, HEAD_TOTAL, HEAD), key_in.reshape(N_SEQ, TOK_DEV, HEAD_TOTAL, HEAD), value.reshape(N_SEQ, TOK_DEV, HEAD_TOTAL, HEAD), decay_log.reshape(N_SEQ, TOK_DEV, HEAD_TOTAL))
    start_state = jnp.zeros((HEAD_TOTAL, HEAD, HEAD), jnp.float32)
    _, attended = lax.scan(attend_block, start_state, blocks)
    attended = attended.reshape(SEQUENCE_LENGTH, HEAD_TOTAL, HEAD)
    inverse_rms = lax.rsqrt(lax.optimization_barrier(jnp.mean(attended * attended, axis=-1, keepdims=True)) + 1e-06)
    gain_f32 = norm_gain.astype(jnp.float32).reshape(HEAD_TOTAL, HEAD)
    normed = (attended * inverse_rms * gain_f32).astype(jnp.bfloat16).reshape(SEQUENCE_LENGTH, ATT)
    mixed = jnp.dot(normed, w_out, preferred_element_type=jnp.float32).astype(jnp.bfloat16)
    logits = jnp.dot(mixed, router, preferred_element_type=jnp.float32)
    picked = jnp.take_along_axis(logits, routes, axis=1)
    raised = jnp.exp(picked)
    gate_probs = raised / lax.optimization_barrier(jnp.sum(raised, axis=-1, keepdims=True))
    block_ids = routes.reshape(N_SEQ, TOK_DEV * TOP)
    onehot = (block_ids[:, :, None] == jnp.arange(EXPERTS, dtype=jnp.int32)[None, None, :]).astype(jnp.int32)
    earlier_hits = jnp.cumsum(onehot, axis=1) - onehot
    slot_index = lax.optimization_barrier(jnp.sum(earlier_hits * onehot, axis=-1))
    target = (jnp.arange(N_SEQ, dtype=jnp.int32)[:, None] * CAP + slot_index).reshape(-1).astype(jnp.int32)
    flat_ids = block_ids.reshape(-1).astype(jnp.int32)
    token_ids = (jnp.arange(SEQUENCE_LENGTH * TOP, dtype=jnp.int32) // TOP).astype(jnp.int32)
    slot_table = jnp.full((EXPERTS, N_SEQ * CAP), -1, jnp.int32).at[flat_ids, target].set(token_ids)
    gate_full = w_gate.reshape(EXPERTS, SLICES, DM, FFW).transpose(0, 2, 1, 3).reshape(EXPERTS, DM, SLICES * FFW)
    up_full = w_up.reshape(EXPERTS, SLICES, DM, FFW).transpose(0, 2, 1, 3).reshape(EXPERTS, DM, SLICES * FFW)
    down_full = w_down.reshape(EXPERTS, SLICES * FFW, DM)

    def expert_run(expert_cols):
        table_row, gate_w, up_w, down_w = expert_cols
        rows = mixed[jnp.maximum(table_row, 0)]
        gate_part = jnp.dot(rows, gate_w, preferred_element_type=jnp.float32)
        up_part = jnp.dot(rows, up_w, preferred_element_type=jnp.float32)
        hidden = (jax.nn.silu(gate_part) * up_part).astype(jnp.bfloat16)
        return jnp.dot(hidden, down_w, preferred_element_type=jnp.float32)
    expert_outs = lax.map(expert_run, (slot_table, gate_full, up_full, down_full))
    row_out = expert_outs[flat_ids, target].reshape(SEQUENCE_LENGTH, TOP, DM)
    combined = lax.optimization_barrier(jnp.sum(row_out * gate_probs[:, :, None], axis=1))
    return (mixed.astype(jnp.float32) + combined).astype(jnp.bfloat16)
```

```python
import functools

import jax
import jax.numpy as jnp
from jax import lax
from jax.experimental import pallas as pl
from jax.experimental.pallas import tpu as pltpu
from jax.sharding import PartitionSpec as P

F32 = jnp.float32
BF16 = jnp.bfloat16
TILE_ROWS = 16
COLUMNS = 512
VMEM_LIMIT = 40 * 1024 * 1024


def plain_plan(query, key_in, value, decay_log, norm_gain, w_out, router, routes, w_gate, w_up, w_down):
    tok_count = query.shape[0]
    head_count = decay_log.shape[1]
    head_size = query.shape[1] // head_count
    top_count = routes.shape[1]
    expert_count = router.shape[1]
    capacity = max(2, 3 * tok_count * top_count // (2 * expert_count))
    exp_count = lax.axis_size("exp")
    slice_count = exp_count // expert_count
    queries = query.reshape(tok_count, head_count, head_size)
    keys_local = key_in.reshape(tok_count, head_count, head_size)
    values_local = value.reshape(tok_count, head_count, head_size)
    cumulative = jnp.cumsum(decay_log, axis=0)
    scores = jnp.einsum("thd,shd->hts", queries, keys_local, preferred_element_type=jnp.float32)
    spread = cumulative.T[:, :, None] - cumulative.T[:, None, :]
    causal = jnp.arange(tok_count)[:, None] >= jnp.arange(tok_count)[None, :]
    weights = jnp.where(causal, jnp.exp(jnp.where(causal, spread, 0.0)), 0.0)
    attend = (scores * weights / head_size).astype(jnp.bfloat16)
    intra_part = jnp.einsum(
        "hts,she->the", attend, values_local, preferred_element_type=jnp.float32
    )
    totals = cumulative[-1]
    tail_decay = jnp.exp(totals[None, :] - cumulative)
    state_delta = jnp.einsum(
        "shd,she->hde",
        keys_local.astype(jnp.float32) * tail_decay[:, :, None],
        values_local.astype(jnp.float32),
        precision=lax.Precision.HIGHEST,
    )
    decay_rows = lax.all_gather(totals[None, :], "seq", axis=0, tiled=True)
    my_rank = lax.axis_index("seq")
    seq_ranks = jnp.arange(decay_rows.shape[0])
    state_piece = lax.all_gather(
        state_delta[None].astype(jnp.bfloat16), "seq", axis=0, tiled=True
    ).astype(jnp.float32)
    piece_rank = jnp.arange(state_piece.shape[0])
    between = (seq_ranks[None, :] > piece_rank[:, None]) & (seq_ranks[None, :] < my_rank)
    logsum = jnp.dot(between.astype(jnp.float32), decay_rows, precision=lax.Precision.HIGHEST)
    factor = jnp.where((piece_rank < my_rank)[:, None], jnp.exp(logsum), 0.0)
    incoming = jnp.zeros_like(state_delta) + jnp.einsum(
        "ih,ihde->hde", factor, state_piece, precision=lax.Precision.HIGHEST
    )
    inter_part = (
        jnp.exp(cumulative)[:, :, None]
        * jnp.einsum(
            "thd,hde->the", queries.astype(jnp.float32), incoming, precision=lax.Precision.HIGHEST
        )
        / head_size
    )
    attended = intra_part + inter_part
    inverse_rms = lax.rsqrt(jnp.mean(attended * attended, axis=-1, keepdims=True) + 1e-06)
    gain_f32 = norm_gain.astype(jnp.float32).reshape(head_count, head_size)
    normed = (
        (attended * inverse_rms * gain_f32)
        .astype(jnp.bfloat16)
        .reshape(tok_count, head_count * head_size)
    )
    own_mixed = lax.psum_scatter(
        jnp.dot(normed, w_out, preferred_element_type=jnp.float32),
        "exp",
        scatter_dimension=0,
        tiled=True,
    ).astype(jnp.bfloat16)
    mixed = lax.all_gather(own_mixed, "exp", axis=0, tiled=True)
    logits = jnp.dot(mixed, router, preferred_element_type=jnp.float32)
    member = routes[:, :, None] == jnp.arange(expert_count)[None, None, :]
    picked = jnp.sum(jnp.where(member, logits[:, None, :], 0.0), axis=-1)
    raised = jnp.exp(picked)
    gate_probs = raised / jnp.sum(raised, axis=-1, keepdims=True)
    my_expert = lax.axis_index("exp") // slice_count
    flat_hit = (routes.reshape(-1) == my_expert).astype(jnp.int32)
    slot_flat = jnp.cumsum(flat_hit) - flat_hit
    slot_match = (slot_flat[:, None] == jnp.arange(capacity)[None, :]) & (flat_hit[:, None] > 0)
    token_select = jnp.sum(
        slot_match.reshape(tok_count, top_count, capacity).astype(jnp.float32), axis=1
    )
    token_gate = jnp.sum(jnp.where(routes == my_expert, gate_probs, 0.0), axis=1)
    slot_rows = jnp.dot(
        token_select.astype(jnp.bfloat16).T, mixed, preferred_element_type=jnp.float32
    ).astype(jnp.bfloat16)
    gate_part = jnp.dot(slot_rows, w_gate[0], preferred_element_type=jnp.float32)
    up_part = jnp.dot(slot_rows, w_up[0], preferred_element_type=jnp.float32)
    hidden = (jax.nn.silu(gate_part) * up_part).astype(jnp.bfloat16)
    slice_out = jnp.dot(hidden, w_down[0], preferred_element_type=jnp.float32)
    spread_out = jnp.dot(token_select, slice_out, precision=lax.Precision.HIGHEST)
    summed = lax.psum_scatter(
        token_gate[:, None] * spread_out, "exp", scatter_dimension=0, tiled=True
    )
    return (own_mixed.astype(jnp.float32) + summed).astype(jnp.bfloat16)


def iota2(shape, axis):
    return lax.broadcasted_iota(jnp.int32, shape, axis)


def cumulate(decay_row):
    t = decay_row.shape[1]
    row, col = iota2((t, t), 0), iota2((t, t), 1)
    spread = jnp.broadcast_to(decay_row, (t, t))
    column = jnp.sum(jnp.where(col <= row, spread, 0.0), axis=1, keepdims=True)
    own = jnp.sum(jnp.where(col == row, spread, 0.0), axis=1, keepdims=True)
    line = jnp.sum(jnp.where(row <= col, own, 0.0), axis=0, keepdims=True)
    return column, line


def dot_f32(a, b, dims):
    return lax.dot_general(a, b, (dims, ((), ())), preferred_element_type=F32)


def split_dot(a_f32, b, dims):
    high = a_f32.astype(BF16)
    low = (a_f32 - high.astype(F32)).astype(BF16)
    return dot_f32(high, b, dims) + dot_f32(low, b, dims)


def state_kernel(key_ref, value_ref, decay_ref, out_ref):
    t, d = key_ref.shape
    column, _ = cumulate(decay_ref[...])
    total = column[t - 1 :, :]
    keyed = key_ref[...].astype(F32) * jnp.exp(total - column)
    state = split_dot(keyed, value_ref[...], ((0,), (0,)))
    out_ref[0:d, :] = state.astype(BF16)
    wide = jnp.broadcast_to(total, (TILE_ROWS, d))
    part0 = wide.astype(BF16).astype(F32)
    part1 = (wide - part0).astype(BF16).astype(F32)
    part2 = wide - part0 - part1
    row = iota2((TILE_ROWS, d), 0)
    parts = jnp.where(row == 0, part0, jnp.where(row == 1, part1, jnp.where(row == 2, part2, 0.0)))
    out_ref[d:, :] = parts.astype(BF16)


def place_matrix(rows, sign, n_pair, pair, core):
    size = 2 * n_pair * rows
    i, j = iota2((size, size), 0), iota2((size, size), 1)
    half, inner = i // (n_pair * rows), i % (n_pair * rows)
    step, row = inner // rows, inner % rows
    who = (pair + sign * step + n_pair) % n_pair
    source = (2 * who + (core + half) % 2) * rows + row
    return jnp.where(source == j, 1.0, 0.0).astype(BF16)


def project_kernel(n_pair, query_ref, key_ref, value_ref, decay_ref, gain_ref, *refs):
    states = refs[:-4]
    w_ref, mine_ref, theirs_ref, normed_ref = refs[-4:]
    t, d = query_ref.shape
    me = lax.axis_index("seq")
    exp_index = lax.axis_index("exp")
    column, line = cumulate(decay_ref[...])
    query, key, value = query_ref[...], key_ref[...], value_ref[...]
    scores = dot_f32(query, key, ((1,), (1,)))
    causal = iota2((t, t), 0) >= iota2((t, t), 1)
    weights = jnp.where(causal, jnp.exp(jnp.where(causal, column - line, 0.0)), 0.0)
    attend = (scores * weights * (1.0 / d)).astype(BF16)
    attended = dot_f32(attend, value, ((1,), (0,)))

    incoming = jnp.zeros((d, d), F32)
    logsum = jnp.zeros((1, d), F32)
    for k, state_ref in enumerate(states, start=1):
        factor = jnp.where(k <= me, jnp.exp(logsum), 0.0)
        incoming = incoming + factor * state_ref[0:d, :].astype(F32)
        logsum = logsum + jnp.sum(state_ref[d:, :].astype(F32), axis=0, keepdims=True)
    high = incoming.astype(BF16)
    low = (incoming - high.astype(F32)).astype(BF16)
    read = dot_f32(query, high, ((1,), (0,))) + dot_f32(query, low, ((1,), (0,)))
    attended = attended + jnp.exp(column) * read * (1.0 / d)

    inverse = lax.rsqrt(jnp.mean(attended * attended, axis=1, keepdims=True) + 1e-06)
    normed = (attended * inverse * gain_ref[...].astype(F32)).astype(BF16)
    place = place_matrix(t // (2 * n_pair), 1, n_pair, exp_index // 2, exp_index % 2)
    normed_ref[...] = dot_f32(place, normed, ((1,), (0,))).astype(BF16)

    width = w_ref.shape[1]

    def columns(i, _):
        at = pl.ds(pl.multiple_of(i * COLUMNS, COLUMNS), COLUMNS)
        part = dot_f32(normed_ref[...], w_ref[:, at], ((1,), (0,))).astype(BF16)
        mine_ref[:, at] = part[: t // 2]
        theirs_ref[:, at] = part[t // 2 :]
        return 0

    lax.fori_loop(0, width // COLUMNS, columns, 0)


def add_kernel(mine_ref, other_ref, own_ref, *out_refs):
    rows = own_ref.shape[0]
    for r, ref in enumerate((own_ref,) + out_refs):
        at = slice(r * rows, (r + 1) * rows)
        ref[...] = (mine_ref[at, :].astype(F32) + other_ref[at, :].astype(F32)).astype(ref.dtype)


def sum_kernel(*refs):
    total = refs[0][...].astype(F32)
    for ref in refs[1:-1]:
        total = total + ref[...].astype(F32)
    refs[-1][...] = total.astype(refs[-1].dtype)


def expert_kernel(n_pair, slices, *refs):
    blocks = refs[: 2 * n_pair]
    gate_ref, up_ref, down_ref, router_ref, routes_ref, mine_ref, theirs_ref, x_ref, hidden_ref = refs[2 * n_pair :]
    rows, width = blocks[0].shape
    t = 2 * n_pair * rows
    experts = router_ref.shape[0]
    exp_index = lax.axis_index("exp")
    my_expert = exp_index // slices
    for i, ref in enumerate(blocks):
        x_ref[i * rows : (i + 1) * rows, :] = ref[...]

    hits = jnp.zeros((experts, t), F32)
    for k in range(routes_ref.shape[0]):
        hits = hits + jnp.where(routes_ref[k : k + 1, :] == iota2((experts, t), 0), 1.0, 0.0)
    place = place_matrix(rows, -1, n_pair, exp_index // 2, exp_index % 2)
    member = dot_f32(place, hits.astype(BF16), ((1,), (1,)))

    hid = gate_ref.shape[1]

    def depth(i, carry):
        gate, up, logits = carry
        at = pl.ds(pl.multiple_of(i * COLUMNS, COLUMNS), COLUMNS)
        x = x_ref[:, at]
        return (
            gate + dot_f32(x, gate_ref[at, :], ((1,), (0,))),
            up + dot_f32(x, up_ref[at, :], ((1,), (0,))),
            logits + dot_f32(x, router_ref[:, at], ((1,), (1,))),
        )

    zero = jnp.zeros((t, hid), F32)
    gate, up, logits = lax.fori_loop(
        0, width // COLUMNS, depth, (zero, zero, jnp.zeros((t, experts), F32))
    )
    raised = jnp.where(member > 0.5, jnp.exp(logits), 0.0)
    chosen = jnp.sum(jnp.where(iota2((t, experts), 1) == my_expert, raised, 0.0), axis=1, keepdims=True)
    prob = chosen / jnp.sum(raised, axis=1, keepdims=True)
    hidden_ref[...] = (gate / (1.0 + jnp.exp(-gate)) * up).astype(BF16)

    def columns(i, _):
        at = pl.ds(pl.multiple_of(i * COLUMNS, COLUMNS), COLUMNS)
        part = (dot_f32(hidden_ref[...], down_ref[:, at], ((1,), (0,))) * prob).astype(BF16)
        mine_ref[:, at] = part[: t // 2]
        theirs_ref[:, at] = part[t // 2 :]
        return 0

    lax.fori_loop(0, width // COLUMNS, columns, 0)


def call(kernel, outs, args, scratch=(), flops=0):
    whole = pl.BlockSpec(memory_space=pltpu.VMEM)
    size = sum(a.size * a.dtype.itemsize for a in (*args, *outs))
    return pl.pallas_call(
        kernel,
        out_shape=outs,
        in_specs=[whole] * len(args),
        out_specs=[whole] * len(outs),
        scratch_shapes=list(scratch),
        compiler_params=pltpu.CompilerParams(vmem_limit_bytes=VMEM_LIMIT),
        cost_estimate=pl.CostEstimate(flops=flops, bytes_accessed=size, transcendentals=0),
    )(*args)


def local(query, key_in, value, decay_log, norm_gain, w_out, router, routes, w_gate, w_up, w_down):
    t, d = query.shape
    width = w_out.shape[1]
    exp_count, seq_count = lax.axis_size("exp"), lax.axis_size("seq")
    n_pair = exp_count // 2
    rows = t // exp_count
    experts = router.shape[1]
    hid = w_gate.shape[2]
    out = jax.ShapeDtypeStruct

    decay_row = decay_log.T
    (state,) = call(state_kernel, [out((d + TILE_ROWS, d), BF16)], (key_in, value, decay_row))
    states = [
        lax.ppermute(state, "seq", [(i, (i + k) % seq_count) for i in range(seq_count)])
        for k in range(1, seq_count)
    ]

    def along(x, shift):
        pairs = [
            (2 * p + c, 2 * ((p + shift) % n_pair) + c) for p in range(n_pair) for c in range(2)
        ]
        return lax.ppermute(x, "exp", pairs)

    def across(x):
        return lax.ppermute(x, "exp", [(e, e ^ 1) for e in range(exp_count)])

    half = out((t // 2, width), BF16)
    own = out((rows, width), F32)
    block = out((rows, width), BF16)

    def reduce(mine, theirs, sign):
        other = across(theirs)
        parts = call(add_kernel, [own] + [block] * (n_pair - 1), (mine, other))
        return [parts[0]] + [along(parts[r], sign * r) for r in range(1, n_pair)]

    mine, theirs = call(
        functools.partial(project_kernel, n_pair),
        [half, half],
        (query, key_in, value, decay_row, norm_gain[None, :], *states, w_out),
        [pltpu.VMEM((t, d), BF16)],
        2 * t * d * width,
    )
    (mixed,) = call(sum_kernel, [block], reduce(mine, theirs, 1))
    blocks = [mixed] + [along(mixed, r) for r in range(1, n_pair)]
    blocks = blocks + [across(b) for b in blocks]
    mine, theirs = call(
        functools.partial(expert_kernel, n_pair, exp_count // experts),
        [half, half],
        (*blocks, w_gate[0], w_up[0], w_down[0], router.T, routes.T),
        [pltpu.VMEM((t, width), BF16), pltpu.VMEM((t, hid), BF16)],
        6 * t * hid * width,
    )
    (result,) = call(sum_kernel, [block], [mixed] + reduce(mine, theirs, -1))
    return result


def solution(mesh):
    placed = (
        P("seq", "exp"),
        P("seq", "exp"),
        P("seq", "exp"),
        P("seq", "exp"),
        P("exp"),
        P("exp", None),
        P(),
        P("seq", None),
        P("exp", None, None),
        P("exp", None, None),
        P("exp", None, None),
    )

    def pick(query, key_in, value, decay_log, *rest):
        rows = query.shape[0] // lax.axis_size("exp")
        tiled = rows % TILE_ROWS == 0 and decay_log.shape[1] == 1 and lax.axis_size("exp") % 2 == 0
        plan = local if tiled else plain_plan
        return plan(query, key_in, value, decay_log, *rest)

    return jax.shard_map(
        pick, mesh=mesh, in_specs=placed, out_specs=P(("seq", "exp"), None), check_vma=False
    )
```

```python
import functools

import jax
import jax.numpy as jnp
from jax import lax
from jax.experimental import pallas as pl
from jax.experimental.pallas import tpu as pltpu
from jax.sharding import PartitionSpec as P

F32 = jnp.float32
BF16 = jnp.bfloat16
TILE_ROWS = 16
MIX_PARTS = 4
OUT_PARTS = 2
VMEM_LIMIT = 16 * 1024 * 1024


def plain_plan(query, key_in, value, decay_log, norm_gain, w_out, router, routes, w_gate, w_up, w_down):
    tok_count = query.shape[0]
    head_count = decay_log.shape[1]
    head_size = query.shape[1] // head_count
    top_count = routes.shape[1]
    expert_count = router.shape[1]
    capacity = max(2, 3 * tok_count * top_count // (2 * expert_count))
    exp_count = lax.axis_size("exp")
    slice_count = exp_count // expert_count
    queries = query.reshape(tok_count, head_count, head_size)
    keys_local = key_in.reshape(tok_count, head_count, head_size)
    values_local = value.reshape(tok_count, head_count, head_size)
    cumulative = jnp.cumsum(decay_log, axis=0)
    scores = jnp.einsum("thd,shd->hts", queries, keys_local, preferred_element_type=jnp.float32)
    spread = cumulative.T[:, :, None] - cumulative.T[:, None, :]
    causal = jnp.arange(tok_count)[:, None] >= jnp.arange(tok_count)[None, :]
    weights = jnp.where(causal, jnp.exp(jnp.where(causal, spread, 0.0)), 0.0)
    attend = (scores * weights / head_size).astype(jnp.bfloat16)
    intra_part = jnp.einsum(
        "hts,she->the", attend, values_local, preferred_element_type=jnp.float32
    )
    totals = cumulative[-1]
    tail_decay = jnp.exp(totals[None, :] - cumulative)
    state_delta = jnp.einsum(
        "shd,she->hde",
        keys_local.astype(jnp.float32) * tail_decay[:, :, None],
        values_local.astype(jnp.float32),
        precision=lax.Precision.HIGHEST,
    )
    decay_rows = lax.all_gather(totals[None, :], "seq", axis=0, tiled=True)
    my_rank = lax.axis_index("seq")
    seq_ranks = jnp.arange(decay_rows.shape[0])
    state_piece = lax.all_gather(
        state_delta[None].astype(jnp.bfloat16), "seq", axis=0, tiled=True
    ).astype(jnp.float32)
    piece_rank = jnp.arange(state_piece.shape[0])
    between = (seq_ranks[None, :] > piece_rank[:, None]) & (seq_ranks[None, :] < my_rank)
    logsum = jnp.dot(between.astype(jnp.float32), decay_rows, precision=lax.Precision.HIGHEST)
    factor = jnp.where((piece_rank < my_rank)[:, None], jnp.exp(logsum), 0.0)
    incoming = jnp.zeros_like(state_delta) + jnp.einsum(
        "ih,ihde->hde", factor, state_piece, precision=lax.Precision.HIGHEST
    )
    inter_part = (
        jnp.exp(cumulative)[:, :, None]
        * jnp.einsum(
            "thd,hde->the", queries.astype(jnp.float32), incoming, precision=lax.Precision.HIGHEST
        )
        / head_size
    )
    attended = intra_part + inter_part
    inverse_rms = lax.rsqrt(jnp.mean(attended * attended, axis=-1, keepdims=True) + 1e-06)
    gain_f32 = norm_gain.astype(jnp.float32).reshape(head_count, head_size)
    normed = (
        (attended * inverse_rms * gain_f32)
        .astype(jnp.bfloat16)
        .reshape(tok_count, head_count * head_size)
    )
    own_mixed = lax.psum_scatter(
        jnp.dot(normed, w_out, preferred_element_type=jnp.float32),
        "exp",
        scatter_dimension=0,
        tiled=True,
    ).astype(jnp.bfloat16)
    mixed = lax.all_gather(own_mixed, "exp", axis=0, tiled=True)
    logits = jnp.dot(mixed, router, preferred_element_type=jnp.float32)
    member = routes[:, :, None] == jnp.arange(expert_count)[None, None, :]
    picked = jnp.sum(jnp.where(member, logits[:, None, :], 0.0), axis=-1)
    raised = jnp.exp(picked)
    gate_probs = raised / jnp.sum(raised, axis=-1, keepdims=True)
    my_expert = lax.axis_index("exp") // slice_count
    flat_hit = (routes.reshape(-1) == my_expert).astype(jnp.int32)
    slot_flat = jnp.cumsum(flat_hit) - flat_hit
    slot_match = (slot_flat[:, None] == jnp.arange(capacity)[None, :]) & (flat_hit[:, None] > 0)
    token_select = jnp.sum(
        slot_match.reshape(tok_count, top_count, capacity).astype(jnp.float32), axis=1
    )
    token_gate = jnp.sum(jnp.where(routes == my_expert, gate_probs, 0.0), axis=1)
    slot_rows = jnp.dot(
        token_select.astype(jnp.bfloat16).T, mixed, preferred_element_type=jnp.float32
    ).astype(jnp.bfloat16)
    gate_part = jnp.dot(slot_rows, w_gate[0], preferred_element_type=jnp.float32)
    up_part = jnp.dot(slot_rows, w_up[0], preferred_element_type=jnp.float32)
    hidden = (jax.nn.silu(gate_part) * up_part).astype(jnp.bfloat16)
    slice_out = jnp.dot(hidden, w_down[0], preferred_element_type=jnp.float32)
    spread_out = jnp.dot(token_select, slice_out, precision=lax.Precision.HIGHEST)
    summed = lax.psum_scatter(
        token_gate[:, None] * spread_out, "exp", scatter_dimension=0, tiled=True
    )
    return (own_mixed.astype(jnp.float32) + summed).astype(jnp.bfloat16)


def iota2(shape, axis):
    return lax.broadcasted_iota(jnp.int32, shape, axis)


def cumulate(decay_row):
    t = decay_row.shape[1]
    row, col = iota2((t, t), 0), iota2((t, t), 1)
    spread = jnp.broadcast_to(decay_row, (t, t))
    column = jnp.sum(jnp.where(col <= row, spread, 0.0), axis=1, keepdims=True)
    own = jnp.sum(jnp.where(col == row, spread, 0.0), axis=1, keepdims=True)
    line = jnp.sum(jnp.where(row <= col, own, 0.0), axis=0, keepdims=True)
    return column, line


def dot_f32(a, b, dims):
    return lax.dot_general(a, b, (dims, ((), ())), preferred_element_type=F32)


def split_dot(a_f32, b, dims):
    high = a_f32.astype(BF16)
    low = (a_f32 - high.astype(F32)).astype(BF16)
    return dot_f32(high, b, dims) + dot_f32(low, b, dims)


def dma_in(sems, pairs):
    copies = [pltpu.make_async_copy(a, b, sems.at[i]) for i, (a, b) in enumerate(pairs)]
    for copy in copies:
        copy.start()
    return copies


def state_kernel(key_hbm, value_hbm, decay_hbm, out_ref, key_ref, value_ref, decay_ref, sems):
    t, d = key_ref.shape
    copies = dma_in(sems, [(decay_hbm, decay_ref), (key_hbm, key_ref), (value_hbm, value_ref)])
    for copy in copies:
        copy.wait()
    column, _ = cumulate(decay_ref[...])
    total = column[t - 1 :, :]
    keyed = key_ref[...].astype(F32) * jnp.exp(total - column)
    state = split_dot(keyed, value_ref[...], ((0,), (0,)))
    out_ref[0:d, :] = state.astype(BF16)
    wide = jnp.broadcast_to(total, (TILE_ROWS, d))
    part0 = wide.astype(BF16).astype(F32)
    part1 = (wide - part0).astype(BF16).astype(F32)
    part2 = wide - part0 - part1
    row = iota2((TILE_ROWS, d), 0)
    parts = jnp.where(row == 0, part0, jnp.where(row == 1, part1, jnp.where(row == 2, part2, 0.0)))
    out_ref[d:, :] = parts.astype(BF16)


def within_kernel(
    query_hbm, key_hbm, value_hbm, decay_hbm, gain_hbm, router_hbm, w_out_hbm, gate_hbm, up_hbm, down_hbm, _,
    intra_ref, grown_ref, query_ref, gain_ref, w_out_ref, in_ref, down_ref,
    key_ref, value_ref, decay_ref, gain_in_ref, router_ref, sems,
):
    t, d = query_ref.shape
    hid = gate_hbm.shape[0]
    copies = dma_in(
        sems,
        [
            (decay_hbm, decay_ref),
            (query_hbm, query_ref),
            (key_hbm, key_ref),
            (value_hbm, value_ref),
            (gain_hbm, gain_in_ref),
            (router_hbm, router_ref),
            (w_out_hbm, w_out_ref),
            (gate_hbm, in_ref.at[0:hid]),
            (up_hbm, in_ref.at[hid : 2 * hid]),
            (down_hbm, down_ref),
        ],
    )
    for copy in copies[:6]:
        copy.wait()
    column, line = cumulate(decay_ref[...])
    query, key, value = query_ref[...], key_ref[...], value_ref[...]
    scores = dot_f32(query, key, ((1,), (1,)))
    causal = iota2((t, t), 0) >= iota2((t, t), 1)
    weights = jnp.where(causal, jnp.exp(jnp.where(causal, column - line, 0.0)), 0.0)
    attend = (scores * weights * (1.0 / d)).astype(BF16)
    intra_ref[...] = dot_f32(attend, value, ((1,), (0,)))
    grown_ref[...] = jnp.broadcast_to(jnp.exp(column) * (1.0 / d), (t, d))
    gain_ref[...] = jnp.broadcast_to(gain_in_ref[...].astype(F32), gain_ref.shape)
    experts = router_ref.shape[0]
    in_ref[2 * hid :, :] = jnp.zeros((TILE_ROWS, in_ref.shape[1]), BF16)
    in_ref[2 * hid : 2 * hid + experts, :] = router_ref[...]
    for copy in copies[6:]:
        copy.wait()


def place_matrix(rows, n_pair, core):
    size = 2 * n_pair * rows
    i, j = iota2((size, size), 0), iota2((size, size), 1)
    half, inner = i // (n_pair * rows), i % (n_pair * rows)
    source = (2 * (inner // rows) + (core + half) % 2) * rows + inner % rows
    return jnp.where(source == j, 1.0, 0.0).astype(BF16)


def normed_kernel(n_pair, *refs):
    states = refs[:-5]
    intra_ref, grown_ref, query_ref, gain_ref, out_ref = refs[-5:]
    t, d = query_ref.shape
    me = lax.axis_index("seq")
    incoming = jnp.zeros((d, d), F32)
    logsum = jnp.zeros((1, d), F32)
    for k, state_ref in enumerate(states, start=1):
        factor = jnp.where(k <= me, jnp.exp(logsum), 0.0)
        incoming = incoming + factor * state_ref[0:d, :].astype(F32)
        logsum = logsum + jnp.sum(state_ref[d:, :].astype(F32), axis=0, keepdims=True)
    high = incoming.astype(BF16)
    low = (incoming - high.astype(F32)).astype(BF16)
    query = query_ref[...]
    read = dot_f32(query, high, ((1,), (0,))) + dot_f32(query, low, ((1,), (0,)))
    attended = intra_ref[...] + grown_ref[...] * read
    inverse = lax.rsqrt(jnp.mean(attended * attended, axis=1, keepdims=True) + 1e-06)
    normed = (attended * inverse * gain_ref[0:1, :]).astype(BF16)
    place = place_matrix(t // (2 * n_pair), n_pair, lax.axis_index("exp") % 2)
    out_ref[...] = dot_f32(place, normed, ((1,), (0,))).astype(BF16)


def project_kernel(at, normed_ref, w_ref, mine_ref, theirs_ref):
    half = mine_ref.shape[0]
    part = dot_f32(normed_ref[...], w_ref[:, at], ((1,), (0,))).astype(BF16)
    mine_ref[...] = part[:half]
    theirs_ref[...] = part[half:]


def add_kernel(a_ref, b_ref, out_ref):
    out_ref[...] = (a_ref[...].astype(F32) + b_ref[...].astype(F32)).astype(out_ref.dtype)


def choose_kernel(places, own_ref, other_ref, out_ref):
    pair = lax.axis_index("exp") // 2
    given = functools.reduce(jnp.logical_or, [pair == p for p in places])

    @pl.when(given)
    def _():
        out_ref[...] = other_ref[...]

    @pl.when(jnp.logical_not(given))
    def _():
        out_ref[...] = own_ref[...]


def enter_kernel(at, own_ref, other_ref, in_ref, *refs):
    x = jnp.concatenate([own_ref[...], other_ref[...]], axis=0)
    part = dot_f32(in_ref[:, at], x, ((1,), (1,)))
    if len(refs) == 2:
        part = part + refs[0][...]
    refs[-1][...] = part


def hidden_kernel(n_pair, slices, total_ref, routes_ref, out_ref):
    hid, t = out_ref.shape
    exp_index = lax.axis_index("exp")
    my_expert = exp_index // slices
    experts = lax.axis_size("exp") // slices
    hits = jnp.zeros((experts, t), F32)
    for k in range(routes_ref.shape[0]):
        hits = hits + jnp.where(routes_ref[k : k + 1, :] == iota2((experts, t), 0), 1.0, 0.0)
    place = place_matrix(t // (2 * n_pair), n_pair, exp_index % 2)
    member = dot_f32(hits.astype(BF16), place, ((1,), (1,)))
    raised = jnp.where(member > 0.5, jnp.exp(total_ref[2 * hid : 2 * hid + experts, :]), 0.0)
    chosen = jnp.sum(jnp.where(iota2((experts, t), 0) == my_expert, raised, 0.0), axis=0, keepdims=True)
    prob = chosen / jnp.sum(raised, axis=0, keepdims=True)
    gate, up = total_ref[0:hid, :], total_ref[hid : 2 * hid, :]
    out_ref[...] = (gate / (1.0 + jnp.exp(-gate)) * up * prob).astype(BF16)


def leave_kernel(at, hidden_ref, down_ref, mine_ref, theirs_ref):
    half = mine_ref.shape[0]
    part = dot_f32(hidden_ref[...], down_ref[:, at], ((0,), (0,))).astype(BF16)
    mine_ref[...] = part[:half]
    theirs_ref[...] = part[half:]


def relay_kernel(n_pair, step, sum_ref, *refs):
    right_ref, left_ref = refs[-2:]
    rows = right_ref.shape[0]
    pair = lax.axis_index("exp") // 2
    to_right = jnp.clip(n_pair - step + pair, 0, n_pair - 1)
    to_left = jnp.clip(step - n_pair + pair, 0, n_pair - 1)
    for n, (place, ref) in enumerate(((to_right, right_ref), (to_left, left_ref))):
        part = sum_ref[pl.ds(pl.multiple_of(place * rows, rows), rows), :]
        if len(refs) > 2:
            part = (part.astype(F32) + refs[n][...].astype(F32)).astype(BF16)
        ref[...] = part


def result_kernel(counts, *refs):
    out_ref = refs[-1]
    rows = out_ref.shape[0]
    own = pl.ds(pl.multiple_of(lax.axis_index("exp") // 2 * rows, rows), rows)
    n_mixed, n_sum = counts
    mixed, sums = refs[:n_mixed], refs[n_mixed : n_mixed + 3 * n_sum]
    wide, narrow = sums[0].shape[1], mixed[0].shape[1]
    for i in range(n_sum):
        total = sums[3 * i][own, :].astype(F32)
        total = total + sums[3 * i + 1][...].astype(F32) + sums[3 * i + 2][...].astype(F32)
        for j in range(wide // narrow):
            at = slice(j * narrow, (j + 1) * narrow)
            full = total[:, at] + mixed[i * (wide // narrow) + j][own, :].astype(F32)
            out_ref[:, i * wide + j * narrow : i * wide + (j + 1) * narrow] = full.astype(BF16)


def call(kernel, outs, args, scratch=(), flops=0, far=0):
    whole = pl.BlockSpec(memory_space=pltpu.VMEM)
    size = sum(a.size * a.dtype.itemsize for a in (*args, *outs))
    if far:
        args = [pltpu.with_memory_space_constraint(a, pltpu.HBM) for a in args[:far]] + list(args[far:])
    return pl.pallas_call(
        kernel,
        out_shape=outs,
        in_specs=[pl.BlockSpec(memory_space=pltpu.HBM) if far else whole] * len(args),
        out_specs=[whole] * len(outs),
        scratch_shapes=list(scratch),
        compiler_params=pltpu.CompilerParams(vmem_limit_bytes=VMEM_LIMIT),
        cost_estimate=pl.CostEstimate(flops=flops, bytes_accessed=size, transcendentals=0),
    )(*args)


def local(query, key_in, value, decay_log, norm_gain, w_out, router, routes, w_gate, w_up, w_down):
    t, d = query.shape
    width = w_out.shape[1]
    exp_count, seq_count = lax.axis_size("exp"), lax.axis_size("seq")
    n_pair = exp_count // 2
    rows = t // exp_count
    experts = router.shape[1]
    slices = exp_count // experts
    hid = w_gate.shape[2]
    out = jax.ShapeDtypeStruct
    dma = pltpu.SemaphoreType.DMA

    def line(x, moves):
        pairs = [(2 * a + c, 2 * b + c) for a, b in moves for c in range(2)]
        return lax.ppermute(x, "exp", pairs)

    def across(x):
        return lax.ppermute(x, "exp", [(e, e ^ 1) for e in range(exp_count)])

    def add(a, b):
        return call(add_kernel, [out(a.shape, BF16)], (a, b))[0]

    decay_row = decay_log.T
    block = pltpu.VMEM((t, d), BF16)
    decay_block = pltpu.VMEM((1, t), F32)
    (state,) = call(
        state_kernel,
        [out((d + TILE_ROWS, d), BF16)],
        (key_in, value, decay_row),
        [block, block, decay_block, dma((3,))],
        far=3,
    )
    states = [
        lax.ppermute(state, "seq", [(i, (i + k) % seq_count) for i in range(seq_count)])
        for k in range(1, seq_count)
    ]
    intra, grown, query_near, gain, w_out_near, w_in, w_down_near = call(
        within_kernel,
        [
            out((t, d), F32),
            out((t, d), F32),
            out((t, d), BF16),
            out((8, d), F32),
            out(w_out.shape, BF16),
            out((2 * hid + TILE_ROWS, width), BF16),
            out((hid, width), BF16),
        ],
        (query, key_in, value, decay_row, norm_gain[None, :], router.T, w_out, w_gate[0].T, w_up[0].T, w_down[0], state),
        [block, block, decay_block, pltpu.VMEM((1, d), BF16), pltpu.VMEM((experts, width), BF16), dma((10,))],
        far=10,
    )
    (normed,) = call(
        functools.partial(normed_kernel, n_pair),
        [out((t, d), BF16)],
        (*states, intra, grown, query_near, gain),
    )

    mixed = []
    total = None
    size = width // MIX_PARTS
    half = out((t // 2, size), BF16)
    for i in range(MIX_PARTS):
        at = slice(i * size, (i + 1) * size)
        mine, theirs = call(
            functools.partial(project_kernel, at), [half, half], (normed, w_out_near), flops=2 * t * d * size
        )
        part = add(mine, across(theirs))
        for j in range(1, n_pair // 2):
            part = add(part, line(part, [(j - 1, j), (n_pair - j, n_pair - 1 - j)]))
        left, right = n_pair // 2 - 1, n_pair // 2
        part = add(part, line(part, [(left, right), (right, left)]))
        for j in reversed(range(1, n_pair // 2)):
            moved = line(part, [(j, j - 1), (n_pair - 1 - j, n_pair - j)])
            (part,) = call(functools.partial(choose_kernel, (j - 1, n_pair - j)), [half], (part, moved))
        mixed.append(part)
        before = () if total is None else (total,)
        (total,) = call(
            functools.partial(enter_kernel, at),
            [out((2 * hid + TILE_ROWS, t), F32)],
            (part, across(part), w_in, *before),
            flops=4 * t * hid * size,
        )

    (hidden,) = call(
        functools.partial(hidden_kernel, n_pair, slices), [out((hid, t), BF16)], (total, routes.T)
    )
    sums = []
    size = width // OUT_PARTS
    half = out((t // 2, size), BF16)
    block = out((rows, size), BF16)
    for i in range(OUT_PARTS):
        at = slice(i * size, (i + 1) * size)
        mine, theirs = call(
            functools.partial(leave_kernel, at), [half, half], (hidden, w_down_near), flops=2 * t * hid * size
        )
        part = add(mine, across(theirs))
        moved = ()
        for step in range(1, n_pair):
            right, left = call(
                functools.partial(relay_kernel, n_pair, step), [block, block], (part, *moved)
            )
            moved = (
                line(right, [(z, z + 1) for z in range(step)]),
                line(left, [(n_pair - 1 - z, n_pair - 2 - z) for z in range(step)]),
            )
        sums += [part, *moved]
    (result,) = call(
        functools.partial(result_kernel, (len(mixed), OUT_PARTS)), [out((rows, width), BF16)], (*mixed, *sums)
    )
    return result


def solution(mesh):
    placed = (
        P("seq", "exp"),
        P("seq", "exp"),
        P("seq", "exp"),
        P("seq", "exp"),
        P("exp"),
        P("exp", None),
        P(),
        P("seq", None),
        P("exp", None, None),
        P("exp", None, None),
        P("exp", None, None),
    )

    def pick(query, key_in, value, decay_log, *rest):
        rows = query.shape[0] // lax.axis_size("exp")
        tiled = rows % TILE_ROWS == 0 and decay_log.shape[1] == 1 and lax.axis_size("exp") % 4 == 0
        plan = local if tiled else plain_plan
        return plan(query, key_in, value, decay_log, *rest)

    return jax.shard_map(
        pick, mesh=mesh, in_specs=placed, out_specs=P(("seq", "exp"), None), check_vma=False
    )
```

```python
import functools

import jax
import jax.numpy as jnp
from jax import lax
from jax.experimental import pallas as pl
from jax.experimental.pallas import tpu as pltpu
from jax.sharding import PartitionSpec as P

F32 = jnp.float32
BF16 = jnp.bfloat16
TILE_ROWS = 16
VMEM_LIMIT = 16 * 1024 * 1024


def plain_plan(query, key_in, value, decay_log, norm_gain, w_out, router, routes, w_gate, w_up, w_down):
    tok_count = query.shape[0]
    head_count = decay_log.shape[1]
    head_size = query.shape[1] // head_count
    top_count = routes.shape[1]
    expert_count = router.shape[1]
    capacity = max(2, 3 * tok_count * top_count // (2 * expert_count))
    exp_count = lax.axis_size("exp")
    slice_count = exp_count // expert_count
    queries = query.reshape(tok_count, head_count, head_size)
    keys_local = key_in.reshape(tok_count, head_count, head_size)
    values_local = value.reshape(tok_count, head_count, head_size)
    cumulative = jnp.cumsum(decay_log, axis=0)
    scores = jnp.einsum("thd,shd->hts", queries, keys_local, preferred_element_type=jnp.float32)
    spread = cumulative.T[:, :, None] - cumulative.T[:, None, :]
    causal = jnp.arange(tok_count)[:, None] >= jnp.arange(tok_count)[None, :]
    weights = jnp.where(causal, jnp.exp(jnp.where(causal, spread, 0.0)), 0.0)
    attend = (scores * weights / head_size).astype(jnp.bfloat16)
    intra_part = jnp.einsum(
        "hts,she->the", attend, values_local, preferred_element_type=jnp.float32
    )
    totals = cumulative[-1]
    tail_decay = jnp.exp(totals[None, :] - cumulative)
    state_delta = jnp.einsum(
        "shd,she->hde",
        keys_local.astype(jnp.float32) * tail_decay[:, :, None],
        values_local.astype(jnp.float32),
        precision=lax.Precision.HIGHEST,
    )
    decay_rows = lax.all_gather(totals[None, :], "seq", axis=0, tiled=True)
    my_rank = lax.axis_index("seq")
    seq_ranks = jnp.arange(decay_rows.shape[0])
    state_piece = lax.all_gather(
        state_delta[None].astype(jnp.bfloat16), "seq", axis=0, tiled=True
    ).astype(jnp.float32)
    piece_rank = jnp.arange(state_piece.shape[0])
    between = (seq_ranks[None, :] > piece_rank[:, None]) & (seq_ranks[None, :] < my_rank)
    logsum = jnp.dot(between.astype(jnp.float32), decay_rows, precision=lax.Precision.HIGHEST)
    factor = jnp.where((piece_rank < my_rank)[:, None], jnp.exp(logsum), 0.0)
    incoming = jnp.zeros_like(state_delta) + jnp.einsum(
        "ih,ihde->hde", factor, state_piece, precision=lax.Precision.HIGHEST
    )
    inter_part = (
        jnp.exp(cumulative)[:, :, None]
        * jnp.einsum(
            "thd,hde->the", queries.astype(jnp.float32), incoming, precision=lax.Precision.HIGHEST
        )
        / head_size
    )
    attended = intra_part + inter_part
    inverse_rms = lax.rsqrt(jnp.mean(attended * attended, axis=-1, keepdims=True) + 1e-06)
    gain_f32 = norm_gain.astype(jnp.float32).reshape(head_count, head_size)
    normed = (
        (attended * inverse_rms * gain_f32)
        .astype(jnp.bfloat16)
        .reshape(tok_count, head_count * head_size)
    )
    own_mixed = lax.psum_scatter(
        jnp.dot(normed, w_out, preferred_element_type=jnp.float32),
        "exp",
        scatter_dimension=0,
        tiled=True,
    ).astype(jnp.bfloat16)
    mixed = lax.all_gather(own_mixed, "exp", axis=0, tiled=True)
    logits = jnp.dot(mixed, router, preferred_element_type=jnp.float32)
    member = routes[:, :, None] == jnp.arange(expert_count)[None, None, :]
    picked = jnp.sum(jnp.where(member, logits[:, None, :], 0.0), axis=-1)
    raised = jnp.exp(picked)
    gate_probs = raised / jnp.sum(raised, axis=-1, keepdims=True)
    my_expert = lax.axis_index("exp") // slice_count
    flat_hit = (routes.reshape(-1) == my_expert).astype(jnp.int32)
    slot_flat = jnp.cumsum(flat_hit) - flat_hit
    slot_match = (slot_flat[:, None] == jnp.arange(capacity)[None, :]) & (flat_hit[:, None] > 0)
    token_select = jnp.sum(
        slot_match.reshape(tok_count, top_count, capacity).astype(jnp.float32), axis=1
    )
    token_gate = jnp.sum(jnp.where(routes == my_expert, gate_probs, 0.0), axis=1)
    slot_rows = jnp.dot(
        token_select.astype(jnp.bfloat16).T, mixed, preferred_element_type=jnp.float32
    ).astype(jnp.bfloat16)
    gate_part = jnp.dot(slot_rows, w_gate[0], preferred_element_type=jnp.float32)
    up_part = jnp.dot(slot_rows, w_up[0], preferred_element_type=jnp.float32)
    hidden = (jax.nn.silu(gate_part) * up_part).astype(jnp.bfloat16)
    slice_out = jnp.dot(hidden, w_down[0], preferred_element_type=jnp.float32)
    spread_out = jnp.dot(token_select, slice_out, precision=lax.Precision.HIGHEST)
    summed = lax.psum_scatter(
        token_gate[:, None] * spread_out, "exp", scatter_dimension=0, tiled=True
    )
    return (own_mixed.astype(jnp.float32) + summed).astype(jnp.bfloat16)


def iota2(shape, axis):
    return lax.broadcasted_iota(jnp.int32, shape, axis)


def cumulate(decay_row):
    t = decay_row.shape[1]
    row, col = iota2((t, t), 0), iota2((t, t), 1)
    spread = jnp.broadcast_to(decay_row, (t, t))
    column = jnp.sum(jnp.where(col <= row, spread, 0.0), axis=1, keepdims=True)
    own = jnp.sum(jnp.where(col == row, spread, 0.0), axis=1, keepdims=True)
    line = jnp.sum(jnp.where(row <= col, own, 0.0), axis=0, keepdims=True)
    return column, line


def dot_f32(a, b, dims):
    return lax.dot_general(a, b, (dims, ((), ())), preferred_element_type=F32)


def split_dot(a_f32, b, dims):
    high = a_f32.astype(BF16)
    low = (a_f32 - high.astype(F32)).astype(BF16)
    return dot_f32(high, b, dims) + dot_f32(low, b, dims)


def dma_in(sems, pairs):
    copies = [pltpu.make_async_copy(a, b, sems.at[i]) for i, (a, b) in enumerate(pairs)]
    for copy in copies:
        copy.start()
    return copies


def state_kernel(key_hbm, value_hbm, decay_hbm, out_ref, key_ref, value_ref, decay_ref, sems):
    t, d = key_ref.shape
    copies = dma_in(sems, [(decay_hbm, decay_ref), (key_hbm, key_ref), (value_hbm, value_ref)])
    for copy in copies:
        copy.wait()
    column, _ = cumulate(decay_ref[...])
    total = column[t - 1 :, :]
    keyed = key_ref[...].astype(F32) * jnp.exp(total - column)
    state = split_dot(keyed, value_ref[...], ((0,), (0,)))
    out_ref[0:d, :] = state.astype(BF16)
    wide = jnp.broadcast_to(total, (TILE_ROWS, d))
    part0 = wide.astype(BF16).astype(F32)
    part1 = (wide - part0).astype(BF16).astype(F32)
    part2 = wide - part0 - part1
    row = iota2((TILE_ROWS, d), 0)
    parts = jnp.where(row == 0, part0, jnp.where(row == 1, part1, jnp.where(row == 2, part2, 0.0)))
    out_ref[d:, :] = parts.astype(BF16)


def within_kernel(
    query_hbm, key_hbm, value_hbm, decay_hbm, gain_hbm, w_out_hbm, _,
    intra_ref, grown_ref, query_ref, gain_ref, w_out_ref,
    key_ref, value_ref, decay_ref, gain_in_ref, sems,
):
    t, d = query_ref.shape
    copies = dma_in(
        sems,
        [
            (decay_hbm, decay_ref),
            (query_hbm, query_ref),
            (key_hbm, key_ref),
            (value_hbm, value_ref),
            (gain_hbm, gain_in_ref),
            (w_out_hbm, w_out_ref),
        ],
    )
    for copy in copies[:5]:
        copy.wait()
    column, line = cumulate(decay_ref[...])
    query, key, value = query_ref[...], key_ref[...], value_ref[...]
    scores = dot_f32(query, key, ((1,), (1,)))
    causal = iota2((t, t), 0) >= iota2((t, t), 1)
    weights = jnp.where(causal, jnp.exp(jnp.where(causal, column - line, 0.0)), 0.0)
    attend = (scores * weights * (1.0 / d)).astype(BF16)
    intra_ref[...] = dot_f32(attend, value, ((1,), (0,)))
    grown_ref[...] = jnp.broadcast_to(jnp.exp(column) * (1.0 / d), (t, d))
    gain_ref[...] = jnp.broadcast_to(gain_in_ref[...].astype(F32), gain_ref.shape)
    copies[5].wait()


def fetch_kernel(router_hbm, gate_hbm, up_hbm, down_hbm, _, in_ref, down_ref, token_ref, router_ref, sems):
    hid = gate_hbm.shape[0]
    copies = dma_in(
        sems,
        [
            (router_hbm, router_ref),
            (gate_hbm, in_ref.at[0:hid]),
            (up_hbm, in_ref.at[hid : 2 * hid]),
            (down_hbm, down_ref),
        ],
    )
    copies[0].wait()
    experts = router_ref.shape[0]
    in_ref[2 * hid :, :] = jnp.zeros((TILE_ROWS, in_ref.shape[1]), BF16)
    in_ref[2 * hid : 2 * hid + experts, :] = router_ref[...]
    token_ref[...] = jnp.zeros(token_ref.shape, F32)
    for copy in copies[1:]:
        copy.wait()


def place_matrix(rows, n_pair, pair, core):
    size = 2 * n_pair * rows
    i, j = iota2((size, size), 0), iota2((size, size), 1)
    half, inner = i // (n_pair * rows), i % (n_pair * rows)
    who = jnp.bitwise_xor(inner // rows, pair)
    source = (2 * who + (core + half) % 2) * rows + inner % rows
    return jnp.where(source == j, 1.0, 0.0).astype(BF16)


def normed_kernel(n_pair, moves, *refs):
    states = refs[: len(moves)]
    intra_ref, grown_ref, query_ref, gain_ref, out_ref = refs[len(moves) :]
    t, d = query_ref.shape
    me, count = lax.axis_index("seq"), lax.axis_size("seq")
    ranks = [move(me) for move in moves]
    totals = [jnp.sum(ref[d:, :].astype(F32), axis=0, keepdims=True) for ref in states]
    incoming = jnp.zeros((d, d), F32)
    for rank, state_ref in zip(ranks, states):
        logsum = jnp.zeros((1, d), F32)
        for other, total in zip(ranks, totals):
            logsum = logsum + jnp.where(jnp.logical_and(rank < other, other < me), total, 0.0)
        factor = jnp.where(rank < me, jnp.exp(logsum), 0.0)
        incoming = incoming + factor * state_ref[0:d, :].astype(F32)
    high = incoming.astype(BF16)
    low = (incoming - high.astype(F32)).astype(BF16)
    query = query_ref[...]
    read = dot_f32(query, high, ((1,), (0,))) + dot_f32(query, low, ((1,), (0,)))
    attended = intra_ref[...] + grown_ref[...] * read
    inverse = lax.rsqrt(jnp.mean(attended * attended, axis=1, keepdims=True) + 1e-06)
    normed = (attended * inverse * gain_ref[0:1, :]).astype(BF16)
    exp_index = lax.axis_index("exp")
    place = place_matrix(t // (2 * n_pair), n_pair, exp_index // 2, exp_index % 2)
    out_ref[...] = dot_f32(place, normed, ((1,), (0,))).astype(BF16)


def project_kernel(at, normed_ref, w_ref, mine_ref, theirs_ref):
    half = mine_ref.shape[0]
    part = dot_f32(normed_ref[...], w_ref[:, at], ((1,), (0,))).astype(BF16)
    mine_ref[...] = part[:half]
    theirs_ref[...] = part[half:]


def add_kernel(groups, a_ref, b_ref, *refs):
    outs = refs[-len(groups) :]
    rows = outs[0].shape[0] // len(groups[0])
    for group, ref in zip(groups, outs):
        for i, block in enumerate(group):
            at = slice(block * rows, (block + 1) * rows)
            total = a_ref[at, :].astype(F32) + b_ref[at, :].astype(F32)
            ref[i * rows : (i + 1) * rows, :] = total.astype(ref.dtype)


def join_kernel(*refs):
    start = 0
    for ref in refs[:-1]:
        refs[-1][start : start + ref.shape[0], :] = ref[...]
        start += ref.shape[0]


def enter_kernel(at, order, rows, in_ref, *refs):
    n_parts = 2 * len({part for part, _ in order})
    parts, before = refs[:n_parts], refs[n_parts:-1]
    half = n_parts // 2
    blocks = [
        parts[core * half + part][i * rows : (i + 1) * rows, :] for core in range(2) for part, i in order
    ]
    total = dot_f32(in_ref[:, at], jnp.concatenate(blocks, axis=0), ((1,), (1,)))
    for ref in before:
        total = total + ref[...]
    refs[-1][...] = total


def hidden_kernel(n_pair, slices, total_ref, routes_ref, out_ref):
    hid, t = out_ref.shape
    exp_index = lax.axis_index("exp")
    my_expert = exp_index // slices
    experts = lax.axis_size("exp") // slices
    hits = jnp.zeros((experts, t), F32)
    for k in range(routes_ref.shape[0]):
        hits = hits + jnp.where(routes_ref[k : k + 1, :] == iota2((experts, t), 0), 1.0, 0.0)
    place = place_matrix(t // (2 * n_pair), n_pair, exp_index // 2, exp_index % 2)
    member = dot_f32(hits.astype(BF16), place, ((1,), (1,)))
    raised = jnp.where(member > 0.5, jnp.exp(total_ref[2 * hid : 2 * hid + experts, :]), 0.0)
    chosen = jnp.sum(jnp.where(iota2((experts, t), 0) == my_expert, raised, 0.0), axis=0, keepdims=True)
    prob = chosen / jnp.sum(raised, axis=0, keepdims=True)
    gate, up = total_ref[0:hid, :], total_ref[hid : 2 * hid, :]
    out_ref[...] = (gate / (1.0 + jnp.exp(-gate)) * up * prob).astype(BF16)


def leave_kernel(at, hidden_ref, down_ref, mine_ref, theirs_ref):
    half = mine_ref.shape[0]
    part = dot_f32(hidden_ref[...], down_ref[:, at], ((0,), (0,))).astype(BF16)
    mine_ref[...] = part[:half]
    theirs_ref[...] = part[half:]


def result_kernel(*refs):
    out_ref = refs[-1]
    width = refs[0].shape[1]
    for i in range(len(refs) // 3):
        kept, moved, mixed = refs[3 * i : 3 * i + 3]
        total = kept[...].astype(F32) + moved[...].astype(F32) + mixed[...].astype(F32)
        out_ref[:, i * width : (i + 1) * width] = total.astype(BF16)


def call(kernel, outs, args, scratch=(), flops=0, far=0):
    whole = pl.BlockSpec(memory_space=pltpu.VMEM)
    size = sum(a.size * a.dtype.itemsize for a in (*args, *outs))
    if far:
        args = [pltpu.with_memory_space_constraint(a, pltpu.HBM) for a in args[:far]] + list(args[far:])
    return pl.pallas_call(
        kernel,
        out_shape=outs,
        in_specs=[pl.BlockSpec(memory_space=pl.ANY) if far else whole] * len(args),
        out_specs=[whole] * len(outs),
        scratch_shapes=list(scratch),
        compiler_params=pltpu.CompilerParams(vmem_limit_bytes=VMEM_LIMIT),
        cost_estimate=pl.CostEstimate(flops=flops, bytes_accessed=size, transcendentals=0),
    )(*args)


def local(query, key_in, value, decay_log, norm_gain, w_out, router, routes, w_gate, w_up, w_down):
    t, d = query.shape
    width = w_out.shape[1]
    exp_count, seq_count = lax.axis_size("exp"), lax.axis_size("seq")
    n_pair = exp_count // 2
    rows = t // exp_count
    experts = router.shape[1]
    slices = exp_count // experts
    hid = w_gate.shape[2]
    out = jax.ShapeDtypeStruct
    dma = pltpu.SemaphoreType.DMA

    def swap(x, bit):
        return lax.ppermute(x, "exp", [(e, e ^ (2 * bit)) for e in range(exp_count)])

    def across(x):
        return lax.ppermute(x, "exp", [(e, e ^ 1) for e in range(exp_count)])

    def deal(held, bit):
        stay = [i for i, r in enumerate(held) if not r & bit]
        return stay, [i for i, r in enumerate(held) if r & bit]

    def add(a, b, groups, dtype=BF16, after=()):
        outs = [out((len(group) * rows, a.shape[1]), dtype) for group in groups]
        return call(functools.partial(add_kernel, groups), outs, (a, b, *after))

    bits = [1 << i for i in range(n_pair.bit_length() - 1)]
    orders = [bits, bits[::-1]]
    size = width // len(orders)
    ranges = [slice(i * size, (i + 1) * size) for i in range(len(orders))]
    half = out((t // 2, size), BF16)

    def begin(mine, theirs, order):
        stay, go = deal(list(range(n_pair)), order[0])
        return [stay] + list(add(mine, across(theirs), [stay, go]))

    def proceed(held, kept, moved, bit, after=()):
        stay, go = deal(held, bit)
        return [[held[i] for i in stay]] + list(add(kept, moved, [stay, go], after=after))

    decay_row = decay_log.T
    block = pltpu.VMEM((t, d), BF16)
    decay_block = pltpu.VMEM((1, t), F32)
    (state,) = call(
        state_kernel,
        [out((d + TILE_ROWS, d), BF16)],
        (key_in, value, decay_row),
        [block, block, decay_block, dma((3,))],
        far=3,
    )
    if seq_count & (seq_count - 1):
        moves = [lambda i, k=k: (i + k) % seq_count for k in range(1, seq_count)]
    else:
        moves = [lambda i, k=k: i ^ k for k in range(1, seq_count)]
    states = [lax.ppermute(state, "seq", [(move(i), i) for i in range(seq_count)]) for move in moves]
    intra, grown, query_near, gain, w_out_near = call(
        within_kernel,
        [out((t, d), F32), out((t, d), F32), out((t, d), BF16), out((8, d), F32), out(w_out.shape, BF16)],
        (query, key_in, value, decay_row, norm_gain[None, :], w_out, state),
        [block, block, decay_block, pltpu.VMEM((1, d), BF16), dma((6,))],
        far=6,
    )
    (normed,) = call(
        functools.partial(normed_kernel, n_pair, moves),
        [out((t, d), BF16)],
        (*states, intra, grown, query_near, gain),
    )

    terms = [
        call(functools.partial(project_kernel, at), [half, half], (normed, w_out_near), flops=2 * t * d * size)
        for at in ranges
    ]
    terms = [begin(mine, theirs, order) for (mine, theirs), order in zip(terms, orders)]
    moved = [swap(go, order[0]) for (_, _, go), order in zip(terms, orders)]
    w_in, w_down_near, token = call(
        fetch_kernel,
        [out((2 * hid + TILE_ROWS, width), BF16), out((hid, width), BF16), out((8, 128), F32)],
        (router.T, w_gate[0].T, w_up[0].T, w_down[0], terms[-1][2]),
        [pltpu.VMEM((experts, width), BF16), dma((4,))],
        far=4,
    )
    for step in range(1, len(bits)):
        terms = [
            proceed(held, kept, came, order[step], (token,))
            for (held, kept, _), came, order in zip(terms, moved, orders)
        ]
        moved = [swap(go, order[step]) for (_, _, go), order in zip(terms, orders)]
    mixed = [add(kept, came, [[0]])[0] for (_, kept, _), came in zip(terms, moved)]

    held = [[0], [0]]
    parts = [[m] for m in mixed]
    others = [[], []]
    whole = mixed
    for step in range(len(bits)):
        moved = [swap(w, order[-1 - step]) for w, order in zip(whole, orders)]
        others = [o + [across(p[-1])] for o, p in zip(others, parts)]
        held = [h + [r ^ order[-1 - step] for r in h] for h, order in zip(held, orders)]
        parts = [p + [m] for p, m in zip(parts, moved)]
        if step + 1 < len(bits):
            whole = [
                call(join_kernel, [out((2 * w.shape[0], size), BF16)], (w, m))[0] for w, m in zip(whole, moved)
            ]
    others = [o + [across(p[-1])] for o, p in zip(others, parts)]

    total = ()
    for at, h, p, o in zip(ranges, held, parts, others):
        spots = [(n, i) for n, part in enumerate(p) for i in range(part.shape[0] // rows)]
        order = [spots[h.index(r)] for r in range(n_pair)]
        total = call(
            functools.partial(enter_kernel, at, order, rows),
            [out((2 * hid + TILE_ROWS, t), F32)],
            (w_in, *p, *o, *total),
            flops=4 * t * hid * size,
        )
    (hidden,) = call(
        functools.partial(hidden_kernel, n_pair, slices), [out((hid, t), BF16)], (*total, routes.T)
    )

    terms = [
        call(functools.partial(leave_kernel, at), [half, half], (hidden, w_down_near), flops=2 * t * hid * size)
        for at in ranges
    ]
    terms = [begin(mine, theirs, order) for (mine, theirs), order in zip(terms, orders)]
    for step in range(len(bits)):
        moved = [swap(go, order[step]) for (_, _, go), order in zip(terms, orders)]
        if step + 1 < len(bits):
            terms = [
                proceed(held, kept, came, order[step + 1])
                for (held, kept, _), came, order in zip(terms, moved, orders)
            ]
    args = [x for (_, kept, _), came, m in zip(terms, moved, mixed) for x in (kept, came, m)]
    (result,) = call(result_kernel, [out((rows, width), BF16)], args)
    return result


def solution(mesh):
    placed = (
        P("seq", "exp"),
        P("seq", "exp"),
        P("seq", "exp"),
        P("seq", "exp"),
        P("exp"),
        P("exp", None),
        P(),
        P("seq", None),
        P("exp", None, None),
        P("exp", None, None),
        P("exp", None, None),
    )

    def pick(query, key_in, value, decay_log, *rest):
        rows = query.shape[0] // lax.axis_size("exp")
        exp_count = lax.axis_size("exp")
        tiled = rows % TILE_ROWS == 0 and decay_log.shape[1] == 1
        tiled = tiled and exp_count >= 4 and exp_count & (exp_count - 1) == 0
        plan = local if tiled else plain_plan
        return plan(query, key_in, value, decay_log, *rest)

    return jax.shard_map(
        pick, mesh=mesh, in_specs=placed, out_specs=P(("seq", "exp"), None), check_vma=False
    )
```

```python
import functools

import jax
import jax.numpy as jnp
from jax import lax
from jax.experimental import pallas as pl
from jax.experimental.pallas import tpu as pltpu
from jax.sharding import PartitionSpec as P

F32 = jnp.float32
BF16 = jnp.bfloat16
TILE_ROWS = 16
COLUMNS = 1024
VMEM_LIMIT = 16 * 1024 * 1024


def plain_plan(query, key_in, value, decay_log, norm_gain, w_out, router, routes, w_gate, w_up, w_down):
    tok_count = query.shape[0]
    head_count = decay_log.shape[1]
    head_size = query.shape[1] // head_count
    top_count = routes.shape[1]
    expert_count = router.shape[1]
    capacity = max(2, 3 * tok_count * top_count // (2 * expert_count))
    exp_count = lax.axis_size("exp")
    slice_count = exp_count // expert_count
    queries = query.reshape(tok_count, head_count, head_size)
    keys_local = key_in.reshape(tok_count, head_count, head_size)
    values_local = value.reshape(tok_count, head_count, head_size)
    cumulative = jnp.cumsum(decay_log, axis=0)
    scores = jnp.einsum("thd,shd->hts", queries, keys_local, preferred_element_type=jnp.float32)
    spread = cumulative.T[:, :, None] - cumulative.T[:, None, :]
    causal = jnp.arange(tok_count)[:, None] >= jnp.arange(tok_count)[None, :]
    weights = jnp.where(causal, jnp.exp(jnp.where(causal, spread, 0.0)), 0.0)
    attend = (scores * weights / head_size).astype(jnp.bfloat16)
    intra_part = jnp.einsum(
        "hts,she->the", attend, values_local, preferred_element_type=jnp.float32
    )
    totals = cumulative[-1]
    tail_decay = jnp.exp(totals[None, :] - cumulative)
    state_delta = jnp.einsum(
        "shd,she->hde",
        keys_local.astype(jnp.float32) * tail_decay[:, :, None],
        values_local.astype(jnp.float32),
        precision=lax.Precision.HIGHEST,
    )
    decay_rows = lax.all_gather(totals[None, :], "seq", axis=0, tiled=True)
    my_rank = lax.axis_index("seq")
    seq_ranks = jnp.arange(decay_rows.shape[0])
    state_piece = lax.all_gather(
        state_delta[None].astype(jnp.bfloat16), "seq", axis=0, tiled=True
    ).astype(jnp.float32)
    piece_rank = jnp.arange(state_piece.shape[0])
    between = (seq_ranks[None, :] > piece_rank[:, None]) & (seq_ranks[None, :] < my_rank)
    logsum = jnp.dot(between.astype(jnp.float32), decay_rows, precision=lax.Precision.HIGHEST)
    factor = jnp.where((piece_rank < my_rank)[:, None], jnp.exp(logsum), 0.0)
    incoming = jnp.zeros_like(state_delta) + jnp.einsum(
        "ih,ihde->hde", factor, state_piece, precision=lax.Precision.HIGHEST
    )
    inter_part = (
        jnp.exp(cumulative)[:, :, None]
        * jnp.einsum(
            "thd,hde->the", queries.astype(jnp.float32), incoming, precision=lax.Precision.HIGHEST
        )
        / head_size
    )
    attended = intra_part + inter_part
    inverse_rms = lax.rsqrt(jnp.mean(attended * attended, axis=-1, keepdims=True) + 1e-06)
    gain_f32 = norm_gain.astype(jnp.float32).reshape(head_count, head_size)
    normed = (
        (attended * inverse_rms * gain_f32)
        .astype(jnp.bfloat16)
        .reshape(tok_count, head_count * head_size)
    )
    own_mixed = lax.psum_scatter(
        jnp.dot(normed, w_out, preferred_element_type=jnp.float32),
        "exp",
        scatter_dimension=0,
        tiled=True,
    ).astype(jnp.bfloat16)
    mixed = lax.all_gather(own_mixed, "exp", axis=0, tiled=True)
    logits = jnp.dot(mixed, router, preferred_element_type=jnp.float32)
    member = routes[:, :, None] == jnp.arange(expert_count)[None, None, :]
    picked = jnp.sum(jnp.where(member, logits[:, None, :], 0.0), axis=-1)
    raised = jnp.exp(picked)
    gate_probs = raised / jnp.sum(raised, axis=-1, keepdims=True)
    my_expert = lax.axis_index("exp") // slice_count
    flat_hit = (routes.reshape(-1) == my_expert).astype(jnp.int32)
    slot_flat = jnp.cumsum(flat_hit) - flat_hit
    slot_match = (slot_flat[:, None] == jnp.arange(capacity)[None, :]) & (flat_hit[:, None] > 0)
    token_select = jnp.sum(
        slot_match.reshape(tok_count, top_count, capacity).astype(jnp.float32), axis=1
    )
    token_gate = jnp.sum(jnp.where(routes == my_expert, gate_probs, 0.0), axis=1)
    slot_rows = jnp.dot(
        token_select.astype(jnp.bfloat16).T, mixed, preferred_element_type=jnp.float32
    ).astype(jnp.bfloat16)
    gate_part = jnp.dot(slot_rows, w_gate[0], preferred_element_type=jnp.float32)
    up_part = jnp.dot(slot_rows, w_up[0], preferred_element_type=jnp.float32)
    hidden = (jax.nn.silu(gate_part) * up_part).astype(jnp.bfloat16)
    slice_out = jnp.dot(hidden, w_down[0], preferred_element_type=jnp.float32)
    spread_out = jnp.dot(token_select, slice_out, precision=lax.Precision.HIGHEST)
    summed = lax.psum_scatter(
        token_gate[:, None] * spread_out, "exp", scatter_dimension=0, tiled=True
    )
    return (own_mixed.astype(jnp.float32) + summed).astype(jnp.bfloat16)


def iota2(shape, axis):
    return lax.broadcasted_iota(jnp.int32, shape, axis)


def cumulate(decay_row):
    t = decay_row.shape[1]
    row, col = iota2((t, t), 0), iota2((t, t), 1)
    spread = jnp.broadcast_to(decay_row, (t, t))
    column = jnp.sum(jnp.where(col <= row, spread, 0.0), axis=1, keepdims=True)
    own = jnp.sum(jnp.where(col == row, spread, 0.0), axis=1, keepdims=True)
    line = jnp.sum(jnp.where(row <= col, own, 0.0), axis=0, keepdims=True)
    return column, line


def dot_f32(a, b, dims):
    return lax.dot_general(a, b, (dims, ((), ())), preferred_element_type=F32)


def split_dot(a_f32, b, dims):
    high = a_f32.astype(BF16)
    low = (a_f32 - high.astype(F32)).astype(BF16)
    return dot_f32(high, b, dims) + dot_f32(low, b, dims)


def dma_in(sems, pairs):
    copies = [pltpu.make_async_copy(a, b, sems.at[i]) for i, (a, b) in enumerate(pairs)]
    for copy in copies:
        copy.start()
    return copies


def put_state(out_ref, state, total):
    d = state.shape[1]
    out_ref[0:d, :] = state.astype(BF16)
    wide = jnp.broadcast_to(total, (TILE_ROWS, d))
    part0 = wide.astype(BF16).astype(F32)
    part1 = (wide - part0).astype(BF16).astype(F32)
    part2 = wide - part0 - part1
    row = iota2((TILE_ROWS, d), 0)
    parts = jnp.where(row == 0, part0, jnp.where(row == 1, part1, jnp.where(row == 2, part2, 0.0)))
    out_ref[d:, :] = parts.astype(BF16)


def get_state(ref):
    d = ref.shape[1]
    return ref[0:d, :].astype(F32), jnp.sum(ref[d:, :].astype(F32), axis=0, keepdims=True)


def state_kernel(key_hbm, value_hbm, decay_hbm, out_ref, key_ref, value_ref, decay_ref, sems):
    t, d = key_ref.shape
    copies = dma_in(sems, [(decay_hbm, decay_ref), (key_hbm, key_ref), (value_hbm, value_ref)])
    for copy in copies:
        copy.wait()
    column, _ = cumulate(decay_ref[...])
    total = column[t - 1 :, :]
    keyed = key_ref[...].astype(F32) * jnp.exp(total - column)
    put_state(out_ref, split_dot(keyed, value_ref[...], ((0,), (0,))), jnp.broadcast_to(total, (1, d)))


def take_before(bit, other_ref, before):
    state, total = get_state(other_ref)
    incoming, log = before
    earlier = jnp.bitwise_and(lax.axis_index("seq"), bit) > 0
    grown = jnp.where(earlier, jnp.exp(log) * state, 0.0)
    more = jnp.where(earlier, total, 0.0)
    if incoming is None:
        return grown, more
    return incoming + grown, log + more


def merge_kernel(bit, mine_ref, other_ref, *refs):
    out_ref, incoming_ref, log_ref = refs[-3:]
    d = incoming_ref.shape[1]
    before = (None, jnp.zeros((1, d), F32)) if len(refs) == 3 else (refs[0][...], refs[1][0:1, :])
    incoming, log = take_before(bit, other_ref, before)
    incoming_ref[...] = incoming
    log_ref[...] = jnp.broadcast_to(log, log_ref.shape)
    mine, my_total = get_state(mine_ref)
    other, other_total = get_state(other_ref)
    earlier = jnp.bitwise_and(lax.axis_index("seq"), bit) > 0
    later_total = jnp.where(earlier, my_total, other_total)
    merged = jnp.exp(later_total) * jnp.where(earlier, other, mine) + jnp.where(earlier, mine, other)
    put_state(out_ref, merged, my_total + other_total)


def within_kernel(
    query_hbm, key_hbm, value_hbm, decay_hbm, gain_hbm, w_out_hbm, _,
    intra_ref, grown_ref, query_ref, gain_ref, w_out_ref,
    key_ref, value_ref, decay_ref, gain_in_ref, sems,
):
    t, d = query_ref.shape
    copies = dma_in(
        sems,
        [
            (decay_hbm, decay_ref),
            (query_hbm, query_ref),
            (key_hbm, key_ref),
            (value_hbm, value_ref),
            (gain_hbm, gain_in_ref),
            (w_out_hbm, w_out_ref),
        ],
    )
    for copy in copies[:5]:
        copy.wait()
    column, line = cumulate(decay_ref[...])
    query, key, value = query_ref[...], key_ref[...], value_ref[...]
    scores = dot_f32(query, key, ((1,), (1,)))
    causal = iota2((t, t), 0) >= iota2((t, t), 1)
    weights = jnp.where(causal, jnp.exp(jnp.where(causal, column - line, 0.0)), 0.0)
    attend = (scores * weights * (1.0 / d)).astype(BF16)
    intra_ref[...] = dot_f32(attend, value, ((1,), (0,)))
    grown_ref[...] = jnp.broadcast_to(jnp.exp(column) * (1.0 / d), (t, d))
    gain_ref[...] = jnp.broadcast_to(gain_in_ref[...].astype(F32), gain_ref.shape)
    copies[5].wait()


def places(step, core, n_pair):
    bits = n_pair.bit_length() - 1
    flipped = sum(((step >> i) & 1) << (bits - 1 - i) for i in range(bits))
    return step + core * (flipped - step)


def place_matrix(rows, n_pair, pair, core):
    size = 2 * n_pair * rows
    i, j = iota2((size, size), 0), iota2((size, size), 1)
    half, inner = i // (n_pair * rows), i % (n_pair * rows)
    whose = (core + half) % 2
    who = jnp.bitwise_xor(places(inner // rows, whose, n_pair), pair)
    source = (2 * who + whose) * rows + inner % rows
    return jnp.where(source == j, 1.0, 0.0).astype(BF16)


def fetch_kernel(
    n_pair, slices, router_hbm, routes_hbm, gate_hbm, up_hbm, down_hbm, _,
    in_ref, down_ref, member_ref, router_ref, routes_ref, sems,
):
    hid = gate_hbm.shape[0]
    copies = dma_in(
        sems,
        [
            (router_hbm, router_ref),
            (routes_hbm, routes_ref),
            (gate_hbm, in_ref.at[0:hid]),
            (up_hbm, in_ref.at[hid : 2 * hid]),
            (down_hbm, down_ref),
        ],
    )
    for copy in copies[:2]:
        copy.wait()
    experts, t = router_ref.shape[0], routes_ref.shape[1]
    in_ref[2 * hid :, :] = jnp.zeros((TILE_ROWS, in_ref.shape[1]), BF16)
    in_ref[2 * hid : 2 * hid + experts, :] = router_ref[...]
    padded = member_ref.shape[0]
    hits = jnp.zeros((padded, t), F32)
    for k in range(routes_ref.shape[0]):
        hits = hits + jnp.where(routes_ref[k : k + 1, :] == iota2((padded, t), 0), 1.0, 0.0)
    exp_index = lax.axis_index("exp")
    place = place_matrix(t // (2 * n_pair), n_pair, exp_index // 2, exp_index % 2)
    member_ref[...] = dot_f32(hits.astype(BF16), place, ((1,), (1,)))
    for copy in copies[2:]:
        copy.wait()


def project_kernel(
    n_pair, bit, other_ref, incoming_ref, log_ref, intra_ref, grown_ref, query_ref, gain_ref, w_ref, mine_ref, theirs_ref
):
    t, d = query_ref.shape
    incoming, _ = take_before(bit, other_ref, (incoming_ref[...], log_ref[0:1, :]))
    high = incoming.astype(BF16)
    low = (incoming - high.astype(F32)).astype(BF16)
    query = query_ref[...]
    read = dot_f32(query, high, ((1,), (0,))) + dot_f32(query, low, ((1,), (0,)))
    attended = intra_ref[...] + grown_ref[...] * read
    inverse = lax.rsqrt(jnp.mean(attended * attended, axis=1, keepdims=True) + 1e-06)
    normed = (attended * inverse * gain_ref[0:1, :]).astype(BF16)
    exp_index = lax.axis_index("exp")
    place = place_matrix(t // (2 * n_pair), n_pair, exp_index // 2, exp_index % 2)
    normed = dot_f32(place, normed, ((1,), (0,))).astype(BF16)
    for at in chunks(w_ref.shape[1]):
        part = dot_f32(normed, w_ref[:, at], ((1,), (0,))).astype(BF16)
        mine_ref[:, at] = part[: t // 2]
        theirs_ref[:, at] = part[t // 2 :]


def chunks(width):
    size = min(width, COLUMNS)
    return [slice(i, i + size) for i in range(0, width, size)]


def add_kernel(groups, a_ref, b_ref, *refs):
    outs = refs[-len(groups) :]
    rows = outs[0].shape[0] // len(groups[0])
    for group, ref in zip(groups, outs):
        for i, block in enumerate(group):
            at = slice(block * rows, (block + 1) * rows)
            total = a_ref[at, :].astype(F32) + b_ref[at, :].astype(F32)
            ref[i * rows : (i + 1) * rows, :] = total.astype(ref.dtype)


def join_kernel(*refs):
    start = 0
    for ref in refs[:-1]:
        refs[-1][start : start + ref.shape[0], :] = ref[...]
        start += ref.shape[0]


def expert_kernel(slices, experts, order, rows, in_ref, down_ref, member_ref, *refs):
    parts, (mine_ref, theirs_ref) = refs[:-2], refs[-2:]
    half = len(parts) // 2
    hid, width = down_ref.shape
    t = member_ref.shape[1]
    total = jnp.zeros((in_ref.shape[0], t), F32)
    for at in chunks(width):
        blocks = [
            parts[core * half + part][i * rows : (i + 1) * rows, at] for core in range(2) for part, i in order
        ]
        total = total + dot_f32(in_ref[:, at], jnp.concatenate(blocks, axis=0), ((1,), (1,)))
    gate, up, logits = total[0:hid], total[hid : 2 * hid], total[2 * hid : 2 * hid + experts]
    raised = jnp.where(member_ref[0:experts, :] > 0.5, jnp.exp(logits), 0.0)
    mine = iota2((experts, t), 0) == lax.axis_index("exp") // slices
    prob = jnp.sum(jnp.where(mine, raised, 0.0), axis=0, keepdims=True) / jnp.sum(raised, axis=0, keepdims=True)
    hidden = (gate / (1.0 + jnp.exp(-gate)) * up * prob).astype(BF16)
    for at in chunks(width):
        part = dot_f32(hidden, down_ref[:, at], ((0,), (0,))).astype(BF16)
        mine_ref[:, at] = part[: t // 2]
        theirs_ref[:, at] = part[t // 2 :]


def result_kernel(kept_ref, moved_ref, mixed_ref, out_ref):
    total = kept_ref[...].astype(F32) + moved_ref[...].astype(F32) + mixed_ref[...].astype(F32)
    out_ref[...] = total.astype(BF16)


def call(kernel, outs, args, scratch=(), flops=0, far=0):
    whole = pl.BlockSpec(memory_space=pltpu.VMEM)
    size = sum(a.size * a.dtype.itemsize for a in (*args, *outs))
    if far:
        args = [pltpu.with_memory_space_constraint(a, pltpu.HBM) for a in args[:far]] + list(args[far:])
    return pl.pallas_call(
        kernel,
        out_shape=outs,
        in_specs=[pl.BlockSpec(memory_space=pl.ANY) if far else whole] * len(args),
        out_specs=[whole] * len(outs),
        scratch_shapes=list(scratch),
        compiler_params=pltpu.CompilerParams(vmem_limit_bytes=VMEM_LIMIT),
        cost_estimate=pl.CostEstimate(flops=flops, bytes_accessed=size, transcendentals=0),
    )(*args)


def local(query, key_in, value, decay_log, norm_gain, w_out, router, routes, w_gate, w_up, w_down):
    t, d = query.shape
    width = w_out.shape[1]
    exp_count, seq_count = lax.axis_size("exp"), lax.axis_size("seq")
    n_pair = exp_count // 2
    rows = t // exp_count
    experts = router.shape[1]
    slices = exp_count // experts
    hid = w_gate.shape[2]
    out = jax.ShapeDtypeStruct
    dma = pltpu.SemaphoreType.DMA
    bits = [1 << i for i in range(n_pair.bit_length() - 1)]

    def swap(x, bit):
        flips = (2 * bit, 2 * places(bit, 1, n_pair))
        return lax.ppermute(x, "exp", [(e, e ^ flips[e % 2]) for e in range(exp_count)])

    def across(x):
        return lax.ppermute(x, "exp", [(e, e ^ 1) for e in range(exp_count)])

    def add(a, b, groups, after=()):
        outs = [out((len(group) * rows, width), BF16) for group in groups]
        return call(functools.partial(add_kernel, groups), outs, (a, b, *after))

    def deal(held, bit):
        return [[i for i, r in enumerate(held) if bool(r & bit) == gone] for gone in (False, True)]

    decay_row = decay_log.T
    block = pltpu.VMEM((t, d), BF16)
    decay_block = pltpu.VMEM((1, t), F32)
    group = out((d + TILE_ROWS, d), BF16)
    (state,) = call(
        state_kernel, [group], (key_in, value, decay_row), [block, block, decay_block, dma((3,))], far=3
    )

    def from_rank(x, bit):
        return lax.ppermute(x, "seq", [(i, i ^ bit) for i in range(seq_count)])

    seq_bits = [1 << i for i in range(seq_count.bit_length() - 1)]
    other = from_rank(state, seq_bits[0])
    intra, grown, query_near, gain, w_out_near = call(
        within_kernel,
        [out((t, d), F32), out((t, d), F32), out((t, d), BF16), out((8, d), F32), out(w_out.shape, BF16)],
        (query, key_in, value, decay_row, norm_gain[None, :], w_out, state),
        [block, block, decay_block, pltpu.VMEM((1, d), BF16), dma((6,))],
        far=6,
    )
    before = ()
    for bit, later in zip(seq_bits, seq_bits[1:]):
        state, *before = call(
            functools.partial(merge_kernel, bit), [group, out((d, d), F32), out((8, d), F32)], (state, other, *before)
        )
        other = from_rank(state, later)
    half = out((t // 2, width), BF16)
    mine, theirs = call(
        functools.partial(project_kernel, n_pair, seq_bits[-1]),
        [half, half],
        (other, *before, intra, grown, query_near, gain, w_out_near),
        flops=2 * t * d * width,
    )

    def reduce(mine, theirs, after):
        held = list(range(n_pair))
        kept, moved = mine, across(theirs)
        extra = ()
        for step, bit in enumerate(bits):
            groups = deal(held, bit)
            kept, go = add(kept, moved, groups, extra)
            held = [held[i] for i in groups[0]]
            moved = swap(go, bit)
            if step == 0:
                extra = after(go)
        return kept, moved

    near = []

    def fetch(go):
        near.extend(
            call(
                functools.partial(fetch_kernel, n_pair, slices),
                [out((2 * hid + TILE_ROWS, width), BF16), out((hid, width), BF16), out((-(-experts // 8) * 8, t), F32)],
                (router.T, routes.T, w_gate[0].T, w_up[0].T, w_down[0], go),
                [pltpu.VMEM((experts, width), BF16), pltpu.VMEM((routes.shape[1], t), jnp.int32), dma((5,))],
                far=5,
            )
        )
        return (near[2],)

    (mixed,) = add(*reduce(mine, theirs, fetch), [[0]])

    held = [0]
    whole = mixed
    for step, bit in enumerate(reversed(bits)):
        moved = swap(whole, bit)
        held = held + [r ^ bit for r in held]
        if step + 1 < len(bits):
            (whole,) = call(join_kernel, [out((2 * whole.shape[0], width), BF16)], (whole, moved))
    parts = [whole, moved]
    spots = [(n, i) for n, part in enumerate(parts) for i in range(part.shape[0] // rows)]
    order = [spots[held.index(r)] for r in range(n_pair)]
    mine, theirs = call(
        functools.partial(expert_kernel, slices, experts, order, rows),
        [half, half],
        (*near, *parts, *[across(part) for part in parts]),
        flops=6 * t * hid * width,
    )
    kept, moved = reduce(mine, theirs, lambda go: ())
    return call(result_kernel, [out((rows, width), BF16)], (kept, moved, mixed))[0]


def solution(mesh):
    placed = (
        P("seq", "exp"),
        P("seq", "exp"),
        P("seq", "exp"),
        P("seq", "exp"),
        P("exp"),
        P("exp", None),
        P(),
        P("seq", None),
        P("exp", None, None),
        P("exp", None, None),
        P("exp", None, None),
    )

    def pick(query, key_in, value, decay_log, *rest):
        rows = query.shape[0] // lax.axis_size("exp")
        exp_count = lax.axis_size("exp")
        tiled = rows % TILE_ROWS == 0 and decay_log.shape[1] == 1
        for count in (exp_count, lax.axis_size("seq")):
            tiled = tiled and count >= 4 and count & (count - 1) == 0
        plan = local if tiled else plain_plan
        return plan(query, key_in, value, decay_log, *rest)

    return jax.shard_map(
        pick, mesh=mesh, in_specs=placed, out_specs=P(("seq", "exp"), None), check_vma=False
    )
```

```python
import functools

import jax
import jax.numpy as jnp
from jax import lax
from jax.experimental import pallas as pl
from jax.experimental.pallas import tpu as pltpu
from jax.sharding import PartitionSpec as P

F32 = jnp.float32
BF16 = jnp.bfloat16
TILE_ROWS = 16
COLUMNS = 1024
VMEM_LIMIT = 16 * 1024 * 1024


def plain_plan(query, key_in, value, decay_log, norm_gain, w_out, router, routes, w_gate, w_up, w_down):
    tok_count = query.shape[0]
    head_count = decay_log.shape[1]
    head_size = query.shape[1] // head_count
    top_count = routes.shape[1]
    expert_count = router.shape[1]
    capacity = max(2, 3 * tok_count * top_count // (2 * expert_count))
    exp_count = lax.axis_size("exp")
    slice_count = exp_count // expert_count
    queries = query.reshape(tok_count, head_count, head_size)
    keys_local = key_in.reshape(tok_count, head_count, head_size)
    values_local = value.reshape(tok_count, head_count, head_size)
    cumulative = jnp.cumsum(decay_log, axis=0)
    scores = jnp.einsum("thd,shd->hts", queries, keys_local, preferred_element_type=jnp.float32)
    spread = cumulative.T[:, :, None] - cumulative.T[:, None, :]
    causal = jnp.arange(tok_count)[:, None] >= jnp.arange(tok_count)[None, :]
    weights = jnp.where(causal, jnp.exp(jnp.where(causal, spread, 0.0)), 0.0)
    attend = (scores * weights / head_size).astype(jnp.bfloat16)
    intra_part = jnp.einsum(
        "hts,she->the", attend, values_local, preferred_element_type=jnp.float32
    )
    totals = cumulative[-1]
    tail_decay = jnp.exp(totals[None, :] - cumulative)
    state_delta = jnp.einsum(
        "shd,she->hde",
        keys_local.astype(jnp.float32) * tail_decay[:, :, None],
        values_local.astype(jnp.float32),
        precision=lax.Precision.HIGHEST,
    )
    decay_rows = lax.all_gather(totals[None, :], "seq", axis=0, tiled=True)
    my_rank = lax.axis_index("seq")
    seq_ranks = jnp.arange(decay_rows.shape[0])
    state_piece = lax.all_gather(
        state_delta[None].astype(jnp.bfloat16), "seq", axis=0, tiled=True
    ).astype(jnp.float32)
    piece_rank = jnp.arange(state_piece.shape[0])
    between = (seq_ranks[None, :] > piece_rank[:, None]) & (seq_ranks[None, :] < my_rank)
    logsum = jnp.dot(between.astype(jnp.float32), decay_rows, precision=lax.Precision.HIGHEST)
    factor = jnp.where((piece_rank < my_rank)[:, None], jnp.exp(logsum), 0.0)
    incoming = jnp.zeros_like(state_delta) + jnp.einsum(
        "ih,ihde->hde", factor, state_piece, precision=lax.Precision.HIGHEST
    )
    inter_part = (
        jnp.exp(cumulative)[:, :, None]
        * jnp.einsum(
            "thd,hde->the", queries.astype(jnp.float32), incoming, precision=lax.Precision.HIGHEST
        )
        / head_size
    )
    attended = intra_part + inter_part
    inverse_rms = lax.rsqrt(jnp.mean(attended * attended, axis=-1, keepdims=True) + 1e-06)
    gain_f32 = norm_gain.astype(jnp.float32).reshape(head_count, head_size)
    normed = (
        (attended * inverse_rms * gain_f32)
        .astype(jnp.bfloat16)
        .reshape(tok_count, head_count * head_size)
    )
    own_mixed = lax.psum_scatter(
        jnp.dot(normed, w_out, preferred_element_type=jnp.float32),
        "exp",
        scatter_dimension=0,
        tiled=True,
    ).astype(jnp.bfloat16)
    mixed = lax.all_gather(own_mixed, "exp", axis=0, tiled=True)
    logits = jnp.dot(mixed, router, preferred_element_type=jnp.float32)
    member = routes[:, :, None] == jnp.arange(expert_count)[None, None, :]
    picked = jnp.sum(jnp.where(member, logits[:, None, :], 0.0), axis=-1)
    raised = jnp.exp(picked)
    gate_probs = raised / jnp.sum(raised, axis=-1, keepdims=True)
    my_expert = lax.axis_index("exp") // slice_count
    flat_hit = (routes.reshape(-1) == my_expert).astype(jnp.int32)
    slot_flat = jnp.cumsum(flat_hit) - flat_hit
    slot_match = (slot_flat[:, None] == jnp.arange(capacity)[None, :]) & (flat_hit[:, None] > 0)
    token_select = jnp.sum(
        slot_match.reshape(tok_count, top_count, capacity).astype(jnp.float32), axis=1
    )
    token_gate = jnp.sum(jnp.where(routes == my_expert, gate_probs, 0.0), axis=1)
    slot_rows = jnp.dot(
        token_select.astype(jnp.bfloat16).T, mixed, preferred_element_type=jnp.float32
    ).astype(jnp.bfloat16)
    gate_part = jnp.dot(slot_rows, w_gate[0], preferred_element_type=jnp.float32)
    up_part = jnp.dot(slot_rows, w_up[0], preferred_element_type=jnp.float32)
    hidden = (jax.nn.silu(gate_part) * up_part).astype(jnp.bfloat16)
    slice_out = jnp.dot(hidden, w_down[0], preferred_element_type=jnp.float32)
    spread_out = jnp.dot(token_select, slice_out, precision=lax.Precision.HIGHEST)
    summed = lax.psum_scatter(
        token_gate[:, None] * spread_out, "exp", scatter_dimension=0, tiled=True
    )
    return (own_mixed.astype(jnp.float32) + summed).astype(jnp.bfloat16)


def iota2(shape, axis):
    return lax.broadcasted_iota(jnp.int32, shape, axis)


def cumulate(decay_row):
    t = decay_row.shape[1]
    row, col = iota2((t, t), 0), iota2((t, t), 1)
    spread = jnp.broadcast_to(decay_row, (t, t))
    column = jnp.sum(jnp.where(col <= row, spread, 0.0), axis=1, keepdims=True)
    own = jnp.sum(jnp.where(col == row, spread, 0.0), axis=1, keepdims=True)
    line = jnp.sum(jnp.where(row <= col, own, 0.0), axis=0, keepdims=True)
    return column, line


def dot_f32(a, b, dims):
    return lax.dot_general(a, b, (dims, ((), ())), preferred_element_type=F32)


def split_dot(a_f32, b, dims):
    high = a_f32.astype(BF16)
    low = (a_f32 - high.astype(F32)).astype(BF16)
    return dot_f32(high, b, dims) + dot_f32(low, b, dims)


def dma_in(sems, pairs):
    copies = [pltpu.make_async_copy(a, b, sems.at[i]) for i, (a, b) in enumerate(pairs)]
    for copy in copies:
        copy.start()
    return copies


def put_state(out_ref, state, total):
    d = state.shape[1]
    out_ref[0:d, :] = state.astype(BF16)
    wide = jnp.broadcast_to(total, (TILE_ROWS, d))
    part0 = wide.astype(BF16).astype(F32)
    part1 = (wide - part0).astype(BF16).astype(F32)
    part2 = wide - part0 - part1
    row = iota2((TILE_ROWS, d), 0)
    parts = jnp.where(row == 0, part0, jnp.where(row == 1, part1, jnp.where(row == 2, part2, 0.0)))
    out_ref[d:, :] = parts.astype(BF16)


def get_state(ref):
    d = ref.shape[1]
    return ref[0:d, :].astype(F32), jnp.sum(ref[d:, :].astype(F32), axis=0, keepdims=True)


def state_kernel(key_hbm, value_hbm, decay_hbm, out_ref, key_ref, value_ref, decay_ref, sems):
    t, d = key_ref.shape
    copies = dma_in(sems, [(decay_hbm, decay_ref), (key_hbm, key_ref), (value_hbm, value_ref)])
    for copy in copies:
        copy.wait()
    column, _ = cumulate(decay_ref[...])
    total = column[t - 1 :, :]
    keyed = key_ref[...].astype(F32) * jnp.exp(total - column)
    put_state(out_ref, split_dot(keyed, value_ref[...], ((0,), (0,))), jnp.broadcast_to(total, (1, d)))


def within_kernel(
    query_hbm, key_hbm, value_hbm, decay_hbm, gain_hbm, w_out_hbm, _,
    intra_ref, grown_ref, query_ref, gain_ref, w_out_ref,
    key_ref, value_ref, decay_ref, gain_in_ref, sems,
):
    t, d = query_ref.shape
    copies = dma_in(
        sems,
        [
            (decay_hbm, decay_ref),
            (query_hbm, query_ref),
            (key_hbm, key_ref),
            (value_hbm, value_ref),
            (gain_hbm, gain_in_ref),
            (w_out_hbm, w_out_ref),
        ],
    )
    for copy in copies[:5]:
        copy.wait()
    column, line = cumulate(decay_ref[...])
    query, key, value = query_ref[...], key_ref[...], value_ref[...]
    scores = dot_f32(query, key, ((1,), (1,)))
    causal = iota2((t, t), 0) >= iota2((t, t), 1)
    weights = jnp.where(causal, jnp.exp(jnp.where(causal, column - line, 0.0)), 0.0)
    attend = (scores * weights * (1.0 / d)).astype(BF16)
    intra_ref[...] = dot_f32(attend, value, ((1,), (0,)))
    grown_ref[...] = jnp.broadcast_to(jnp.exp(column) * (1.0 / d), (t, d))
    gain_ref[...] = jnp.broadcast_to(gain_in_ref[...].astype(F32), gain_ref.shape)
    copies[5].wait()


def place_matrix(rows, n_pair, pair, core):
    size = 2 * n_pair * rows
    i, j = iota2((size, size), 0), iota2((size, size), 1)
    half, inner = i // (n_pair * rows), i % (n_pair * rows)
    who = jnp.bitwise_xor(inner // rows, pair)
    source = (2 * who + (core + half) % 2) * rows + inner % rows
    return jnp.where(source == j, 1.0, 0.0).astype(BF16)


def fetch_kernel(
    n_pair, groups, router_hbm, routes_hbm, gate_hbm, up_hbm, down_hbm, _, in_ref, down_ref, *refs
):
    member_refs, (router_ref, routes_ref, sems) = refs[:-3], refs[-3:]
    hid = gate_hbm.shape[0]
    copies = dma_in(
        sems,
        [
            (router_hbm, router_ref),
            (routes_hbm, routes_ref),
            (gate_hbm, in_ref.at[0:hid]),
            (up_hbm, in_ref.at[hid : 2 * hid]),
            (down_hbm, down_ref),
        ],
    )
    for copy in copies[:2]:
        copy.wait()
    experts, t = router_ref.shape[0], routes_ref.shape[1]
    rows = t // (2 * n_pair)
    in_ref[2 * hid :, :] = jnp.zeros((TILE_ROWS, in_ref.shape[1]), BF16)
    in_ref[2 * hid : 2 * hid + experts, :] = router_ref[...]
    padded = member_refs[0].shape[0]
    hits = jnp.zeros((padded, t), F32)
    for k in range(routes_ref.shape[0]):
        hits = hits + jnp.where(routes_ref[k : k + 1, :] == iota2((padded, t), 0), 1.0, 0.0)
    exp_index = lax.axis_index("exp")
    place = place_matrix(rows, n_pair, exp_index // 2, exp_index % 2)
    for group, ref in zip(groups, member_refs):
        blocks = [half * n_pair + r for half in range(2) for r in group]
        some = jnp.concatenate([place[b * rows : (b + 1) * rows] for b in blocks], axis=0)
        ref[...] = dot_f32(hits.astype(BF16), some, ((1,), (1,)))
    for copy in copies[2:]:
        copy.wait()


def project_kernel(n_pair, moves, *refs):
    states = refs[: len(moves)]
    intra_ref, grown_ref, query_ref, gain_ref, w_ref, mine_ref, theirs_ref = refs[len(moves) :]
    t, d = query_ref.shape
    me = lax.axis_index("seq")
    ranks = [move(me) for move in moves]
    parts = [get_state(ref) for ref in states]
    incoming = jnp.zeros((d, d), F32)
    for rank, (state, _) in zip(ranks, parts):
        logsum = jnp.zeros((1, d), F32)
        for other, (_, total) in zip(ranks, parts):
            logsum = logsum + jnp.where(jnp.logical_and(rank < other, other < me), total, 0.0)
        incoming = incoming + jnp.where(rank < me, jnp.exp(logsum), 0.0) * state
    high = incoming.astype(BF16)
    low = (incoming - high.astype(F32)).astype(BF16)
    query = query_ref[...]
    read = dot_f32(query, high, ((1,), (0,))) + dot_f32(query, low, ((1,), (0,)))
    attended = intra_ref[...] + grown_ref[...] * read
    inverse = lax.rsqrt(jnp.mean(attended * attended, axis=1, keepdims=True) + 1e-06)
    normed = (attended * inverse * gain_ref[0:1, :]).astype(BF16)
    exp_index = lax.axis_index("exp")
    place = place_matrix(t // (2 * n_pair), n_pair, exp_index // 2, exp_index % 2)
    normed = dot_f32(place, normed, ((1,), (0,))).astype(BF16)
    for at in chunks(w_ref.shape[1]):
        part = dot_f32(normed, w_ref[:, at], ((1,), (0,))).astype(BF16)
        mine_ref[:, at] = part[: t // 2]
        theirs_ref[:, at] = part[t // 2 :]


def chunks(width):
    size = min(width, COLUMNS)
    return [slice(i, i + size) for i in range(0, width, size)]


def add_kernel(groups, a_ref, b_ref, *refs):
    outs = refs[-len(groups) :]
    rows = outs[0].shape[0] // len(groups[0])
    for group, ref in zip(groups, outs):
        for i, block in enumerate(group):
            at = slice(block * rows, (block + 1) * rows)
            total = a_ref[at, :].astype(F32) + b_ref[at, :].astype(F32)
            ref[i * rows : (i + 1) * rows, :] = total.astype(ref.dtype)


def sum_kernel(count, *refs):
    total = refs[0][...].astype(F32)
    for ref in refs[1:count]:
        total = total + ref[...].astype(F32)
    refs[-1][...] = total.astype(BF16)


def expert_kernel(slices, experts, count, in_ref, down_ref, member_ref, *refs):
    parts, (mine_ref, theirs_ref) = refs[:count], refs[-2:]
    hid, width = down_ref.shape
    t = member_ref.shape[1]
    total = jnp.zeros((in_ref.shape[0], t), F32)
    for at in chunks(width):
        x = jnp.concatenate([part[:, at] for part in parts], axis=0)
        total = total + dot_f32(in_ref[:, at], x, ((1,), (1,)))
    gate, up, logits = total[0:hid], total[hid : 2 * hid], total[2 * hid : 2 * hid + experts]
    raised = jnp.where(member_ref[0:experts, :] > 0.5, jnp.exp(logits), 0.0)
    mine = iota2((experts, t), 0) == lax.axis_index("exp") // slices
    prob = jnp.sum(jnp.where(mine, raised, 0.0), axis=0, keepdims=True) / jnp.sum(raised, axis=0, keepdims=True)
    hidden = (gate / (1.0 + jnp.exp(-gate)) * up * prob).astype(BF16)
    for at in chunks(width):
        part = dot_f32(hidden, down_ref[:, at], ((0,), (0,))).astype(BF16)
        mine_ref[:, at] = part[: t // 2]
        theirs_ref[:, at] = part[t // 2 :]


def call(kernel, outs, args, scratch=(), flops=0, far=0):
    whole = pl.BlockSpec(memory_space=pltpu.VMEM)
    size = sum(a.size * a.dtype.itemsize for a in (*args, *outs))
    if far:
        args = [pltpu.with_memory_space_constraint(a, pltpu.HBM) for a in args[:far]] + list(args[far:])
    return pl.pallas_call(
        kernel,
        out_shape=outs,
        in_specs=[pl.BlockSpec(memory_space=pl.ANY) if far else whole] * len(args),
        out_specs=[whole] * len(outs),
        scratch_shapes=list(scratch),
        compiler_params=pltpu.CompilerParams(vmem_limit_bytes=VMEM_LIMIT),
        cost_estimate=pl.CostEstimate(flops=0, bytes_accessed=0, transcendentals=0),
    )(*args)


def local(query, key_in, value, decay_log, norm_gain, w_out, router, routes, w_gate, w_up, w_down):
    t, d = query.shape
    width = w_out.shape[1]
    exp_count, seq_count = lax.axis_size("exp"), lax.axis_size("seq")
    n_pair = exp_count // 2
    rows = t // exp_count
    experts = router.shape[1]
    slices = exp_count // experts
    hid = w_gate.shape[2]
    out = jax.ShapeDtypeStruct
    dma = pltpu.SemaphoreType.DMA

    def swap(x, r):
        return lax.ppermute(x, "exp", [(e, e ^ (2 * r)) for e in range(exp_count)])

    def across(x):
        return lax.ppermute(x, "exp", [(e, e ^ 1) for e in range(exp_count)])

    def rows_of(count):
        return out((count * rows, width), BF16)

    decay_row = decay_log.T
    block = pltpu.VMEM((t, d), BF16)
    decay_block = pltpu.VMEM((1, t), F32)
    (state,) = call(
        state_kernel,
        [out((d + TILE_ROWS, d), BF16)],
        (key_in, value, decay_row),
        [block, block, decay_block, dma((3,))],
        far=3,
    )
    moves = [lambda i, k=k: i ^ k for k in range(1, seq_count)]
    states = [lax.ppermute(state, "seq", [(move(i), i) for i in range(seq_count)]) for move in moves]
    intra, grown, query_near, gain, w_out_near = call(
        within_kernel,
        [out((t, d), F32), out((t, d), F32), out((t, d), BF16), out((8, d), F32), out(w_out.shape, BF16)],
        (query, key_in, value, decay_row, norm_gain[None, :], w_out, state),
        [block, block, decay_block, pltpu.VMEM((1, d), BF16), dma((6,))],
        far=6,
    )
    mine, theirs = call(
        functools.partial(project_kernel, n_pair, moves),
        [rows_of(n_pair), rows_of(n_pair)],
        (*states, intra, grown, query_near, gain, w_out_near),
        flops=2 * t * d * width,
    )
    terms = call(
        functools.partial(add_kernel, [[r] for r in range(n_pair)]),
        [rows_of(1)] * n_pair,
        (mine, across(theirs)),
    )
    moved = [swap(terms[r], r) for r in range(1, n_pair)]

    groups = [list(range(n_pair))]
    w_in, w_down_near, *members = call(
        functools.partial(fetch_kernel, n_pair, groups),
        [out((2 * hid + TILE_ROWS, width), BF16), out((hid, width), BF16)]
        + [out((-(-experts // 8) * 8, 2 * len(group) * rows), F32) for group in groups],
        (router.T, routes.T, w_gate[0].T, w_up[0].T, w_down[0], terms[1]),
        [pltpu.VMEM((experts, width), BF16), pltpu.VMEM((routes.shape[1], t), jnp.int32), dma((5,))],
        far=5,
    )
    (mixed,) = call(functools.partial(sum_kernel, n_pair), [rows_of(1)], (terms[0], *moved, members[0]))

    gathered = {0: mixed}
    for group in groups:
        for r in group:
            if r:
                gathered[r] = swap(mixed, r)
    sums = [mixed]
    mine, parts = None, ()
    for group, member in zip(groups, members):
        near = [gathered[r] for r in group]
        if parts:
            near = list(lax.optimization_barrier((*near, mine)))[:-1]
        mine, theirs = call(
            functools.partial(expert_kernel, slices, experts, 2 * len(group)),
            [rows_of(len(group))] * 2,
            (w_in, w_down_near, member, *near, *[across(x) for x in near], *parts),
            flops=6 * 2 * len(group) * rows * hid * width,
        )
        parts = call(
            functools.partial(add_kernel, [[i] for i in range(len(group))]),
            [rows_of(1)] * len(group),
            (mine, across(theirs)),
        )
        sums += [swap(part, r) if r else part for part, r in zip(parts, group)]
    return call(functools.partial(sum_kernel, len(sums)), [rows_of(1)], sums)[0]


def solution(mesh):
    placed = (
        P("seq", "exp"),
        P("seq", "exp"),
        P("seq", "exp"),
        P("seq", "exp"),
        P("exp"),
        P("exp", None),
        P(),
        P("seq", None),
        P("exp", None, None),
        P("exp", None, None),
        P("exp", None, None),
    )

    def pick(query, key_in, value, decay_log, *rest):
        rows = query.shape[0] // lax.axis_size("exp")
        exp_count = lax.axis_size("exp")
        tiled = rows % TILE_ROWS == 0 and decay_log.shape[1] == 1
        for count in (exp_count, lax.axis_size("seq")):
            tiled = tiled and count >= 4 and count & (count - 1) == 0
        plan = local if tiled else plain_plan
        return plan(query, key_in, value, decay_log, *rest)

    return jax.shard_map(
        pick, mesh=mesh, in_specs=placed, out_specs=P(("seq", "exp"), None), check_vma=False
    )
```

```python
import functools

import jax
import jax.numpy as jnp
from jax import lax
from jax.experimental import pallas as pl
from jax.experimental.pallas import tpu as pltpu
from jax.sharding import PartitionSpec as P

F32 = jnp.float32
BF16 = jnp.bfloat16
TILE_ROWS = 16
COLUMNS = 1024
VMEM_LIMIT = 16 * 1024 * 1024


def plain_plan(query, key_in, value, decay_log, norm_gain, w_out, router, routes, w_gate, w_up, w_down):
    tok_count = query.shape[0]
    head_count = decay_log.shape[1]
    head_size = query.shape[1] // head_count
    top_count = routes.shape[1]
    expert_count = router.shape[1]
    capacity = max(2, 3 * tok_count * top_count // (2 * expert_count))
    exp_count = lax.axis_size("exp")
    slice_count = exp_count // expert_count
    queries = query.reshape(tok_count, head_count, head_size)
    keys_local = key_in.reshape(tok_count, head_count, head_size)
    values_local = value.reshape(tok_count, head_count, head_size)
    cumulative = jnp.cumsum(decay_log, axis=0)
    scores = jnp.einsum("thd,shd->hts", queries, keys_local, preferred_element_type=jnp.float32)
    spread = cumulative.T[:, :, None] - cumulative.T[:, None, :]
    causal = jnp.arange(tok_count)[:, None] >= jnp.arange(tok_count)[None, :]
    weights = jnp.where(causal, jnp.exp(jnp.where(causal, spread, 0.0)), 0.0)
    attend = (scores * weights / head_size).astype(jnp.bfloat16)
    intra_part = jnp.einsum(
        "hts,she->the", attend, values_local, preferred_element_type=jnp.float32
    )
    totals = cumulative[-1]
    tail_decay = jnp.exp(totals[None, :] - cumulative)
    state_delta = jnp.einsum(
        "shd,she->hde",
        keys_local.astype(jnp.float32) * tail_decay[:, :, None],
        values_local.astype(jnp.float32),
        precision=lax.Precision.HIGHEST,
    )
    decay_rows = lax.all_gather(totals[None, :], "seq", axis=0, tiled=True)
    my_rank = lax.axis_index("seq")
    seq_ranks = jnp.arange(decay_rows.shape[0])
    state_piece = lax.all_gather(
        state_delta[None].astype(jnp.bfloat16), "seq", axis=0, tiled=True
    ).astype(jnp.float32)
    piece_rank = jnp.arange(state_piece.shape[0])
    between = (seq_ranks[None, :] > piece_rank[:, None]) & (seq_ranks[None, :] < my_rank)
    logsum = jnp.dot(between.astype(jnp.float32), decay_rows, precision=lax.Precision.HIGHEST)
    factor = jnp.where((piece_rank < my_rank)[:, None], jnp.exp(logsum), 0.0)
    incoming = jnp.zeros_like(state_delta) + jnp.einsum(
        "ih,ihde->hde", factor, state_piece, precision=lax.Precision.HIGHEST
    )
    inter_part = (
        jnp.exp(cumulative)[:, :, None]
        * jnp.einsum(
            "thd,hde->the", queries.astype(jnp.float32), incoming, precision=lax.Precision.HIGHEST
        )
        / head_size
    )
    attended = intra_part + inter_part
    inverse_rms = lax.rsqrt(jnp.mean(attended * attended, axis=-1, keepdims=True) + 1e-06)
    gain_f32 = norm_gain.astype(jnp.float32).reshape(head_count, head_size)
    normed = (
        (attended * inverse_rms * gain_f32)
        .astype(jnp.bfloat16)
        .reshape(tok_count, head_count * head_size)
    )
    own_mixed = lax.psum_scatter(
        jnp.dot(normed, w_out, preferred_element_type=jnp.float32),
        "exp",
        scatter_dimension=0,
        tiled=True,
    ).astype(jnp.bfloat16)
    mixed = lax.all_gather(own_mixed, "exp", axis=0, tiled=True)
    logits = jnp.dot(mixed, router, preferred_element_type=jnp.float32)
    member = routes[:, :, None] == jnp.arange(expert_count)[None, None, :]
    picked = jnp.sum(jnp.where(member, logits[:, None, :], 0.0), axis=-1)
    raised = jnp.exp(picked)
    gate_probs = raised / jnp.sum(raised, axis=-1, keepdims=True)
    my_expert = lax.axis_index("exp") // slice_count
    flat_hit = (routes.reshape(-1) == my_expert).astype(jnp.int32)
    slot_flat = jnp.cumsum(flat_hit) - flat_hit
    slot_match = (slot_flat[:, None] == jnp.arange(capacity)[None, :]) & (flat_hit[:, None] > 0)
    token_select = jnp.sum(
        slot_match.reshape(tok_count, top_count, capacity).astype(jnp.float32), axis=1
    )
    token_gate = jnp.sum(jnp.where(routes == my_expert, gate_probs, 0.0), axis=1)
    slot_rows = jnp.dot(
        token_select.astype(jnp.bfloat16).T, mixed, preferred_element_type=jnp.float32
    ).astype(jnp.bfloat16)
    gate_part = jnp.dot(slot_rows, w_gate[0], preferred_element_type=jnp.float32)
    up_part = jnp.dot(slot_rows, w_up[0], preferred_element_type=jnp.float32)
    hidden = (jax.nn.silu(gate_part) * up_part).astype(jnp.bfloat16)
    slice_out = jnp.dot(hidden, w_down[0], preferred_element_type=jnp.float32)
    spread_out = jnp.dot(token_select, slice_out, precision=lax.Precision.HIGHEST)
    summed = lax.psum_scatter(
        token_gate[:, None] * spread_out, "exp", scatter_dimension=0, tiled=True
    )
    return (own_mixed.astype(jnp.float32) + summed).astype(jnp.bfloat16)


def iota2(shape, axis):
    return lax.broadcasted_iota(jnp.int32, shape, axis)


def cumulate(decay_row):
    t = decay_row.shape[1]
    row, col = iota2((t, t), 0), iota2((t, t), 1)
    spread = jnp.broadcast_to(decay_row, (t, t))
    column = jnp.sum(jnp.where(col <= row, spread, 0.0), axis=1, keepdims=True)
    own = jnp.sum(jnp.where(col == row, spread, 0.0), axis=1, keepdims=True)
    line = jnp.sum(jnp.where(row <= col, own, 0.0), axis=0, keepdims=True)
    return column, line


def dot_f32(a, b, dims):
    return lax.dot_general(a, b, (dims, ((), ())), preferred_element_type=F32)


def split_dot(a_f32, b, dims):
    high = a_f32.astype(BF16)
    low = (a_f32 - high.astype(F32)).astype(BF16)
    return dot_f32(high, b, dims) + dot_f32(low, b, dims)


def dma_in(sems, pairs):
    copies = [pltpu.make_async_copy(a, b, sems.at[i]) for i, (a, b) in enumerate(pairs)]
    for copy in copies:
        copy.start()
    return copies


def put_state(out_ref, state, total):
    d = state.shape[1]
    out_ref[0:d, :] = state.astype(BF16)
    wide = jnp.broadcast_to(total, (TILE_ROWS, d))
    part0 = wide.astype(BF16).astype(F32)
    part1 = (wide - part0).astype(BF16).astype(F32)
    part2 = wide - part0 - part1
    row = iota2((TILE_ROWS, d), 0)
    parts = jnp.where(row == 0, part0, jnp.where(row == 1, part1, jnp.where(row == 2, part2, 0.0)))
    out_ref[d:, :] = parts.astype(BF16)


def get_state(ref):
    d = ref.shape[1]
    return ref[0:d, :].astype(F32), jnp.sum(ref[d:, :].astype(F32), axis=0, keepdims=True)


def state_kernel(key_hbm, value_hbm, decay_hbm, out_ref, key_ref, value_ref, decay_ref, sems):
    t, d = key_ref.shape
    copies = dma_in(sems, [(decay_hbm, decay_ref), (key_hbm, key_ref), (value_hbm, value_ref)])
    for copy in copies:
        copy.wait()
    column, _ = cumulate(decay_ref[...])
    total = column[t - 1 :, :]
    keyed = key_ref[...].astype(F32) * jnp.exp(total - column)
    put_state(out_ref, split_dot(keyed, value_ref[...], ((0,), (0,))), jnp.broadcast_to(total, (1, d)))


def within_kernel(
    query_hbm, key_hbm, value_hbm, decay_hbm, gain_hbm, w_out_hbm, _,
    intra_ref, grown_ref, query_ref, gain_ref, w_out_ref,
    key_ref, value_ref, decay_ref, gain_in_ref, sems,
):
    t, d = query_ref.shape
    copies = dma_in(
        sems,
        [
            (decay_hbm, decay_ref),
            (query_hbm, query_ref),
            (key_hbm, key_ref),
            (value_hbm, value_ref),
            (gain_hbm, gain_in_ref),
            (w_out_hbm, w_out_ref),
        ],
    )
    for copy in copies[:5]:
        copy.wait()
    column, line = cumulate(decay_ref[...])
    query, key, value = query_ref[...], key_ref[...], value_ref[...]
    scores = dot_f32(query, key, ((1,), (1,)))
    causal = iota2((t, t), 0) >= iota2((t, t), 1)
    weights = jnp.where(causal, jnp.exp(jnp.where(causal, column - line, 0.0)), 0.0)
    attend = (scores * weights * (1.0 / d)).astype(BF16)
    intra_ref[...] = dot_f32(attend, value, ((1,), (0,)))
    grown_ref[...] = jnp.broadcast_to(jnp.exp(column) * (1.0 / d), (t, d))
    gain_ref[...] = jnp.broadcast_to(gain_in_ref[...].astype(F32), gain_ref.shape)
    copies[5].wait()


def place_matrix(rows, n_pair, pair, core):
    size = 2 * n_pair * rows
    i, j = iota2((size, size), 0), iota2((size, size), 1)
    half, inner = i // (n_pair * rows), i % (n_pair * rows)
    who = (inner // rows + pair) % n_pair
    source = (2 * who + (core + half) % 2) * rows + inner % rows
    return jnp.where(source == j, 1.0, 0.0).astype(BF16)


def fetch_kernel(
    n_pair, groups, router_hbm, routes_hbm, gate_hbm, up_hbm, down_hbm, _, in_ref, down_ref, *refs
):
    member_refs, (router_ref, routes_ref, sems) = refs[:-3], refs[-3:]
    hid = gate_hbm.shape[0]
    copies = dma_in(
        sems,
        [
            (router_hbm, router_ref),
            (routes_hbm, routes_ref),
            (gate_hbm, in_ref.at[0:hid]),
            (up_hbm, in_ref.at[hid : 2 * hid]),
            (down_hbm, down_ref),
        ],
    )
    for copy in copies[:2]:
        copy.wait()
    experts, t = router_ref.shape[0], routes_ref.shape[1]
    rows = t // (2 * n_pair)
    in_ref[2 * hid :, :] = jnp.zeros((TILE_ROWS, in_ref.shape[1]), BF16)
    in_ref[2 * hid : 2 * hid + experts, :] = router_ref[...]
    padded = member_refs[0].shape[0]
    hits = jnp.zeros((padded, t), F32)
    for k in range(routes_ref.shape[0]):
        hits = hits + jnp.where(routes_ref[k : k + 1, :] == iota2((padded, t), 0), 1.0, 0.0)
    exp_index = lax.axis_index("exp")
    place = place_matrix(rows, n_pair, exp_index // 2, exp_index % 2)
    for group, ref in zip(groups, member_refs):
        blocks = [half * n_pair + r for half in range(2) for r in group]
        some = jnp.concatenate([place[b * rows : (b + 1) * rows] for b in blocks], axis=0)
        ref[...] = dot_f32(hits.astype(BF16), some, ((1,), (1,)))
    for copy in copies[2:]:
        copy.wait()


def project_kernel(n_pair, moves, *refs):
    states = refs[: len(moves)]
    intra_ref, grown_ref, query_ref, gain_ref, w_ref, mine_ref, theirs_ref = refs[len(moves) :]
    t, d = query_ref.shape
    me = lax.axis_index("seq")
    ranks = [move(me) for move in moves]
    parts = [get_state(ref) for ref in states]
    incoming = jnp.zeros((d, d), F32)
    for rank, (state, _) in zip(ranks, parts):
        logsum = jnp.zeros((1, d), F32)
        for other, (_, total) in zip(ranks, parts):
            logsum = logsum + jnp.where(jnp.logical_and(rank < other, other < me), total, 0.0)
        incoming = incoming + jnp.where(rank < me, jnp.exp(logsum), 0.0) * state
    high = incoming.astype(BF16)
    low = (incoming - high.astype(F32)).astype(BF16)
    query = query_ref[...]
    read = dot_f32(query, high, ((1,), (0,))) + dot_f32(query, low, ((1,), (0,)))
    attended = intra_ref[...] + grown_ref[...] * read
    inverse = lax.rsqrt(jnp.mean(attended * attended, axis=1, keepdims=True) + 1e-06)
    normed = (attended * inverse * gain_ref[0:1, :]).astype(BF16)
    exp_index = lax.axis_index("exp")
    place = place_matrix(t // (2 * n_pair), n_pair, exp_index // 2, exp_index % 2)
    normed = dot_f32(place, normed, ((1,), (0,))).astype(BF16)
    for at in chunks(w_ref.shape[1]):
        part = dot_f32(normed, w_ref[:, at], ((1,), (0,))).astype(BF16)
        mine_ref[:, at] = part[: t // 2]
        theirs_ref[:, at] = part[t // 2 :]


def chunks(width):
    size = min(width, COLUMNS)
    return [slice(i, i + size) for i in range(0, width, size)]


def add_kernel(groups, a_ref, b_ref, *refs):
    outs = refs[-len(groups) :]
    rows = outs[0].shape[0] // len(groups[0])
    for group, ref in zip(groups, outs):
        for i, block in enumerate(group):
            at = slice(block * rows, (block + 1) * rows)
            total = a_ref[at, :].astype(F32) + b_ref[at, :].astype(F32)
            ref[i * rows : (i + 1) * rows, :] = total.astype(ref.dtype)


def sum_kernel(count, *refs):
    total = refs[0][...].astype(F32)
    for ref in refs[1:count]:
        total = total + ref[...].astype(F32)
    refs[-1][...] = total.astype(BF16)


def expert_kernel(slices, experts, count, in_ref, down_ref, member_ref, *refs):
    parts, (mine_ref, theirs_ref) = refs[:count], refs[-2:]
    hid, width = down_ref.shape
    t = member_ref.shape[1]
    total = jnp.zeros((in_ref.shape[0], t), F32)
    for at in chunks(width):
        x = jnp.concatenate([part[:, at] for part in parts], axis=0)
        total = total + dot_f32(in_ref[:, at], x, ((1,), (1,)))
    gate, up, logits = total[0:hid], total[hid : 2 * hid], total[2 * hid : 2 * hid + experts]
    raised = jnp.where(member_ref[0:experts, :] > 0.5, jnp.exp(logits), 0.0)
    mine = iota2((experts, t), 0) == lax.axis_index("exp") // slices
    prob = jnp.sum(jnp.where(mine, raised, 0.0), axis=0, keepdims=True) / jnp.sum(raised, axis=0, keepdims=True)
    hidden = (gate / (1.0 + jnp.exp(-gate)) * up * prob).astype(BF16)
    for at in chunks(width):
        part = dot_f32(hidden, down_ref[:, at], ((0,), (0,))).astype(BF16)
        mine_ref[:, at] = part[: t // 2]
        theirs_ref[:, at] = part[t // 2 :]


def call(kernel, outs, args, scratch=(), flops=0, far=0):
    whole = pl.BlockSpec(memory_space=pltpu.VMEM)
    size = sum(a.size * a.dtype.itemsize for a in (*args, *outs))
    if far:
        args = [pltpu.with_memory_space_constraint(a, pltpu.HBM) for a in args[:far]] + list(args[far:])
    return pl.pallas_call(
        kernel,
        out_shape=outs,
        in_specs=[pl.BlockSpec(memory_space=pl.ANY) if far else whole] * len(args),
        out_specs=[whole] * len(outs),
        scratch_shapes=list(scratch),
        compiler_params=pltpu.CompilerParams(vmem_limit_bytes=VMEM_LIMIT),
        cost_estimate=pl.CostEstimate(flops=0, bytes_accessed=0, transcendentals=0),
    )(*args)


def local(query, key_in, value, decay_log, norm_gain, w_out, router, routes, w_gate, w_up, w_down):
    t, d = query.shape
    width = w_out.shape[1]
    exp_count, seq_count = lax.axis_size("exp"), lax.axis_size("seq")
    n_pair = exp_count // 2
    rows = t // exp_count
    experts = router.shape[1]
    slices = exp_count // experts
    hid = w_gate.shape[2]
    out = jax.ShapeDtypeStruct
    dma = pltpu.SemaphoreType.DMA

    def shift(x, r):
        return lax.ppermute(x, "exp", [(e, (e + 2 * r) % exp_count) for e in range(exp_count)])

    def across(x):
        return lax.ppermute(x, "exp", [(e, e ^ 1) for e in range(exp_count)])

    def rows_of(count):
        return out((count * rows, width), BF16)

    decay_row = decay_log.T
    block = pltpu.VMEM((t, d), BF16)
    decay_block = pltpu.VMEM((1, t), F32)
    (state,) = call(
        state_kernel,
        [out((d + TILE_ROWS, d), BF16)],
        (key_in, value, decay_row),
        [block, block, decay_block, dma((3,))],
        far=3,
    )
    moves = [lambda i, k=k: i ^ k for k in reversed(range(1, seq_count))]
    states = [lax.ppermute(state, "seq", [(move(i), i) for i in range(seq_count)]) for move in moves]
    intra, grown, query_near, gain, w_out_near = call(
        within_kernel,
        [out((t, d), F32), out((t, d), F32), out((t, d), BF16), out((8, d), F32), out(w_out.shape, BF16)],
        (query, key_in, value, decay_row, norm_gain[None, :], w_out, state),
        [block, block, decay_block, pltpu.VMEM((1, d), BF16), dma((6,))],
        far=6,
    )
    mine, theirs = call(
        functools.partial(project_kernel, n_pair, moves),
        [rows_of(n_pair), rows_of(n_pair)],
        (*states, intra, grown, query_near, gain, w_out_near),
        flops=2 * t * d * width,
    )
    terms = call(
        functools.partial(add_kernel, [[r] for r in range(n_pair)]),
        [rows_of(1)] * n_pair,
        (mine, across(theirs)),
    )
    moved = [shift(terms[r], r) for r in range(1, n_pair)]

    groups = [list(range(n_pair))]
    w_in, w_down_near, *members = call(
        functools.partial(fetch_kernel, n_pair, groups),
        [out((2 * hid + TILE_ROWS, width), BF16), out((hid, width), BF16)]
        + [out((-(-experts // 8) * 8, 2 * len(group) * rows), F32) for group in groups],
        (router.T, routes.T, w_gate[0].T, w_up[0].T, w_down[0], terms[-1]),
        [pltpu.VMEM((experts, width), BF16), pltpu.VMEM((routes.shape[1], t), jnp.int32), dma((5,))],
        far=5,
    )
    (mixed,) = call(functools.partial(sum_kernel, n_pair), [rows_of(1)], (terms[0], *moved, members[0]))

    gathered = {r: shift(mixed, -r) if r else mixed for r in reversed(range(n_pair))}
    sums = [mixed]
    mine, parts = None, ()
    for group, member in zip(groups, members):
        near = [gathered[r] for r in group]
        if parts:
            near = list(lax.optimization_barrier((*near, mine)))[:-1]
        mine, theirs = call(
            functools.partial(expert_kernel, slices, experts, 2 * len(group)),
            [rows_of(len(group))] * 2,
            (w_in, w_down_near, member, *near, *[across(x) for x in near], *parts),
            flops=6 * 2 * len(group) * rows * hid * width,
        )
        parts = call(
            functools.partial(add_kernel, [[i] for i in range(len(group))]),
            [rows_of(1)] * len(group),
            (mine, across(theirs)),
        )
        sums += [shift(part, r) if r else part for part, r in zip(parts, group)]
    return call(functools.partial(sum_kernel, len(sums)), [rows_of(1)], sums)[0]


def solution(mesh):
    placed = (
        P("seq", "exp"),
        P("seq", "exp"),
        P("seq", "exp"),
        P("seq", "exp"),
        P("exp"),
        P("exp", None),
        P(),
        P("seq", None),
        P("exp", None, None),
        P("exp", None, None),
        P("exp", None, None),
    )

    def pick(query, key_in, value, decay_log, *rest):
        rows = query.shape[0] // lax.axis_size("exp")
        exp_count = lax.axis_size("exp")
        tiled = rows % TILE_ROWS == 0 and decay_log.shape[1] == 1
        for count in (exp_count, lax.axis_size("seq")):
            tiled = tiled and count >= 4 and count & (count - 1) == 0
        plan = local if tiled else plain_plan
        return plan(query, key_in, value, decay_log, *rest)

    return jax.shard_map(
        pick, mesh=mesh, in_specs=placed, out_specs=P(("seq", "exp"), None), check_vma=False
    )
```

```python
import functools

import jax
import jax.numpy as jnp
from jax import lax
from jax.experimental import pallas as pl
from jax.experimental.pallas import tpu as pltpu
from jax.sharding import PartitionSpec as P

F32 = jnp.float32
BF16 = jnp.bfloat16
TILE_ROWS = 16
COLUMNS = 512
VMEM_LIMIT = 16 * 1024 * 1024


def plain_plan(query, key_in, value, decay_log, norm_gain, w_out, router, routes, w_gate, w_up, w_down):
    tok_count = query.shape[0]
    head_count = decay_log.shape[1]
    head_size = query.shape[1] // head_count
    top_count = routes.shape[1]
    expert_count = router.shape[1]
    capacity = max(2, 3 * tok_count * top_count // (2 * expert_count))
    exp_count = lax.axis_size("exp")
    slice_count = exp_count // expert_count
    queries = query.reshape(tok_count, head_count, head_size)
    keys_local = key_in.reshape(tok_count, head_count, head_size)
    values_local = value.reshape(tok_count, head_count, head_size)
    cumulative = jnp.cumsum(decay_log, axis=0)
    scores = jnp.einsum("thd,shd->hts", queries, keys_local, preferred_element_type=jnp.float32)
    spread = cumulative.T[:, :, None] - cumulative.T[:, None, :]
    causal = jnp.arange(tok_count)[:, None] >= jnp.arange(tok_count)[None, :]
    weights = jnp.where(causal, jnp.exp(jnp.where(causal, spread, 0.0)), 0.0)
    attend = (scores * weights / head_size).astype(jnp.bfloat16)
    intra_part = jnp.einsum(
        "hts,she->the", attend, values_local, preferred_element_type=jnp.float32
    )
    totals = cumulative[-1]
    tail_decay = jnp.exp(totals[None, :] - cumulative)
    state_delta = jnp.einsum(
        "shd,she->hde",
        keys_local.astype(jnp.float32) * tail_decay[:, :, None],
        values_local.astype(jnp.float32),
        precision=lax.Precision.HIGHEST,
    )
    decay_rows = lax.all_gather(totals[None, :], "seq", axis=0, tiled=True)
    my_rank = lax.axis_index("seq")
    seq_ranks = jnp.arange(decay_rows.shape[0])
    state_piece = lax.all_gather(
        state_delta[None].astype(jnp.bfloat16), "seq", axis=0, tiled=True
    ).astype(jnp.float32)
    piece_rank = jnp.arange(state_piece.shape[0])
    between = (seq_ranks[None, :] > piece_rank[:, None]) & (seq_ranks[None, :] < my_rank)
    logsum = jnp.dot(between.astype(jnp.float32), decay_rows, precision=lax.Precision.HIGHEST)
    factor = jnp.where((piece_rank < my_rank)[:, None], jnp.exp(logsum), 0.0)
    incoming = jnp.zeros_like(state_delta) + jnp.einsum(
        "ih,ihde->hde", factor, state_piece, precision=lax.Precision.HIGHEST
    )
    inter_part = (
        jnp.exp(cumulative)[:, :, None]
        * jnp.einsum(
            "thd,hde->the", queries.astype(jnp.float32), incoming, precision=lax.Precision.HIGHEST
        )
        / head_size
    )
    attended = intra_part + inter_part
    inverse_rms = lax.rsqrt(jnp.mean(attended * attended, axis=-1, keepdims=True) + 1e-06)
    gain_f32 = norm_gain.astype(jnp.float32).reshape(head_count, head_size)
    normed = (
        (attended * inverse_rms * gain_f32)
        .astype(jnp.bfloat16)
        .reshape(tok_count, head_count * head_size)
    )
    own_mixed = lax.psum_scatter(
        jnp.dot(normed, w_out, preferred_element_type=jnp.float32),
        "exp",
        scatter_dimension=0,
        tiled=True,
    ).astype(jnp.bfloat16)
    mixed = lax.all_gather(own_mixed, "exp", axis=0, tiled=True)
    logits = jnp.dot(mixed, router, preferred_element_type=jnp.float32)
    member = routes[:, :, None] == jnp.arange(expert_count)[None, None, :]
    picked = jnp.sum(jnp.where(member, logits[:, None, :], 0.0), axis=-1)
    raised = jnp.exp(picked)
    gate_probs = raised / jnp.sum(raised, axis=-1, keepdims=True)
    my_expert = lax.axis_index("exp") // slice_count
    flat_hit = (routes.reshape(-1) == my_expert).astype(jnp.int32)
    slot_flat = jnp.cumsum(flat_hit) - flat_hit
    slot_match = (slot_flat[:, None] == jnp.arange(capacity)[None, :]) & (flat_hit[:, None] > 0)
    token_select = jnp.sum(
        slot_match.reshape(tok_count, top_count, capacity).astype(jnp.float32), axis=1
    )
    token_gate = jnp.sum(jnp.where(routes == my_expert, gate_probs, 0.0), axis=1)
    slot_rows = jnp.dot(
        token_select.astype(jnp.bfloat16).T, mixed, preferred_element_type=jnp.float32
    ).astype(jnp.bfloat16)
    gate_part = jnp.dot(slot_rows, w_gate[0], preferred_element_type=jnp.float32)
    up_part = jnp.dot(slot_rows, w_up[0], preferred_element_type=jnp.float32)
    hidden = (jax.nn.silu(gate_part) * up_part).astype(jnp.bfloat16)
    slice_out = jnp.dot(hidden, w_down[0], preferred_element_type=jnp.float32)
    spread_out = jnp.dot(token_select, slice_out, precision=lax.Precision.HIGHEST)
    summed = lax.psum_scatter(
        token_gate[:, None] * spread_out, "exp", scatter_dimension=0, tiled=True
    )
    return (own_mixed.astype(jnp.float32) + summed).astype(jnp.bfloat16)


def iota2(shape, axis):
    return lax.broadcasted_iota(jnp.int32, shape, axis)


def cumulate(decay_row):
    t = decay_row.shape[1]
    row, col = iota2((t, t), 0), iota2((t, t), 1)
    spread = jnp.broadcast_to(decay_row, (t, t))
    column = jnp.sum(jnp.where(col <= row, spread, 0.0), axis=1, keepdims=True)
    own = jnp.sum(jnp.where(col == row, spread, 0.0), axis=1, keepdims=True)
    line = jnp.sum(jnp.where(row <= col, own, 0.0), axis=0, keepdims=True)
    return column, line


def dot_f32(a, b, dims):
    return lax.dot_general(a, b, (dims, ((), ())), preferred_element_type=F32)


def split_dot(a_f32, b, dims):
    high = a_f32.astype(BF16)
    low = (a_f32 - high.astype(F32)).astype(BF16)
    return dot_f32(high, b, dims) + dot_f32(low, b, dims)


def dma_in(sems, pairs):
    copies = [pltpu.make_async_copy(a, b, sems.at[i]) for i, (a, b) in enumerate(pairs)]
    for copy in copies:
        copy.start()
    return copies


def put_state(out_ref, state, total):
    d = state.shape[1]
    out_ref[0:d, :] = state.astype(BF16)
    wide = jnp.broadcast_to(total, (TILE_ROWS, d))
    part0 = wide.astype(BF16).astype(F32)
    part1 = (wide - part0).astype(BF16).astype(F32)
    part2 = wide - part0 - part1
    row = iota2((TILE_ROWS, d), 0)
    parts = jnp.where(row == 0, part0, jnp.where(row == 1, part1, jnp.where(row == 2, part2, 0.0)))
    out_ref[d:, :] = parts.astype(BF16)


def get_state(ref):
    d = ref.shape[1]
    return ref[0:d, :].astype(F32), jnp.sum(ref[d:, :].astype(F32), axis=0, keepdims=True)


def state_kernel(key_hbm, value_hbm, decay_hbm, out_ref, key_ref, value_ref, decay_ref, sems):
    t, d = key_ref.shape
    copies = dma_in(sems, [(decay_hbm, decay_ref), (key_hbm, key_ref), (value_hbm, value_ref)])
    for copy in copies:
        copy.wait()
    column, _ = cumulate(decay_ref[...])
    total = column[t - 1 :, :]
    keyed = key_ref[...].astype(F32) * jnp.exp(total - column)
    put_state(out_ref, split_dot(keyed, value_ref[...], ((0,), (0,))), jnp.broadcast_to(total, (1, d)))


def within_kernel(
    query_hbm, key_hbm, value_hbm, decay_hbm, gain_hbm, w_out_hbm, _,
    intra_ref, grown_ref, query_ref, gain_ref, w_out_ref,
    key_ref, value_ref, decay_ref, gain_in_ref, sems,
):
    t, d = query_ref.shape
    copies = dma_in(
        sems,
        [
            (decay_hbm, decay_ref),
            (query_hbm, query_ref),
            (key_hbm, key_ref),
            (value_hbm, value_ref),
            (gain_hbm, gain_in_ref),
            (w_out_hbm, w_out_ref),
        ],
    )
    for copy in copies[:5]:
        copy.wait()
    column, line = cumulate(decay_ref[...])
    query, key, value = query_ref[...], key_ref[...], value_ref[...]
    scores = dot_f32(query, key, ((1,), (1,)))
    causal = iota2((t, t), 0) >= iota2((t, t), 1)
    weights = jnp.where(causal, jnp.exp(jnp.where(causal, column - line, 0.0)), 0.0)
    attend = (scores * weights * (1.0 / d)).astype(BF16)
    intra_ref[...] = dot_f32(attend, value, ((1,), (0,)))
    grown_ref[...] = jnp.broadcast_to(jnp.exp(column) * (1.0 / d), (t, d))
    gain_ref[...] = jnp.broadcast_to(gain_in_ref[...].astype(F32), gain_ref.shape)
    copies[5].wait()


def place_matrix(rows, n_pair, pair, core):
    size = 2 * n_pair * rows
    i, j = iota2((size, size), 0), iota2((size, size), 1)
    half, inner = i // (n_pair * rows), i % (n_pair * rows)
    who = (inner // rows + pair) % n_pair
    source = (2 * who + (core + half) % 2) * rows + inner % rows
    return jnp.where(source == j, 1.0, 0.0).astype(BF16)


def fetch_kernel(
    n_pair, groups, router_hbm, routes_hbm, gate_hbm, up_hbm, down_hbm, _, in_ref, down_ref, *refs
):
    member_refs, (router_ref, routes_ref, sems) = refs[:-3], refs[-3:]
    hid = gate_hbm.shape[0]
    copies = dma_in(
        sems,
        [
            (router_hbm, router_ref),
            (routes_hbm, routes_ref),
            (gate_hbm, in_ref.at[0:hid]),
            (up_hbm, in_ref.at[hid : 2 * hid]),
            (down_hbm, down_ref),
        ],
    )
    for copy in copies[:2]:
        copy.wait()
    experts, t = router_ref.shape[0], routes_ref.shape[1]
    rows = t // (2 * n_pair)
    in_ref[2 * hid :, :] = jnp.zeros((TILE_ROWS, in_ref.shape[1]), BF16)
    in_ref[2 * hid : 2 * hid + experts, :] = router_ref[...]
    padded = member_refs[0].shape[0]
    hits = jnp.zeros((padded, t), F32)
    for k in range(routes_ref.shape[0]):
        hits = hits + jnp.where(routes_ref[k : k + 1, :] == iota2((padded, t), 0), 1.0, 0.0)
    exp_index = lax.axis_index("exp")
    place = place_matrix(rows, n_pair, exp_index // 2, exp_index % 2)
    for group, ref in zip(groups, member_refs):
        blocks = [half * n_pair + r for half in range(2) for r in group]
        some = jnp.concatenate([place[b * rows : (b + 1) * rows] for b in blocks], axis=0)
        ref[...] = dot_f32(hits.astype(BF16), some, ((1,), (1,)))
    for copy in copies[2:]:
        copy.wait()


def project_kernel(n_pair, moves, *refs):
    states = refs[: len(moves)]
    intra_ref, grown_ref, query_ref, gain_ref, w_ref, mine_ref, theirs_ref = refs[len(moves) :]
    t, d = query_ref.shape
    me = lax.axis_index("seq")
    ranks = [move(me) for move in moves]
    parts = [get_state(ref) for ref in states]
    incoming = jnp.zeros((d, d), F32)
    for rank, (state, _) in zip(ranks, parts):
        logsum = jnp.zeros((1, d), F32)
        for other, (_, total) in zip(ranks, parts):
            logsum = logsum + jnp.where(jnp.logical_and(rank < other, other < me), total, 0.0)
        incoming = incoming + jnp.where(rank < me, jnp.exp(logsum), 0.0) * state
    high = incoming.astype(BF16)
    low = (incoming - high.astype(F32)).astype(BF16)
    query = query_ref[...]
    read = dot_f32(query, high, ((1,), (0,))) + dot_f32(query, low, ((1,), (0,)))
    attended = intra_ref[...] + grown_ref[...] * read
    inverse = lax.rsqrt(jnp.mean(attended * attended, axis=1, keepdims=True) + 1e-06)
    normed = (attended * inverse * gain_ref[0:1, :]).astype(BF16)
    exp_index = lax.axis_index("exp")
    place = place_matrix(t // (2 * n_pair), n_pair, exp_index // 2, exp_index % 2)
    normed = dot_f32(place, normed, ((1,), (0,))).astype(BF16)

    def project(at):
        part = dot_f32(normed, w_ref[:, at], ((1,), (0,))).astype(BF16)
        mine_ref[:, at] = part[: t // 2]
        theirs_ref[:, at] = part[t // 2 :]

    over_columns(w_ref.shape[1], project)


def over_columns(width, body):
    size = min(width, COLUMNS)

    def step(i, carry):
        body(pl.ds(pl.multiple_of(i * size, size), size))
        return carry

    lax.fori_loop(0, width // size, step, 0)


def add_kernel(groups, a_ref, b_ref, *refs):
    outs = refs[-len(groups) :]
    rows = outs[0].shape[0] // len(groups[0])

    def add(at):
        for group, ref in zip(groups, outs):
            for i, block in enumerate(group):
                some = slice(block * rows, (block + 1) * rows)
                total = a_ref[some, at].astype(F32) + b_ref[some, at].astype(F32)
                ref[i * rows : (i + 1) * rows, at] = total.astype(ref.dtype)

    over_columns(a_ref.shape[1], add)


def sum_kernel(count, *refs):
    def add(at):
        total = refs[0][:, at].astype(F32)
        for ref in refs[1:count]:
            total = total + ref[:, at].astype(F32)
        refs[-1][:, at] = total.astype(BF16)

    over_columns(refs[0].shape[1], add)


def expert_kernel(slices, experts, count, in_ref, down_ref, member_ref, *refs):
    parts, (mine_ref, theirs_ref, total_ref) = refs[:count], refs[-3:]
    hid, width = down_ref.shape
    t = member_ref.shape[1]
    total_ref[...] = jnp.zeros(total_ref.shape, F32)

    def enter(at):
        x = jnp.concatenate([part[:, at] for part in parts], axis=0)
        total_ref[...] += dot_f32(in_ref[:, at], x, ((1,), (1,)))

    over_columns(width, enter)
    gate, up, logits = total_ref[0:hid], total_ref[hid : 2 * hid], total_ref[2 * hid : 2 * hid + experts]
    raised = jnp.where(member_ref[0:experts, :] > 0.5, jnp.exp(logits), 0.0)
    mine = iota2((experts, t), 0) == lax.axis_index("exp") // slices
    prob = jnp.sum(jnp.where(mine, raised, 0.0), axis=0, keepdims=True) / jnp.sum(raised, axis=0, keepdims=True)
    hidden = (gate / (1.0 + jnp.exp(-gate)) * up * prob).astype(BF16)
    hidden = hidden.T

    def leave(at):
        part = dot_f32(hidden, down_ref[:, at], ((1,), (0,))).astype(BF16)
        mine_ref[:, at] = part[: t // 2]
        theirs_ref[:, at] = part[t // 2 :]

    over_columns(width, leave)


def call(kernel, outs, args, scratch=(), flops=0, far=0):
    whole = pl.BlockSpec(memory_space=pltpu.VMEM)
    size = sum(a.size * a.dtype.itemsize for a in (*args, *outs))
    if far:
        args = [pltpu.with_memory_space_constraint(a, pltpu.HBM) for a in args[:far]] + list(args[far:])
    return pl.pallas_call(
        kernel,
        out_shape=outs,
        in_specs=[pl.BlockSpec(memory_space=pl.ANY) if far else whole] * len(args),
        out_specs=[whole] * len(outs),
        scratch_shapes=list(scratch),
        compiler_params=pltpu.CompilerParams(vmem_limit_bytes=VMEM_LIMIT),
        cost_estimate=pl.CostEstimate(flops=0, bytes_accessed=0, transcendentals=0),
    )(*args)


def local(query, key_in, value, decay_log, norm_gain, w_out, router, routes, w_gate, w_up, w_down):
    t, d = query.shape
    width = w_out.shape[1]
    exp_count, seq_count = lax.axis_size("exp"), lax.axis_size("seq")
    n_pair = exp_count // 2
    rows = t // exp_count
    experts = router.shape[1]
    slices = exp_count // experts
    hid = w_gate.shape[2]
    out = jax.ShapeDtypeStruct
    dma = pltpu.SemaphoreType.DMA

    def shift(x, r):
        return lax.ppermute(x, "exp", [(e, (e + 2 * r) % exp_count) for e in range(exp_count)])

    def across(x):
        return lax.ppermute(x, "exp", [(e, e ^ 1) for e in range(exp_count)])

    def rows_of(count):
        return out((count * rows, width), BF16)

    decay_row = decay_log.T
    block = pltpu.VMEM((t, d), BF16)
    decay_block = pltpu.VMEM((1, t), F32)
    (state,) = call(
        state_kernel,
        [out((d + TILE_ROWS, d), BF16)],
        (key_in, value, decay_row),
        [block, block, decay_block, dma((3,))],
        far=3,
    )
    moves = [lambda i, k=k: i ^ k for k in range(1, seq_count)]
    states = [lax.ppermute(state, "seq", [(move(i), i) for i in range(seq_count)]) for move in moves]
    intra, grown, query_near, gain, w_out_near = call(
        within_kernel,
        [out((t, d), F32), out((t, d), F32), out((t, d), BF16), out((8, d), F32), out(w_out.shape, BF16)],
        (query, key_in, value, decay_row, norm_gain[None, :], w_out, state),
        [block, block, decay_block, pltpu.VMEM((1, d), BF16), dma((6,))],
        far=6,
    )
    mine, theirs = call(
        functools.partial(project_kernel, n_pair, moves),
        [rows_of(n_pair), rows_of(n_pair)],
        (*states, intra, grown, query_near, gain, w_out_near),
        flops=2 * t * d * width,
    )
    terms = call(
        functools.partial(add_kernel, [[r] for r in range(n_pair)]),
        [rows_of(1)] * n_pair,
        (mine, across(theirs)),
    )
    moved = [shift(terms[r], r) for r in range(1, n_pair)]

    groups = [list(range(n_pair))]
    w_in, w_down_near, *members = call(
        functools.partial(fetch_kernel, n_pair, groups),
        [out((2 * hid + TILE_ROWS, width), BF16), out((hid, width), BF16)]
        + [out((-(-experts // 8) * 8, 2 * len(group) * rows), F32) for group in groups],
        (router.T, routes.T, w_gate[0].T, w_up[0].T, w_down[0], terms[-1]),
        [pltpu.VMEM((experts, width), BF16), pltpu.VMEM((routes.shape[1], t), jnp.int32), dma((5,))],
        far=5,
    )
    (mixed,) = call(functools.partial(sum_kernel, n_pair), [rows_of(1)], (terms[0], *moved, members[0]))

    gathered = {r: shift(mixed, -r) if r else mixed for r in reversed(range(n_pair))}
    sums = [mixed]
    mine, parts = None, ()
    for group, member in zip(groups, members):
        near = [gathered[r] for r in group]
        if parts:
            near = list(lax.optimization_barrier((*near, mine)))[:-1]
        mine, theirs = call(
            functools.partial(expert_kernel, slices, experts, 2 * len(group)),
            [rows_of(len(group))] * 2,
            (w_in, w_down_near, member, *near, *[across(x) for x in near], *parts),
            [pltpu.VMEM((2 * hid + TILE_ROWS, 2 * len(group) * rows), F32)],
            flops=6 * 2 * len(group) * rows * hid * width,
        )
        parts = call(
            functools.partial(add_kernel, [[i] for i in range(len(group))]),
            [rows_of(1)] * len(group),
            (mine, across(theirs)),
        )
        sums += [shift(part, r) if r else part for part, r in zip(parts, group)]
    return call(functools.partial(sum_kernel, len(sums)), [rows_of(1)], sums)[0]


def solution(mesh):
    placed = (
        P("seq", "exp"),
        P("seq", "exp"),
        P("seq", "exp"),
        P("seq", "exp"),
        P("exp"),
        P("exp", None),
        P(),
        P("seq", None),
        P("exp", None, None),
        P("exp", None, None),
        P("exp", None, None),
    )

    def pick(query, key_in, value, decay_log, *rest):
        rows = query.shape[0] // lax.axis_size("exp")
        exp_count = lax.axis_size("exp")
        tiled = rows % TILE_ROWS == 0 and decay_log.shape[1] == 1
        for count in (exp_count, lax.axis_size("seq")):
            tiled = tiled and count >= 4 and count & (count - 1) == 0
        plan = local if tiled else plain_plan
        return plan(query, key_in, value, decay_log, *rest)

    return jax.shard_map(
        pick, mesh=mesh, in_specs=placed, out_specs=P(("seq", "exp"), None), check_vma=False
    )
```

```python
import functools

import jax
import jax.numpy as jnp
from jax import lax
from jax.experimental import pallas as pl
from jax.experimental.pallas import tpu as pltpu
from jax.sharding import PartitionSpec as P

F32 = jnp.float32
BF16 = jnp.bfloat16
TILE_ROWS = 16
COLUMNS = 1024
VMEM_LIMIT = 16 * 1024 * 1024


def plain_plan(query, key_in, value, decay_log, norm_gain, w_out, router, routes, w_gate, w_up, w_down):
    tok_count = query.shape[0]
    head_count = decay_log.shape[1]
    head_size = query.shape[1] // head_count
    top_count = routes.shape[1]
    expert_count = router.shape[1]
    capacity = max(2, 3 * tok_count * top_count // (2 * expert_count))
    exp_count = lax.axis_size("exp")
    slice_count = exp_count // expert_count
    queries = query.reshape(tok_count, head_count, head_size)
    keys_local = key_in.reshape(tok_count, head_count, head_size)
    values_local = value.reshape(tok_count, head_count, head_size)
    cumulative = jnp.cumsum(decay_log, axis=0)
    scores = jnp.einsum("thd,shd->hts", queries, keys_local, preferred_element_type=jnp.float32)
    spread = cumulative.T[:, :, None] - cumulative.T[:, None, :]
    causal = jnp.arange(tok_count)[:, None] >= jnp.arange(tok_count)[None, :]
    weights = jnp.where(causal, jnp.exp(jnp.where(causal, spread, 0.0)), 0.0)
    attend = (scores * weights / head_size).astype(jnp.bfloat16)
    intra_part = jnp.einsum(
        "hts,she->the", attend, values_local, preferred_element_type=jnp.float32
    )
    totals = cumulative[-1]
    tail_decay = jnp.exp(totals[None, :] - cumulative)
    state_delta = jnp.einsum(
        "shd,she->hde",
        keys_local.astype(jnp.float32) * tail_decay[:, :, None],
        values_local.astype(jnp.float32),
        precision=lax.Precision.HIGHEST,
    )
    decay_rows = lax.all_gather(totals[None, :], "seq", axis=0, tiled=True)
    my_rank = lax.axis_index("seq")
    seq_ranks = jnp.arange(decay_rows.shape[0])
    state_piece = lax.all_gather(
        state_delta[None].astype(jnp.bfloat16), "seq", axis=0, tiled=True
    ).astype(jnp.float32)
    piece_rank = jnp.arange(state_piece.shape[0])
    between = (seq_ranks[None, :] > piece_rank[:, None]) & (seq_ranks[None, :] < my_rank)
    logsum = jnp.dot(between.astype(jnp.float32), decay_rows, precision=lax.Precision.HIGHEST)
    factor = jnp.where((piece_rank < my_rank)[:, None], jnp.exp(logsum), 0.0)
    incoming = jnp.zeros_like(state_delta) + jnp.einsum(
        "ih,ihde->hde", factor, state_piece, precision=lax.Precision.HIGHEST
    )
    inter_part = (
        jnp.exp(cumulative)[:, :, None]
        * jnp.einsum(
            "thd,hde->the", queries.astype(jnp.float32), incoming, precision=lax.Precision.HIGHEST
        )
        / head_size
    )
    attended = intra_part + inter_part
    inverse_rms = lax.rsqrt(jnp.mean(attended * attended, axis=-1, keepdims=True) + 1e-06)
    gain_f32 = norm_gain.astype(jnp.float32).reshape(head_count, head_size)
    normed = (
        (attended * inverse_rms * gain_f32)
        .astype(jnp.bfloat16)
        .reshape(tok_count, head_count * head_size)
    )
    own_mixed = lax.psum_scatter(
        jnp.dot(normed, w_out, preferred_element_type=jnp.float32),
        "exp",
        scatter_dimension=0,
        tiled=True,
    ).astype(jnp.bfloat16)
    mixed = lax.all_gather(own_mixed, "exp", axis=0, tiled=True)
    logits = jnp.dot(mixed, router, preferred_element_type=jnp.float32)
    member = routes[:, :, None] == jnp.arange(expert_count)[None, None, :]
    picked = jnp.sum(jnp.where(member, logits[:, None, :], 0.0), axis=-1)
    raised = jnp.exp(picked)
    gate_probs = raised / jnp.sum(raised, axis=-1, keepdims=True)
    my_expert = lax.axis_index("exp") // slice_count
    flat_hit = (routes.reshape(-1) == my_expert).astype(jnp.int32)
    slot_flat = jnp.cumsum(flat_hit) - flat_hit
    slot_match = (slot_flat[:, None] == jnp.arange(capacity)[None, :]) & (flat_hit[:, None] > 0)
    token_select = jnp.sum(
        slot_match.reshape(tok_count, top_count, capacity).astype(jnp.float32), axis=1
    )
    token_gate = jnp.sum(jnp.where(routes == my_expert, gate_probs, 0.0), axis=1)
    slot_rows = jnp.dot(
        token_select.astype(jnp.bfloat16).T, mixed, preferred_element_type=jnp.float32
    ).astype(jnp.bfloat16)
    gate_part = jnp.dot(slot_rows, w_gate[0], preferred_element_type=jnp.float32)
    up_part = jnp.dot(slot_rows, w_up[0], preferred_element_type=jnp.float32)
    hidden = (jax.nn.silu(gate_part) * up_part).astype(jnp.bfloat16)
    slice_out = jnp.dot(hidden, w_down[0], preferred_element_type=jnp.float32)
    spread_out = jnp.dot(token_select, slice_out, precision=lax.Precision.HIGHEST)
    summed = lax.psum_scatter(
        token_gate[:, None] * spread_out, "exp", scatter_dimension=0, tiled=True
    )
    return (own_mixed.astype(jnp.float32) + summed).astype(jnp.bfloat16)


def iota2(shape, axis):
    return lax.broadcasted_iota(jnp.int32, shape, axis)


def cumulate(decay_row):
    t = decay_row.shape[1]
    row, col = iota2((t, t), 0), iota2((t, t), 1)
    spread = jnp.broadcast_to(decay_row, (t, t))
    column = jnp.sum(jnp.where(col <= row, spread, 0.0), axis=1, keepdims=True)
    own = jnp.sum(jnp.where(col == row, spread, 0.0), axis=1, keepdims=True)
    line = jnp.sum(jnp.where(row <= col, own, 0.0), axis=0, keepdims=True)
    return column, line


def dot_f32(a, b, dims):
    return lax.dot_general(a, b, (dims, ((), ())), preferred_element_type=F32)


def split_dot(a_f32, b, dims):
    high = a_f32.astype(BF16)
    low = (a_f32 - high.astype(F32)).astype(BF16)
    return dot_f32(high, b, dims) + dot_f32(low, b, dims)


def dma_in(sems, pairs):
    copies = [pltpu.make_async_copy(a, b, sems.at[i]) for i, (a, b) in enumerate(pairs)]
    for copy in copies:
        copy.start()
    return copies


def put_state(out_ref, state, total):
    d = state.shape[1]
    out_ref[0:d, :] = state.astype(BF16)
    wide = jnp.broadcast_to(total, (TILE_ROWS, d))
    part0 = wide.astype(BF16).astype(F32)
    part1 = (wide - part0).astype(BF16).astype(F32)
    part2 = wide - part0 - part1
    row = iota2((TILE_ROWS, d), 0)
    parts = jnp.where(row == 0, part0, jnp.where(row == 1, part1, jnp.where(row == 2, part2, 0.0)))
    out_ref[d:, :] = parts.astype(BF16)


def get_state(ref):
    d = ref.shape[1]
    return ref[0:d, :].astype(F32), jnp.sum(ref[d:, :].astype(F32), axis=0, keepdims=True)


def state_kernel(key_hbm, value_hbm, decay_hbm, out_ref, key_ref, value_ref, decay_ref, sems):
    t, d = key_ref.shape
    copies = dma_in(sems, [(decay_hbm, decay_ref), (key_hbm, key_ref), (value_hbm, value_ref)])
    for copy in copies:
        copy.wait()
    column, _ = cumulate(decay_ref[...])
    total = column[t - 1 :, :]
    keyed = key_ref[...].astype(F32) * jnp.exp(total - column)
    put_state(out_ref, split_dot(keyed, value_ref[...], ((0,), (0,))), jnp.broadcast_to(total, (1, d)))


def within_kernel(
    query_hbm, key_hbm, value_hbm, decay_hbm, gain_hbm, w_out_hbm, _,
    intra_ref, grown_ref, query_ref, gain_ref, w_out_ref,
    key_ref, value_ref, decay_ref, gain_in_ref, sems,
):
    t, d = query_ref.shape
    copies = dma_in(
        sems,
        [
            (decay_hbm, decay_ref),
            (query_hbm, query_ref),
            (key_hbm, key_ref),
            (value_hbm, value_ref),
            (gain_hbm, gain_in_ref),
            (w_out_hbm, w_out_ref),
        ],
    )
    for copy in copies[:5]:
        copy.wait()
    column, line = cumulate(decay_ref[...])
    query, key, value = query_ref[...], key_ref[...], value_ref[...]
    scores = dot_f32(query, key, ((1,), (1,)))
    causal = iota2((t, t), 0) >= iota2((t, t), 1)
    weights = jnp.where(causal, jnp.exp(jnp.where(causal, column - line, 0.0)), 0.0)
    attend = (scores * weights * (1.0 / d)).astype(BF16)
    intra_ref[...] = dot_f32(attend, value, ((1,), (0,)))
    grown_ref[...] = jnp.broadcast_to(jnp.exp(column) * (1.0 / d), (t, d))
    gain_ref[...] = jnp.broadcast_to(gain_in_ref[...].astype(F32), gain_ref.shape)
    copies[5].wait()


def place_matrix(rows, n_pair, pair, core):
    size = 2 * n_pair * rows
    i, j = iota2((size, size), 0), iota2((size, size), 1)
    half, inner = i // (n_pair * rows), i % (n_pair * rows)
    who = (inner // rows + pair) % n_pair
    source = (2 * who + (core + half) % 2) * rows + inner % rows
    return jnp.where(source == j, 1.0, 0.0).astype(BF16)


def fetch_kernel(
    n_pair, groups, router_hbm, routes_hbm, gate_hbm, up_hbm, down_hbm, _, in_ref, down_ref, *refs
):
    member_refs, (router_ref, routes_ref, sems) = refs[:-3], refs[-3:]
    hid = gate_hbm.shape[0]
    copies = dma_in(
        sems,
        [
            (router_hbm, router_ref),
            (routes_hbm, routes_ref),
            (gate_hbm, in_ref.at[0:hid]),
            (up_hbm, in_ref.at[hid : 2 * hid]),
            (down_hbm, down_ref),
        ],
    )
    for copy in copies[:2]:
        copy.wait()
    experts, t = router_ref.shape[0], routes_ref.shape[1]
    rows = t // (2 * n_pair)
    in_ref[2 * hid :, :] = jnp.zeros((TILE_ROWS, in_ref.shape[1]), BF16)
    in_ref[2 * hid : 2 * hid + experts, :] = router_ref[...]
    padded = member_refs[0].shape[0]
    hits = jnp.zeros((padded, t), F32)
    for k in range(routes_ref.shape[0]):
        hits = hits + jnp.where(routes_ref[k : k + 1, :] == iota2((padded, t), 0), 1.0, 0.0)
    exp_index = lax.axis_index("exp")
    place = place_matrix(rows, n_pair, exp_index // 2, exp_index % 2)
    for group, ref in zip(groups, member_refs):
        blocks = [half * n_pair + r for half in range(2) for r in group]
        some = jnp.concatenate([place[b * rows : (b + 1) * rows] for b in blocks], axis=0)
        ref[...] = dot_f32(hits.astype(BF16), some, ((1,), (1,)))
    for copy in copies[2:]:
        copy.wait()


def project_kernel(n_pair, moves, *refs):
    states = refs[: len(moves)]
    intra_ref, grown_ref, query_ref, gain_ref, w_ref, mine_ref, theirs_ref = refs[len(moves) :]
    t, d = query_ref.shape
    me = lax.axis_index("seq")
    ranks = [move(me) for move in moves]
    parts = [get_state(ref) for ref in states]
    incoming = jnp.zeros((d, d), F32)
    for rank, (state, _) in zip(ranks, parts):
        logsum = jnp.zeros((1, d), F32)
        for other, (_, total) in zip(ranks, parts):
            logsum = logsum + jnp.where(jnp.logical_and(rank < other, other < me), total, 0.0)
        incoming = incoming + jnp.where(rank < me, jnp.exp(logsum), 0.0) * state
    high = incoming.astype(BF16)
    low = (incoming - high.astype(F32)).astype(BF16)
    query = query_ref[...]
    read = dot_f32(query, high, ((1,), (0,))) + dot_f32(query, low, ((1,), (0,)))
    attended = intra_ref[...] + grown_ref[...] * read
    inverse = lax.rsqrt(jnp.mean(attended * attended, axis=1, keepdims=True) + 1e-06)
    normed = (attended * inverse * gain_ref[0:1, :]).astype(BF16)
    exp_index = lax.axis_index("exp")
    place = place_matrix(t // (2 * n_pair), n_pair, exp_index // 2, exp_index % 2)
    normed = dot_f32(place, normed, ((1,), (0,))).astype(BF16)
    for at in chunks(w_ref.shape[1]):
        part = dot_f32(normed, w_ref[:, at], ((1,), (0,))).astype(BF16)
        mine_ref[:, at] = part[: t // 2]
        theirs_ref[:, at] = part[t // 2 :]


def chunks(width):
    size = min(width, COLUMNS)
    return [slice(i, i + size) for i in range(0, width, size)]


def add_kernel(groups, a_ref, b_ref, *refs):
    outs = refs[-len(groups) :]
    rows = outs[0].shape[0] // len(groups[0])
    for group, ref in zip(groups, outs):
        for i, block in enumerate(group):
            at = slice(block * rows, (block + 1) * rows)
            total = a_ref[at, :].astype(F32) + b_ref[at, :].astype(F32)
            ref[i * rows : (i + 1) * rows, :] = total.astype(ref.dtype)


def sum_kernel(count, *refs):
    total = refs[0][...].astype(F32)
    for ref in refs[1:count]:
        total = total + ref[...].astype(F32)
    refs[-1][...] = total.astype(BF16)


def expert_kernel(slices, experts, count, in_ref, down_ref, member_ref, *refs):
    parts, (mine_ref, theirs_ref) = refs[:count], refs[-2:]
    hid, width = down_ref.shape
    t = member_ref.shape[1]
    x = jnp.concatenate([part[...] for part in parts], axis=0)
    total = dot_f32(in_ref[...], x, ((1,), (1,)))
    gate, up, logits = total[0:hid], total[hid : 2 * hid], total[2 * hid : 2 * hid + experts]
    raised = jnp.where(member_ref[0:experts, :] > 0.5, jnp.exp(logits), 0.0)
    mine = iota2((experts, t), 0) == lax.axis_index("exp") // slices
    prob = jnp.sum(jnp.where(mine, raised, 0.0), axis=0, keepdims=True) / jnp.sum(raised, axis=0, keepdims=True)
    hidden = (gate / (1.0 + jnp.exp(-gate)) * up * prob).T.astype(BF16)
    for at in chunks(width):
        part = dot_f32(hidden, down_ref[:, at], ((1,), (0,))).astype(BF16)
        mine_ref[:, at] = part[: t // 2]
        theirs_ref[:, at] = part[t // 2 :]


def call(kernel, outs, args, scratch=(), flops=0, far=0):
    whole = pl.BlockSpec(memory_space=pltpu.VMEM)
    size = sum(a.size * a.dtype.itemsize for a in (*args, *outs))
    if far:
        args = [pltpu.with_memory_space_constraint(a, pltpu.HBM) for a in args[:far]] + list(args[far:])
    return pl.pallas_call(
        kernel,
        out_shape=outs,
        in_specs=[pl.BlockSpec(memory_space=pl.ANY) if far else whole] * len(args),
        out_specs=[whole] * len(outs),
        scratch_shapes=list(scratch),
        compiler_params=pltpu.CompilerParams(vmem_limit_bytes=VMEM_LIMIT),
        cost_estimate=pl.CostEstimate(flops=0, bytes_accessed=0, transcendentals=0),
    )(*args)


def local(query, key_in, value, decay_log, norm_gain, w_out, router, routes, w_gate, w_up, w_down):
    t, d = query.shape
    width = w_out.shape[1]
    exp_count, seq_count = lax.axis_size("exp"), lax.axis_size("seq")
    n_pair = exp_count // 2
    rows = t // exp_count
    experts = router.shape[1]
    slices = exp_count // experts
    hid = w_gate.shape[2]
    out = jax.ShapeDtypeStruct
    dma = pltpu.SemaphoreType.DMA

    def shift(x, r):
        return lax.ppermute(x, "exp", [(e, (e + 2 * r) % exp_count) for e in range(exp_count)])

    def across(x):
        return lax.ppermute(x, "exp", [(e, e ^ 1) for e in range(exp_count)])

    def rows_of(count):
        return out((count * rows, width), BF16)

    decay_row = decay_log.T
    block = pltpu.VMEM((t, d), BF16)
    decay_block = pltpu.VMEM((1, t), F32)
    (state,) = call(
        state_kernel,
        [out((d + TILE_ROWS, d), BF16)],
        (key_in, value, decay_row),
        [block, block, decay_block, dma((3,))],
        far=3,
    )
    moves = [lambda i, k=k: i ^ k for k in range(1, seq_count)]
    states = [lax.ppermute(state, "seq", [(move(i), i) for i in range(seq_count)]) for move in moves]
    intra, grown, query_near, gain, w_out_near = call(
        within_kernel,
        [out((t, d), F32), out((t, d), F32), out((t, d), BF16), out((8, d), F32), out(w_out.shape, BF16)],
        (query, key_in, value, decay_row, norm_gain[None, :], w_out, state),
        [block, block, decay_block, pltpu.VMEM((1, d), BF16), dma((6,))],
        far=6,
    )
    mine, theirs = call(
        functools.partial(project_kernel, n_pair, moves),
        [rows_of(n_pair), rows_of(n_pair)],
        (*states, intra, grown, query_near, gain, w_out_near),
        flops=2 * t * d * width,
    )
    terms = call(
        functools.partial(add_kernel, [[r] for r in range(n_pair)]),
        [rows_of(1)] * n_pair,
        (mine, across(theirs)),
    )
    moved = [shift(terms[r], r) for r in range(1, n_pair)]

    groups = [list(range(n_pair))]
    w_in, w_down_near, *members = call(
        functools.partial(fetch_kernel, n_pair, groups),
        [out((2 * hid + TILE_ROWS, width), BF16), out((hid, width), BF16)]
        + [out((-(-experts // 8) * 8, 2 * len(group) * rows), F32) for group in groups],
        (router.T, routes.T, w_gate[0].T, w_up[0].T, w_down[0], terms[-1]),
        [pltpu.VMEM((experts, width), BF16), pltpu.VMEM((routes.shape[1], t), jnp.int32), dma((5,))],
        far=5,
    )
    (mixed,) = call(functools.partial(sum_kernel, n_pair), [rows_of(1)], (terms[0], *moved, members[0]))

    gathered = {r: shift(mixed, -r) if r else mixed for r in reversed(range(n_pair))}
    sums = [mixed]
    mine, parts = None, ()
    for group, member in zip(groups, members):
        near = [gathered[r] for r in group]
        if parts:
            near = list(lax.optimization_barrier((*near, mine)))[:-1]
        mine, theirs = call(
            functools.partial(expert_kernel, slices, experts, 2 * len(group)),
            [rows_of(len(group))] * 2,
            (w_in, w_down_near, member, *near, *[across(x) for x in near], *parts),
            flops=6 * 2 * len(group) * rows * hid * width,
        )
        parts = call(
            functools.partial(add_kernel, [[i] for i in range(len(group))]),
            [rows_of(1)] * len(group),
            (mine, across(theirs)),
        )
        sums += [shift(part, r) if r else part for part, r in zip(parts[::-1], group[::-1])]
    return call(functools.partial(sum_kernel, len(sums)), [rows_of(1)], sums)[0]


def solution(mesh):
    placed = (
        P("seq", "exp"),
        P("seq", "exp"),
        P("seq", "exp"),
        P("seq", "exp"),
        P("exp"),
        P("exp", None),
        P(),
        P("seq", None),
        P("exp", None, None),
        P("exp", None, None),
        P("exp", None, None),
    )

    def pick(query, key_in, value, decay_log, *rest):
        rows = query.shape[0] // lax.axis_size("exp")
        exp_count = lax.axis_size("exp")
        tiled = rows % TILE_ROWS == 0 and decay_log.shape[1] == 1
        for count in (exp_count, lax.axis_size("seq")):
            tiled = tiled and count >= 4 and count & (count - 1) == 0
        plan = local if tiled else plain_plan
        return plan(query, key_in, value, decay_log, *rest)

    return jax.shard_map(
        pick, mesh=mesh, in_specs=placed, out_specs=P(("seq", "exp"), None), check_vma=False
    )
```

```python
import functools

import jax
import jax.numpy as jnp
from jax import lax
from jax.experimental import pallas as pl
from jax.experimental.pallas import tpu as pltpu
from jax.sharding import PartitionSpec as P

F32 = jnp.float32
BF16 = jnp.bfloat16
TILE_ROWS = 16
COLUMNS = 1024
VMEM_LIMIT = 16 * 1024 * 1024


def plain_plan(query, key_in, value, decay_log, norm_gain, w_out, router, routes, w_gate, w_up, w_down):
    tok_count = query.shape[0]
    head_count = decay_log.shape[1]
    head_size = query.shape[1] // head_count
    top_count = routes.shape[1]
    expert_count = router.shape[1]
    capacity = max(2, 3 * tok_count * top_count // (2 * expert_count))
    exp_count = lax.axis_size("exp")
    slice_count = exp_count // expert_count
    queries = query.reshape(tok_count, head_count, head_size)
    keys_local = key_in.reshape(tok_count, head_count, head_size)
    values_local = value.reshape(tok_count, head_count, head_size)
    cumulative = jnp.cumsum(decay_log, axis=0)
    scores = jnp.einsum("thd,shd->hts", queries, keys_local, preferred_element_type=jnp.float32)
    spread = cumulative.T[:, :, None] - cumulative.T[:, None, :]
    causal = jnp.arange(tok_count)[:, None] >= jnp.arange(tok_count)[None, :]
    weights = jnp.where(causal, jnp.exp(jnp.where(causal, spread, 0.0)), 0.0)
    attend = (scores * weights / head_size).astype(jnp.bfloat16)
    intra_part = jnp.einsum(
        "hts,she->the", attend, values_local, preferred_element_type=jnp.float32
    )
    totals = cumulative[-1]
    tail_decay = jnp.exp(totals[None, :] - cumulative)
    state_delta = jnp.einsum(
        "shd,she->hde",
        keys_local.astype(jnp.float32) * tail_decay[:, :, None],
        values_local.astype(jnp.float32),
        precision=lax.Precision.HIGHEST,
    )
    decay_rows = lax.all_gather(totals[None, :], "seq", axis=0, tiled=True)
    my_rank = lax.axis_index("seq")
    seq_ranks = jnp.arange(decay_rows.shape[0])
    state_piece = lax.all_gather(
        state_delta[None].astype(jnp.bfloat16), "seq", axis=0, tiled=True
    ).astype(jnp.float32)
    piece_rank = jnp.arange(state_piece.shape[0])
    between = (seq_ranks[None, :] > piece_rank[:, None]) & (seq_ranks[None, :] < my_rank)
    logsum = jnp.dot(between.astype(jnp.float32), decay_rows, precision=lax.Precision.HIGHEST)
    factor = jnp.where((piece_rank < my_rank)[:, None], jnp.exp(logsum), 0.0)
    incoming = jnp.zeros_like(state_delta) + jnp.einsum(
        "ih,ihde->hde", factor, state_piece, precision=lax.Precision.HIGHEST
    )
    inter_part = (
        jnp.exp(cumulative)[:, :, None]
        * jnp.einsum(
            "thd,hde->the", queries.astype(jnp.float32), incoming, precision=lax.Precision.HIGHEST
        )
        / head_size
    )
    attended = intra_part + inter_part
    inverse_rms = lax.rsqrt(jnp.mean(attended * attended, axis=-1, keepdims=True) + 1e-06)
    gain_f32 = norm_gain.astype(jnp.float32).reshape(head_count, head_size)
    normed = (
        (attended * inverse_rms * gain_f32)
        .astype(jnp.bfloat16)
        .reshape(tok_count, head_count * head_size)
    )
    own_mixed = lax.psum_scatter(
        jnp.dot(normed, w_out, preferred_element_type=jnp.float32),
        "exp",
        scatter_dimension=0,
        tiled=True,
    ).astype(jnp.bfloat16)
    mixed = lax.all_gather(own_mixed, "exp", axis=0, tiled=True)
    logits = jnp.dot(mixed, router, preferred_element_type=jnp.float32)
    member = routes[:, :, None] == jnp.arange(expert_count)[None, None, :]
    picked = jnp.sum(jnp.where(member, logits[:, None, :], 0.0), axis=-1)
    raised = jnp.exp(picked)
    gate_probs = raised / jnp.sum(raised, axis=-1, keepdims=True)
    my_expert = lax.axis_index("exp") // slice_count
    flat_hit = (routes.reshape(-1) == my_expert).astype(jnp.int32)
    slot_flat = jnp.cumsum(flat_hit) - flat_hit
    slot_match = (slot_flat[:, None] == jnp.arange(capacity)[None, :]) & (flat_hit[:, None] > 0)
    token_select = jnp.sum(
        slot_match.reshape(tok_count, top_count, capacity).astype(jnp.float32), axis=1
    )
    token_gate = jnp.sum(jnp.where(routes == my_expert, gate_probs, 0.0), axis=1)
    slot_rows = jnp.dot(
        token_select.astype(jnp.bfloat16).T, mixed, preferred_element_type=jnp.float32
    ).astype(jnp.bfloat16)
    gate_part = jnp.dot(slot_rows, w_gate[0], preferred_element_type=jnp.float32)
    up_part = jnp.dot(slot_rows, w_up[0], preferred_element_type=jnp.float32)
    hidden = (jax.nn.silu(gate_part) * up_part).astype(jnp.bfloat16)
    slice_out = jnp.dot(hidden, w_down[0], preferred_element_type=jnp.float32)
    spread_out = jnp.dot(token_select, slice_out, precision=lax.Precision.HIGHEST)
    summed = lax.psum_scatter(
        token_gate[:, None] * spread_out, "exp", scatter_dimension=0, tiled=True
    )
    return (own_mixed.astype(jnp.float32) + summed).astype(jnp.bfloat16)


def iota2(shape, axis):
    return lax.broadcasted_iota(jnp.int32, shape, axis)


def cumulate(decay_row):
    t = decay_row.shape[1]
    row, col = iota2((t, t), 0), iota2((t, t), 1)
    spread = jnp.broadcast_to(decay_row, (t, t))
    column = jnp.sum(jnp.where(col <= row, spread, 0.0), axis=1, keepdims=True)
    own = jnp.sum(jnp.where(col == row, spread, 0.0), axis=1, keepdims=True)
    line = jnp.sum(jnp.where(row <= col, own, 0.0), axis=0, keepdims=True)
    return column, line


def dot_f32(a, b, dims):
    return lax.dot_general(a, b, (dims, ((), ())), preferred_element_type=F32)


def split_dot(a_f32, b, dims):
    high = a_f32.astype(BF16)
    low = (a_f32 - high.astype(F32)).astype(BF16)
    return dot_f32(high, b, dims) + dot_f32(low, b, dims)


def dma_in(sems, pairs):
    copies = [pltpu.make_async_copy(a, b, sems.at[i]) for i, (a, b) in enumerate(pairs)]
    for copy in copies:
        copy.start()
    return copies


def put_state(out_ref, state, total):
    d = state.shape[1]
    out_ref[0:d, :] = state.astype(BF16)
    wide = jnp.broadcast_to(total, (TILE_ROWS, d))
    part0 = wide.astype(BF16).astype(F32)
    part1 = (wide - part0).astype(BF16).astype(F32)
    part2 = wide - part0 - part1
    row = iota2((TILE_ROWS, d), 0)
    parts = jnp.where(row == 0, part0, jnp.where(row == 1, part1, jnp.where(row == 2, part2, 0.0)))
    out_ref[d:, :] = parts.astype(BF16)


def get_state(ref):
    d = ref.shape[1]
    return ref[0:d, :].astype(F32), jnp.sum(ref[d:, :].astype(F32), axis=0, keepdims=True)


def state_kernel(key_hbm, value_hbm, decay_hbm, out_ref, key_ref, value_ref, decay_ref, sems):
    t, d = key_ref.shape
    copies = dma_in(sems, [(decay_hbm, decay_ref), (key_hbm, key_ref), (value_hbm, value_ref)])
    for copy in copies:
        copy.wait()
    column, _ = cumulate(decay_ref[...])
    total = column[t - 1 :, :]
    keyed = key_ref[...].astype(F32) * jnp.exp(total - column)
    put_state(out_ref, split_dot(keyed, value_ref[...], ((0,), (0,))), jnp.broadcast_to(total, (1, d)))


def within_kernel(
    query_hbm, key_hbm, value_hbm, decay_hbm, gain_hbm, w_out_hbm, _,
    intra_ref, grown_ref, query_ref, gain_ref, w_out_ref,
    key_ref, value_ref, decay_ref, gain_in_ref, sems,
):
    t, d = query_ref.shape
    copies = dma_in(
        sems,
        [
            (decay_hbm, decay_ref),
            (query_hbm, query_ref),
            (key_hbm, key_ref),
            (value_hbm, value_ref),
            (gain_hbm, gain_in_ref),
            (w_out_hbm, w_out_ref),
        ],
    )
    for copy in copies[:5]:
        copy.wait()
    column, line = cumulate(decay_ref[...])
    query, key, value = query_ref[...], key_ref[...], value_ref[...]
    scores = dot_f32(query, key, ((1,), (1,)))
    causal = iota2((t, t), 0) >= iota2((t, t), 1)
    weights = jnp.where(causal, jnp.exp(jnp.where(causal, column - line, 0.0)), 0.0)
    attend = (scores * weights * (1.0 / d)).astype(BF16)
    intra_ref[...] = dot_f32(attend, value, ((1,), (0,)))
    grown_ref[...] = jnp.broadcast_to(jnp.exp(column) * (1.0 / d), (t, d))
    gain_ref[...] = jnp.broadcast_to(gain_in_ref[...].astype(F32), gain_ref.shape)
    copies[5].wait()


def place_matrix(rows, n_pair, core):
    size = 2 * n_pair * rows
    i, j = iota2((size, size), 0), iota2((size, size), 1)
    half, inner = i // (n_pair * rows), i % (n_pair * rows)
    who = inner // rows
    source = (2 * who + (core + half) % 2) * rows + inner % rows
    return jnp.where(source == j, 1.0, 0.0).astype(BF16)


def fetch_in_kernel(
    n_pair, router_hbm, routes_hbm, gate_hbm, up_hbm, _, in_ref, member_ref, router_ref, routes_ref, sems
):
    hid = gate_hbm.shape[0]
    copies = dma_in(
        sems,
        [
            (router_hbm, router_ref),
            (routes_hbm, routes_ref),
            (gate_hbm, in_ref.at[0:hid]),
            (up_hbm, in_ref.at[hid : 2 * hid]),
        ],
    )
    for copy in copies[:2]:
        copy.wait()
    experts, t = router_ref.shape[0], routes_ref.shape[1]
    in_ref[2 * hid :, :] = jnp.zeros((TILE_ROWS, in_ref.shape[1]), BF16)
    in_ref[2 * hid : 2 * hid + experts, :] = router_ref[...]
    padded = member_ref.shape[0]
    hits = jnp.zeros((padded, t), F32)
    for k in range(routes_ref.shape[0]):
        hits = hits + jnp.where(routes_ref[k : k + 1, :] == iota2((padded, t), 0), 1.0, 0.0)
    place = place_matrix(t // (2 * n_pair), n_pair, lax.axis_index("exp") % 2)
    member_ref[...] = dot_f32(hits.astype(BF16), place, ((1,), (1,)))
    for copy in copies[2:]:
        copy.wait()


def fetch_down_kernel(down_hbm, _, down_ref, sem):
    copy = pltpu.make_async_copy(down_hbm, down_ref, sem)
    copy.start()
    copy.wait()


def project_kernel(n_pair, moves, *refs):
    states = refs[: len(moves)]
    intra_ref, grown_ref, query_ref, gain_ref, w_ref, mine_ref, theirs_ref = refs[len(moves) :]
    t, d = query_ref.shape
    me = lax.axis_index("seq")
    ranks = [move(me) for move in moves]
    parts = [get_state(ref) for ref in states]
    incoming = jnp.zeros((d, d), F32)
    for rank, (state, _) in zip(ranks, parts):
        logsum = jnp.zeros((1, d), F32)
        for other, (_, total) in zip(ranks, parts):
            logsum = logsum + jnp.where(jnp.logical_and(rank < other, other < me), total, 0.0)
        incoming = incoming + jnp.where(rank < me, jnp.exp(logsum), 0.0) * state
    high = incoming.astype(BF16)
    low = (incoming - high.astype(F32)).astype(BF16)
    query = query_ref[...]
    read = dot_f32(query, high, ((1,), (0,))) + dot_f32(query, low, ((1,), (0,)))
    attended = intra_ref[...] + grown_ref[...] * read
    inverse = lax.rsqrt(jnp.mean(attended * attended, axis=1, keepdims=True) + 1e-06)
    normed = (attended * inverse * gain_ref[0:1, :]).astype(BF16)
    exp_index = lax.axis_index("exp")
    place = place_matrix(t // (2 * n_pair), n_pair, exp_index % 2)
    normed = dot_f32(place, normed, ((1,), (0,))).astype(BF16)
    for at in chunks(w_ref.shape[1]):
        part = dot_f32(normed, w_ref[:, at], ((1,), (0,))).astype(BF16)
        mine_ref[:, at] = part[: t // 2]
        theirs_ref[:, at] = part[t // 2 :]


def chunks(width):
    size = min(width, COLUMNS)
    return [slice(i, i + size) for i in range(0, width, size)]


def add_kernel(a_ref, b_ref, *refs):
    refs[-1][...] = (a_ref[...].astype(F32) + b_ref[...].astype(F32)).astype(BF16)


def sum_blocks(count, ref):
    rows = ref.shape[0] // count
    total = ref[0:rows, :].astype(F32)
    for i in range(1, count):
        total = total + ref[i * rows : (i + 1) * rows, :].astype(F32)
    return total


def sum_kernel(count, terms_ref, out_ref, copies_ref):
    total = sum_blocks(count, terms_ref).astype(BF16)
    out_ref[...] = total
    rows = total.shape[0]
    for i in range(count):
        copies_ref[i * rows : (i + 1) * rows, :] = total


def result_kernel(count, terms_ref, mixed_ref, out_ref):
    out_ref[...] = (sum_blocks(count, terms_ref) + mixed_ref[...].astype(F32)).astype(BF16)


def expert_kernel(slices, experts, in_ref, down_ref, member_ref, *refs):
    parts, (mine_ref, theirs_ref) = refs[:-2], refs[-2:]
    hid, width = down_ref.shape
    t = member_ref.shape[1]
    total = dot_f32(in_ref[...], jnp.concatenate([part[...] for part in parts], axis=0), ((1,), (1,)))
    gate, up, logits = total[0:hid], total[hid : 2 * hid], total[2 * hid : 2 * hid + experts]
    raised = jnp.where(member_ref[0:experts, :] > 0.5, jnp.exp(logits), 0.0)
    mine = iota2((experts, t), 0) == lax.axis_index("exp") // slices
    prob = jnp.sum(jnp.where(mine, raised, 0.0), axis=0, keepdims=True) / jnp.sum(raised, axis=0, keepdims=True)
    hidden = (gate / (1.0 + jnp.exp(-gate)) * up * prob).T.astype(BF16)
    for at in chunks(width):
        part = dot_f32(hidden, down_ref[:, at], ((1,), (0,))).astype(BF16)
        mine_ref[:, at] = part[: t // 2]
        theirs_ref[:, at] = part[t // 2 :]


def call(kernel, outs, args, scratch=(), flops=0, far=0):
    whole = pl.BlockSpec(memory_space=pltpu.VMEM)
    size = sum(a.size * a.dtype.itemsize for a in (*args, *outs))
    if far:
        args = [pltpu.with_memory_space_constraint(a, pltpu.HBM) for a in args[:far]] + list(args[far:])
    return pl.pallas_call(
        kernel,
        out_shape=outs,
        in_specs=[pl.BlockSpec(memory_space=pl.ANY) if far else whole] * len(args),
        out_specs=[whole] * len(outs),
        scratch_shapes=list(scratch),
        compiler_params=pltpu.CompilerParams(vmem_limit_bytes=VMEM_LIMIT),
        cost_estimate=pl.CostEstimate(flops=0, bytes_accessed=0, transcendentals=0),
    )(*args)


def local(query, key_in, value, decay_log, norm_gain, w_out, router, routes, w_gate, w_up, w_down):
    t, d = query.shape
    width = w_out.shape[1]
    exp_count, seq_count = lax.axis_size("exp"), lax.axis_size("seq")
    n_pair = exp_count // 2
    rows = t // exp_count
    experts = router.shape[1]
    slices = exp_count // experts
    hid = w_gate.shape[2]
    out = jax.ShapeDtypeStruct
    dma = pltpu.SemaphoreType.DMA

    def trade(x):
        line = [[2 * p + c for p in range(n_pair)] for c in range(2)]
        return lax.all_to_all(x, "exp", 0, 0, axis_index_groups=line, tiled=True)

    def across(x):
        return lax.ppermute(x, "exp", [(e, e ^ 1) for e in range(exp_count)])

    def rows_of(count):
        return out((count * rows, width), BF16)

    decay_row = decay_log.T
    block = pltpu.VMEM((t, d), BF16)
    decay_block = pltpu.VMEM((1, t), F32)
    (state,) = call(
        state_kernel,
        [out((d + TILE_ROWS, d), BF16)],
        (key_in, value, decay_row),
        [block, block, decay_block, dma((3,))],
        far=3,
    )
    moves = [lambda i, k=k: i ^ k for k in range(1, seq_count)]
    states = [lax.ppermute(state, "seq", [(move(i), i) for i in range(seq_count)]) for move in moves]
    intra, grown, query_near, gain, w_out_near = call(
        within_kernel,
        [out((t, d), F32), out((t, d), F32), out((t, d), BF16), out((8, d), F32), out(w_out.shape, BF16)],
        (query, key_in, value, decay_row, norm_gain[None, :], w_out, state),
        [block, block, decay_block, pltpu.VMEM((1, d), BF16), dma((6,))],
        far=6,
    )
    mine, theirs = call(
        functools.partial(project_kernel, n_pair, moves),
        [rows_of(n_pair), rows_of(n_pair)],
        (*states, intra, grown, query_near, gain, w_out_near),
        flops=2 * t * d * width,
    )
    def reduce(mine, theirs, *after):
        return trade(call(add_kernel, [rows_of(n_pair)], (mine, across(theirs), *after))[0])

    w_in, member = call(
        functools.partial(fetch_in_kernel, n_pair),
        [out((2 * hid + TILE_ROWS, width), BF16), out((-(-experts // 8) * 8, t), F32)],
        (router.T, routes.T, w_gate[0].T, w_up[0].T, theirs),
        [pltpu.VMEM((experts, width), BF16), pltpu.VMEM((routes.shape[1], t), jnp.int32), dma((4,))],
        far=4,
    )
    mixed, copies = call(
        functools.partial(sum_kernel, n_pair), [rows_of(1), rows_of(n_pair)], (reduce(mine, theirs, member),)
    )
    own = trade(copies)
    (w_down_near,) = call(fetch_down_kernel, [out((hid, width), BF16)], (w_down[0], own), [dma], far=1)
    mine, theirs = call(
        functools.partial(expert_kernel, slices, experts),
        [rows_of(n_pair)] * 2,
        (w_in, w_down_near, member, own, across(own)),
        flops=6 * t * hid * width,
    )
    return call(functools.partial(result_kernel, n_pair), [rows_of(1)], (reduce(mine, theirs), mixed))[0]


def solution(mesh):
    placed = (
        P("seq", "exp"),
        P("seq", "exp"),
        P("seq", "exp"),
        P("seq", "exp"),
        P("exp"),
        P("exp", None),
        P(),
        P("seq", None),
        P("exp", None, None),
        P("exp", None, None),
        P("exp", None, None),
    )

    def pick(query, key_in, value, decay_log, *rest):
        rows = query.shape[0] // lax.axis_size("exp")
        exp_count = lax.axis_size("exp")
        tiled = rows % TILE_ROWS == 0 and decay_log.shape[1] == 1
        for count in (exp_count, lax.axis_size("seq")):
            tiled = tiled and count >= 4 and count & (count - 1) == 0
        plan = local if tiled else plain_plan
        return plan(query, key_in, value, decay_log, *rest)

    return jax.shard_map(
        pick, mesh=mesh, in_specs=placed, out_specs=P(("seq", "exp"), None), check_vma=False
    )
```

```python
import functools

import jax
import jax.numpy as jnp
from jax import lax
from jax.experimental import pallas as pl
from jax.experimental.pallas import tpu as pltpu
from jax.sharding import PartitionSpec as P

F32 = jnp.float32
BF16 = jnp.bfloat16
TILE_ROWS = 16
COLUMNS = 1024
PARTS = 2
VMEM_LIMIT = 16 * 1024 * 1024


def plain_plan(query, key_in, value, decay_log, norm_gain, w_out, router, routes, w_gate, w_up, w_down):
    tok_count = query.shape[0]
    head_count = decay_log.shape[1]
    head_size = query.shape[1] // head_count
    top_count = routes.shape[1]
    expert_count = router.shape[1]
    capacity = max(2, 3 * tok_count * top_count // (2 * expert_count))
    exp_count = lax.axis_size("exp")
    slice_count = exp_count // expert_count
    queries = query.reshape(tok_count, head_count, head_size)
    keys_local = key_in.reshape(tok_count, head_count, head_size)
    values_local = value.reshape(tok_count, head_count, head_size)
    cumulative = jnp.cumsum(decay_log, axis=0)
    scores = jnp.einsum("thd,shd->hts", queries, keys_local, preferred_element_type=jnp.float32)
    spread = cumulative.T[:, :, None] - cumulative.T[:, None, :]
    causal = jnp.arange(tok_count)[:, None] >= jnp.arange(tok_count)[None, :]
    weights = jnp.where(causal, jnp.exp(jnp.where(causal, spread, 0.0)), 0.0)
    attend = (scores * weights / head_size).astype(jnp.bfloat16)
    intra_part = jnp.einsum(
        "hts,she->the", attend, values_local, preferred_element_type=jnp.float32
    )
    totals = cumulative[-1]
    tail_decay = jnp.exp(totals[None, :] - cumulative)
    state_delta = jnp.einsum(
        "shd,she->hde",
        keys_local.astype(jnp.float32) * tail_decay[:, :, None],
        values_local.astype(jnp.float32),
        precision=lax.Precision.HIGHEST,
    )
    decay_rows = lax.all_gather(totals[None, :], "seq", axis=0, tiled=True)
    my_rank = lax.axis_index("seq")
    seq_ranks = jnp.arange(decay_rows.shape[0])
    state_piece = lax.all_gather(
        state_delta[None].astype(jnp.bfloat16), "seq", axis=0, tiled=True
    ).astype(jnp.float32)
    piece_rank = jnp.arange(state_piece.shape[0])
    between = (seq_ranks[None, :] > piece_rank[:, None]) & (seq_ranks[None, :] < my_rank)
    logsum = jnp.dot(between.astype(jnp.float32), decay_rows, precision=lax.Precision.HIGHEST)
    factor = jnp.where((piece_rank < my_rank)[:, None], jnp.exp(logsum), 0.0)
    incoming = jnp.zeros_like(state_delta) + jnp.einsum(
        "ih,ihde->hde", factor, state_piece, precision=lax.Precision.HIGHEST
    )
    inter_part = (
        jnp.exp(cumulative)[:, :, None]
        * jnp.einsum(
            "thd,hde->the", queries.astype(jnp.float32), incoming, precision=lax.Precision.HIGHEST
        )
        / head_size
    )
    attended = intra_part + inter_part
    inverse_rms = lax.rsqrt(jnp.mean(attended * attended, axis=-1, keepdims=True) + 1e-06)
    gain_f32 = norm_gain.astype(jnp.float32).reshape(head_count, head_size)
    normed = (
        (attended * inverse_rms * gain_f32)
        .astype(jnp.bfloat16)
        .reshape(tok_count, head_count * head_size)
    )
    own_mixed = lax.psum_scatter(
        jnp.dot(normed, w_out, preferred_element_type=jnp.float32),
        "exp",
        scatter_dimension=0,
        tiled=True,
    ).astype(jnp.bfloat16)
    mixed = lax.all_gather(own_mixed, "exp", axis=0, tiled=True)
    logits = jnp.dot(mixed, router, preferred_element_type=jnp.float32)
    member = routes[:, :, None] == jnp.arange(expert_count)[None, None, :]
    picked = jnp.sum(jnp.where(member, logits[:, None, :], 0.0), axis=-1)
    raised = jnp.exp(picked)
    gate_probs = raised / jnp.sum(raised, axis=-1, keepdims=True)
    my_expert = lax.axis_index("exp") // slice_count
    flat_hit = (routes.reshape(-1) == my_expert).astype(jnp.int32)
    slot_flat = jnp.cumsum(flat_hit) - flat_hit
    slot_match = (slot_flat[:, None] == jnp.arange(capacity)[None, :]) & (flat_hit[:, None] > 0)
    token_select = jnp.sum(
        slot_match.reshape(tok_count, top_count, capacity).astype(jnp.float32), axis=1
    )
    token_gate = jnp.sum(jnp.where(routes == my_expert, gate_probs, 0.0), axis=1)
    slot_rows = jnp.dot(
        token_select.astype(jnp.bfloat16).T, mixed, preferred_element_type=jnp.float32
    ).astype(jnp.bfloat16)
    gate_part = jnp.dot(slot_rows, w_gate[0], preferred_element_type=jnp.float32)
    up_part = jnp.dot(slot_rows, w_up[0], preferred_element_type=jnp.float32)
    hidden = (jax.nn.silu(gate_part) * up_part).astype(jnp.bfloat16)
    slice_out = jnp.dot(hidden, w_down[0], preferred_element_type=jnp.float32)
    spread_out = jnp.dot(token_select, slice_out, precision=lax.Precision.HIGHEST)
    summed = lax.psum_scatter(
        token_gate[:, None] * spread_out, "exp", scatter_dimension=0, tiled=True
    )
    return (own_mixed.astype(jnp.float32) + summed).astype(jnp.bfloat16)


def iota2(shape, axis):
    return lax.broadcasted_iota(jnp.int32, shape, axis)


def cumulate(decay_row):
    t = decay_row.shape[1]
    row, col = iota2((t, t), 0), iota2((t, t), 1)
    spread = jnp.broadcast_to(decay_row, (t, t))
    column = jnp.sum(jnp.where(col <= row, spread, 0.0), axis=1, keepdims=True)
    own = jnp.sum(jnp.where(col == row, spread, 0.0), axis=1, keepdims=True)
    line = jnp.sum(jnp.where(row <= col, own, 0.0), axis=0, keepdims=True)
    return column, line


def dot_f32(a, b, dims):
    return lax.dot_general(a, b, (dims, ((), ())), preferred_element_type=F32)


def split_dot(a_f32, b, dims):
    high = a_f32.astype(BF16)
    low = (a_f32 - high.astype(F32)).astype(BF16)
    return dot_f32(high, b, dims) + dot_f32(low, b, dims)


def dma_in(sems, pairs):
    copies = [pltpu.make_async_copy(a, b, sems.at[i]) for i, (a, b) in enumerate(pairs)]
    for copy in copies:
        copy.start()
    return copies


def put_state(out_ref, state, total):
    d = state.shape[1]
    out_ref[0:d, :] = state.astype(BF16)
    wide = jnp.broadcast_to(total, (TILE_ROWS, d))
    part0 = wide.astype(BF16).astype(F32)
    part1 = (wide - part0).astype(BF16).astype(F32)
    part2 = wide - part0 - part1
    row = iota2((TILE_ROWS, d), 0)
    parts = jnp.where(row == 0, part0, jnp.where(row == 1, part1, jnp.where(row == 2, part2, 0.0)))
    out_ref[d:, :] = parts.astype(BF16)


def get_state(ref):
    d = ref.shape[1]
    return ref[0:d, :].astype(F32), jnp.sum(ref[d:, :].astype(F32), axis=0, keepdims=True)


def state_kernel(key_hbm, value_hbm, decay_hbm, out_ref, key_ref, value_ref, decay_ref, sems):
    t, d = key_ref.shape
    copies = dma_in(sems, [(decay_hbm, decay_ref), (key_hbm, key_ref), (value_hbm, value_ref)])
    for copy in copies:
        copy.wait()
    column, _ = cumulate(decay_ref[...])
    total = column[t - 1 :, :]
    keyed = key_ref[...].astype(F32) * jnp.exp(total - column)
    put_state(out_ref, split_dot(keyed, value_ref[...], ((0,), (0,))), jnp.broadcast_to(total, (1, d)))


def within_kernel(
    query_hbm, key_hbm, value_hbm, decay_hbm, gain_hbm, w_out_hbm, _,
    intra_ref, grown_ref, query_ref, gain_ref, w_out_ref,
    key_ref, value_ref, decay_ref, gain_in_ref, sems,
):
    t, d = query_ref.shape
    copies = dma_in(
        sems,
        [
            (decay_hbm, decay_ref),
            (query_hbm, query_ref),
            (key_hbm, key_ref),
            (value_hbm, value_ref),
            (gain_hbm, gain_in_ref),
            (w_out_hbm, w_out_ref),
        ],
    )
    for copy in copies[:5]:
        copy.wait()
    column, line = cumulate(decay_ref[...])
    query, key, value = query_ref[...], key_ref[...], value_ref[...]
    scores = dot_f32(query, key, ((1,), (1,)))
    causal = iota2((t, t), 0) >= iota2((t, t), 1)
    weights = jnp.where(causal, jnp.exp(jnp.where(causal, column - line, 0.0)), 0.0)
    attend = (scores * weights * (1.0 / d)).astype(BF16)
    intra_ref[...] = dot_f32(attend, value, ((1,), (0,)))
    grown_ref[...] = jnp.broadcast_to(jnp.exp(column) * (1.0 / d), (t, d))
    gain_ref[...] = jnp.broadcast_to(gain_in_ref[...].astype(F32), gain_ref.shape)
    copies[5].wait()


def place_matrix(rows, n_pair, pair, core):
    size = 2 * n_pair * rows
    i, j = iota2((size, size), 0), iota2((size, size), 1)
    half, inner = i // (n_pair * rows), i % (n_pair * rows)
    who = (inner // rows + pair) % n_pair
    source = (2 * who + (core + half) % 2) * rows + inner % rows
    return jnp.where(source == j, 1.0, 0.0).astype(BF16)


def fetch_kernel(
    n_pair, router_hbm, routes_hbm, gate_hbm, up_hbm, down_hbm, _,
    in_ref, down_ref, member_ref, router_ref, routes_ref, sems,
):
    hid = gate_hbm.shape[0]
    copies = dma_in(
        sems,
        [
            (router_hbm, router_ref),
            (routes_hbm, routes_ref),
            (gate_hbm, in_ref.at[0:hid]),
            (up_hbm, in_ref.at[hid : 2 * hid]),
            (down_hbm, down_ref),
        ],
    )
    for copy in copies[:2]:
        copy.wait()
    experts, t = router_ref.shape[0], routes_ref.shape[1]
    rows = t // (2 * n_pair)
    in_ref[2 * hid :, :] = jnp.zeros((TILE_ROWS, in_ref.shape[1]), BF16)
    in_ref[2 * hid : 2 * hid + experts, :] = router_ref[...]
    padded = member_ref.shape[0]
    hits = jnp.zeros((padded, t), F32)
    for k in range(routes_ref.shape[0]):
        hits = hits + jnp.where(routes_ref[k : k + 1, :] == iota2((padded, t), 0), 1.0, 0.0)
    exp_index = lax.axis_index("exp")
    place = place_matrix(rows, n_pair, exp_index // 2, exp_index % 2)
    member_ref[...] = dot_f32(hits.astype(BF16), place, ((1,), (1,)))
    for copy in copies[2:]:
        copy.wait()


def normed_kernel(n_pair, moves, *refs):
    states = refs[: len(moves)]
    intra_ref, grown_ref, query_ref, gain_ref, out_ref = refs[len(moves) :]
    t, d = query_ref.shape
    me = lax.axis_index("seq")
    ranks = [move(me) for move in moves]
    parts = [get_state(ref) for ref in states]
    incoming = jnp.zeros((d, d), F32)
    for rank, (state, _) in zip(ranks, parts):
        logsum = jnp.zeros((1, d), F32)
        for other, (_, total) in zip(ranks, parts):
            logsum = logsum + jnp.where(jnp.logical_and(rank < other, other < me), total, 0.0)
        incoming = incoming + jnp.where(rank < me, jnp.exp(logsum), 0.0) * state
    high = incoming.astype(BF16)
    low = (incoming - high.astype(F32)).astype(BF16)
    query = query_ref[...]
    read = dot_f32(query, high, ((1,), (0,))) + dot_f32(query, low, ((1,), (0,)))
    attended = intra_ref[...] + grown_ref[...] * read
    inverse = lax.rsqrt(jnp.mean(attended * attended, axis=1, keepdims=True) + 1e-06)
    normed = (attended * inverse * gain_ref[0:1, :]).astype(BF16)
    exp_index = lax.axis_index("exp")
    place = place_matrix(t // (2 * n_pair), n_pair, exp_index // 2, exp_index % 2)
    out_ref[...] = dot_f32(place, normed, ((1,), (0,))).astype(BF16)


def product_kernel(at, x_ref, w_ref, mine_ref, theirs_ref):
    half = mine_ref.shape[0]
    for i in range(at.start, at.stop, COLUMNS):
        part = dot_f32(x_ref[...], w_ref[:, i : i + COLUMNS], ((1,), (0,))).astype(BF16)
        mine_ref[:, i - at.start : i - at.start + COLUMNS] = part[:half]
        theirs_ref[:, i - at.start : i - at.start + COLUMNS] = part[half:]


def add_kernel(groups, a_ref, b_ref, *refs):
    outs = refs[-len(groups) :]
    rows = outs[0].shape[0] // len(groups[0])
    for group, ref in zip(groups, outs):
        for i, block in enumerate(group):
            at = slice(block * rows, (block + 1) * rows)
            total = a_ref[at, :].astype(F32) + b_ref[at, :].astype(F32)
            ref[i * rows : (i + 1) * rows, :] = total.astype(ref.dtype)


def sum_kernel(count, *refs):
    total = refs[0][...].astype(F32)
    for ref in refs[1:count]:
        total = total + ref[...].astype(F32)
    refs[-1][...] = total.astype(BF16)


def join_kernel(*refs):
    start = 0
    for ref in refs[:-1]:
        refs[-1][start : start + ref.shape[0], :] = ref[...]
        start += ref.shape[0]


def enter_part(at, in_ref, own_ref, other_ref):
    x = jnp.concatenate([own_ref[...], other_ref[...]], axis=0)
    return dot_f32(in_ref[:, at], x, ((1,), (1,)))


def enter_kernel(at, in_ref, own_ref, other_ref, out_ref):
    out_ref[...] = enter_part(at, in_ref, own_ref, other_ref)


def hidden_kernel(at, slices, experts, in_ref, own_ref, other_ref, before_ref, member_ref, out_ref):
    total = before_ref[...] + enter_part(at, in_ref, own_ref, other_ref)
    t, hid = out_ref.shape
    gate, up, logits = total[0:hid], total[hid : 2 * hid], total[2 * hid : 2 * hid + experts]
    raised = jnp.where(member_ref[0:experts, :] > 0.5, jnp.exp(logits), 0.0)
    mine = iota2((experts, t), 0) == lax.axis_index("exp") // slices
    prob = jnp.sum(jnp.where(mine, raised, 0.0), axis=0, keepdims=True) / jnp.sum(raised, axis=0, keepdims=True)
    out_ref[...] = (gate / (1.0 + jnp.exp(-gate)) * up * prob).T.astype(BF16)


def result_kernel(count, *refs):
    out_ref = refs[-1]
    width = refs[0].shape[1]
    for i in range(len(refs) // count):
        total = refs[i * count][...].astype(F32)
        for ref in refs[i * count + 1 : (i + 1) * count]:
            total = total + ref[...].astype(F32)
        out_ref[:, i * width : (i + 1) * width] = total.astype(BF16)


def call(kernel, outs, args, scratch=(), far=0):
    whole = pl.BlockSpec(memory_space=pltpu.VMEM)
    if far:
        args = [pltpu.with_memory_space_constraint(a, pltpu.HBM) for a in args[:far]] + list(args[far:])
    return pl.pallas_call(
        kernel,
        out_shape=outs,
        in_specs=[pl.BlockSpec(memory_space=pl.ANY) if far else whole] * len(args),
        out_specs=[whole] * len(outs),
        scratch_shapes=list(scratch),
        compiler_params=pltpu.CompilerParams(vmem_limit_bytes=VMEM_LIMIT),
        cost_estimate=pl.CostEstimate(flops=0, bytes_accessed=0, transcendentals=0),
    )(*args)


def local(query, key_in, value, decay_log, norm_gain, w_out, router, routes, w_gate, w_up, w_down):
    t, d = query.shape
    width = w_out.shape[1]
    exp_count, seq_count = lax.axis_size("exp"), lax.axis_size("seq")
    n_pair = exp_count // 2
    rows = t // exp_count
    experts = router.shape[1]
    slices = exp_count // experts
    hid = w_gate.shape[2]
    out = jax.ShapeDtypeStruct
    dma = pltpu.SemaphoreType.DMA

    def shift(x, r):
        return lax.ppermute(x, "exp", [(e, (e + 2 * r) % exp_count) for e in range(exp_count)])

    def across(x):
        return lax.ppermute(x, "exp", [(e, e ^ 1) for e in range(exp_count)])

    size = width // PARTS
    ranges = [slice(i * size, (i + 1) * size) for i in range(PARTS)]

    def rows_of(count):
        return out((count * rows, size), BF16)

    def reduce(products):
        others = [across(theirs) for _, theirs in products]
        terms = [
            call(functools.partial(add_kernel, [[r] for r in range(n_pair)]), [rows_of(1)] * n_pair, (mine, other))
            for (mine, _), other in zip(products, others)
        ]
        return [[term[0]] + [shift(term[r], r) for r in range(1, n_pair)] for term in terms], terms[-1][-1]

    def products_of(x, w):
        return [call(functools.partial(product_kernel, at), [rows_of(n_pair)] * 2, (x, w)) for at in ranges]

    decay_row = decay_log.T
    block = pltpu.VMEM((t, d), BF16)
    decay_block = pltpu.VMEM((1, t), F32)
    (state,) = call(
        state_kernel,
        [out((d + TILE_ROWS, d), BF16)],
        (key_in, value, decay_row),
        [block, block, decay_block, dma((3,))],
        far=3,
    )
    moves = [lambda i, k=k: i ^ k for k in range(1, seq_count)]
    states = [lax.ppermute(state, "seq", [(move(i), i) for i in range(seq_count)]) for move in moves]
    intra, grown, query_near, gain, w_out_near = call(
        within_kernel,
        [out((t, d), F32), out((t, d), F32), out((t, d), BF16), out((8, d), F32), out(w_out.shape, BF16)],
        (query, key_in, value, decay_row, norm_gain[None, :], w_out, state),
        [block, block, decay_block, pltpu.VMEM((1, d), BF16), dma((6,))],
        far=6,
    )
    (normed,) = call(
        functools.partial(normed_kernel, n_pair, moves),
        [out((t, d), BF16)],
        (*states, intra, grown, query_near, gain),
    )
    terms, last = reduce(products_of(normed, w_out_near))
    w_in, w_down_near, member = call(
        functools.partial(fetch_kernel, n_pair),
        [
            out((2 * hid + TILE_ROWS, width), BF16),
            out((hid, width), BF16),
            out((-(-experts // 8) * 8, t), F32),
        ],
        (router.T, routes.T, w_gate[0].T, w_up[0].T, w_down[0], last),
        [pltpu.VMEM((experts, width), BF16), pltpu.VMEM((routes.shape[1], t), jnp.int32), dma((5,))],
        far=5,
    )
    mixed = [call(functools.partial(sum_kernel, n_pair), [rows_of(1)], (*term, member))[0] for term in terms]
    gathered = [[shift(m, -r) if r else m for r in range(n_pair)] for m in mixed]
    own = [call(join_kernel, [rows_of(n_pair)], blocks)[0] for blocks in gathered]
    total = ()
    for at, x in zip(ranges, own):
        if at.stop < width:
            kernel, shape = functools.partial(enter_kernel, at), out((w_in.shape[0], t), F32)
        else:
            kernel, shape = functools.partial(hidden_kernel, at, slices, experts), out((t, hid), BF16)
            total = (*total, member)
        total = call(kernel, [shape], (w_in, x, across(x), *total))
    sums, _ = reduce(products_of(total[0], w_down_near))
    args = [x for some, m in zip(sums, mixed) for x in (*some, m)]
    return call(functools.partial(result_kernel, n_pair + 1), [out((rows, width), BF16)], args)[0]


def solution(mesh):
    placed = (
        P("seq", "exp"),
        P("seq", "exp"),
        P("seq", "exp"),
        P("seq", "exp"),
        P("exp"),
        P("exp", None),
        P(),
        P("seq", None),
        P("exp", None, None),
        P("exp", None, None),
        P("exp", None, None),
    )

    def pick(query, key_in, value, decay_log, *rest):
        rows = query.shape[0] // lax.axis_size("exp")
        exp_count = lax.axis_size("exp")
        tiled = rows % TILE_ROWS == 0 and decay_log.shape[1] == 1
        for count in (exp_count, lax.axis_size("seq")):
            tiled = tiled and count >= 4 and count & (count - 1) == 0
        plan = local if tiled else plain_plan
        return plan(query, key_in, value, decay_log, *rest)

    return jax.shard_map(
        pick, mesh=mesh, in_specs=placed, out_specs=P(("seq", "exp"), None), check_vma=False
    )
```

```python
import functools

import jax
import jax.numpy as jnp
from jax import lax
from jax.experimental import pallas as pl
from jax.experimental.pallas import tpu as pltpu
from jax.sharding import PartitionSpec as P

F32 = jnp.float32
BF16 = jnp.bfloat16
TILE_ROWS = 16
COLUMNS = 1024
VMEM_LIMIT = 16 * 1024 * 1024


def plain_plan(query, key_in, value, decay_log, norm_gain, w_out, router, routes, w_gate, w_up, w_down):
    tok_count = query.shape[0]
    head_count = decay_log.shape[1]
    head_size = query.shape[1] // head_count
    top_count = routes.shape[1]
    expert_count = router.shape[1]
    capacity = max(2, 3 * tok_count * top_count // (2 * expert_count))
    exp_count = lax.axis_size("exp")
    slice_count = exp_count // expert_count
    queries = query.reshape(tok_count, head_count, head_size)
    keys_local = key_in.reshape(tok_count, head_count, head_size)
    values_local = value.reshape(tok_count, head_count, head_size)
    cumulative = jnp.cumsum(decay_log, axis=0)
    scores = jnp.einsum("thd,shd->hts", queries, keys_local, preferred_element_type=jnp.float32)
    spread = cumulative.T[:, :, None] - cumulative.T[:, None, :]
    causal = jnp.arange(tok_count)[:, None] >= jnp.arange(tok_count)[None, :]
    weights = jnp.where(causal, jnp.exp(jnp.where(causal, spread, 0.0)), 0.0)
    attend = (scores * weights / head_size).astype(jnp.bfloat16)
    intra_part = jnp.einsum(
        "hts,she->the", attend, values_local, preferred_element_type=jnp.float32
    )
    totals = cumulative[-1]
    tail_decay = jnp.exp(totals[None, :] - cumulative)
    state_delta = jnp.einsum(
        "shd,she->hde",
        keys_local.astype(jnp.float32) * tail_decay[:, :, None],
        values_local.astype(jnp.float32),
        precision=lax.Precision.HIGHEST,
    )
    decay_rows = lax.all_gather(totals[None, :], "seq", axis=0, tiled=True)
    my_rank = lax.axis_index("seq")
    seq_ranks = jnp.arange(decay_rows.shape[0])
    state_piece = lax.all_gather(
        state_delta[None].astype(jnp.bfloat16), "seq", axis=0, tiled=True
    ).astype(jnp.float32)
    piece_rank = jnp.arange(state_piece.shape[0])
    between = (seq_ranks[None, :] > piece_rank[:, None]) & (seq_ranks[None, :] < my_rank)
    logsum = jnp.dot(between.astype(jnp.float32), decay_rows, precision=lax.Precision.HIGHEST)
    factor = jnp.where((piece_rank < my_rank)[:, None], jnp.exp(logsum), 0.0)
    incoming = jnp.zeros_like(state_delta) + jnp.einsum(
        "ih,ihde->hde", factor, state_piece, precision=lax.Precision.HIGHEST
    )
    inter_part = (
        jnp.exp(cumulative)[:, :, None]
        * jnp.einsum(
            "thd,hde->the", queries.astype(jnp.float32), incoming, precision=lax.Precision.HIGHEST
        )
        / head_size
    )
    attended = intra_part + inter_part
    inverse_rms = lax.rsqrt(jnp.mean(attended * attended, axis=-1, keepdims=True) + 1e-06)
    gain_f32 = norm_gain.astype(jnp.float32).reshape(head_count, head_size)
    normed = (
        (attended * inverse_rms * gain_f32)
        .astype(jnp.bfloat16)
        .reshape(tok_count, head_count * head_size)
    )
    own_mixed = lax.psum_scatter(
        jnp.dot(normed, w_out, preferred_element_type=jnp.float32),
        "exp",
        scatter_dimension=0,
        tiled=True,
    ).astype(jnp.bfloat16)
    mixed = lax.all_gather(own_mixed, "exp", axis=0, tiled=True)
    logits = jnp.dot(mixed, router, preferred_element_type=jnp.float32)
    member = routes[:, :, None] == jnp.arange(expert_count)[None, None, :]
    picked = jnp.sum(jnp.where(member, logits[:, None, :], 0.0), axis=-1)
    raised = jnp.exp(picked)
    gate_probs = raised / jnp.sum(raised, axis=-1, keepdims=True)
    my_expert = lax.axis_index("exp") // slice_count
    flat_hit = (routes.reshape(-1) == my_expert).astype(jnp.int32)
    slot_flat = jnp.cumsum(flat_hit) - flat_hit
    slot_match = (slot_flat[:, None] == jnp.arange(capacity)[None, :]) & (flat_hit[:, None] > 0)
    token_select = jnp.sum(
        slot_match.reshape(tok_count, top_count, capacity).astype(jnp.float32), axis=1
    )
    token_gate = jnp.sum(jnp.where(routes == my_expert, gate_probs, 0.0), axis=1)
    slot_rows = jnp.dot(
        token_select.astype(jnp.bfloat16).T, mixed, preferred_element_type=jnp.float32
    ).astype(jnp.bfloat16)
    gate_part = jnp.dot(slot_rows, w_gate[0], preferred_element_type=jnp.float32)
    up_part = jnp.dot(slot_rows, w_up[0], preferred_element_type=jnp.float32)
    hidden = (jax.nn.silu(gate_part) * up_part).astype(jnp.bfloat16)
    slice_out = jnp.dot(hidden, w_down[0], preferred_element_type=jnp.float32)
    spread_out = jnp.dot(token_select, slice_out, precision=lax.Precision.HIGHEST)
    summed = lax.psum_scatter(
        token_gate[:, None] * spread_out, "exp", scatter_dimension=0, tiled=True
    )
    return (own_mixed.astype(jnp.float32) + summed).astype(jnp.bfloat16)


def iota2(shape, axis):
    return lax.broadcasted_iota(jnp.int32, shape, axis)


def cumulate(decay_row):
    t = decay_row.shape[1]
    row, col = iota2((t, t), 0), iota2((t, t), 1)
    spread = jnp.broadcast_to(decay_row, (t, t))
    column = jnp.sum(jnp.where(col <= row, spread, 0.0), axis=1, keepdims=True)
    own = jnp.sum(jnp.where(col == row, spread, 0.0), axis=1, keepdims=True)
    line = jnp.sum(jnp.where(row <= col, own, 0.0), axis=0, keepdims=True)
    return column, line


def dot_f32(a, b, dims):
    return lax.dot_general(a, b, (dims, ((), ())), preferred_element_type=F32)


def split_dot(a_f32, b, dims):
    high = a_f32.astype(BF16)
    low = (a_f32 - high.astype(F32)).astype(BF16)
    return dot_f32(high, b, dims) + dot_f32(low, b, dims)


def dma_in(sems, pairs):
    copies = [pltpu.make_async_copy(a, b, sems.at[i]) for i, (a, b) in enumerate(pairs)]
    for copy in copies:
        copy.start()
    return copies


def put_state(out_ref, state, total):
    d = state.shape[1]
    out_ref[0:d, :] = state.astype(BF16)
    wide = jnp.broadcast_to(total, (TILE_ROWS, d))
    part0 = wide.astype(BF16).astype(F32)
    part1 = (wide - part0).astype(BF16).astype(F32)
    part2 = wide - part0 - part1
    row = iota2((TILE_ROWS, d), 0)
    parts = jnp.where(row == 0, part0, jnp.where(row == 1, part1, jnp.where(row == 2, part2, 0.0)))
    out_ref[d:, :] = parts.astype(BF16)


def get_state(ref):
    d = ref.shape[1]
    return ref[0:d, :].astype(F32), jnp.sum(ref[d:, :].astype(F32), axis=0, keepdims=True)


def state_kernel(key_hbm, value_hbm, decay_hbm, out_ref, key_ref, value_ref, decay_ref, sems):
    t, d = key_ref.shape
    copies = dma_in(sems, [(decay_hbm, decay_ref), (key_hbm, key_ref), (value_hbm, value_ref)])
    for copy in copies:
        copy.wait()
    column, _ = cumulate(decay_ref[...])
    total = column[t - 1 :, :]
    keyed = key_ref[...].astype(F32) * jnp.exp(total - column)
    put_state(out_ref, split_dot(keyed, value_ref[...], ((0,), (0,))), jnp.broadcast_to(total, (1, d)))


def within_kernel(
    query_hbm, key_hbm, value_hbm, decay_hbm, gain_hbm, w_out_hbm, _,
    intra_ref, grown_ref, query_ref, gain_ref, w_out_ref,
    key_ref, value_ref, decay_ref, gain_in_ref, sems,
):
    t, d = query_ref.shape
    copies = dma_in(
        sems,
        [
            (decay_hbm, decay_ref),
            (query_hbm, query_ref),
            (key_hbm, key_ref),
            (value_hbm, value_ref),
            (gain_hbm, gain_in_ref),
            (w_out_hbm, w_out_ref),
        ],
    )
    for copy in copies[:5]:
        copy.wait()
    column, line = cumulate(decay_ref[...])
    query, key, value = query_ref[...], key_ref[...], value_ref[...]
    scores = dot_f32(query, key, ((1,), (1,)))
    causal = iota2((t, t), 0) >= iota2((t, t), 1)
    weights = jnp.where(causal, jnp.exp(jnp.where(causal, column - line, 0.0)), 0.0)
    attend = (scores * weights * (1.0 / d)).astype(BF16)
    intra_ref[...] = dot_f32(attend, value, ((1,), (0,)))
    grown_ref[...] = jnp.broadcast_to(jnp.exp(column) * (1.0 / d), (t, d))
    gain_ref[...] = jnp.broadcast_to(gain_in_ref[...].astype(F32), gain_ref.shape)
    copies[5].wait()


def place_matrix(rows, n_pair, pair, core):
    size = 2 * n_pair * rows
    i, j = iota2((size, size), 0), iota2((size, size), 1)
    half, inner = i // (n_pair * rows), i % (n_pair * rows)
    who = jnp.bitwise_xor(inner // rows, pair)
    source = (2 * who + (core + half) % 2) * rows + inner % rows
    return jnp.where(source == j, 1.0, 0.0).astype(BF16)


def fetch_in_kernel(
    n_pair, router_hbm, routes_hbm, gate_hbm, up_hbm, _, in_ref, member_ref, router_ref, routes_ref, sems
):
    hid = gate_hbm.shape[0]
    copies = dma_in(
        sems,
        [
            (router_hbm, router_ref),
            (routes_hbm, routes_ref),
            (gate_hbm, in_ref.at[0:hid]),
            (up_hbm, in_ref.at[hid : 2 * hid]),
        ],
    )
    for copy in copies[:2]:
        copy.wait()
    experts, t = router_ref.shape[0], routes_ref.shape[1]
    in_ref[2 * hid :, :] = jnp.zeros((TILE_ROWS, in_ref.shape[1]), BF16)
    in_ref[2 * hid : 2 * hid + experts, :] = router_ref[...]
    padded = member_ref.shape[0]
    hits = jnp.zeros((padded, t), F32)
    for k in range(routes_ref.shape[0]):
        hits = hits + jnp.where(routes_ref[k : k + 1, :] == iota2((padded, t), 0), 1.0, 0.0)
    exp_index = lax.axis_index("exp")
    place = place_matrix(t // (2 * n_pair), n_pair, exp_index // 2, exp_index % 2)
    member_ref[...] = dot_f32(hits.astype(BF16), place, ((1,), (1,)))
    for copy in copies[2:]:
        copy.wait()


def fetch_down_kernel(down_hbm, _, down_ref, token_ref, sem):
    copy = pltpu.make_async_copy(down_hbm, down_ref, sem)
    copy.start()
    token_ref[...] = jnp.zeros(token_ref.shape, F32)
    copy.wait()


def normed_kernel(n_pair, moves, *refs):
    states = refs[: len(moves)]
    intra_ref, grown_ref, query_ref, gain_ref, out_ref = refs[len(moves) :]
    t, d = query_ref.shape
    me = lax.axis_index("seq")
    ranks = [move(me) for move in moves]
    parts = [get_state(ref) for ref in states]
    incoming = jnp.zeros((d, d), F32)
    for rank, (state, _) in zip(ranks, parts):
        logsum = jnp.zeros((1, d), F32)
        for other, (_, total) in zip(ranks, parts):
            logsum = logsum + jnp.where(jnp.logical_and(rank < other, other < me), total, 0.0)
        incoming = incoming + jnp.where(rank < me, jnp.exp(logsum), 0.0) * state
    high = incoming.astype(BF16)
    low = (incoming - high.astype(F32)).astype(BF16)
    query = query_ref[...]
    read = dot_f32(query, high, ((1,), (0,))) + dot_f32(query, low, ((1,), (0,)))
    attended = intra_ref[...] + grown_ref[...] * read
    inverse = lax.rsqrt(jnp.mean(attended * attended, axis=1, keepdims=True) + 1e-06)
    normed = (attended * inverse * gain_ref[0:1, :]).astype(BF16)
    exp_index = lax.axis_index("exp")
    place = place_matrix(t // (2 * n_pair), n_pair, exp_index // 2, exp_index % 2)
    out_ref[...] = dot_f32(place, normed, ((1,), (0,))).astype(BF16)


def product_kernel(at, x_ref, w_ref, mine_ref, theirs_ref):
    half = mine_ref.shape[0]
    for i in range(at.start, at.stop, COLUMNS):
        part = dot_f32(x_ref[...], w_ref[:, i : i + COLUMNS], ((1,), (0,))).astype(BF16)
        mine_ref[:, i - at.start : i - at.start + COLUMNS] = part[:half]
        theirs_ref[:, i - at.start : i - at.start + COLUMNS] = part[half:]


def add_kernel(at, a_ref, b_ref, *refs):
    outs = refs[1:] if at.start else refs
    rows = outs[0].shape[0]
    for r, ref in enumerate(outs):
        some = slice(r * rows, (r + 1) * rows)
        total = (a_ref[some, :].astype(F32) + b_ref[some, :].astype(F32)).astype(BF16)
        if at.start and r == 1:
            ref[:, : at.start] = refs[0][...]
            ref[:, at] = total
        else:
            ref[...] = total


def sum_of(at, own_ref, near_ref, *far_refs):
    total = own_ref[...].astype(F32) + near_ref[:, at].astype(F32)
    for ref in far_refs:
        total = total + ref[...].astype(F32)
    return total


def sum_kernel(at, count, *refs):
    total = sum_of(at, *refs[:count]).astype(BF16)
    if at.start:
        refs[-2][...] = total
        refs[-1][:, : at.start] = refs[count][...]
        refs[-1][:, at] = total
    else:
        refs[-1][...] = total


def join_kernel(at, count, own_ref, near_ref, *refs):
    rows = own_ref.shape[0]
    refs[-1][0:rows, :] = own_ref[...]
    refs[-1][rows : 2 * rows, :] = near_ref[:, at]
    for i, ref in enumerate(refs[: count - 2], start=2):
        refs[-1][i * rows : (i + 1) * rows, :] = ref[...]


def enter_part(at, in_ref, own_ref, other_ref):
    x = jnp.concatenate([own_ref[...], other_ref[...]], axis=0)
    return dot_f32(in_ref[:, at], x, ((1,), (1,)))


def enter_kernel(at, in_ref, own_ref, other_ref, out_ref):
    out_ref[...] = enter_part(at, in_ref, own_ref, other_ref)


def hidden_kernel(at, slices, experts, in_ref, own_ref, other_ref, before_ref, member_ref, out_ref):
    total = before_ref[...] + enter_part(at, in_ref, own_ref, other_ref)
    t, hid = out_ref.shape
    gate, up, logits = total[0:hid], total[hid : 2 * hid], total[2 * hid : 2 * hid + experts]
    raised = jnp.where(member_ref[0:experts, :] > 0.5, jnp.exp(logits), 0.0)
    mine = iota2((experts, t), 0) == lax.axis_index("exp") // slices
    prob = jnp.sum(jnp.where(mine, raised, 0.0), axis=0, keepdims=True) / jnp.sum(raised, axis=0, keepdims=True)
    out_ref[...] = (gate / (1.0 + jnp.exp(-gate)) * up * prob).T.astype(BF16)


def result_kernel(ranges, *refs):
    count = (len(refs) - 1) // len(ranges)
    for i, at in enumerate(ranges):
        *terms, mixed_ref = refs[i * count : (i + 1) * count]
        refs[-1][:, at] = (sum_of(at, *terms) + mixed_ref[...].astype(F32)).astype(BF16)


def call(kernel, outs, args, scratch=(), far=0):
    whole = pl.BlockSpec(memory_space=pltpu.VMEM)
    if far:
        args = [pltpu.with_memory_space_constraint(a, pltpu.HBM) for a in args[:far]] + list(args[far:])
    return pl.pallas_call(
        kernel,
        out_shape=outs,
        in_specs=[pl.BlockSpec(memory_space=pl.ANY) if far else whole] * len(args),
        out_specs=[whole] * len(outs),
        scratch_shapes=list(scratch),
        compiler_params=pltpu.CompilerParams(vmem_limit_bytes=VMEM_LIMIT),
        cost_estimate=pl.CostEstimate(flops=0, bytes_accessed=0, transcendentals=0),
    )(*args)


def local(query, key_in, value, decay_log, norm_gain, w_out, router, routes, w_gate, w_up, w_down):
    t, d = query.shape
    width = w_out.shape[1]
    exp_count, seq_count = lax.axis_size("exp"), lax.axis_size("seq")
    n_pair = exp_count // 2
    rows = t // exp_count
    experts = router.shape[1]
    slices = exp_count // experts
    hid = w_gate.shape[2]
    out = jax.ShapeDtypeStruct
    dma = pltpu.SemaphoreType.DMA

    def swap(x, r):
        return lax.ppermute(x, "exp", [(e, e ^ (2 * r)) for e in range(exp_count)])

    def across(x):
        return lax.ppermute(x, "exp", [(e, e ^ 1) for e in range(exp_count)])

    size = width // 2
    ranges = [slice(0, size), slice(size, width)]
    full = out((rows, width), BF16)

    def rows_of(count):
        return out((count * rows, size), BF16)

    def reduce(products):
        others = [across(theirs) for _, theirs in products]
        terms, first = [], ()
        for at, (mine, _), other in zip(ranges, products, others):
            outs = [rows_of(1)] * n_pair
            if first:
                outs[1] = full
            terms.append(call(functools.partial(add_kernel, at), outs, (mine, other, *first)))
            first = (terms[-1][1],)
        far = [[swap(term[r], r) for r in range(2, n_pair)] for term in terms]
        near = swap(first[0], 1)
        return [[term[0], near, *some] for term, some in zip(terms, far)], terms[-1][-1]

    def products_of(x, w):
        return [call(functools.partial(product_kernel, at), [rows_of(n_pair)] * 2, (x, w)) for at in ranges]

    decay_row = decay_log.T
    block = pltpu.VMEM((t, d), BF16)
    decay_block = pltpu.VMEM((1, t), F32)
    (state,) = call(
        state_kernel,
        [out((d + TILE_ROWS, d), BF16)],
        (key_in, value, decay_row),
        [block, block, decay_block, dma((3,))],
        far=3,
    )
    moves = [lambda i, k=k: i ^ k for k in range(1, seq_count)]
    states = [lax.ppermute(state, "seq", [(move(i), i) for i in range(seq_count)]) for move in moves]
    intra, grown, query_near, gain, w_out_near = call(
        within_kernel,
        [out((t, d), F32), out((t, d), F32), out((t, d), BF16), out((8, d), F32), out(w_out.shape, BF16)],
        (query, key_in, value, decay_row, norm_gain[None, :], w_out, state),
        [block, block, decay_block, pltpu.VMEM((1, d), BF16), dma((6,))],
        far=6,
    )
    (normed,) = call(
        functools.partial(normed_kernel, n_pair, moves),
        [out((t, d), BF16)],
        (*states, intra, grown, query_near, gain),
    )
    terms, last = reduce(products_of(normed, w_out_near))
    w_in, member = call(
        functools.partial(fetch_in_kernel, n_pair),
        [out((2 * hid + TILE_ROWS, width), BF16), out((-(-experts // 8) * 8, t), F32)],
        (router.T, routes.T, w_gate[0].T, w_up[0].T, last),
        [pltpu.VMEM((experts, width), BF16), pltpu.VMEM((routes.shape[1], t), jnp.int32), dma((4,))],
        far=4,
    )
    left, right = ranges
    (mixed,) = call(functools.partial(sum_kernel, left, n_pair), [rows_of(1)], (*terms[0], member))
    mixed = [mixed]
    other, whole = call(
        functools.partial(sum_kernel, right, n_pair), [rows_of(1), full], (*terms[1], mixed[0])
    )
    mixed.append(other)
    far = [[swap(m, r) for r in range(2, n_pair)] for m in mixed]
    near = swap(whole, 1)
    (own,) = call(
        functools.partial(join_kernel, left, n_pair), [rows_of(n_pair)], (mixed[0], near, *far[0])
    )
    w_down_near, token = call(
        fetch_down_kernel, [out((hid, width), BF16), out((8, 128), F32)], (w_down[0], own), [dma], far=1
    )
    (own_right,) = call(
        functools.partial(join_kernel, right, n_pair), [rows_of(n_pair)], (mixed[1], near, *far[1], token)
    )
    (total,) = call(
        functools.partial(enter_kernel, left), [out((w_in.shape[0], t), F32)], (w_in, own, across(own))
    )
    (hidden,) = call(
        functools.partial(hidden_kernel, right, slices, experts),
        [out((t, hid), BF16)],
        (w_in, own_right, across(own_right), total, member),
    )
    sums, _ = reduce(products_of(hidden, w_down_near))
    args = [x for some, m in zip(sums, mixed) for x in (*some, m)]
    return call(functools.partial(result_kernel, ranges), [full], args)[0]


def solution(mesh):
    placed = (
        P("seq", "exp"),
        P("seq", "exp"),
        P("seq", "exp"),
        P("seq", "exp"),
        P("exp"),
        P("exp", None),
        P(),
        P("seq", None),
        P("exp", None, None),
        P("exp", None, None),
        P("exp", None, None),
    )

    def pick(query, key_in, value, decay_log, *rest):
        rows = query.shape[0] // lax.axis_size("exp")
        exp_count = lax.axis_size("exp")
        tiled = rows % TILE_ROWS == 0 and decay_log.shape[1] == 1
        for count in (exp_count, lax.axis_size("seq")):
            tiled = tiled and count >= 4 and count & (count - 1) == 0
        plan = local if tiled else plain_plan
        return plan(query, key_in, value, decay_log, *rest)

    return jax.shard_map(
        pick, mesh=mesh, in_specs=placed, out_specs=P(("seq", "exp"), None), check_vma=False
    )
```

```python
import functools

import jax
import jax.numpy as jnp
from jax import lax
from jax.experimental import pallas as pl
from jax.experimental.pallas import tpu as pltpu
from jax.sharding import PartitionSpec as P

F32 = jnp.float32
BF16 = jnp.bfloat16
TILE_ROWS = 16
COLUMNS = 1024
PARTS = 2
VMEM_LIMIT = 16 * 1024 * 1024


def plain_plan(query, key_in, value, decay_log, norm_gain, w_out, router, routes, w_gate, w_up, w_down):
    tok_count = query.shape[0]
    head_count = decay_log.shape[1]
    head_size = query.shape[1] // head_count
    top_count = routes.shape[1]
    expert_count = router.shape[1]
    capacity = max(2, 3 * tok_count * top_count // (2 * expert_count))
    exp_count = lax.axis_size("exp")
    slice_count = exp_count // expert_count
    queries = query.reshape(tok_count, head_count, head_size)
    keys_local = key_in.reshape(tok_count, head_count, head_size)
    values_local = value.reshape(tok_count, head_count, head_size)
    cumulative = jnp.cumsum(decay_log, axis=0)
    scores = jnp.einsum("thd,shd->hts", queries, keys_local, preferred_element_type=jnp.float32)
    spread = cumulative.T[:, :, None] - cumulative.T[:, None, :]
    causal = jnp.arange(tok_count)[:, None] >= jnp.arange(tok_count)[None, :]
    weights = jnp.where(causal, jnp.exp(jnp.where(causal, spread, 0.0)), 0.0)
    attend = (scores * weights / head_size).astype(jnp.bfloat16)
    intra_part = jnp.einsum(
        "hts,she->the", attend, values_local, preferred_element_type=jnp.float32
    )
    totals = cumulative[-1]
    tail_decay = jnp.exp(totals[None, :] - cumulative)
    state_delta = jnp.einsum(
        "shd,she->hde",
        keys_local.astype(jnp.float32) * tail_decay[:, :, None],
        values_local.astype(jnp.float32),
        precision=lax.Precision.HIGHEST,
    )
    decay_rows = lax.all_gather(totals[None, :], "seq", axis=0, tiled=True)
    my_rank = lax.axis_index("seq")
    seq_ranks = jnp.arange(decay_rows.shape[0])
    state_piece = lax.all_gather(
        state_delta[None].astype(jnp.bfloat16), "seq", axis=0, tiled=True
    ).astype(jnp.float32)
    piece_rank = jnp.arange(state_piece.shape[0])
    between = (seq_ranks[None, :] > piece_rank[:, None]) & (seq_ranks[None, :] < my_rank)
    logsum = jnp.dot(between.astype(jnp.float32), decay_rows, precision=lax.Precision.HIGHEST)
    factor = jnp.where((piece_rank < my_rank)[:, None], jnp.exp(logsum), 0.0)
    incoming = jnp.zeros_like(state_delta) + jnp.einsum(
        "ih,ihde->hde", factor, state_piece, precision=lax.Precision.HIGHEST
    )
    inter_part = (
        jnp.exp(cumulative)[:, :, None]
        * jnp.einsum(
            "thd,hde->the", queries.astype(jnp.float32), incoming, precision=lax.Precision.HIGHEST
        )
        / head_size
    )
    attended = intra_part + inter_part
    inverse_rms = lax.rsqrt(jnp.mean(attended * attended, axis=-1, keepdims=True) + 1e-06)
    gain_f32 = norm_gain.astype(jnp.float32).reshape(head_count, head_size)
    normed = (
        (attended * inverse_rms * gain_f32)
        .astype(jnp.bfloat16)
        .reshape(tok_count, head_count * head_size)
    )
    own_mixed = lax.psum_scatter(
        jnp.dot(normed, w_out, preferred_element_type=jnp.float32),
        "exp",
        scatter_dimension=0,
        tiled=True,
    ).astype(jnp.bfloat16)
    mixed = lax.all_gather(own_mixed, "exp", axis=0, tiled=True)
    logits = jnp.dot(mixed, router, preferred_element_type=jnp.float32)
    member = routes[:, :, None] == jnp.arange(expert_count)[None, None, :]
    picked = jnp.sum(jnp.where(member, logits[:, None, :], 0.0), axis=-1)
    raised = jnp.exp(picked)
    gate_probs = raised / jnp.sum(raised, axis=-1, keepdims=True)
    my_expert = lax.axis_index("exp") // slice_count
    flat_hit = (routes.reshape(-1) == my_expert).astype(jnp.int32)
    slot_flat = jnp.cumsum(flat_hit) - flat_hit
    slot_match = (slot_flat[:, None] == jnp.arange(capacity)[None, :]) & (flat_hit[:, None] > 0)
    token_select = jnp.sum(
        slot_match.reshape(tok_count, top_count, capacity).astype(jnp.float32), axis=1
    )
    token_gate = jnp.sum(jnp.where(routes == my_expert, gate_probs, 0.0), axis=1)
    slot_rows = jnp.dot(
        token_select.astype(jnp.bfloat16).T, mixed, preferred_element_type=jnp.float32
    ).astype(jnp.bfloat16)
    gate_part = jnp.dot(slot_rows, w_gate[0], preferred_element_type=jnp.float32)
    up_part = jnp.dot(slot_rows, w_up[0], preferred_element_type=jnp.float32)
    hidden = (jax.nn.silu(gate_part) * up_part).astype(jnp.bfloat16)
    slice_out = jnp.dot(hidden, w_down[0], preferred_element_type=jnp.float32)
    spread_out = jnp.dot(token_select, slice_out, precision=lax.Precision.HIGHEST)
    summed = lax.psum_scatter(
        token_gate[:, None] * spread_out, "exp", scatter_dimension=0, tiled=True
    )
    return (own_mixed.astype(jnp.float32) + summed).astype(jnp.bfloat16)


def iota2(shape, axis):
    return lax.broadcasted_iota(jnp.int32, shape, axis)


def cumulate(decay_row):
    t = decay_row.shape[1]
    row, col = iota2((t, t), 0), iota2((t, t), 1)
    spread = jnp.broadcast_to(decay_row, (t, t))
    column = jnp.sum(jnp.where(col <= row, spread, 0.0), axis=1, keepdims=True)
    own = jnp.sum(jnp.where(col == row, spread, 0.0), axis=1, keepdims=True)
    line = jnp.sum(jnp.where(row <= col, own, 0.0), axis=0, keepdims=True)
    return column, line


def dot_f32(a, b, dims):
    return lax.dot_general(a, b, (dims, ((), ())), preferred_element_type=F32)


def split_dot(a_f32, b, dims):
    high = a_f32.astype(BF16)
    low = (a_f32 - high.astype(F32)).astype(BF16)
    return dot_f32(high, b, dims) + dot_f32(low, b, dims)


def dma_in(sems, pairs):
    copies = [pltpu.make_async_copy(a, b, sems.at[i]) for i, (a, b) in enumerate(pairs)]
    for copy in copies:
        copy.start()
    return copies


def put_state(out_ref, state, total):
    d = state.shape[1]
    out_ref[0:d, :] = state.astype(BF16)
    wide = jnp.broadcast_to(total, (TILE_ROWS, d))
    part0 = wide.astype(BF16).astype(F32)
    part1 = (wide - part0).astype(BF16).astype(F32)
    part2 = wide - part0 - part1
    row = iota2((TILE_ROWS, d), 0)
    parts = jnp.where(row == 0, part0, jnp.where(row == 1, part1, jnp.where(row == 2, part2, 0.0)))
    out_ref[d:, :] = parts.astype(BF16)


def get_state(ref):
    d = ref.shape[1]
    return ref[0:d, :].astype(F32), jnp.sum(ref[d:, :].astype(F32), axis=0, keepdims=True)


def state_kernel(key_hbm, value_hbm, decay_hbm, out_ref, key_ref, value_ref, decay_ref, sems):
    t, d = key_ref.shape
    copies = dma_in(sems, [(decay_hbm, decay_ref), (key_hbm, key_ref), (value_hbm, value_ref)])
    for copy in copies:
        copy.wait()
    column, _ = cumulate(decay_ref[...])
    total = column[t - 1 :, :]
    keyed = key_ref[...].astype(F32) * jnp.exp(total - column)
    put_state(out_ref, split_dot(keyed, value_ref[...], ((0,), (0,))), jnp.broadcast_to(total, (1, d)))


def within_kernel(
    n_pair, query_hbm, key_hbm, value_hbm, decay_hbm, gain_hbm, router_hbm, routes_hbm, w_out_hbm, gate_hbm, up_hbm, _,
    intra_ref, grown_ref, query_ref, gain_ref, w_out_ref, in_ref, member_ref,
    key_ref, value_ref, decay_ref, gain_in_ref, router_ref, routes_ref, sems,
):
    t, d = query_ref.shape
    hid = gate_hbm.shape[0]
    copies = dma_in(
        sems,
        [
            (decay_hbm, decay_ref),
            (query_hbm, query_ref),
            (key_hbm, key_ref),
            (value_hbm, value_ref),
            (gain_hbm, gain_in_ref),
            (router_hbm, router_ref),
            (routes_hbm, routes_ref),
            (w_out_hbm, w_out_ref),
            (gate_hbm, in_ref.at[0:hid]),
            (up_hbm, in_ref.at[hid : 2 * hid]),
        ],
    )
    for copy in copies[:7]:
        copy.wait()
    column, line = cumulate(decay_ref[...])
    query, key, value = query_ref[...], key_ref[...], value_ref[...]
    scores = dot_f32(query, key, ((1,), (1,)))
    causal = iota2((t, t), 0) >= iota2((t, t), 1)
    weights = jnp.where(causal, jnp.exp(jnp.where(causal, column - line, 0.0)), 0.0)
    attend = (scores * weights * (1.0 / d)).astype(BF16)
    intra_ref[...] = dot_f32(attend, value, ((1,), (0,)))
    grown_ref[...] = jnp.broadcast_to(jnp.exp(column) * (1.0 / d), (t, d))
    gain_ref[...] = jnp.broadcast_to(gain_in_ref[...].astype(F32), gain_ref.shape)
    experts = router_ref.shape[0]
    in_ref[2 * hid :, :] = jnp.zeros((TILE_ROWS, in_ref.shape[1]), BF16)
    in_ref[2 * hid : 2 * hid + experts, :] = router_ref[...]
    padded = member_ref.shape[0]
    hits = jnp.zeros((padded, t), F32)
    for k in range(routes_ref.shape[0]):
        hits = hits + jnp.where(routes_ref[k : k + 1, :] == iota2((padded, t), 0), 1.0, 0.0)
    exp_index = lax.axis_index("exp")
    place = place_matrix(t // (2 * n_pair), n_pair, exp_index // 2, exp_index % 2)
    member_ref[...] = dot_f32(hits.astype(BF16), place, ((1,), (1,)))
    for copy in copies[7:]:
        copy.wait()


def place_matrix(rows, n_pair, pair, core):
    size = 2 * n_pair * rows
    i, j = iota2((size, size), 0), iota2((size, size), 1)
    half, inner = i // (n_pair * rows), i % (n_pair * rows)
    who = (inner // rows + pair) % n_pair
    source = (2 * who + (core + half) % 2) * rows + inner % rows
    return jnp.where(source == j, 1.0, 0.0).astype(BF16)


def fetch_down_kernel(down_hbm, _, down_ref, token_ref, sem):
    copy = pltpu.make_async_copy(down_hbm, down_ref, sem)
    copy.start()
    token_ref[...] = jnp.zeros(token_ref.shape, F32)
    copy.wait()


def normed_kernel(n_pair, moves, *refs):
    states = refs[: len(moves)]
    intra_ref, grown_ref, query_ref, gain_ref, out_ref = refs[len(moves) :]
    t, d = query_ref.shape
    me = lax.axis_index("seq")
    ranks = [move(me) for move in moves]
    parts = [get_state(ref) for ref in states]
    incoming = jnp.zeros((d, d), F32)
    for rank, (state, _) in zip(ranks, parts):
        logsum = jnp.zeros((1, d), F32)
        for other, (_, total) in zip(ranks, parts):
            logsum = logsum + jnp.where(jnp.logical_and(rank < other, other < me), total, 0.0)
        incoming = incoming + jnp.where(rank < me, jnp.exp(logsum), 0.0) * state
    high = incoming.astype(BF16)
    low = (incoming - high.astype(F32)).astype(BF16)
    query = query_ref[...]
    read = dot_f32(query, high, ((1,), (0,))) + dot_f32(query, low, ((1,), (0,)))
    attended = intra_ref[...] + grown_ref[...] * read
    inverse = lax.rsqrt(jnp.mean(attended * attended, axis=1, keepdims=True) + 1e-06)
    normed = (attended * inverse * gain_ref[0:1, :]).astype(BF16)
    exp_index = lax.axis_index("exp")
    place = place_matrix(t // (2 * n_pair), n_pair, exp_index // 2, exp_index % 2)
    out_ref[...] = dot_f32(place, normed, ((1,), (0,))).astype(BF16)


def product_kernel(at, x_ref, w_ref, mine_ref, theirs_ref):
    half = mine_ref.shape[0]
    for i in range(at.start, at.stop, COLUMNS):
        part = dot_f32(x_ref[...], w_ref[:, i : i + COLUMNS], ((1,), (0,))).astype(BF16)
        mine_ref[:, i - at.start : i - at.start + COLUMNS] = part[:half]
        theirs_ref[:, i - at.start : i - at.start + COLUMNS] = part[half:]


def add_kernel(groups, a_ref, b_ref, *refs):
    outs = refs[-len(groups) :]
    rows = outs[0].shape[0] // len(groups[0])
    for group, ref in zip(groups, outs):
        for i, block in enumerate(group):
            at = slice(block * rows, (block + 1) * rows)
            total = a_ref[at, :].astype(F32) + b_ref[at, :].astype(F32)
            ref[i * rows : (i + 1) * rows, :] = total.astype(ref.dtype)


def sum_kernel(count, *refs):
    total = refs[0][...].astype(F32)
    for ref in refs[1:count]:
        total = total + ref[...].astype(F32)
    refs[-1][...] = total.astype(BF16)


def join_kernel(count, *refs):
    start = 0
    for ref in refs[:count]:
        refs[-1][start : start + ref.shape[0], :] = ref[...]
        start += ref.shape[0]


def enter_part(at, in_ref, own_ref, other_ref):
    x = jnp.concatenate([own_ref[...], other_ref[...]], axis=0)
    return dot_f32(in_ref[:, at], x, ((1,), (1,)))


def enter_kernel(at, in_ref, own_ref, other_ref, out_ref):
    out_ref[...] = enter_part(at, in_ref, own_ref, other_ref)


def hidden_kernel(at, slices, experts, in_ref, own_ref, other_ref, before_ref, member_ref, out_ref):
    total = before_ref[...] + enter_part(at, in_ref, own_ref, other_ref)
    t, hid = out_ref.shape
    gate, up, logits = total[0:hid], total[hid : 2 * hid], total[2 * hid : 2 * hid + experts]
    raised = jnp.where(member_ref[0:experts, :] > 0.5, jnp.exp(logits), 0.0)
    mine = iota2((experts, t), 0) == lax.axis_index("exp") // slices
    prob = jnp.sum(jnp.where(mine, raised, 0.0), axis=0, keepdims=True) / jnp.sum(raised, axis=0, keepdims=True)
    out_ref[...] = (gate / (1.0 + jnp.exp(-gate)) * up * prob).T.astype(BF16)


def result_kernel(count, *refs):
    out_ref = refs[-1]
    width = refs[0].shape[1]
    for i in range(len(refs) // count):
        total = refs[i * count][...].astype(F32)
        for ref in refs[i * count + 1 : (i + 1) * count]:
            total = total + ref[...].astype(F32)
        out_ref[:, i * width : (i + 1) * width] = total.astype(BF16)


def call(kernel, outs, args, scratch=(), far=0):
    whole = pl.BlockSpec(memory_space=pltpu.VMEM)
    if far:
        args = [pltpu.with_memory_space_constraint(a, pltpu.HBM) for a in args[:far]] + list(args[far:])
    return pl.pallas_call(
        kernel,
        out_shape=outs,
        in_specs=[pl.BlockSpec(memory_space=pl.ANY) if far else whole] * len(args),
        out_specs=[whole] * len(outs),
        scratch_shapes=list(scratch),
        compiler_params=pltpu.CompilerParams(vmem_limit_bytes=VMEM_LIMIT),
        cost_estimate=pl.CostEstimate(flops=0, bytes_accessed=0, transcendentals=0),
    )(*args)


def local(query, key_in, value, decay_log, norm_gain, w_out, router, routes, w_gate, w_up, w_down):
    t, d = query.shape
    width = w_out.shape[1]
    exp_count, seq_count = lax.axis_size("exp"), lax.axis_size("seq")
    n_pair = exp_count // 2
    rows = t // exp_count
    experts = router.shape[1]
    slices = exp_count // experts
    hid = w_gate.shape[2]
    out = jax.ShapeDtypeStruct
    dma = pltpu.SemaphoreType.DMA

    def shift(x, r):
        return lax.ppermute(x, "exp", [(e, (e + 2 * r) % exp_count) for e in range(exp_count)])

    def across(x):
        return lax.ppermute(x, "exp", [(e, e ^ 1) for e in range(exp_count)])

    size = width // PARTS
    ranges = [slice(i * size, (i + 1) * size) for i in range(PARTS)]

    def rows_of(count):
        return out((count * rows, size), BF16)

    def reduce(products):
        others = [across(theirs) for _, theirs in products]
        terms = [
            call(functools.partial(add_kernel, [[r] for r in range(n_pair)]), [rows_of(1)] * n_pair, (mine, other))
            for (mine, _), other in zip(products, others)
        ]
        return [[term[0]] + [shift(term[r], r) for r in range(1, n_pair)] for term in terms]

    def products_of(x, w):
        return [call(functools.partial(product_kernel, at), [rows_of(n_pair)] * 2, (x, w)) for at in ranges]

    decay_row = decay_log.T
    block = pltpu.VMEM((t, d), BF16)
    decay_block = pltpu.VMEM((1, t), F32)
    (state,) = call(
        state_kernel,
        [out((d + TILE_ROWS, d), BF16)],
        (key_in, value, decay_row),
        [block, block, decay_block, dma((3,))],
        far=3,
    )
    moves = [lambda i, k=k: i ^ k for k in range(1, seq_count)]
    states = [lax.ppermute(state, "seq", [(move(i), i) for i in range(seq_count)]) for move in moves]
    intra, grown, query_near, gain, w_out_near, w_in, member = call(
        functools.partial(within_kernel, n_pair),
        [
            out((t, d), F32),
            out((t, d), F32),
            out((t, d), BF16),
            out((8, d), F32),
            out(w_out.shape, BF16),
            out((2 * hid + TILE_ROWS, width), BF16),
            out((-(-experts // 8) * 8, t), F32),
        ],
        (query, key_in, value, decay_row, norm_gain[None, :], router.T, routes.T, w_out, w_gate[0].T, w_up[0].T, state),
        [
            block,
            block,
            decay_block,
            pltpu.VMEM((1, d), BF16),
            pltpu.VMEM((experts, width), BF16),
            pltpu.VMEM((routes.shape[1], t), jnp.int32),
            dma((10,)),
        ],
        far=10,
    )
    (normed,) = call(
        functools.partial(normed_kernel, n_pair, moves),
        [out((t, d), BF16)],
        (*states, intra, grown, query_near, gain),
    )
    terms = reduce(products_of(normed, w_out_near))
    mixed = [call(functools.partial(sum_kernel, n_pair), [rows_of(1)], term)[0] for term in terms]
    gathered = [[shift(m, -r) if r else m for r in range(n_pair)] for m in mixed]
    own, after = [], ()
    for blocks in gathered:
        own += call(functools.partial(join_kernel, n_pair), [rows_of(n_pair)], (*blocks, *after))
        if not after:
            w_down_near, token = call(
                fetch_down_kernel, [out((hid, width), BF16), out((8, 128), F32)], (w_down[0], own[0]), [dma], far=1
            )
            after = (token,)
    total = ()
    for at, x in zip(ranges, own):
        if at.stop < width:
            kernel, shape = functools.partial(enter_kernel, at), out((w_in.shape[0], t), F32)
        else:
            kernel, shape = functools.partial(hidden_kernel, at, slices, experts), out((t, hid), BF16)
            total = (*total, member)
        total = call(kernel, [shape], (w_in, x, across(x), *total))
    sums = reduce(products_of(total[0], w_down_near))
    args = [x for some, m in zip(sums, mixed) for x in (*some, m)]
    return call(functools.partial(result_kernel, n_pair + 1), [out((rows, width), BF16)], args)[0]


def solution(mesh):
    placed = (
        P("seq", "exp"),
        P("seq", "exp"),
        P("seq", "exp"),
        P("seq", "exp"),
        P("exp"),
        P("exp", None),
        P(),
        P("seq", None),
        P("exp", None, None),
        P("exp", None, None),
        P("exp", None, None),
    )

    def pick(query, key_in, value, decay_log, *rest):
        rows = query.shape[0] // lax.axis_size("exp")
        exp_count = lax.axis_size("exp")
        tiled = rows % TILE_ROWS == 0 and decay_log.shape[1] == 1
        for count in (exp_count, lax.axis_size("seq")):
            tiled = tiled and count >= 4 and count & (count - 1) == 0
        plan = local if tiled else plain_plan
        return plan(query, key_in, value, decay_log, *rest)

    return jax.shard_map(
        pick, mesh=mesh, in_specs=placed, out_specs=P(("seq", "exp"), None), check_vma=False
    )
```

```python
import functools

import jax
import jax.numpy as jnp
from jax import lax
from jax.experimental import pallas as pl
from jax.experimental.pallas import tpu as pltpu
from jax.sharding import PartitionSpec as P

F32 = jnp.float32
BF16 = jnp.bfloat16
TILE_ROWS = 16
COLUMNS = 1024
PARTS = 2
VMEM_LIMIT = 16 * 1024 * 1024


def plain_plan(query, key_in, value, decay_log, norm_gain, w_out, router, routes, w_gate, w_up, w_down):
    tok_count = query.shape[0]
    head_count = decay_log.shape[1]
    head_size = query.shape[1] // head_count
    top_count = routes.shape[1]
    expert_count = router.shape[1]
    capacity = max(2, 3 * tok_count * top_count // (2 * expert_count))
    exp_count = lax.axis_size("exp")
    slice_count = exp_count // expert_count
    queries = query.reshape(tok_count, head_count, head_size)
    keys_local = key_in.reshape(tok_count, head_count, head_size)
    values_local = value.reshape(tok_count, head_count, head_size)
    cumulative = jnp.cumsum(decay_log, axis=0)
    scores = jnp.einsum("thd,shd->hts", queries, keys_local, preferred_element_type=jnp.float32)
    spread = cumulative.T[:, :, None] - cumulative.T[:, None, :]
    causal = jnp.arange(tok_count)[:, None] >= jnp.arange(tok_count)[None, :]
    weights = jnp.where(causal, jnp.exp(jnp.where(causal, spread, 0.0)), 0.0)
    attend = (scores * weights / head_size).astype(jnp.bfloat16)
    intra_part = jnp.einsum(
        "hts,she->the", attend, values_local, preferred_element_type=jnp.float32
    )
    totals = cumulative[-1]
    tail_decay = jnp.exp(totals[None, :] - cumulative)
    state_delta = jnp.einsum(
        "shd,she->hde",
        keys_local.astype(jnp.float32) * tail_decay[:, :, None],
        values_local.astype(jnp.float32),
        precision=lax.Precision.HIGHEST,
    )
    decay_rows = lax.all_gather(totals[None, :], "seq", axis=0, tiled=True)
    my_rank = lax.axis_index("seq")
    seq_ranks = jnp.arange(decay_rows.shape[0])
    state_piece = lax.all_gather(
        state_delta[None].astype(jnp.bfloat16), "seq", axis=0, tiled=True
    ).astype(jnp.float32)
    piece_rank = jnp.arange(state_piece.shape[0])
    between = (seq_ranks[None, :] > piece_rank[:, None]) & (seq_ranks[None, :] < my_rank)
    logsum = jnp.dot(between.astype(jnp.float32), decay_rows, precision=lax.Precision.HIGHEST)
    factor = jnp.where((piece_rank < my_rank)[:, None], jnp.exp(logsum), 0.0)
    incoming = jnp.zeros_like(state_delta) + jnp.einsum(
        "ih,ihde->hde", factor, state_piece, precision=lax.Precision.HIGHEST
    )
    inter_part = (
        jnp.exp(cumulative)[:, :, None]
        * jnp.einsum(
            "thd,hde->the", queries.astype(jnp.float32), incoming, precision=lax.Precision.HIGHEST
        )
        / head_size
    )
    attended = intra_part + inter_part
    inverse_rms = lax.rsqrt(jnp.mean(attended * attended, axis=-1, keepdims=True) + 1e-06)
    gain_f32 = norm_gain.astype(jnp.float32).reshape(head_count, head_size)
    normed = (
        (attended * inverse_rms * gain_f32)
        .astype(jnp.bfloat16)
        .reshape(tok_count, head_count * head_size)
    )
    own_mixed = lax.psum_scatter(
        jnp.dot(normed, w_out, preferred_element_type=jnp.float32),
        "exp",
        scatter_dimension=0,
        tiled=True,
    ).astype(jnp.bfloat16)
    mixed = lax.all_gather(own_mixed, "exp", axis=0, tiled=True)
    logits = jnp.dot(mixed, router, preferred_element_type=jnp.float32)
    member = routes[:, :, None] == jnp.arange(expert_count)[None, None, :]
    picked = jnp.sum(jnp.where(member, logits[:, None, :], 0.0), axis=-1)
    raised = jnp.exp(picked)
    gate_probs = raised / jnp.sum(raised, axis=-1, keepdims=True)
    my_expert = lax.axis_index("exp") // slice_count
    flat_hit = (routes.reshape(-1) == my_expert).astype(jnp.int32)
    slot_flat = jnp.cumsum(flat_hit) - flat_hit
    slot_match = (slot_flat[:, None] == jnp.arange(capacity)[None, :]) & (flat_hit[:, None] > 0)
    token_select = jnp.sum(
        slot_match.reshape(tok_count, top_count, capacity).astype(jnp.float32), axis=1
    )
    token_gate = jnp.sum(jnp.where(routes == my_expert, gate_probs, 0.0), axis=1)
    slot_rows = jnp.dot(
        token_select.astype(jnp.bfloat16).T, mixed, preferred_element_type=jnp.float32
    ).astype(jnp.bfloat16)
    gate_part = jnp.dot(slot_rows, w_gate[0], preferred_element_type=jnp.float32)
    up_part = jnp.dot(slot_rows, w_up[0], preferred_element_type=jnp.float32)
    hidden = (jax.nn.silu(gate_part) * up_part).astype(jnp.bfloat16)
    slice_out = jnp.dot(hidden, w_down[0], preferred_element_type=jnp.float32)
    spread_out = jnp.dot(token_select, slice_out, precision=lax.Precision.HIGHEST)
    summed = lax.psum_scatter(
        token_gate[:, None] * spread_out, "exp", scatter_dimension=0, tiled=True
    )
    return (own_mixed.astype(jnp.float32) + summed).astype(jnp.bfloat16)


def iota2(shape, axis):
    return lax.broadcasted_iota(jnp.int32, shape, axis)


def cumulate(decay_row):
    t = decay_row.shape[1]
    row, col = iota2((t, t), 0), iota2((t, t), 1)
    spread = jnp.broadcast_to(decay_row, (t, t))
    column = jnp.sum(jnp.where(col <= row, spread, 0.0), axis=1, keepdims=True)
    own = jnp.sum(jnp.where(col == row, spread, 0.0), axis=1, keepdims=True)
    line = jnp.sum(jnp.where(row <= col, own, 0.0), axis=0, keepdims=True)
    return column, line


def dot_f32(a, b, dims):
    return lax.dot_general(a, b, (dims, ((), ())), preferred_element_type=F32)


def split_dot(a_f32, b, dims):
    high = a_f32.astype(BF16)
    low = (a_f32 - high.astype(F32)).astype(BF16)
    return dot_f32(high, b, dims) + dot_f32(low, b, dims)


def dma_in(sems, pairs):
    copies = [pltpu.make_async_copy(a, b, sems.at[i]) for i, (a, b) in enumerate(pairs)]
    for copy in copies:
        copy.start()
    return copies


def put_state(out_ref, state, total):
    d = state.shape[1]
    out_ref[0:d, :] = state.astype(BF16)
    wide = jnp.broadcast_to(total, (TILE_ROWS, d))
    part0 = wide.astype(BF16).astype(F32)
    part1 = (wide - part0).astype(BF16).astype(F32)
    part2 = wide - part0 - part1
    row = iota2((TILE_ROWS, d), 0)
    parts = jnp.where(row == 0, part0, jnp.where(row == 1, part1, jnp.where(row == 2, part2, 0.0)))
    out_ref[d:, :] = parts.astype(BF16)


def get_state(ref):
    d = ref.shape[1]
    return ref[0:d, :].astype(F32), jnp.sum(ref[d:, :].astype(F32), axis=0, keepdims=True)


def state_kernel(key_hbm, value_hbm, decay_hbm, out_ref, key_ref, value_ref, decay_ref, sems):
    t, d = key_ref.shape
    copies = dma_in(sems, [(decay_hbm, decay_ref), (key_hbm, key_ref), (value_hbm, value_ref)])
    for copy in copies:
        copy.wait()
    column, _ = cumulate(decay_ref[...])
    total = column[t - 1 :, :]
    keyed = key_ref[...].astype(F32) * jnp.exp(total - column)
    put_state(out_ref, split_dot(keyed, value_ref[...], ((0,), (0,))), jnp.broadcast_to(total, (1, d)))


def within_kernel(
    n_pair, query_hbm, key_hbm, value_hbm, decay_hbm, gain_hbm, router_hbm, routes_hbm, w_out_hbm, gate_hbm, up_hbm, _,
    intra_ref, grown_ref, query_ref, gain_ref, w_out_ref, in_ref, member_ref,
    key_ref, value_ref, decay_ref, gain_in_ref, router_ref, routes_ref, sems,
):
    t, d = query_ref.shape
    hid = gate_hbm.shape[0]
    copies = dma_in(
        sems,
        [
            (decay_hbm, decay_ref),
            (query_hbm, query_ref),
            (key_hbm, key_ref),
            (value_hbm, value_ref),
            (gain_hbm, gain_in_ref),
            (router_hbm, router_ref),
            (routes_hbm, routes_ref),
            (w_out_hbm, w_out_ref),
            (gate_hbm, in_ref.at[0:hid]),
            (up_hbm, in_ref.at[hid : 2 * hid]),
        ],
    )
    for copy in copies[:7]:
        copy.wait()
    column, line = cumulate(decay_ref[...])
    query, key, value = query_ref[...], key_ref[...], value_ref[...]
    scores = dot_f32(query, key, ((1,), (1,)))
    causal = iota2((t, t), 0) >= iota2((t, t), 1)
    weights = jnp.where(causal, jnp.exp(jnp.where(causal, column - line, 0.0)), 0.0)
    attend = (scores * weights * (1.0 / d)).astype(BF16)
    intra_ref[...] = dot_f32(attend, value, ((1,), (0,)))
    grown_ref[...] = jnp.broadcast_to(jnp.exp(column) * (1.0 / d), (t, d))
    gain_ref[...] = jnp.broadcast_to(gain_in_ref[...].astype(F32), gain_ref.shape)
    experts = router_ref.shape[0]
    in_ref[2 * hid :, :] = jnp.zeros((TILE_ROWS, in_ref.shape[1]), BF16)
    in_ref[2 * hid : 2 * hid + experts, :] = router_ref[...]
    padded = member_ref.shape[0]
    hits = jnp.zeros((padded, t), F32)
    for k in range(routes_ref.shape[0]):
        hits = hits + jnp.where(routes_ref[k : k + 1, :] == iota2((padded, t), 0), 1.0, 0.0)
    exp_index = lax.axis_index("exp")
    place = place_matrix(t // (2 * n_pair), n_pair, exp_index // 2, exp_index % 2)
    member_ref[...] = dot_f32(hits.astype(BF16), place, ((1,), (1,)))
    for copy in copies[7:]:
        copy.wait()


def place_matrix(rows, n_pair, pair, core):
    size = 2 * n_pair * rows
    i, j = iota2((size, size), 0), iota2((size, size), 1)
    half, inner = i // (n_pair * rows), i % (n_pair * rows)
    who = jnp.bitwise_xor((n_pair - inner // rows) % n_pair, pair)
    source = (2 * who + (core + half) % 2) * rows + inner % rows
    return jnp.where(source == j, 1.0, 0.0).astype(BF16)


def fetch_down_kernel(down_hbm, _, down_ref, token_ref, sem):
    copy = pltpu.make_async_copy(down_hbm, down_ref, sem)
    copy.start()
    token_ref[...] = jnp.zeros(token_ref.shape, F32)
    copy.wait()


def normed_kernel(n_pair, moves, *refs):
    states = refs[: len(moves)]
    intra_ref, grown_ref, query_ref, gain_ref, out_ref = refs[len(moves) :]
    t, d = query_ref.shape
    me = lax.axis_index("seq")
    ranks = [move(me) for move in moves]
    parts = [get_state(ref) for ref in states]
    incoming = jnp.zeros((d, d), F32)
    for rank, (state, _) in zip(ranks, parts):
        logsum = jnp.zeros((1, d), F32)
        for other, (_, total) in zip(ranks, parts):
            logsum = logsum + jnp.where(jnp.logical_and(rank < other, other < me), total, 0.0)
        incoming = incoming + jnp.where(rank < me, jnp.exp(logsum), 0.0) * state
    high = incoming.astype(BF16)
    low = (incoming - high.astype(F32)).astype(BF16)
    query = query_ref[...]
    read = dot_f32(query, high, ((1,), (0,))) + dot_f32(query, low, ((1,), (0,)))
    attended = intra_ref[...] + grown_ref[...] * read
    inverse = lax.rsqrt(jnp.mean(attended * attended, axis=1, keepdims=True) + 1e-06)
    normed = (attended * inverse * gain_ref[0:1, :]).astype(BF16)
    exp_index = lax.axis_index("exp")
    place = place_matrix(t // (2 * n_pair), n_pair, exp_index // 2, exp_index % 2)
    out_ref[...] = dot_f32(place, normed, ((1,), (0,))).astype(BF16)


def product_kernel(at, x_ref, w_ref, mine_ref, theirs_ref):
    half = mine_ref.shape[0]
    for i in range(at.start, at.stop, COLUMNS):
        part = dot_f32(x_ref[...], w_ref[:, i : i + COLUMNS], ((1,), (0,))).astype(BF16)
        mine_ref[:, i - at.start : i - at.start + COLUMNS] = part[:half]
        theirs_ref[:, i - at.start : i - at.start + COLUMNS] = part[half:]


def add_kernel(groups, a_ref, b_ref, *refs):
    outs = refs[-len(groups) :]
    rows = outs[0].shape[0] // len(groups[0])
    for group, ref in zip(groups, outs):
        for i, block in enumerate(group):
            at = slice(block * rows, (block + 1) * rows)
            total = a_ref[at, :].astype(F32) + b_ref[at, :].astype(F32)
            ref[i * rows : (i + 1) * rows, :] = total.astype(ref.dtype)


def sum_kernel(count, *refs):
    total = refs[0][...].astype(F32)
    for ref in refs[1:count]:
        total = total + ref[...].astype(F32)
    refs[-1][...] = total.astype(BF16)


def join_kernel(count, *refs):
    start = 0
    for ref in refs[:count]:
        refs[-1][start : start + ref.shape[0], :] = ref[...]
        start += ref.shape[0]


def enter_part(at, in_ref, own_ref, other_ref):
    x = jnp.concatenate([own_ref[...], other_ref[...]], axis=0)
    return dot_f32(in_ref[:, at], x, ((1,), (1,)))


def enter_kernel(at, in_ref, own_ref, other_ref, out_ref):
    out_ref[...] = enter_part(at, in_ref, own_ref, other_ref)


def hidden_kernel(at, slices, experts, in_ref, own_ref, other_ref, before_ref, member_ref, out_ref):
    total = before_ref[...] + enter_part(at, in_ref, own_ref, other_ref)
    t, hid = out_ref.shape
    gate, up, logits = total[0:hid], total[hid : 2 * hid], total[2 * hid : 2 * hid + experts]
    raised = jnp.where(member_ref[0:experts, :] > 0.5, jnp.exp(logits), 0.0)
    mine = iota2((experts, t), 0) == lax.axis_index("exp") // slices
    prob = jnp.sum(jnp.where(mine, raised, 0.0), axis=0, keepdims=True) / jnp.sum(raised, axis=0, keepdims=True)
    out_ref[...] = (gate / (1.0 + jnp.exp(-gate)) * up * prob).T.astype(BF16)


def result_kernel(count, *refs):
    out_ref = refs[-1]
    width = refs[0].shape[1]
    for i in range(len(refs) // count):
        total = refs[i * count][...].astype(F32)
        for ref in refs[i * count + 1 : (i + 1) * count]:
            total = total + ref[...].astype(F32)
        out_ref[:, i * width : (i + 1) * width] = total.astype(BF16)


def call(kernel, outs, args, scratch=(), far=0):
    whole = pl.BlockSpec(memory_space=pltpu.VMEM)
    if far:
        args = [pltpu.with_memory_space_constraint(a, pltpu.HBM) for a in args[:far]] + list(args[far:])
    return pl.pallas_call(
        kernel,
        out_shape=outs,
        in_specs=[pl.BlockSpec(memory_space=pl.ANY) if far else whole] * len(args),
        out_specs=[whole] * len(outs),
        scratch_shapes=list(scratch),
        compiler_params=pltpu.CompilerParams(vmem_limit_bytes=VMEM_LIMIT),
        cost_estimate=pl.CostEstimate(flops=0, bytes_accessed=0, transcendentals=0),
    )(*args)


def local(query, key_in, value, decay_log, norm_gain, w_out, router, routes, w_gate, w_up, w_down):
    t, d = query.shape
    width = w_out.shape[1]
    exp_count, seq_count = lax.axis_size("exp"), lax.axis_size("seq")
    n_pair = exp_count // 2
    rows = t // exp_count
    experts = router.shape[1]
    slices = exp_count // experts
    hid = w_gate.shape[2]
    out = jax.ShapeDtypeStruct
    dma = pltpu.SemaphoreType.DMA

    def swap(x, r):
        flip = 2 * (n_pair - r)
        return lax.ppermute(x, "exp", [(e, e ^ flip) for e in range(exp_count)])

    def across(x):
        return lax.ppermute(x, "exp", [(e, e ^ 1) for e in range(exp_count)])

    size = width // PARTS
    ranges = [slice(i * size, (i + 1) * size) for i in range(PARTS)]

    def rows_of(count):
        return out((count * rows, size), BF16)

    def reduce(products):
        others = [across(theirs) for _, theirs in products]
        terms = [
            call(functools.partial(add_kernel, [[r] for r in range(n_pair)]), [rows_of(1)] * n_pair, (mine, other))
            for (mine, _), other in zip(products, others)
        ]
        return [[term[0]] + [swap(term[r], r) for r in reversed(range(1, n_pair))] for term in terms]

    def products_of(x, w):
        return [call(functools.partial(product_kernel, at), [rows_of(n_pair)] * 2, (x, w)) for at in ranges]

    decay_row = decay_log.T
    block = pltpu.VMEM((t, d), BF16)
    decay_block = pltpu.VMEM((1, t), F32)
    (state,) = call(
        state_kernel,
        [out((d + TILE_ROWS, d), BF16)],
        (key_in, value, decay_row),
        [block, block, decay_block, dma((3,))],
        far=3,
    )
    moves = [lambda i, k=k: i ^ k for k in range(1, seq_count)]
    states = [lax.ppermute(state, "seq", [(move(i), i) for i in range(seq_count)]) for move in moves]
    intra, grown, query_near, gain, w_out_near, w_in, member = call(
        functools.partial(within_kernel, n_pair),
        [
            out((t, d), F32),
            out((t, d), F32),
            out((t, d), BF16),
            out((8, d), F32),
            out(w_out.shape, BF16),
            out((2 * hid + TILE_ROWS, width), BF16),
            out((-(-experts // 8) * 8, t), F32),
        ],
        (query, key_in, value, decay_row, norm_gain[None, :], router.T, routes.T, w_out, w_gate[0].T, w_up[0].T, state),
        [
            block,
            block,
            decay_block,
            pltpu.VMEM((1, d), BF16),
            pltpu.VMEM((experts, width), BF16),
            pltpu.VMEM((routes.shape[1], t), jnp.int32),
            dma((10,)),
        ],
        far=10,
    )
    (normed,) = call(
        functools.partial(normed_kernel, n_pair, moves),
        [out((t, d), BF16)],
        (*states, intra, grown, query_near, gain),
    )
    terms = reduce(products_of(normed, w_out_near))
    mixed = [call(functools.partial(sum_kernel, n_pair), [rows_of(1)], term)[0] for term in terms]
    gathered = [[swap(m, r) if r else m for r in range(n_pair)] for m in mixed]
    own, after = [], ()
    for blocks in gathered:
        own += call(functools.partial(join_kernel, n_pair), [rows_of(n_pair)], (*blocks, *after))
        if not after:
            w_down_near, token = call(
                fetch_down_kernel, [out((hid, width), BF16), out((8, 128), F32)], (w_down[0], own[0]), [dma], far=1
            )
            after = (token,)
    total = ()
    for at, x in zip(ranges, own):
        if at.stop < width:
            kernel, shape = functools.partial(enter_kernel, at), out((w_in.shape[0], t), F32)
        else:
            kernel, shape = functools.partial(hidden_kernel, at, slices, experts), out((t, hid), BF16)
            total = (*total, member)
        total = call(kernel, [shape], (w_in, x, across(x), *total))
    sums = reduce(products_of(total[0], w_down_near))
    args = [x for some, m in zip(sums, mixed) for x in (*some, m)]
    return call(functools.partial(result_kernel, n_pair + 1), [out((rows, width), BF16)], args)[0]


def solution(mesh):
    placed = (
        P("seq", "exp"),
        P("seq", "exp"),
        P("seq", "exp"),
        P("seq", "exp"),
        P("exp"),
        P("exp", None),
        P(),
        P("seq", None),
        P("exp", None, None),
        P("exp", None, None),
        P("exp", None, None),
    )

    def pick(query, key_in, value, decay_log, *rest):
        rows = query.shape[0] // lax.axis_size("exp")
        exp_count = lax.axis_size("exp")
        tiled = rows % TILE_ROWS == 0 and decay_log.shape[1] == 1
        for count in (exp_count, lax.axis_size("seq")):
            tiled = tiled and count >= 4 and count & (count - 1) == 0
        plan = local if tiled else plain_plan
        return plan(query, key_in, value, decay_log, *rest)

    return jax.shard_map(
        pick, mesh=mesh, in_specs=placed, out_specs=P(("seq", "exp"), None), check_vma=False
    )
```

```python
import functools

import jax
import jax.numpy as jnp
from jax import lax
from jax.experimental import pallas as pl
from jax.experimental.pallas import tpu as pltpu
from jax.sharding import PartitionSpec as P

F32 = jnp.float32
BF16 = jnp.bfloat16
TILE_ROWS = 16
COLUMNS = 1024
LANES = 128
MIX_PARTS = 3
OUT_PARTS = 2
VMEM_LIMIT = 16 * 1024 * 1024


def plain_plan(query, key_in, value, decay_log, norm_gain, w_out, router, routes, w_gate, w_up, w_down):
    tok_count = query.shape[0]
    head_count = decay_log.shape[1]
    head_size = query.shape[1] // head_count
    top_count = routes.shape[1]
    expert_count = router.shape[1]
    capacity = max(2, 3 * tok_count * top_count // (2 * expert_count))
    exp_count = lax.axis_size("exp")
    slice_count = exp_count // expert_count
    queries = query.reshape(tok_count, head_count, head_size)
    keys_local = key_in.reshape(tok_count, head_count, head_size)
    values_local = value.reshape(tok_count, head_count, head_size)
    cumulative = jnp.cumsum(decay_log, axis=0)
    scores = jnp.einsum("thd,shd->hts", queries, keys_local, preferred_element_type=jnp.float32)
    spread = cumulative.T[:, :, None] - cumulative.T[:, None, :]
    causal = jnp.arange(tok_count)[:, None] >= jnp.arange(tok_count)[None, :]
    weights = jnp.where(causal, jnp.exp(jnp.where(causal, spread, 0.0)), 0.0)
    attend = (scores * weights / head_size).astype(jnp.bfloat16)
    intra_part = jnp.einsum(
        "hts,she->the", attend, values_local, preferred_element_type=jnp.float32
    )
    totals = cumulative[-1]
    tail_decay = jnp.exp(totals[None, :] - cumulative)
    state_delta = jnp.einsum(
        "shd,she->hde",
        keys_local.astype(jnp.float32) * tail_decay[:, :, None],
        values_local.astype(jnp.float32),
        precision=lax.Precision.HIGHEST,
    )
    decay_rows = lax.all_gather(totals[None, :], "seq", axis=0, tiled=True)
    my_rank = lax.axis_index("seq")
    seq_ranks = jnp.arange(decay_rows.shape[0])
    state_piece = lax.all_gather(
        state_delta[None].astype(jnp.bfloat16), "seq", axis=0, tiled=True
    ).astype(jnp.float32)
    piece_rank = jnp.arange(state_piece.shape[0])
    between = (seq_ranks[None, :] > piece_rank[:, None]) & (seq_ranks[None, :] < my_rank)
    logsum = jnp.dot(between.astype(jnp.float32), decay_rows, precision=lax.Precision.HIGHEST)
    factor = jnp.where((piece_rank < my_rank)[:, None], jnp.exp(logsum), 0.0)
    incoming = jnp.zeros_like(state_delta) + jnp.einsum(
        "ih,ihde->hde", factor, state_piece, precision=lax.Precision.HIGHEST
    )
    inter_part = (
        jnp.exp(cumulative)[:, :, None]
        * jnp.einsum(
            "thd,hde->the", queries.astype(jnp.float32), incoming, precision=lax.Precision.HIGHEST
        )
        / head_size
    )
    attended = intra_part + inter_part
    inverse_rms = lax.rsqrt(jnp.mean(attended * attended, axis=-1, keepdims=True) + 1e-06)
    gain_f32 = norm_gain.astype(jnp.float32).reshape(head_count, head_size)
    normed = (
        (attended * inverse_rms * gain_f32)
        .astype(jnp.bfloat16)
        .reshape(tok_count, head_count * head_size)
    )
    own_mixed = lax.psum_scatter(
        jnp.dot(normed, w_out, preferred_element_type=jnp.float32),
        "exp",
        scatter_dimension=0,
        tiled=True,
    ).astype(jnp.bfloat16)
    mixed = lax.all_gather(own_mixed, "exp", axis=0, tiled=True)
    logits = jnp.dot(mixed, router, preferred_element_type=jnp.float32)
    member = routes[:, :, None] == jnp.arange(expert_count)[None, None, :]
    picked = jnp.sum(jnp.where(member, logits[:, None, :], 0.0), axis=-1)
    raised = jnp.exp(picked)
    gate_probs = raised / jnp.sum(raised, axis=-1, keepdims=True)
    my_expert = lax.axis_index("exp") // slice_count
    flat_hit = (routes.reshape(-1) == my_expert).astype(jnp.int32)
    slot_flat = jnp.cumsum(flat_hit) - flat_hit
    slot_match = (slot_flat[:, None] == jnp.arange(capacity)[None, :]) & (flat_hit[:, None] > 0)
    token_select = jnp.sum(
        slot_match.reshape(tok_count, top_count, capacity).astype(jnp.float32), axis=1
    )
    token_gate = jnp.sum(jnp.where(routes == my_expert, gate_probs, 0.0), axis=1)
    slot_rows = jnp.dot(
        token_select.astype(jnp.bfloat16).T, mixed, preferred_element_type=jnp.float32
    ).astype(jnp.bfloat16)
    gate_part = jnp.dot(slot_rows, w_gate[0], preferred_element_type=jnp.float32)
    up_part = jnp.dot(slot_rows, w_up[0], preferred_element_type=jnp.float32)
    hidden = (jax.nn.silu(gate_part) * up_part).astype(jnp.bfloat16)
    slice_out = jnp.dot(hidden, w_down[0], preferred_element_type=jnp.float32)
    spread_out = jnp.dot(token_select, slice_out, precision=lax.Precision.HIGHEST)
    summed = lax.psum_scatter(
        token_gate[:, None] * spread_out, "exp", scatter_dimension=0, tiled=True
    )
    return (own_mixed.astype(jnp.float32) + summed).astype(jnp.bfloat16)


def iota2(shape, axis):
    return lax.broadcasted_iota(jnp.int32, shape, axis)


def cumulate(decay_row):
    t = decay_row.shape[1]
    row, col = iota2((t, t), 0), iota2((t, t), 1)
    spread = jnp.broadcast_to(decay_row, (t, t))
    column = jnp.sum(jnp.where(col <= row, spread, 0.0), axis=1, keepdims=True)
    own = jnp.sum(jnp.where(col == row, spread, 0.0), axis=1, keepdims=True)
    line = jnp.sum(jnp.where(row <= col, own, 0.0), axis=0, keepdims=True)
    return column, line


def dot_f32(a, b, dims):
    return lax.dot_general(a, b, (dims, ((), ())), preferred_element_type=F32)


def split_dot(a_f32, b, dims):
    high = a_f32.astype(BF16)
    low = (a_f32 - high.astype(F32)).astype(BF16)
    return dot_f32(high, b, dims) + dot_f32(low, b, dims)


def dma_in(sems, pairs):
    copies = [pltpu.make_async_copy(a, b, sems.at[i]) for i, (a, b) in enumerate(pairs)]
    for copy in copies:
        copy.start()
    return copies


def put_state(out_ref, state, total):
    d = state.shape[1]
    out_ref[0:d, :] = state.astype(BF16)
    wide = jnp.broadcast_to(total, (TILE_ROWS, d))
    part0 = wide.astype(BF16).astype(F32)
    part1 = (wide - part0).astype(BF16).astype(F32)
    part2 = wide - part0 - part1
    row = iota2((TILE_ROWS, d), 0)
    parts = jnp.where(row == 0, part0, jnp.where(row == 1, part1, jnp.where(row == 2, part2, 0.0)))
    out_ref[d:, :] = parts.astype(BF16)


def get_state(ref):
    d = ref.shape[1]
    return ref[0:d, :].astype(F32), jnp.sum(ref[d:, :].astype(F32), axis=0, keepdims=True)


def state_kernel(key_hbm, value_hbm, decay_hbm, out_ref, key_ref, value_ref, decay_ref, sems):
    t, d = key_ref.shape
    copies = dma_in(sems, [(decay_hbm, decay_ref), (key_hbm, key_ref), (value_hbm, value_ref)])
    for copy in copies:
        copy.wait()
    column, _ = cumulate(decay_ref[...])
    total = column[t - 1 :, :]
    keyed = key_ref[...].astype(F32) * jnp.exp(total - column)
    put_state(out_ref, split_dot(keyed, value_ref[...], ((0,), (0,))), jnp.broadcast_to(total, (1, d)))


def within_kernel(
    n_pair, query_hbm, key_hbm, value_hbm, decay_hbm, gain_hbm, router_hbm, routes_hbm, w_out_hbm, gate_hbm, up_hbm, _,
    intra_ref, grown_ref, query_ref, gain_ref, w_out_ref, in_ref, member_ref,
    key_ref, value_ref, decay_ref, gain_in_ref, router_ref, routes_ref, sems,
):
    t, d = query_ref.shape
    hid = gate_hbm.shape[0]
    copies = dma_in(
        sems,
        [
            (decay_hbm, decay_ref),
            (query_hbm, query_ref),
            (key_hbm, key_ref),
            (value_hbm, value_ref),
            (gain_hbm, gain_in_ref),
            (router_hbm, router_ref),
            (routes_hbm, routes_ref),
            (w_out_hbm, w_out_ref),
            (gate_hbm, in_ref.at[0:hid]),
            (up_hbm, in_ref.at[hid : 2 * hid]),
        ],
    )
    for copy in copies[:7]:
        copy.wait()
    column, line = cumulate(decay_ref[...])
    query, key, value = query_ref[...], key_ref[...], value_ref[...]
    scores = dot_f32(query, key, ((1,), (1,)))
    causal = iota2((t, t), 0) >= iota2((t, t), 1)
    weights = jnp.where(causal, jnp.exp(jnp.where(causal, column - line, 0.0)), 0.0)
    attend = (scores * weights * (1.0 / d)).astype(BF16)
    intra_ref[...] = dot_f32(attend, value, ((1,), (0,)))
    grown_ref[...] = jnp.broadcast_to(jnp.exp(column) * (1.0 / d), (t, d))
    gain_ref[...] = jnp.broadcast_to(gain_in_ref[...].astype(F32), gain_ref.shape)
    experts = router_ref.shape[0]
    in_ref[2 * hid :, :] = jnp.zeros((TILE_ROWS, in_ref.shape[1]), BF16)
    in_ref[2 * hid : 2 * hid + experts, :] = router_ref[...]
    padded = member_ref.shape[0]
    hits = jnp.zeros((padded, t), F32)
    for k in range(routes_ref.shape[0]):
        hits = hits + jnp.where(routes_ref[k : k + 1, :] == iota2((padded, t), 0), 1.0, 0.0)
    exp_index = lax.axis_index("exp")
    place = place_matrix(t // (2 * n_pair), n_pair, exp_index // 2, exp_index % 2)
    member_ref[...] = dot_f32(hits.astype(BF16), place, ((1,), (1,)))
    for copy in copies[7:]:
        copy.wait()


def place_matrix(rows, n_pair, pair, core):
    size = 2 * n_pair * rows
    i, j = iota2((size, size), 0), iota2((size, size), 1)
    half, inner = i // (n_pair * rows), i % (n_pair * rows)
    who = (inner // rows + pair) % n_pair
    source = (2 * who + (core + half) % 2) * rows + inner % rows
    return jnp.where(source == j, 1.0, 0.0).astype(BF16)


def fetch_down_kernel(down_hbm, _, down_ref, token_ref, sem):
    copy = pltpu.make_async_copy(down_hbm, down_ref, sem)
    copy.start()
    token_ref[...] = jnp.zeros(token_ref.shape, F32)
    copy.wait()


def normed_kernel(n_pair, moves, *refs):
    states = refs[: len(moves)]
    intra_ref, grown_ref, query_ref, gain_ref, out_ref = refs[len(moves) :]
    t, d = query_ref.shape
    me = lax.axis_index("seq")
    ranks = [move(me) for move in moves]
    parts = [get_state(ref) for ref in states]
    incoming = jnp.zeros((d, d), F32)
    for rank, (state, _) in zip(ranks, parts):
        logsum = jnp.zeros((1, d), F32)
        for other, (_, total) in zip(ranks, parts):
            logsum = logsum + jnp.where(jnp.logical_and(rank < other, other < me), total, 0.0)
        incoming = incoming + jnp.where(rank < me, jnp.exp(logsum), 0.0) * state
    high = incoming.astype(BF16)
    low = (incoming - high.astype(F32)).astype(BF16)
    query = query_ref[...]
    read = dot_f32(query, high, ((1,), (0,))) + dot_f32(query, low, ((1,), (0,)))
    attended = intra_ref[...] + grown_ref[...] * read
    inverse = lax.rsqrt(jnp.mean(attended * attended, axis=1, keepdims=True) + 1e-06)
    normed = (attended * inverse * gain_ref[0:1, :]).astype(BF16)
    exp_index = lax.axis_index("exp")
    place = place_matrix(t // (2 * n_pair), n_pair, exp_index // 2, exp_index % 2)
    out_ref[...] = dot_f32(place, normed, ((1,), (0,))).astype(BF16)


def product_kernel(at, x_ref, w_ref, mine_ref, theirs_ref):
    half = mine_ref.shape[0]
    for i in range(at.start, at.stop, COLUMNS):
        j = min(i + COLUMNS, at.stop)
        part = dot_f32(x_ref[...], w_ref[:, i:j], ((1,), (0,))).astype(BF16)
        mine_ref[:, i - at.start : j - at.start] = part[:half]
        theirs_ref[:, i - at.start : j - at.start] = part[half:]


def add_kernel(groups, a_ref, b_ref, *refs):
    outs = refs[-len(groups) :]
    rows = outs[0].shape[0] // len(groups[0])
    for group, ref in zip(groups, outs):
        for i, block in enumerate(group):
            at = slice(block * rows, (block + 1) * rows)
            total = a_ref[at, :].astype(F32) + b_ref[at, :].astype(F32)
            ref[i * rows : (i + 1) * rows, :] = total.astype(ref.dtype)


def sum_kernel(count, *refs):
    total = refs[0][...].astype(F32)
    for ref in refs[1:count]:
        total = total + ref[...].astype(F32)
    refs[-1][...] = total.astype(BF16)


def join_kernel(count, *refs):
    start = 0
    for ref in refs[:count]:
        refs[-1][start : start + ref.shape[0], :] = ref[...]
        start += ref.shape[0]


def enter_part(at, in_ref, own_ref, other_ref):
    x = jnp.concatenate([own_ref[...], other_ref[...]], axis=0)
    return dot_f32(in_ref[:, at], x, ((1,), (1,)))


def enter_kernel(at, in_ref, own_ref, other_ref, *refs):
    total = enter_part(at, in_ref, own_ref, other_ref)
    for ref in refs[:-1]:
        total = total + ref[...]
    refs[-1][...] = total


def hidden_kernel(at, slices, experts, in_ref, own_ref, other_ref, before_ref, member_ref, out_ref):
    total = before_ref[...] + enter_part(at, in_ref, own_ref, other_ref)
    t, hid = out_ref.shape
    gate, up, logits = total[0:hid], total[hid : 2 * hid], total[2 * hid : 2 * hid + experts]
    raised = jnp.where(member_ref[0:experts, :] > 0.5, jnp.exp(logits), 0.0)
    mine = iota2((experts, t), 0) == lax.axis_index("exp") // slices
    prob = jnp.sum(jnp.where(mine, raised, 0.0), axis=0, keepdims=True) / jnp.sum(raised, axis=0, keepdims=True)
    out_ref[...] = (gate / (1.0 + jnp.exp(-gate)) * up * prob).T.astype(BF16)


def result_kernel(out_ranges, mix_ranges, *refs):
    out_ref, mixed = refs[-1], refs[-1 - len(mix_ranges) : -1]
    count = (len(refs) - 1 - len(mixed)) // len(out_ranges)
    edges = sorted({at.start for at in out_ranges + mix_ranges} | {out_ref.shape[1]})
    for start, stop in zip(edges, edges[1:]):
        ((i, at),) = [(i, at) for i, at in enumerate(out_ranges) if at.start <= start < at.stop]
        ((m, by),) = [(ref, by) for ref, by in zip(mixed, mix_ranges) if by.start <= start < by.stop]
        total = m[:, start - by.start : stop - by.start].astype(F32)
        for ref in refs[i * count : (i + 1) * count]:
            total = total + ref[:, start - at.start : stop - at.start].astype(F32)
        out_ref[:, start:stop] = total.astype(BF16)


def split(width, parts):
    edges = [-(-width * i // parts // LANES) * LANES for i in range(parts)] + [width]
    return [slice(a, b) for a, b in zip(edges, edges[1:])]


def call(kernel, outs, args, scratch=(), far=0):
    whole = pl.BlockSpec(memory_space=pltpu.VMEM)
    if far:
        args = [pltpu.with_memory_space_constraint(a, pltpu.HBM) for a in args[:far]] + list(args[far:])
    return pl.pallas_call(
        kernel,
        out_shape=outs,
        in_specs=[pl.BlockSpec(memory_space=pl.ANY) if far else whole] * len(args),
        out_specs=[whole] * len(outs),
        scratch_shapes=list(scratch),
        compiler_params=pltpu.CompilerParams(vmem_limit_bytes=VMEM_LIMIT),
        cost_estimate=pl.CostEstimate(flops=0, bytes_accessed=0, transcendentals=0),
    )(*args)


def local(query, key_in, value, decay_log, norm_gain, w_out, router, routes, w_gate, w_up, w_down):
    t, d = query.shape
    width = w_out.shape[1]
    exp_count, seq_count = lax.axis_size("exp"), lax.axis_size("seq")
    n_pair = exp_count // 2
    rows = t // exp_count
    experts = router.shape[1]
    slices = exp_count // experts
    hid = w_gate.shape[2]
    out = jax.ShapeDtypeStruct
    dma = pltpu.SemaphoreType.DMA

    def shift(x, r):
        return lax.ppermute(x, "exp", [(e, (e + 2 * r) % exp_count) for e in range(exp_count)])

    def across(x):
        return lax.ppermute(x, "exp", [(e, e ^ 1) for e in range(exp_count)])

    mix_ranges, out_ranges = split(width, MIX_PARTS), split(width, OUT_PARTS)

    def rows_of(count, at):
        return out((count * rows, at.stop - at.start), BF16)

    def reduce(x, w, ranges):
        products = [call(functools.partial(product_kernel, at), [rows_of(n_pair, at)] * 2, (x, w)) for at in ranges]
        others = [across(theirs) for _, theirs in products]
        terms = [
            call(functools.partial(add_kernel, [[r] for r in range(n_pair)]), [rows_of(1, at)] * n_pair, (mine, other))
            for at, (mine, _), other in zip(ranges, products, others)
        ]
        return [[term[0]] + [shift(term[r], r) for r in range(1, n_pair)] for term in terms]

    decay_row = decay_log.T
    block = pltpu.VMEM((t, d), BF16)
    decay_block = pltpu.VMEM((1, t), F32)
    (state,) = call(
        state_kernel,
        [out((d + TILE_ROWS, d), BF16)],
        (key_in, value, decay_row),
        [block, block, decay_block, dma((3,))],
        far=3,
    )
    moves = [lambda i, k=k: i ^ k for k in range(1, seq_count)]
    states = [lax.ppermute(state, "seq", [(move(i), i) for i in range(seq_count)]) for move in moves]
    intra, grown, query_near, gain, w_out_near, w_in, member = call(
        functools.partial(within_kernel, n_pair),
        [
            out((t, d), F32),
            out((t, d), F32),
            out((t, d), BF16),
            out((8, d), F32),
            out(w_out.shape, BF16),
            out((2 * hid + TILE_ROWS, width), BF16),
            out((-(-experts // 8) * 8, t), F32),
        ],
        (query, key_in, value, decay_row, norm_gain[None, :], router.T, routes.T, w_out, w_gate[0].T, w_up[0].T, state),
        [
            block,
            block,
            decay_block,
            pltpu.VMEM((1, d), BF16),
            pltpu.VMEM((experts, width), BF16),
            pltpu.VMEM((routes.shape[1], t), jnp.int32),
            dma((10,)),
        ],
        far=10,
    )
    (normed,) = call(
        functools.partial(normed_kernel, n_pair, moves),
        [out((t, d), BF16)],
        (*states, intra, grown, query_near, gain),
    )
    terms = reduce(normed, w_out_near, mix_ranges)
    mixed = [
        call(functools.partial(sum_kernel, n_pair), [rows_of(1, at)], term)[0] for at, term in zip(mix_ranges, terms)
    ]
    gathered = [[shift(m, -r) if r else m for r in range(n_pair)] for m in mixed]
    (own,) = call(functools.partial(join_kernel, n_pair), [rows_of(n_pair, mix_ranges[0])], gathered[0])
    w_down_near, token = call(
        fetch_down_kernel, [out((hid, width), BF16), out((8, 128), F32)], (w_down[0], own), [dma], far=1
    )
    whole = [own]
    for at, blocks in zip(mix_ranges[1:], gathered[1:]):
        whole += call(functools.partial(join_kernel, n_pair), [rows_of(n_pair, at)], (*blocks, token))
    total = ()
    for at, own in zip(mix_ranges[:-1], whole):
        total = call(
            functools.partial(enter_kernel, at),
            [out((w_in.shape[0], t), F32)],
            (w_in, own, across(own), *total),
        )
    (hidden,) = call(
        functools.partial(hidden_kernel, mix_ranges[-1], slices, experts),
        [out((t, hid), BF16)],
        (w_in, whole[-1], across(whole[-1]), *total, member),
    )
    sums = reduce(hidden, w_down_near, out_ranges)
    return call(
        functools.partial(result_kernel, out_ranges, mix_ranges),
        [out((rows, width), BF16)],
        [x for some in sums for x in some] + mixed,
    )[0]


def solution(mesh):
    placed = (
        P("seq", "exp"),
        P("seq", "exp"),
        P("seq", "exp"),
        P("seq", "exp"),
        P("exp"),
        P("exp", None),
        P(),
        P("seq", None),
        P("exp", None, None),
        P("exp", None, None),
        P("exp", None, None),
    )

    def pick(query, key_in, value, decay_log, *rest):
        rows = query.shape[0] // lax.axis_size("exp")
        exp_count = lax.axis_size("exp")
        tiled = rows % TILE_ROWS == 0 and decay_log.shape[1] == 1
        for count in (exp_count, lax.axis_size("seq")):
            tiled = tiled and count >= 4 and count & (count - 1) == 0
        plan = local if tiled else plain_plan
        return plan(query, key_in, value, decay_log, *rest)

    return jax.shard_map(
        pick, mesh=mesh, in_specs=placed, out_specs=P(("seq", "exp"), None), check_vma=False
    )
```

```python
import functools

import jax
import jax.numpy as jnp
from jax import lax
from jax.experimental import pallas as pl
from jax.experimental.pallas import tpu as pltpu
from jax.sharding import PartitionSpec as P

F32 = jnp.float32
BF16 = jnp.bfloat16
TILE_ROWS = 16
COLUMNS = 1024
VMEM_LIMIT = 16 * 1024 * 1024


def plain_plan(query, key_in, value, decay_log, norm_gain, w_out, router, routes, w_gate, w_up, w_down):
    tok_count = query.shape[0]
    head_count = decay_log.shape[1]
    head_size = query.shape[1] // head_count
    top_count = routes.shape[1]
    expert_count = router.shape[1]
    capacity = max(2, 3 * tok_count * top_count // (2 * expert_count))
    exp_count = lax.axis_size("exp")
    slice_count = exp_count // expert_count
    queries = query.reshape(tok_count, head_count, head_size)
    keys_local = key_in.reshape(tok_count, head_count, head_size)
    values_local = value.reshape(tok_count, head_count, head_size)
    cumulative = jnp.cumsum(decay_log, axis=0)
    scores = jnp.einsum("thd,shd->hts", queries, keys_local, preferred_element_type=jnp.float32)
    spread = cumulative.T[:, :, None] - cumulative.T[:, None, :]
    causal = jnp.arange(tok_count)[:, None] >= jnp.arange(tok_count)[None, :]
    weights = jnp.where(causal, jnp.exp(jnp.where(causal, spread, 0.0)), 0.0)
    attend = (scores * weights / head_size).astype(jnp.bfloat16)
    intra_part = jnp.einsum(
        "hts,she->the", attend, values_local, preferred_element_type=jnp.float32
    )
    totals = cumulative[-1]
    tail_decay = jnp.exp(totals[None, :] - cumulative)
    state_delta = jnp.einsum(
        "shd,she->hde",
        keys_local.astype(jnp.float32) * tail_decay[:, :, None],
        values_local.astype(jnp.float32),
        precision=lax.Precision.HIGHEST,
    )
    decay_rows = lax.all_gather(totals[None, :], "seq", axis=0, tiled=True)
    my_rank = lax.axis_index("seq")
    seq_ranks = jnp.arange(decay_rows.shape[0])
    state_piece = lax.all_gather(
        state_delta[None].astype(jnp.bfloat16), "seq", axis=0, tiled=True
    ).astype(jnp.float32)
    piece_rank = jnp.arange(state_piece.shape[0])
    between = (seq_ranks[None, :] > piece_rank[:, None]) & (seq_ranks[None, :] < my_rank)
    logsum = jnp.dot(between.astype(jnp.float32), decay_rows, precision=lax.Precision.HIGHEST)
    factor = jnp.where((piece_rank < my_rank)[:, None], jnp.exp(logsum), 0.0)
    incoming = jnp.zeros_like(state_delta) + jnp.einsum(
        "ih,ihde->hde", factor, state_piece, precision=lax.Precision.HIGHEST
    )
    inter_part = (
        jnp.exp(cumulative)[:, :, None]
        * jnp.einsum(
            "thd,hde->the", queries.astype(jnp.float32), incoming, precision=lax.Precision.HIGHEST
        )
        / head_size
    )
    attended = intra_part + inter_part
    inverse_rms = lax.rsqrt(jnp.mean(attended * attended, axis=-1, keepdims=True) + 1e-06)
    gain_f32 = norm_gain.astype(jnp.float32).reshape(head_count, head_size)
    normed = (
        (attended * inverse_rms * gain_f32)
        .astype(jnp.bfloat16)
        .reshape(tok_count, head_count * head_size)
    )
    own_mixed = lax.psum_scatter(
        jnp.dot(normed, w_out, preferred_element_type=jnp.float32),
        "exp",
        scatter_dimension=0,
        tiled=True,
    ).astype(jnp.bfloat16)
    mixed = lax.all_gather(own_mixed, "exp", axis=0, tiled=True)
    logits = jnp.dot(mixed, router, preferred_element_type=jnp.float32)
    member = routes[:, :, None] == jnp.arange(expert_count)[None, None, :]
    picked = jnp.sum(jnp.where(member, logits[:, None, :], 0.0), axis=-1)
    raised = jnp.exp(picked)
    gate_probs = raised / jnp.sum(raised, axis=-1, keepdims=True)
    my_expert = lax.axis_index("exp") // slice_count
    flat_hit = (routes.reshape(-1) == my_expert).astype(jnp.int32)
    slot_flat = jnp.cumsum(flat_hit) - flat_hit
    slot_match = (slot_flat[:, None] == jnp.arange(capacity)[None, :]) & (flat_hit[:, None] > 0)
    token_select = jnp.sum(
        slot_match.reshape(tok_count, top_count, capacity).astype(jnp.float32), axis=1
    )
    token_gate = jnp.sum(jnp.where(routes == my_expert, gate_probs, 0.0), axis=1)
    slot_rows = jnp.dot(
        token_select.astype(jnp.bfloat16).T, mixed, preferred_element_type=jnp.float32
    ).astype(jnp.bfloat16)
    gate_part = jnp.dot(slot_rows, w_gate[0], preferred_element_type=jnp.float32)
    up_part = jnp.dot(slot_rows, w_up[0], preferred_element_type=jnp.float32)
    hidden = (jax.nn.silu(gate_part) * up_part).astype(jnp.bfloat16)
    slice_out = jnp.dot(hidden, w_down[0], preferred_element_type=jnp.float32)
    spread_out = jnp.dot(token_select, slice_out, precision=lax.Precision.HIGHEST)
    summed = lax.psum_scatter(
        token_gate[:, None] * spread_out, "exp", scatter_dimension=0, tiled=True
    )
    return (own_mixed.astype(jnp.float32) + summed).astype(jnp.bfloat16)


def iota2(shape, axis):
    return lax.broadcasted_iota(jnp.int32, shape, axis)


def cumulate(decay_row):
    t = decay_row.shape[1]
    row, col = iota2((t, t), 0), iota2((t, t), 1)
    spread = jnp.broadcast_to(decay_row, (t, t))
    column = jnp.sum(jnp.where(col <= row, spread, 0.0), axis=1, keepdims=True)
    own = jnp.sum(jnp.where(col == row, spread, 0.0), axis=1, keepdims=True)
    line = jnp.sum(jnp.where(row <= col, own, 0.0), axis=0, keepdims=True)
    return column, line


def dot_f32(a, b, dims):
    return lax.dot_general(a, b, (dims, ((), ())), preferred_element_type=F32)


def split_dot(a_f32, b, dims):
    high = a_f32.astype(BF16)
    low = (a_f32 - high.astype(F32)).astype(BF16)
    return dot_f32(high, b, dims) + dot_f32(low, b, dims)


def dma_in(sems, pairs):
    copies = [pltpu.make_async_copy(a, b, sems.at[i]) for i, (a, b) in enumerate(pairs)]
    for copy in copies:
        copy.start()
    return copies


def put_state(out_ref, state, total):
    d = state.shape[1]
    out_ref[0:d, :] = state.astype(BF16)
    wide = jnp.broadcast_to(total, (TILE_ROWS, d))
    part0 = wide.astype(BF16).astype(F32)
    part1 = (wide - part0).astype(BF16).astype(F32)
    part2 = wide - part0 - part1
    row = iota2((TILE_ROWS, d), 0)
    parts = jnp.where(row == 0, part0, jnp.where(row == 1, part1, jnp.where(row == 2, part2, 0.0)))
    out_ref[d:, :] = parts.astype(BF16)


def get_state(ref):
    d = ref.shape[1]
    return ref[0:d, :].astype(F32), jnp.sum(ref[d:, :].astype(F32), axis=0, keepdims=True)


def state_kernel(key_hbm, value_hbm, decay_hbm, out_ref, key_ref, value_ref, decay_ref, sems):
    t, d = key_ref.shape
    copies = dma_in(sems, [(decay_hbm, decay_ref), (key_hbm, key_ref), (value_hbm, value_ref)])
    for copy in copies:
        copy.wait()
    column, _ = cumulate(decay_ref[...])
    total = column[t - 1 :, :]
    keyed = key_ref[...].astype(F32) * jnp.exp(total - column)
    put_state(out_ref, split_dot(keyed, value_ref[...], ((0,), (0,))), jnp.broadcast_to(total, (1, d)))


def within_kernel(
    n_pair, query_hbm, key_hbm, value_hbm, decay_hbm, gain_hbm, router_hbm, routes_hbm, w_out_hbm, gate_hbm, up_hbm, _,
    intra_ref, grown_ref, query_ref, gain_ref, w_out_ref, in_ref, member_ref,
    key_ref, value_ref, decay_ref, gain_in_ref, router_ref, routes_ref, sems,
):
    t, d = query_ref.shape
    hid = gate_hbm.shape[0]
    copies = dma_in(
        sems,
        [
            (decay_hbm, decay_ref),
            (query_hbm, query_ref),
            (key_hbm, key_ref),
            (value_hbm, value_ref),
            (gain_hbm, gain_in_ref),
            (router_hbm, router_ref),
            (routes_hbm, routes_ref),
            (w_out_hbm, w_out_ref),
            (gate_hbm, in_ref.at[0:hid]),
            (up_hbm, in_ref.at[hid : 2 * hid]),
        ],
    )
    for copy in copies[:7]:
        copy.wait()
    column, line = cumulate(decay_ref[...])
    query, key, value = query_ref[...], key_ref[...], value_ref[...]
    scores = dot_f32(query, key, ((1,), (1,)))
    causal = iota2((t, t), 0) >= iota2((t, t), 1)
    weights = jnp.where(causal, jnp.exp(jnp.where(causal, column - line, 0.0)), 0.0)
    attend = (scores * weights * (1.0 / d)).astype(BF16)
    intra_ref[...] = dot_f32(attend, value, ((1,), (0,)))
    grown_ref[...] = jnp.broadcast_to(jnp.exp(column) * (1.0 / d), (t, d))
    gain_ref[...] = jnp.broadcast_to(gain_in_ref[...].astype(F32), gain_ref.shape)
    experts = router_ref.shape[0]
    in_ref[2 * hid :, :] = jnp.zeros((TILE_ROWS, in_ref.shape[1]), BF16)
    in_ref[2 * hid : 2 * hid + experts, :] = router_ref[...]
    padded = member_ref.shape[0]
    hits = jnp.zeros((padded, t), F32)
    for k in range(routes_ref.shape[0]):
        hits = hits + jnp.where(routes_ref[k : k + 1, :] == iota2((padded, t), 0), 1.0, 0.0)
    exp_index = lax.axis_index("exp")
    place = place_matrix(t // (2 * n_pair), n_pair, exp_index // 2, exp_index % 2)
    member_ref[...] = dot_f32(hits.astype(BF16), place, ((1,), (1,)))
    for copy in copies[7:]:
        copy.wait()


def place_matrix(rows, n_pair, pair, core):
    size = 2 * n_pair * rows
    i, j = iota2((size, size), 0), iota2((size, size), 1)
    half, inner = i // (n_pair * rows), i % (n_pair * rows)
    who = (inner // rows + pair) % n_pair
    source = (2 * who + (core + half) % 2) * rows + inner % rows
    return jnp.where(source == j, 1.0, 0.0).astype(BF16)


def fetch_down_kernel(down_hbm, _, down_ref, token_ref, sem):
    copy = pltpu.make_async_copy(down_hbm, down_ref, sem)
    copy.start()
    token_ref[...] = jnp.zeros(token_ref.shape, F32)
    copy.wait()


def normed_kernel(n_pair, moves, *refs):
    states = refs[: len(moves)]
    intra_ref, grown_ref, query_ref, gain_ref, mine_ref, theirs_ref = refs[len(moves) : len(moves) + 4] + refs[-2:]
    t, d = query_ref.shape
    me = lax.axis_index("seq")
    ranks = [move(me) for move in moves]
    parts = [get_state(ref) for ref in states]
    incoming = jnp.zeros((d, d), F32)
    for rank, (state, _) in zip(ranks, parts):
        logsum = jnp.zeros((1, d), F32)
        for other, (_, total) in zip(ranks, parts):
            logsum = logsum + jnp.where(jnp.logical_and(rank < other, other < me), total, 0.0)
        incoming = incoming + jnp.where(rank < me, jnp.exp(logsum), 0.0) * state
    high = incoming.astype(BF16)
    low = (incoming - high.astype(F32)).astype(BF16)
    query = query_ref[...]
    read = dot_f32(query, high, ((1,), (0,))) + dot_f32(query, low, ((1,), (0,)))
    attended = intra_ref[...] + grown_ref[...] * read
    inverse = lax.rsqrt(jnp.mean(attended * attended, axis=1, keepdims=True) + 1e-06)
    normed = (attended * inverse * gain_ref[0:1, :]).astype(BF16)
    exp_index = lax.axis_index("exp")
    place = place_matrix(t // (2 * n_pair), n_pair, exp_index // 2, exp_index % 2)
    normed = dot_f32(place, normed, ((1,), (0,))).astype(BF16)
    mine_ref[...] = normed[: t // 2]
    theirs_ref[...] = normed[t // 2 :]


def product_kernel(at, a_ref, b_ref, wa_ref, wb_ref, *outs):
    rows = outs[0].shape[0]
    for i in range(at.start, at.stop, COLUMNS):
        some, there = slice(i, i + COLUMNS), slice(i - at.start, i - at.start + COLUMNS)
        part = dot_f32(a_ref[...], wa_ref[:, some], ((1,), (0,))) + dot_f32(b_ref[...], wb_ref[:, some], ((1,), (0,)))
        for r, ref in enumerate(outs):
            ref[:, there] = part[r * rows : (r + 1) * rows].astype(BF16)


def sum_kernel(count, *refs):
    total = refs[0][...].astype(F32)
    for ref in refs[1:count]:
        total = total + ref[...].astype(F32)
    refs[-1][...] = total.astype(BF16)


def join_kernel(count, *refs):
    start = 0
    for ref in refs[:count]:
        refs[-1][start : start + ref.shape[0], :] = ref[...]
        start += ref.shape[0]


def enter_part(at, in_ref, own_ref, other_ref):
    x = jnp.concatenate([own_ref[...], other_ref[...]], axis=0)
    return dot_f32(in_ref[:, at], x, ((1,), (1,)))


def enter_kernel(at, in_ref, own_ref, other_ref, out_ref):
    out_ref[...] = enter_part(at, in_ref, own_ref, other_ref)


def hidden_kernel(at, slices, experts, in_ref, own_ref, other_ref, before_ref, member_ref, mine_ref, theirs_ref):
    total = before_ref[...] + enter_part(at, in_ref, own_ref, other_ref)
    half, hid = mine_ref.shape
    t = 2 * half
    gate, up, logits = total[0:hid], total[hid : 2 * hid], total[2 * hid : 2 * hid + experts]
    raised = jnp.where(member_ref[0:experts, :] > 0.5, jnp.exp(logits), 0.0)
    mine = iota2((experts, t), 0) == lax.axis_index("exp") // slices
    prob = jnp.sum(jnp.where(mine, raised, 0.0), axis=0, keepdims=True) / jnp.sum(raised, axis=0, keepdims=True)
    hidden = (gate / (1.0 + jnp.exp(-gate)) * up * prob).T.astype(BF16)
    mine_ref[...] = hidden[:half]
    theirs_ref[...] = hidden[half:]


def result_kernel(count, *refs):
    out_ref = refs[-1]
    width = refs[0].shape[1]
    for i in range(len(refs) // count):
        total = refs[i * count][...].astype(F32)
        for ref in refs[i * count + 1 : (i + 1) * count]:
            total = total + ref[...].astype(F32)
        out_ref[:, i * width : (i + 1) * width] = total.astype(BF16)


def call(kernel, outs, args, scratch=(), far=0):
    whole = pl.BlockSpec(memory_space=pltpu.VMEM)
    if far:
        args = [pltpu.with_memory_space_constraint(a, pltpu.HBM) for a in args[:far]] + list(args[far:])
    return pl.pallas_call(
        kernel,
        out_shape=outs,
        in_specs=[pl.BlockSpec(memory_space=pl.ANY) if far else whole] * len(args),
        out_specs=[whole] * len(outs),
        scratch_shapes=list(scratch),
        compiler_params=pltpu.CompilerParams(vmem_limit_bytes=VMEM_LIMIT),
        cost_estimate=pl.CostEstimate(flops=0, bytes_accessed=0, transcendentals=0),
    )(*args)


def local(query, key_in, value, decay_log, norm_gain, w_out, router, routes, w_gate, w_up, w_down):
    t, d = query.shape
    width = w_out.shape[1]
    exp_count, seq_count = lax.axis_size("exp"), lax.axis_size("seq")
    n_pair = exp_count // 2
    rows = t // exp_count
    experts = router.shape[1]
    slices = exp_count // experts
    hid = w_gate.shape[2]
    out = jax.ShapeDtypeStruct
    dma = pltpu.SemaphoreType.DMA

    def shift(x, r):
        return lax.ppermute(x, "exp", [(e, (e + 2 * r) % exp_count) for e in range(exp_count)])

    def across(x):
        return lax.ppermute(x, "exp", [(e, e ^ 1) for e in range(exp_count)])

    size = width // 2
    ranges = [slice(0, size), slice(size, width)]

    def rows_of(count):
        return out((count * rows, size), BF16)

    def reduce(mine, theirs, w, w_other):
        other = across(theirs)
        terms = [
            call(functools.partial(product_kernel, at), [rows_of(1)] * n_pair, (mine, other, w, w_other)) for at in ranges
        ]
        return [[term[0]] + [shift(term[r], r) for r in range(1, n_pair)] for term in terms]

    decay_row = decay_log.T
    block = pltpu.VMEM((t, d), BF16)
    decay_block = pltpu.VMEM((1, t), F32)
    (state,) = call(
        state_kernel,
        [out((d + TILE_ROWS, d), BF16)],
        (key_in, value, decay_row),
        [block, block, decay_block, dma((3,))],
        far=3,
    )
    moves = [lambda i, k=k: i ^ k for k in range(1, seq_count)]
    states = [lax.ppermute(state, "seq", [(move(i), i) for i in range(seq_count)]) for move in moves]
    intra, grown, query_near, gain, w_out_near, w_in, member = call(
        functools.partial(within_kernel, n_pair),
        [
            out((t, d), F32),
            out((t, d), F32),
            out((t, d), BF16),
            out((8, d), F32),
            out(w_out.shape, BF16),
            out((2 * hid + TILE_ROWS, width), BF16),
            out((-(-experts // 8) * 8, t), F32),
        ],
        (query, key_in, value, decay_row, norm_gain[None, :], router.T, routes.T, w_out, w_gate[0].T, w_up[0].T, state),
        [
            block,
            block,
            decay_block,
            pltpu.VMEM((1, d), BF16),
            pltpu.VMEM((experts, width), BF16),
            pltpu.VMEM((routes.shape[1], t), jnp.int32),
            dma((10,)),
        ],
        far=10,
    )
    w_out_other, w_down_other = across(w_out), across(w_down[0])
    mine, theirs = call(
        functools.partial(normed_kernel, n_pair, moves),
        [out((t // 2, d), BF16)] * 2,
        (*states, intra, grown, query_near, gain, w_down_other),
    )
    terms = reduce(mine, theirs, w_out_near, w_out_other)
    mixed = [call(functools.partial(sum_kernel, n_pair), [rows_of(1)], term)[0] for term in terms]
    gathered = [[shift(m, -r) if r else m for r in range(n_pair)] for m in mixed]
    own, after = [], ()
    for blocks in gathered:
        own += call(functools.partial(join_kernel, n_pair), [rows_of(n_pair)], (*blocks, *after))
        if not after:
            w_down_near, token = call(
                fetch_down_kernel, [out((hid, width), BF16), out((8, 128), F32)], (w_down[0], own[0]), [dma], far=1
            )
            after = (token,)
    left, right = ranges
    (total,) = call(functools.partial(enter_kernel, left), [out((w_in.shape[0], t), F32)], (w_in, own[0], across(own[0])))
    mine, theirs = call(
        functools.partial(hidden_kernel, right, slices, experts),
        [out((t // 2, hid), BF16)] * 2,
        (w_in, own[1], across(own[1]), total, member),
    )
    sums = reduce(mine, theirs, w_down_near, w_down_other)
    args = [x for some, m in zip(sums, mixed) for x in (*some, m)]
    return call(functools.partial(result_kernel, n_pair + 1), [out((rows, width), BF16)], args)[0]


def solution(mesh):
    placed = (
        P("seq", "exp"),
        P("seq", "exp"),
        P("seq", "exp"),
        P("seq", "exp"),
        P("exp"),
        P("exp", None),
        P(),
        P("seq", None),
        P("exp", None, None),
        P("exp", None, None),
        P("exp", None, None),
    )

    def pick(query, key_in, value, decay_log, *rest):
        rows = query.shape[0] // lax.axis_size("exp")
        exp_count = lax.axis_size("exp")
        tiled = rows % TILE_ROWS == 0 and decay_log.shape[1] == 1
        for count in (exp_count, lax.axis_size("seq")):
            tiled = tiled and count >= 4 and count & (count - 1) == 0
        plan = local if tiled else plain_plan
        return plan(query, key_in, value, decay_log, *rest)

    return jax.shard_map(
        pick, mesh=mesh, in_specs=placed, out_specs=P(("seq", "exp"), None), check_vma=False
    )
```

```python
import functools

import jax
import jax.numpy as jnp
from jax import lax
from jax.experimental import pallas as pl
from jax.experimental.pallas import tpu as pltpu
from jax.sharding import PartitionSpec as P

F32 = jnp.float32
BF16 = jnp.bfloat16
TILE_ROWS = 16
COLUMNS = 1024
PARTS = 2
VMEM_LIMIT = 16 * 1024 * 1024


def plain_plan(query, key_in, value, decay_log, norm_gain, w_out, router, routes, w_gate, w_up, w_down):
    tok_count = query.shape[0]
    head_count = decay_log.shape[1]
    head_size = query.shape[1] // head_count
    top_count = routes.shape[1]
    expert_count = router.shape[1]
    capacity = max(2, 3 * tok_count * top_count // (2 * expert_count))
    exp_count = lax.axis_size("exp")
    slice_count = exp_count // expert_count
    queries = query.reshape(tok_count, head_count, head_size)
    keys_local = key_in.reshape(tok_count, head_count, head_size)
    values_local = value.reshape(tok_count, head_count, head_size)
    cumulative = jnp.cumsum(decay_log, axis=0)
    scores = jnp.einsum("thd,shd->hts", queries, keys_local, preferred_element_type=jnp.float32)
    spread = cumulative.T[:, :, None] - cumulative.T[:, None, :]
    causal = jnp.arange(tok_count)[:, None] >= jnp.arange(tok_count)[None, :]
    weights = jnp.where(causal, jnp.exp(jnp.where(causal, spread, 0.0)), 0.0)
    attend = (scores * weights / head_size).astype(jnp.bfloat16)
    intra_part = jnp.einsum(
        "hts,she->the", attend, values_local, preferred_element_type=jnp.float32
    )
    totals = cumulative[-1]
    tail_decay = jnp.exp(totals[None, :] - cumulative)
    state_delta = jnp.einsum(
        "shd,she->hde",
        keys_local.astype(jnp.float32) * tail_decay[:, :, None],
        values_local.astype(jnp.float32),
        precision=lax.Precision.HIGHEST,
    )
    decay_rows = lax.all_gather(totals[None, :], "seq", axis=0, tiled=True)
    my_rank = lax.axis_index("seq")
    seq_ranks = jnp.arange(decay_rows.shape[0])
    state_piece = lax.all_gather(
        state_delta[None].astype(jnp.bfloat16), "seq", axis=0, tiled=True
    ).astype(jnp.float32)
    piece_rank = jnp.arange(state_piece.shape[0])
    between = (seq_ranks[None, :] > piece_rank[:, None]) & (seq_ranks[None, :] < my_rank)
    logsum = jnp.dot(between.astype(jnp.float32), decay_rows, precision=lax.Precision.HIGHEST)
    factor = jnp.where((piece_rank < my_rank)[:, None], jnp.exp(logsum), 0.0)
    incoming = jnp.zeros_like(state_delta) + jnp.einsum(
        "ih,ihde->hde", factor, state_piece, precision=lax.Precision.HIGHEST
    )
    inter_part = (
        jnp.exp(cumulative)[:, :, None]
        * jnp.einsum(
            "thd,hde->the", queries.astype(jnp.float32), incoming, precision=lax.Precision.HIGHEST
        )
        / head_size
    )
    attended = intra_part + inter_part
    inverse_rms = lax.rsqrt(jnp.mean(attended * attended, axis=-1, keepdims=True) + 1e-06)
    gain_f32 = norm_gain.astype(jnp.float32).reshape(head_count, head_size)
    normed = (
        (attended * inverse_rms * gain_f32)
        .astype(jnp.bfloat16)
        .reshape(tok_count, head_count * head_size)
    )
    own_mixed = lax.psum_scatter(
        jnp.dot(normed, w_out, preferred_element_type=jnp.float32),
        "exp",
        scatter_dimension=0,
        tiled=True,
    ).astype(jnp.bfloat16)
    mixed = lax.all_gather(own_mixed, "exp", axis=0, tiled=True)
    logits = jnp.dot(mixed, router, preferred_element_type=jnp.float32)
    member = routes[:, :, None] == jnp.arange(expert_count)[None, None, :]
    picked = jnp.sum(jnp.where(member, logits[:, None, :], 0.0), axis=-1)
    raised = jnp.exp(picked)
    gate_probs = raised / jnp.sum(raised, axis=-1, keepdims=True)
    my_expert = lax.axis_index("exp") // slice_count
    flat_hit = (routes.reshape(-1) == my_expert).astype(jnp.int32)
    slot_flat = jnp.cumsum(flat_hit) - flat_hit
    slot_match = (slot_flat[:, None] == jnp.arange(capacity)[None, :]) & (flat_hit[:, None] > 0)
    token_select = jnp.sum(
        slot_match.reshape(tok_count, top_count, capacity).astype(jnp.float32), axis=1
    )
    token_gate = jnp.sum(jnp.where(routes == my_expert, gate_probs, 0.0), axis=1)
    slot_rows = jnp.dot(
        token_select.astype(jnp.bfloat16).T, mixed, preferred_element_type=jnp.float32
    ).astype(jnp.bfloat16)
    gate_part = jnp.dot(slot_rows, w_gate[0], preferred_element_type=jnp.float32)
    up_part = jnp.dot(slot_rows, w_up[0], preferred_element_type=jnp.float32)
    hidden = (jax.nn.silu(gate_part) * up_part).astype(jnp.bfloat16)
    slice_out = jnp.dot(hidden, w_down[0], preferred_element_type=jnp.float32)
    spread_out = jnp.dot(token_select, slice_out, precision=lax.Precision.HIGHEST)
    summed = lax.psum_scatter(
        token_gate[:, None] * spread_out, "exp", scatter_dimension=0, tiled=True
    )
    return (own_mixed.astype(jnp.float32) + summed).astype(jnp.bfloat16)


def iota2(shape, axis):
    return lax.broadcasted_iota(jnp.int32, shape, axis)


def cumulate(decay_row):
    t = decay_row.shape[1]
    row, col = iota2((t, t), 0), iota2((t, t), 1)
    spread = jnp.broadcast_to(decay_row, (t, t))
    column = jnp.sum(jnp.where(col <= row, spread, 0.0), axis=1, keepdims=True)
    own = jnp.sum(jnp.where(col == row, spread, 0.0), axis=1, keepdims=True)
    line = jnp.sum(jnp.where(row <= col, own, 0.0), axis=0, keepdims=True)
    return column, line


def dot_f32(a, b, dims):
    return lax.dot_general(a, b, (dims, ((), ())), preferred_element_type=F32)


def split_dot(a_f32, b, dims):
    high = a_f32.astype(BF16)
    low = (a_f32 - high.astype(F32)).astype(BF16)
    return dot_f32(high, b, dims) + dot_f32(low, b, dims)


def dma_in(sems, pairs):
    copies = [pltpu.make_async_copy(a, b, sems.at[i]) for i, (a, b) in enumerate(pairs)]
    for copy in copies:
        copy.start()
    return copies


def put_state(out_ref, state, total):
    d = state.shape[1]
    out_ref[0:d, :] = state.astype(BF16)
    wide = jnp.broadcast_to(total, (TILE_ROWS, d))
    part0 = wide.astype(BF16).astype(F32)
    part1 = (wide - part0).astype(BF16).astype(F32)
    part2 = wide - part0 - part1
    row = iota2((TILE_ROWS, d), 0)
    parts = jnp.where(row == 0, part0, jnp.where(row == 1, part1, jnp.where(row == 2, part2, 0.0)))
    out_ref[d:, :] = parts.astype(BF16)


def get_state(ref):
    d = ref.shape[1]
    return ref[0:d, :].astype(F32), jnp.sum(ref[d:, :].astype(F32), axis=0, keepdims=True)


def state_kernel(key_hbm, value_hbm, decay_hbm, out_ref, key_ref, value_ref, decay_ref, sems):
    t, d = key_ref.shape
    copies = dma_in(sems, [(decay_hbm, decay_ref), (key_hbm, key_ref), (value_hbm, value_ref)])
    for copy in copies:
        copy.wait()
    column, _ = cumulate(decay_ref[...])
    total = column[t - 1 :, :]
    keyed = key_ref[...].astype(F32) * jnp.exp(total - column)
    put_state(out_ref, split_dot(keyed, value_ref[...], ((0,), (0,))), jnp.broadcast_to(total, (1, d)))


def within_kernel(
    n_pair, query_hbm, key_hbm, value_hbm, decay_hbm, gain_hbm, router_hbm, routes_hbm, w_out_hbm, gate_hbm, up_hbm, _,
    intra_ref, grown_ref, query_ref, gain_ref, w_out_ref, in_ref, member_ref,
    key_ref, value_ref, decay_ref, gain_in_ref, router_ref, routes_ref, sems,
):
    t, d = query_ref.shape
    hid = gate_hbm.shape[0]
    copies = dma_in(
        sems,
        [
            (decay_hbm, decay_ref),
            (query_hbm, query_ref),
            (key_hbm, key_ref),
            (value_hbm, value_ref),
            (gain_hbm, gain_in_ref),
            (router_hbm, router_ref),
            (routes_hbm, routes_ref),
            (w_out_hbm, w_out_ref),
            (gate_hbm, in_ref.at[0:hid]),
            (up_hbm, in_ref.at[hid : 2 * hid]),
        ],
    )
    for copy in copies[:7]:
        copy.wait()
    column, line = cumulate(decay_ref[...])
    query, key, value = query_ref[...], key_ref[...], value_ref[...]
    scores = dot_f32(query, key, ((1,), (1,)))
    causal = iota2((t, t), 0) >= iota2((t, t), 1)
    weights = jnp.where(causal, jnp.exp(jnp.where(causal, column - line, 0.0)), 0.0)
    attend = (scores * weights * (1.0 / d)).astype(BF16)
    intra_ref[...] = dot_f32(attend, value, ((1,), (0,)))
    grown_ref[...] = jnp.broadcast_to(jnp.exp(column) * (1.0 / d), (t, d))
    gain_ref[...] = jnp.broadcast_to(gain_in_ref[...].astype(F32), gain_ref.shape)
    experts = router_ref.shape[0]
    in_ref[2 * hid :, :] = jnp.zeros((TILE_ROWS, in_ref.shape[1]), BF16)
    in_ref[2 * hid : 2 * hid + experts, :] = router_ref[...]
    padded = member_ref.shape[0]
    hits = jnp.zeros((padded, t), F32)
    for k in range(routes_ref.shape[0]):
        hits = hits + jnp.where(routes_ref[k : k + 1, :] == iota2((padded, t), 0), 1.0, 0.0)
    exp_index = lax.axis_index("exp")
    place = place_matrix(t // (2 * n_pair), n_pair, exp_index // 2, exp_index % 2)
    member_ref[...] = dot_f32(hits.astype(BF16), place, ((1,), (1,)))
    for copy in copies[7:]:
        copy.wait()


def place_matrix(rows, n_pair, pair, core):
    size = 2 * n_pair * rows
    i, j = iota2((size, size), 0), iota2((size, size), 1)
    half, inner = i // (n_pair * rows), i % (n_pair * rows)
    whose = (core + half) % 2
    who = (inner // rows * (1 - 2 * whose) + pair + n_pair) % n_pair
    source = (2 * who + whose) * rows + inner % rows
    return jnp.where(source == j, 1.0, 0.0).astype(BF16)


def fetch_down_kernel(down_hbm, _, down_ref, token_ref, sem):
    copy = pltpu.make_async_copy(down_hbm, down_ref, sem)
    copy.start()
    token_ref[...] = jnp.zeros(token_ref.shape, F32)
    copy.wait()


def normed_kernel(n_pair, moves, *refs):
    states = refs[: len(moves)]
    intra_ref, grown_ref, query_ref, gain_ref, out_ref = refs[len(moves) :]
    t, d = query_ref.shape
    me = lax.axis_index("seq")
    ranks = [move(me) for move in moves]
    parts = [get_state(ref) for ref in states]
    incoming = jnp.zeros((d, d), F32)
    for rank, (state, _) in zip(ranks, parts):
        logsum = jnp.zeros((1, d), F32)
        for other, (_, total) in zip(ranks, parts):
            logsum = logsum + jnp.where(jnp.logical_and(rank < other, other < me), total, 0.0)
        incoming = incoming + jnp.where(rank < me, jnp.exp(logsum), 0.0) * state
    high = incoming.astype(BF16)
    low = (incoming - high.astype(F32)).astype(BF16)
    query = query_ref[...]
    read = dot_f32(query, high, ((1,), (0,))) + dot_f32(query, low, ((1,), (0,)))
    attended = intra_ref[...] + grown_ref[...] * read
    inverse = lax.rsqrt(jnp.mean(attended * attended, axis=1, keepdims=True) + 1e-06)
    normed = (attended * inverse * gain_ref[0:1, :]).astype(BF16)
    exp_index = lax.axis_index("exp")
    place = place_matrix(t // (2 * n_pair), n_pair, exp_index // 2, exp_index % 2)
    out_ref[...] = dot_f32(place, normed, ((1,), (0,))).astype(BF16)


def product_kernel(at, x_ref, w_ref, mine_ref, theirs_ref):
    half = mine_ref.shape[0]
    for i in range(at.start, at.stop, COLUMNS):
        part = dot_f32(x_ref[...], w_ref[:, i : i + COLUMNS], ((1,), (0,))).astype(BF16)
        mine_ref[:, i - at.start : i - at.start + COLUMNS] = part[:half]
        theirs_ref[:, i - at.start : i - at.start + COLUMNS] = part[half:]


def add_kernel(groups, a_ref, b_ref, *refs):
    outs = refs[-len(groups) :]
    rows = outs[0].shape[0] // len(groups[0])
    for group, ref in zip(groups, outs):
        for i, block in enumerate(group):
            at = slice(block * rows, (block + 1) * rows)
            total = a_ref[at, :].astype(F32) + b_ref[at, :].astype(F32)
            ref[i * rows : (i + 1) * rows, :] = total.astype(ref.dtype)


def sum_kernel(count, *refs):
    total = refs[0][...].astype(F32)
    for ref in refs[1:count]:
        total = total + ref[...].astype(F32)
    refs[-1][...] = total.astype(BF16)


def join_kernel(count, *refs):
    start = 0
    for ref in refs[:count]:
        refs[-1][start : start + ref.shape[0], :] = ref[...]
        start += ref.shape[0]


def enter_part(at, in_ref, own_ref, other_ref):
    x = jnp.concatenate([own_ref[...], other_ref[...]], axis=0)
    return dot_f32(in_ref[:, at], x, ((1,), (1,)))


def enter_kernel(at, in_ref, own_ref, other_ref, out_ref):
    out_ref[...] = enter_part(at, in_ref, own_ref, other_ref)


def hidden_kernel(at, slices, experts, in_ref, own_ref, other_ref, before_ref, member_ref, out_ref):
    total = before_ref[...] + enter_part(at, in_ref, own_ref, other_ref)
    t, hid = out_ref.shape
    gate, up, logits = total[0:hid], total[hid : 2 * hid], total[2 * hid : 2 * hid + experts]
    raised = jnp.where(member_ref[0:experts, :] > 0.5, jnp.exp(logits), 0.0)
    mine = iota2((experts, t), 0) == lax.axis_index("exp") // slices
    prob = jnp.sum(jnp.where(mine, raised, 0.0), axis=0, keepdims=True) / jnp.sum(raised, axis=0, keepdims=True)
    out_ref[...] = (gate / (1.0 + jnp.exp(-gate)) * up * prob).T.astype(BF16)


def result_kernel(count, *refs):
    out_ref = refs[-1]
    width = refs[0].shape[1]
    for i in range(len(refs) // count):
        total = refs[i * count][...].astype(F32)
        for ref in refs[i * count + 1 : (i + 1) * count]:
            total = total + ref[...].astype(F32)
        out_ref[:, i * width : (i + 1) * width] = total.astype(BF16)


def call(kernel, outs, args, scratch=(), far=0):
    whole = pl.BlockSpec(memory_space=pltpu.VMEM)
    if far:
        args = [pltpu.with_memory_space_constraint(a, pltpu.HBM) for a in args[:far]] + list(args[far:])
    return pl.pallas_call(
        kernel,
        out_shape=outs,
        in_specs=[pl.BlockSpec(memory_space=pl.ANY) if far else whole] * len(args),
        out_specs=[whole] * len(outs),
        scratch_shapes=list(scratch),
        compiler_params=pltpu.CompilerParams(vmem_limit_bytes=VMEM_LIMIT),
        cost_estimate=pl.CostEstimate(flops=0, bytes_accessed=0, transcendentals=0),
    )(*args)


def local(query, key_in, value, decay_log, norm_gain, w_out, router, routes, w_gate, w_up, w_down):
    t, d = query.shape
    width = w_out.shape[1]
    exp_count, seq_count = lax.axis_size("exp"), lax.axis_size("seq")
    n_pair = exp_count // 2
    rows = t // exp_count
    experts = router.shape[1]
    slices = exp_count // experts
    hid = w_gate.shape[2]
    out = jax.ShapeDtypeStruct
    dma = pltpu.SemaphoreType.DMA

    def shift(x, r):
        return lax.ppermute(x, "exp", [(e, (e + 2 * r * (1 - 2 * (e % 2))) % exp_count) for e in range(exp_count)])

    def across(x):
        return lax.ppermute(x, "exp", [(e, e ^ 1) for e in range(exp_count)])

    size = width // PARTS
    ranges = [slice(i * size, (i + 1) * size) for i in range(PARTS)]

    def rows_of(count):
        return out((count * rows, size), BF16)

    def reduce(products):
        others = [across(theirs) for _, theirs in products]
        terms = [
            call(functools.partial(add_kernel, [[r] for r in range(n_pair)]), [rows_of(1)] * n_pair, (mine, other))
            for (mine, _), other in zip(products, others)
        ]
        return [[term[0]] + [shift(term[r], r) for r in range(1, n_pair)] for term in terms]

    def products_of(x, w):
        return [call(functools.partial(product_kernel, at), [rows_of(n_pair)] * 2, (x, w)) for at in ranges]

    decay_row = decay_log.T
    block = pltpu.VMEM((t, d), BF16)
    decay_block = pltpu.VMEM((1, t), F32)
    (state,) = call(
        state_kernel,
        [out((d + TILE_ROWS, d), BF16)],
        (key_in, value, decay_row),
        [block, block, decay_block, dma((3,))],
        far=3,
    )
    moves = [lambda i, k=k: i ^ k for k in range(1, seq_count)]
    states = [lax.ppermute(state, "seq", [(move(i), i) for i in range(seq_count)]) for move in moves]
    intra, grown, query_near, gain, w_out_near, w_in, member = call(
        functools.partial(within_kernel, n_pair),
        [
            out((t, d), F32),
            out((t, d), F32),
            out((t, d), BF16),
            out((8, d), F32),
            out(w_out.shape, BF16),
            out((2 * hid + TILE_ROWS, width), BF16),
            out((-(-experts // 8) * 8, t), F32),
        ],
        (query, key_in, value, decay_row, norm_gain[None, :], router.T, routes.T, w_out, w_gate[0].T, w_up[0].T, state),
        [
            block,
            block,
            decay_block,
            pltpu.VMEM((1, d), BF16),
            pltpu.VMEM((experts, width), BF16),
            pltpu.VMEM((routes.shape[1], t), jnp.int32),
            dma((10,)),
        ],
        far=10,
    )
    (normed,) = call(
        functools.partial(normed_kernel, n_pair, moves),
        [out((t, d), BF16)],
        (*states, intra, grown, query_near, gain),
    )
    terms = reduce(products_of(normed, w_out_near))
    mixed = [call(functools.partial(sum_kernel, n_pair), [rows_of(1)], term)[0] for term in terms]
    gathered = [[shift(m, -r) if r else m for r in range(n_pair)] for m in mixed]
    own, after = [], ()
    for blocks in gathered:
        own += call(functools.partial(join_kernel, n_pair), [rows_of(n_pair)], (*blocks, *after))
        if not after:
            w_down_near, token = call(
                fetch_down_kernel, [out((hid, width), BF16), out((8, 128), F32)], (w_down[0], own[0]), [dma], far=1
            )
            after = (token,)
    total = ()
    for at, x in zip(ranges, own):
        if at.stop < width:
            kernel, shape = functools.partial(enter_kernel, at), out((w_in.shape[0], t), F32)
        else:
            kernel, shape = functools.partial(hidden_kernel, at, slices, experts), out((t, hid), BF16)
            total = (*total, member)
        total = call(kernel, [shape], (w_in, x, across(x), *total))
    sums = reduce(products_of(total[0], w_down_near))
    args = [x for some, m in zip(sums, mixed) for x in (*some, m)]
    return call(functools.partial(result_kernel, n_pair + 1), [out((rows, width), BF16)], args)[0]


def solution(mesh):
    placed = (
        P("seq", "exp"),
        P("seq", "exp"),
        P("seq", "exp"),
        P("seq", "exp"),
        P("exp"),
        P("exp", None),
        P(),
        P("seq", None),
        P("exp", None, None),
        P("exp", None, None),
        P("exp", None, None),
    )

    def pick(query, key_in, value, decay_log, *rest):
        rows = query.shape[0] // lax.axis_size("exp")
        exp_count = lax.axis_size("exp")
        tiled = rows % TILE_ROWS == 0 and decay_log.shape[1] == 1
        for count in (exp_count, lax.axis_size("seq")):
            tiled = tiled and count >= 4 and count & (count - 1) == 0
        plan = local if tiled else plain_plan
        return plan(query, key_in, value, decay_log, *rest)

    return jax.shard_map(
        pick, mesh=mesh, in_specs=placed, out_specs=P(("seq", "exp"), None), check_vma=False
    )
```

```python
import functools

import jax
import jax.numpy as jnp
from jax import lax
from jax.experimental import pallas as pl
from jax.experimental.pallas import tpu as pltpu
from jax.sharding import PartitionSpec as P

F32 = jnp.float32
BF16 = jnp.bfloat16
TILE_ROWS = 16
COLUMNS = 1024
VMEM_LIMIT = 16 * 1024 * 1024


def plain_plan(query, key_in, value, decay_log, norm_gain, w_out, router, routes, w_gate, w_up, w_down):
    tok_count = query.shape[0]
    head_count = decay_log.shape[1]
    head_size = query.shape[1] // head_count
    top_count = routes.shape[1]
    expert_count = router.shape[1]
    capacity = max(2, 3 * tok_count * top_count // (2 * expert_count))
    exp_count = lax.axis_size("exp")
    slice_count = exp_count // expert_count
    queries = query.reshape(tok_count, head_count, head_size)
    keys_local = key_in.reshape(tok_count, head_count, head_size)
    values_local = value.reshape(tok_count, head_count, head_size)
    cumulative = jnp.cumsum(decay_log, axis=0)
    scores = jnp.einsum("thd,shd->hts", queries, keys_local, preferred_element_type=jnp.float32)
    spread = cumulative.T[:, :, None] - cumulative.T[:, None, :]
    causal = jnp.arange(tok_count)[:, None] >= jnp.arange(tok_count)[None, :]
    weights = jnp.where(causal, jnp.exp(jnp.where(causal, spread, 0.0)), 0.0)
    attend = (scores * weights / head_size).astype(jnp.bfloat16)
    intra_part = jnp.einsum(
        "hts,she->the", attend, values_local, preferred_element_type=jnp.float32
    )
    totals = cumulative[-1]
    tail_decay = jnp.exp(totals[None, :] - cumulative)
    state_delta = jnp.einsum(
        "shd,she->hde",
        keys_local.astype(jnp.float32) * tail_decay[:, :, None],
        values_local.astype(jnp.float32),
        precision=lax.Precision.HIGHEST,
    )
    decay_rows = lax.all_gather(totals[None, :], "seq", axis=0, tiled=True)
    my_rank = lax.axis_index("seq")
    seq_ranks = jnp.arange(decay_rows.shape[0])
    state_piece = lax.all_gather(
        state_delta[None].astype(jnp.bfloat16), "seq", axis=0, tiled=True
    ).astype(jnp.float32)
    piece_rank = jnp.arange(state_piece.shape[0])
    between = (seq_ranks[None, :] > piece_rank[:, None]) & (seq_ranks[None, :] < my_rank)
    logsum = jnp.dot(between.astype(jnp.float32), decay_rows, precision=lax.Precision.HIGHEST)
    factor = jnp.where((piece_rank < my_rank)[:, None], jnp.exp(logsum), 0.0)
    incoming = jnp.zeros_like(state_delta) + jnp.einsum(
        "ih,ihde->hde", factor, state_piece, precision=lax.Precision.HIGHEST
    )
    inter_part = (
        jnp.exp(cumulative)[:, :, None]
        * jnp.einsum(
            "thd,hde->the", queries.astype(jnp.float32), incoming, precision=lax.Precision.HIGHEST
        )
        / head_size
    )
    attended = intra_part + inter_part
    inverse_rms = lax.rsqrt(jnp.mean(attended * attended, axis=-1, keepdims=True) + 1e-06)
    gain_f32 = norm_gain.astype(jnp.float32).reshape(head_count, head_size)
    normed = (
        (attended * inverse_rms * gain_f32)
        .astype(jnp.bfloat16)
        .reshape(tok_count, head_count * head_size)
    )
    own_mixed = lax.psum_scatter(
        jnp.dot(normed, w_out, preferred_element_type=jnp.float32),
        "exp",
        scatter_dimension=0,
        tiled=True,
    ).astype(jnp.bfloat16)
    mixed = lax.all_gather(own_mixed, "exp", axis=0, tiled=True)
    logits = jnp.dot(mixed, router, preferred_element_type=jnp.float32)
    member = routes[:, :, None] == jnp.arange(expert_count)[None, None, :]
    picked = jnp.sum(jnp.where(member, logits[:, None, :], 0.0), axis=-1)
    raised = jnp.exp(picked)
    gate_probs = raised / jnp.sum(raised, axis=-1, keepdims=True)
    my_expert = lax.axis_index("exp") // slice_count
    flat_hit = (routes.reshape(-1) == my_expert).astype(jnp.int32)
    slot_flat = jnp.cumsum(flat_hit) - flat_hit
    slot_match = (slot_flat[:, None] == jnp.arange(capacity)[None, :]) & (flat_hit[:, None] > 0)
    token_select = jnp.sum(
        slot_match.reshape(tok_count, top_count, capacity).astype(jnp.float32), axis=1
    )
    token_gate = jnp.sum(jnp.where(routes == my_expert, gate_probs, 0.0), axis=1)
    slot_rows = jnp.dot(
        token_select.astype(jnp.bfloat16).T, mixed, preferred_element_type=jnp.float32
    ).astype(jnp.bfloat16)
    gate_part = jnp.dot(slot_rows, w_gate[0], preferred_element_type=jnp.float32)
    up_part = jnp.dot(slot_rows, w_up[0], preferred_element_type=jnp.float32)
    hidden = (jax.nn.silu(gate_part) * up_part).astype(jnp.bfloat16)
    slice_out = jnp.dot(hidden, w_down[0], preferred_element_type=jnp.float32)
    spread_out = jnp.dot(token_select, slice_out, precision=lax.Precision.HIGHEST)
    summed = lax.psum_scatter(
        token_gate[:, None] * spread_out, "exp", scatter_dimension=0, tiled=True
    )
    return (own_mixed.astype(jnp.float32) + summed).astype(jnp.bfloat16)


def iota2(shape, axis):
    return lax.broadcasted_iota(jnp.int32, shape, axis)


def cumulate(decay_row):
    t = decay_row.shape[1]
    row, col = iota2((t, t), 0), iota2((t, t), 1)
    spread = jnp.broadcast_to(decay_row, (t, t))
    column = jnp.sum(jnp.where(col <= row, spread, 0.0), axis=1, keepdims=True)
    own = jnp.sum(jnp.where(col == row, spread, 0.0), axis=1, keepdims=True)
    line = jnp.sum(jnp.where(row <= col, own, 0.0), axis=0, keepdims=True)
    return column, line


def dot_f32(a, b, dims):
    return lax.dot_general(a, b, (dims, ((), ())), preferred_element_type=F32)


def split_dot(a_f32, b, dims):
    high = a_f32.astype(BF16)
    low = (a_f32 - high.astype(F32)).astype(BF16)
    return dot_f32(high, b, dims) + dot_f32(low, b, dims)


def dma_in(sems, pairs):
    copies = [pltpu.make_async_copy(a, b, sems.at[i]) for i, (a, b) in enumerate(pairs)]
    for copy in copies:
        copy.start()
    return copies


def put_state(out_ref, state, total):
    d = state.shape[1]
    out_ref[0:d, :] = state.astype(BF16)
    wide = jnp.broadcast_to(total, (TILE_ROWS, d))
    part0 = wide.astype(BF16).astype(F32)
    part1 = (wide - part0).astype(BF16).astype(F32)
    part2 = wide - part0 - part1
    row = iota2((TILE_ROWS, d), 0)
    parts = jnp.where(row == 0, part0, jnp.where(row == 1, part1, jnp.where(row == 2, part2, 0.0)))
    out_ref[d:, :] = parts.astype(BF16)


def get_state(ref):
    d = ref.shape[1]
    return ref[0:d, :].astype(F32), jnp.sum(ref[d:, :].astype(F32), axis=0, keepdims=True)


def state_kernel(key_hbm, value_hbm, decay_hbm, out_ref, key_ref, value_ref, decay_ref, sems):
    t, d = key_ref.shape
    copies = dma_in(sems, [(decay_hbm, decay_ref), (key_hbm, key_ref), (value_hbm, value_ref)])
    for copy in copies:
        copy.wait()
    column, _ = cumulate(decay_ref[...])
    total = column[t - 1 :, :]
    keyed = key_ref[...].astype(F32) * jnp.exp(total - column)
    put_state(out_ref, split_dot(keyed, value_ref[...], ((0,), (0,))), jnp.broadcast_to(total, (1, d)))


def within_kernel(
    n_pair, query_hbm, key_hbm, value_hbm, decay_hbm, gain_hbm, router_hbm, routes_hbm, w_out_hbm, gate_hbm, up_hbm, _,
    intra_ref, grown_ref, query_ref, gain_ref, w_out_ref, in_ref, member_ref,
    key_ref, value_ref, decay_ref, gain_in_ref, router_ref, routes_ref, sems,
):
    t, d = query_ref.shape
    hid = gate_hbm.shape[0]
    copies = dma_in(
        sems,
        [
            (decay_hbm, decay_ref),
            (query_hbm, query_ref),
            (key_hbm, key_ref),
            (value_hbm, value_ref),
            (gain_hbm, gain_in_ref),
            (router_hbm, router_ref),
            (routes_hbm, routes_ref),
            (w_out_hbm, w_out_ref),
            (gate_hbm, in_ref.at[0:hid]),
            (up_hbm, in_ref.at[hid : 2 * hid]),
        ],
    )
    for copy in copies[:7]:
        copy.wait()
    column, line = cumulate(decay_ref[...])
    query, key, value = query_ref[...], key_ref[...], value_ref[...]
    scores = dot_f32(query, key, ((1,), (1,)))
    causal = iota2((t, t), 0) >= iota2((t, t), 1)
    weights = jnp.where(causal, jnp.exp(jnp.where(causal, column - line, 0.0)), 0.0)
    attend = (scores * weights * (1.0 / d)).astype(BF16)
    intra_ref[...] = dot_f32(attend, value, ((1,), (0,)))
    grown_ref[...] = jnp.broadcast_to(jnp.exp(column) * (1.0 / d), (t, d))
    gain_ref[...] = jnp.broadcast_to(gain_in_ref[...].astype(F32), gain_ref.shape)
    experts = router_ref.shape[0]
    in_ref[2 * hid :, :] = jnp.zeros((TILE_ROWS, in_ref.shape[1]), BF16)
    in_ref[2 * hid : 2 * hid + experts, :] = router_ref[...]
    padded = member_ref.shape[0]
    hits = jnp.zeros((padded, t), F32)
    for k in range(routes_ref.shape[0]):
        hits = hits + jnp.where(routes_ref[k : k + 1, :] == iota2((padded, t), 0), 1.0, 0.0)
    exp_index = lax.axis_index("exp")
    place = place_matrix(t // (2 * n_pair), n_pair, exp_index // 2, exp_index % 2)
    member_ref[...] = dot_f32(hits.astype(BF16), place, ((1,), (1,)))
    for copy in copies[7:]:
        copy.wait()


def place_matrix(rows, n_pair, pair, core):
    size = 2 * n_pair * rows
    i, j = iota2((size, size), 0), iota2((size, size), 1)
    half, inner = i // (n_pair * rows), i % (n_pair * rows)
    who = (inner // rows + pair) % n_pair
    source = (2 * who + (core + half) % 2) * rows + inner % rows
    return jnp.where(source == j, 1.0, 0.0).astype(BF16)


def fetch_down_kernel(down_hbm, _, down_ref, token_ref, sem):
    copy = pltpu.make_async_copy(down_hbm, down_ref, sem)
    copy.start()
    token_ref[...] = jnp.zeros(token_ref.shape, F32)
    copy.wait()


def normed_kernel(n_pair, moves, *refs):
    states = refs[: len(moves)]
    intra_ref, grown_ref, query_ref, gain_ref, mine_ref, theirs_ref = refs[len(moves) :]
    t, d = query_ref.shape
    me = lax.axis_index("seq")
    ranks = [move(me) for move in moves]
    parts = [get_state(ref) for ref in states]
    incoming = jnp.zeros((d, d), F32)
    for rank, (state, _) in zip(ranks, parts):
        logsum = jnp.zeros((1, d), F32)
        for other, (_, total) in zip(ranks, parts):
            logsum = logsum + jnp.where(jnp.logical_and(rank < other, other < me), total, 0.0)
        incoming = incoming + jnp.where(rank < me, jnp.exp(logsum), 0.0) * state
    high = incoming.astype(BF16)
    low = (incoming - high.astype(F32)).astype(BF16)
    query = query_ref[...]
    read = dot_f32(query, high, ((1,), (0,))) + dot_f32(query, low, ((1,), (0,)))
    attended = intra_ref[...] + grown_ref[...] * read
    inverse = lax.rsqrt(jnp.mean(attended * attended, axis=1, keepdims=True) + 1e-06)
    normed = (attended * inverse * gain_ref[0:1, :]).astype(BF16)
    exp_index = lax.axis_index("exp")
    place = place_matrix(t // (2 * n_pair), n_pair, exp_index // 2, exp_index % 2)
    normed = dot_f32(place, normed, ((1,), (0,))).astype(BF16)
    mine_ref[...] = normed[: t // 2]
    theirs_ref[...] = normed[t // 2 :]


def product_kernel(at, a_ref, b_ref, wa_ref, wb_ref, *outs):
    rows = outs[0].shape[0]
    for i in range(at.start, at.stop, COLUMNS):
        some, there = slice(i, i + COLUMNS), slice(i - at.start, i - at.start + COLUMNS)
        part = dot_f32(a_ref[...], wa_ref[:, some], ((1,), (0,))) + dot_f32(b_ref[...], wb_ref[:, some], ((1,), (0,)))
        for r, ref in enumerate(outs):
            ref[:, there] = part[r * rows : (r + 1) * rows].astype(BF16)


def halves_kernel(at, x_ref, w_ref, mine_ref, theirs_ref):
    half = mine_ref.shape[0]
    for i in range(at.start, at.stop, COLUMNS):
        part = dot_f32(x_ref[...], w_ref[:, i : i + COLUMNS], ((1,), (0,))).astype(BF16)
        mine_ref[:, i - at.start : i - at.start + COLUMNS] = part[:half]
        theirs_ref[:, i - at.start : i - at.start + COLUMNS] = part[half:]


def add_kernel(groups, a_ref, b_ref, *refs):
    outs = refs[-len(groups) :]
    rows = outs[0].shape[0] // len(groups[0])
    for group, ref in zip(groups, outs):
        for i, block in enumerate(group):
            at = slice(block * rows, (block + 1) * rows)
            total = a_ref[at, :].astype(F32) + b_ref[at, :].astype(F32)
            ref[i * rows : (i + 1) * rows, :] = total.astype(ref.dtype)


def sum_kernel(count, *refs):
    total = refs[0][...].astype(F32)
    for ref in refs[1:count]:
        total = total + ref[...].astype(F32)
    refs[-1][...] = total.astype(BF16)


def join_kernel(count, *refs):
    start = 0
    for ref in refs[:count]:
        refs[-1][start : start + ref.shape[0], :] = ref[...]
        start += ref.shape[0]


def enter_part(at, in_ref, own_ref, other_ref):
    x = jnp.concatenate([own_ref[...], other_ref[...]], axis=0)
    return dot_f32(in_ref[:, at], x, ((1,), (1,)))


def enter_kernel(at, in_ref, own_ref, other_ref, out_ref):
    out_ref[...] = enter_part(at, in_ref, own_ref, other_ref)


def hidden_kernel(at, slices, experts, in_ref, own_ref, other_ref, before_ref, member_ref, out_ref):
    total = before_ref[...] + enter_part(at, in_ref, own_ref, other_ref)
    t, hid = out_ref.shape
    gate, up, logits = total[0:hid], total[hid : 2 * hid], total[2 * hid : 2 * hid + experts]
    raised = jnp.where(member_ref[0:experts, :] > 0.5, jnp.exp(logits), 0.0)
    mine = iota2((experts, t), 0) == lax.axis_index("exp") // slices
    prob = jnp.sum(jnp.where(mine, raised, 0.0), axis=0, keepdims=True) / jnp.sum(raised, axis=0, keepdims=True)
    out_ref[...] = (gate / (1.0 + jnp.exp(-gate)) * up * prob).T.astype(BF16)


def result_kernel(count, *refs):
    out_ref = refs[-1]
    width = refs[0].shape[1]
    for i in range(len(refs) // count):
        total = refs[i * count][...].astype(F32)
        for ref in refs[i * count + 1 : (i + 1) * count]:
            total = total + ref[...].astype(F32)
        out_ref[:, i * width : (i + 1) * width] = total.astype(BF16)


def call(kernel, outs, args, scratch=(), far=0):
    whole = pl.BlockSpec(memory_space=pltpu.VMEM)
    if far:
        args = [pltpu.with_memory_space_constraint(a, pltpu.HBM) for a in args[:far]] + list(args[far:])
    return pl.pallas_call(
        kernel,
        out_shape=outs,
        in_specs=[pl.BlockSpec(memory_space=pl.ANY) if far else whole] * len(args),
        out_specs=[whole] * len(outs),
        scratch_shapes=list(scratch),
        compiler_params=pltpu.CompilerParams(vmem_limit_bytes=VMEM_LIMIT),
        cost_estimate=pl.CostEstimate(flops=0, bytes_accessed=0, transcendentals=0),
    )(*args)


def local(query, key_in, value, decay_log, norm_gain, w_out, router, routes, w_gate, w_up, w_down):
    t, d = query.shape
    width = w_out.shape[1]
    exp_count, seq_count = lax.axis_size("exp"), lax.axis_size("seq")
    n_pair = exp_count // 2
    rows = t // exp_count
    experts = router.shape[1]
    slices = exp_count // experts
    hid = w_gate.shape[2]
    out = jax.ShapeDtypeStruct
    dma = pltpu.SemaphoreType.DMA

    def shift(x, r):
        return lax.ppermute(x, "exp", [(e, (e + 2 * r) % exp_count) for e in range(exp_count)])

    def across(x):
        return lax.ppermute(x, "exp", [(e, e ^ 1) for e in range(exp_count)])

    size = width // 2
    ranges = [slice(0, size), slice(size, width)]

    def rows_of(count):
        return out((count * rows, size), BF16)

    def send(terms):
        return [[term[0]] + [shift(term[r], r) for r in range(1, n_pair)] for term in terms]

    decay_row = decay_log.T
    block = pltpu.VMEM((t, d), BF16)
    decay_block = pltpu.VMEM((1, t), F32)
    (state,) = call(
        state_kernel,
        [out((d + TILE_ROWS, d), BF16)],
        (key_in, value, decay_row),
        [block, block, decay_block, dma((3,))],
        far=3,
    )
    moves = [lambda i, k=k: i ^ k for k in range(1, seq_count)]
    states = [lax.ppermute(state, "seq", [(move(i), i) for i in range(seq_count)]) for move in moves]
    intra, grown, query_near, gain, w_out_near, w_in, member = call(
        functools.partial(within_kernel, n_pair),
        [
            out((t, d), F32),
            out((t, d), F32),
            out((t, d), BF16),
            out((8, d), F32),
            out(w_out.shape, BF16),
            out((2 * hid + TILE_ROWS, width), BF16),
            out((-(-experts // 8) * 8, t), F32),
        ],
        (query, key_in, value, decay_row, norm_gain[None, :], router.T, routes.T, w_out, w_gate[0].T, w_up[0].T, state),
        [
            block,
            block,
            decay_block,
            pltpu.VMEM((1, d), BF16),
            pltpu.VMEM((experts, width), BF16),
            pltpu.VMEM((routes.shape[1], t), jnp.int32),
            dma((10,)),
        ],
        far=10,
    )
    w_out_other = across(w_out)
    mine, theirs = call(
        functools.partial(normed_kernel, n_pair, moves),
        [out((t // 2, d), BF16)] * 2,
        (*states, intra, grown, query_near, gain),
    )
    other = across(theirs)
    terms = send(
        call(functools.partial(product_kernel, at), [rows_of(1)] * n_pair, (mine, other, w_out_near, w_out_other))
        for at in ranges
    )
    mixed = [call(functools.partial(sum_kernel, n_pair), [rows_of(1)], term)[0] for term in terms]
    gathered = [[shift(m, -r) if r else m for r in range(n_pair)] for m in mixed]
    own, after = [], ()
    for blocks in gathered:
        own += call(functools.partial(join_kernel, n_pair), [rows_of(n_pair)], (*blocks, *after))
        if not after:
            w_down_near, token = call(
                fetch_down_kernel, [out((hid, width), BF16), out((8, 128), F32)], (w_down[0], own[0]), [dma], far=1
            )
            after = (token,)
    left, right = ranges
    (total,) = call(functools.partial(enter_kernel, left), [out((w_in.shape[0], t), F32)], (w_in, own[0], across(own[0])))
    (hidden,) = call(
        functools.partial(hidden_kernel, right, slices, experts),
        [out((t, hid), BF16)],
        (w_in, own[1], across(own[1]), total, member),
    )
    products = [
        call(functools.partial(halves_kernel, at), [rows_of(n_pair)] * 2, (hidden, w_down_near)) for at in ranges
    ]
    others = [across(theirs) for _, theirs in products]
    sums = send(
        call(functools.partial(add_kernel, [[r] for r in range(n_pair)]), [rows_of(1)] * n_pair, (mine, other))
        for (mine, _), other in zip(products, others)
    )
    args = [x for some, m in zip(sums, mixed) for x in (*some, m)]
    return call(functools.partial(result_kernel, n_pair + 1), [out((rows, width), BF16)], args)[0]


def solution(mesh):
    placed = (
        P("seq", "exp"),
        P("seq", "exp"),
        P("seq", "exp"),
        P("seq", "exp"),
        P("exp"),
        P("exp", None),
        P(),
        P("seq", None),
        P("exp", None, None),
        P("exp", None, None),
        P("exp", None, None),
    )

    def pick(query, key_in, value, decay_log, *rest):
        rows = query.shape[0] // lax.axis_size("exp")
        exp_count = lax.axis_size("exp")
        tiled = rows % TILE_ROWS == 0 and decay_log.shape[1] == 1
        for count in (exp_count, lax.axis_size("seq")):
            tiled = tiled and count >= 4 and count & (count - 1) == 0
        plan = local if tiled else plain_plan
        return plan(query, key_in, value, decay_log, *rest)

    return jax.shard_map(
        pick, mesh=mesh, in_specs=placed, out_specs=P(("seq", "exp"), None), check_vma=False
    )
```

```python
import functools

import jax
import jax.numpy as jnp
from jax import lax
from jax.experimental import pallas as pl
from jax.experimental.pallas import tpu as pltpu
from jax.sharding import PartitionSpec as P

F32 = jnp.float32
BF16 = jnp.bfloat16
TILE_ROWS = 16
COLUMNS = 1024
VMEM_LIMIT = 16 * 1024 * 1024


def plain_plan(query, key_in, value, decay_log, norm_gain, w_out, router, routes, w_gate, w_up, w_down):
    tok_count = query.shape[0]
    head_count = decay_log.shape[1]
    head_size = query.shape[1] // head_count
    top_count = routes.shape[1]
    expert_count = router.shape[1]
    capacity = max(2, 3 * tok_count * top_count // (2 * expert_count))
    exp_count = lax.axis_size("exp")
    slice_count = exp_count // expert_count
    queries = query.reshape(tok_count, head_count, head_size)
    keys_local = key_in.reshape(tok_count, head_count, head_size)
    values_local = value.reshape(tok_count, head_count, head_size)
    cumulative = jnp.cumsum(decay_log, axis=0)
    scores = jnp.einsum("thd,shd->hts", queries, keys_local, preferred_element_type=jnp.float32)
    spread = cumulative.T[:, :, None] - cumulative.T[:, None, :]
    causal = jnp.arange(tok_count)[:, None] >= jnp.arange(tok_count)[None, :]
    weights = jnp.where(causal, jnp.exp(jnp.where(causal, spread, 0.0)), 0.0)
    attend = (scores * weights / head_size).astype(jnp.bfloat16)
    intra_part = jnp.einsum(
        "hts,she->the", attend, values_local, preferred_element_type=jnp.float32
    )
    totals = cumulative[-1]
    tail_decay = jnp.exp(totals[None, :] - cumulative)
    state_delta = jnp.einsum(
        "shd,she->hde",
        keys_local.astype(jnp.float32) * tail_decay[:, :, None],
        values_local.astype(jnp.float32),
        precision=lax.Precision.HIGHEST,
    )
    decay_rows = lax.all_gather(totals[None, :], "seq", axis=0, tiled=True)
    my_rank = lax.axis_index("seq")
    seq_ranks = jnp.arange(decay_rows.shape[0])
    state_piece = lax.all_gather(
        state_delta[None].astype(jnp.bfloat16), "seq", axis=0, tiled=True
    ).astype(jnp.float32)
    piece_rank = jnp.arange(state_piece.shape[0])
    between = (seq_ranks[None, :] > piece_rank[:, None]) & (seq_ranks[None, :] < my_rank)
    logsum = jnp.dot(between.astype(jnp.float32), decay_rows, precision=lax.Precision.HIGHEST)
    factor = jnp.where((piece_rank < my_rank)[:, None], jnp.exp(logsum), 0.0)
    incoming = jnp.zeros_like(state_delta) + jnp.einsum(
        "ih,ihde->hde", factor, state_piece, precision=lax.Precision.HIGHEST
    )
    inter_part = (
        jnp.exp(cumulative)[:, :, None]
        * jnp.einsum(
            "thd,hde->the", queries.astype(jnp.float32), incoming, precision=lax.Precision.HIGHEST
        )
        / head_size
    )
    attended = intra_part + inter_part
    inverse_rms = lax.rsqrt(jnp.mean(attended * attended, axis=-1, keepdims=True) + 1e-06)
    gain_f32 = norm_gain.astype(jnp.float32).reshape(head_count, head_size)
    normed = (
        (attended * inverse_rms * gain_f32)
        .astype(jnp.bfloat16)
        .reshape(tok_count, head_count * head_size)
    )
    own_mixed = lax.psum_scatter(
        jnp.dot(normed, w_out, preferred_element_type=jnp.float32),
        "exp",
        scatter_dimension=0,
        tiled=True,
    ).astype(jnp.bfloat16)
    mixed = lax.all_gather(own_mixed, "exp", axis=0, tiled=True)
    logits = jnp.dot(mixed, router, preferred_element_type=jnp.float32)
    member = routes[:, :, None] == jnp.arange(expert_count)[None, None, :]
    picked = jnp.sum(jnp.where(member, logits[:, None, :], 0.0), axis=-1)
    raised = jnp.exp(picked)
    gate_probs = raised / jnp.sum(raised, axis=-1, keepdims=True)
    my_expert = lax.axis_index("exp") // slice_count
    flat_hit = (routes.reshape(-1) == my_expert).astype(jnp.int32)
    slot_flat = jnp.cumsum(flat_hit) - flat_hit
    slot_match = (slot_flat[:, None] == jnp.arange(capacity)[None, :]) & (flat_hit[:, None] > 0)
    token_select = jnp.sum(
        slot_match.reshape(tok_count, top_count, capacity).astype(jnp.float32), axis=1
    )
    token_gate = jnp.sum(jnp.where(routes == my_expert, gate_probs, 0.0), axis=1)
    slot_rows = jnp.dot(
        token_select.astype(jnp.bfloat16).T, mixed, preferred_element_type=jnp.float32
    ).astype(jnp.bfloat16)
    gate_part = jnp.dot(slot_rows, w_gate[0], preferred_element_type=jnp.float32)
    up_part = jnp.dot(slot_rows, w_up[0], preferred_element_type=jnp.float32)
    hidden = (jax.nn.silu(gate_part) * up_part).astype(jnp.bfloat16)
    slice_out = jnp.dot(hidden, w_down[0], preferred_element_type=jnp.float32)
    spread_out = jnp.dot(token_select, slice_out, precision=lax.Precision.HIGHEST)
    summed = lax.psum_scatter(
        token_gate[:, None] * spread_out, "exp", scatter_dimension=0, tiled=True
    )
    return (own_mixed.astype(jnp.float32) + summed).astype(jnp.bfloat16)


def iota2(shape, axis):
    return lax.broadcasted_iota(jnp.int32, shape, axis)


def cumulate(decay_row):
    t = decay_row.shape[1]
    row, col = iota2((t, t), 0), iota2((t, t), 1)
    spread = jnp.broadcast_to(decay_row, (t, t))
    column = jnp.sum(jnp.where(col <= row, spread, 0.0), axis=1, keepdims=True)
    own = jnp.sum(jnp.where(col == row, spread, 0.0), axis=1, keepdims=True)
    line = jnp.sum(jnp.where(row <= col, own, 0.0), axis=0, keepdims=True)
    return column, line


def dot_f32(a, b, dims):
    return lax.dot_general(a, b, (dims, ((), ())), preferred_element_type=F32)


def split_dot(a_f32, b, dims):
    high = a_f32.astype(BF16)
    low = (a_f32 - high.astype(F32)).astype(BF16)
    return dot_f32(high, b, dims) + dot_f32(low, b, dims)


def dma_in(sems, pairs):
    copies = [pltpu.make_async_copy(a, b, sems.at[i]) for i, (a, b) in enumerate(pairs)]
    for copy in copies:
        copy.start()
    return copies


def put_state(out_ref, state, total):
    d = state.shape[1]
    out_ref[0:d, :] = state.astype(BF16)
    wide = jnp.broadcast_to(total, (TILE_ROWS, d))
    part0 = wide.astype(BF16).astype(F32)
    part1 = (wide - part0).astype(BF16).astype(F32)
    part2 = wide - part0 - part1
    row = iota2((TILE_ROWS, d), 0)
    parts = jnp.where(row == 0, part0, jnp.where(row == 1, part1, jnp.where(row == 2, part2, 0.0)))
    out_ref[d:, :] = parts.astype(BF16)


def get_state(ref):
    d = ref.shape[1]
    return ref[0:d, :].astype(F32), jnp.sum(ref[d:, :].astype(F32), axis=0, keepdims=True)


def state_kernel(key_hbm, value_hbm, decay_hbm, out_ref, key_ref, value_ref, decay_ref, sems):
    t, d = key_ref.shape
    copies = dma_in(sems, [(decay_hbm, decay_ref), (key_hbm, key_ref), (value_hbm, value_ref)])
    for copy in copies:
        copy.wait()
    column, _ = cumulate(decay_ref[...])
    total = column[t - 1 :, :]
    keyed = key_ref[...].astype(F32) * jnp.exp(total - column)
    put_state(out_ref, split_dot(keyed, value_ref[...], ((0,), (0,))), jnp.broadcast_to(total, (1, d)))


def within_kernel(
    n_pair, query_hbm, key_hbm, value_hbm, decay_hbm, gain_hbm, router_hbm, routes_hbm, w_out_hbm, gate_hbm, up_hbm, _,
    intra_ref, grown_ref, query_ref, gain_ref, w_out_ref, in_ref, member_ref,
    key_ref, value_ref, decay_ref, gain_in_ref, router_ref, routes_ref, sems,
):
    t, d = query_ref.shape
    hid = gate_hbm.shape[0]
    copies = dma_in(
        sems,
        [
            (decay_hbm, decay_ref),
            (query_hbm, query_ref),
            (key_hbm, key_ref),
            (value_hbm, value_ref),
            (gain_hbm, gain_in_ref),
            (router_hbm, router_ref),
            (routes_hbm, routes_ref),
            (w_out_hbm, w_out_ref),
            (gate_hbm, in_ref.at[0:hid]),
            (up_hbm, in_ref.at[hid : 2 * hid]),
        ],
    )
    for copy in copies[:7]:
        copy.wait()
    column, line = cumulate(decay_ref[...])
    query, key, value = query_ref[...], key_ref[...], value_ref[...]
    scores = dot_f32(query, key, ((1,), (1,)))
    causal = iota2((t, t), 0) >= iota2((t, t), 1)
    weights = jnp.where(causal, jnp.exp(jnp.where(causal, column - line, 0.0)), 0.0)
    attend = (scores * weights * (1.0 / d)).astype(BF16)
    intra_ref[...] = dot_f32(attend, value, ((1,), (0,)))
    grown_ref[...] = jnp.broadcast_to(jnp.exp(column) * (1.0 / d), (t, d))
    gain_ref[...] = jnp.broadcast_to(gain_in_ref[...].astype(F32), gain_ref.shape)
    experts = router_ref.shape[0]
    in_ref[2 * hid :, :] = jnp.zeros((TILE_ROWS, in_ref.shape[1]), BF16)
    in_ref[2 * hid : 2 * hid + experts, :] = router_ref[...]
    padded = member_ref.shape[0]
    hits = jnp.zeros((padded, t), F32)
    for k in range(routes_ref.shape[0]):
        hits = hits + jnp.where(routes_ref[k : k + 1, :] == iota2((padded, t), 0), 1.0, 0.0)
    exp_index = lax.axis_index("exp")
    place = place_matrix(t // (2 * n_pair), n_pair, exp_index // 2, exp_index % 2)
    member_ref[...] = dot_f32(hits.astype(BF16), place, ((1,), (1,)))
    for copy in copies[7:]:
        copy.wait()


def place_matrix(rows, n_pair, pair, core):
    size = 2 * n_pair * rows
    i, j = iota2((size, size), 0), iota2((size, size), 1)
    half, inner = i // (n_pair * rows), i % (n_pair * rows)
    who = (inner // rows + pair) % n_pair
    source = (2 * who + (core + half) % 2) * rows + inner % rows
    return jnp.where(source == j, 1.0, 0.0).astype(BF16)


def fetch_down_kernel(down_hbm, _, down_ref, token_ref, sem):
    copy = pltpu.make_async_copy(down_hbm, down_ref, sem)
    copy.start()
    token_ref[...] = jnp.zeros(token_ref.shape, F32)
    copy.wait()


def normed_kernel(n_pair, moves, *refs):
    states = refs[: len(moves)]
    intra_ref, grown_ref, query_ref, gain_ref, mine_ref, theirs_ref = refs[len(moves) :]
    t, d = query_ref.shape
    me = lax.axis_index("seq")
    ranks = [move(me) for move in moves]
    parts = [get_state(ref) for ref in states]
    incoming = jnp.zeros((d, d), F32)
    for rank, (state, _) in zip(ranks, parts):
        logsum = jnp.zeros((1, d), F32)
        for other, (_, total) in zip(ranks, parts):
            logsum = logsum + jnp.where(jnp.logical_and(rank < other, other < me), total, 0.0)
        incoming = incoming + jnp.where(rank < me, jnp.exp(logsum), 0.0) * state
    high = incoming.astype(BF16)
    low = (incoming - high.astype(F32)).astype(BF16)
    query = query_ref[...]
    read = dot_f32(query, high, ((1,), (0,))) + dot_f32(query, low, ((1,), (0,)))
    attended = intra_ref[...] + grown_ref[...] * read
    inverse = lax.rsqrt(jnp.mean(attended * attended, axis=1, keepdims=True) + 1e-06)
    normed = (attended * inverse * gain_ref[0:1, :]).astype(BF16)
    exp_index = lax.axis_index("exp")
    place = place_matrix(t // (2 * n_pair), n_pair, exp_index // 2, exp_index % 2)
    normed = dot_f32(place, normed, ((1,), (0,))).astype(BF16)
    mine_ref[...] = normed[: t // 2]
    theirs_ref[...] = normed[t // 2 :]


def product_kernel(at, a_ref, b_ref, wa_ref, wb_ref, *outs):
    rows = outs[0].shape[0]
    for i in range(at.start, at.stop, COLUMNS):
        some, there = slice(i, i + COLUMNS), slice(i - at.start, i - at.start + COLUMNS)
        part = dot_f32(a_ref[...], wa_ref[:, some], ((1,), (0,))) + dot_f32(b_ref[...], wb_ref[:, some], ((1,), (0,)))
        for r, ref in enumerate(outs):
            ref[:, there] = part[r * rows : (r + 1) * rows].astype(BF16)


def halves_kernel(at, x_ref, w_ref, mine_ref, theirs_ref):
    half = mine_ref.shape[0]
    for i in range(at.start, at.stop, COLUMNS):
        part = dot_f32(x_ref[...], w_ref[:, i : i + COLUMNS], ((1,), (0,))).astype(BF16)
        mine_ref[:, i - at.start : i - at.start + COLUMNS] = part[:half]
        theirs_ref[:, i - at.start : i - at.start + COLUMNS] = part[half:]


def add_kernel(groups, a_ref, b_ref, *refs):
    outs = refs[-len(groups) :]
    rows = outs[0].shape[0] // len(groups[0])
    for group, ref in zip(groups, outs):
        for i, block in enumerate(group):
            at = slice(block * rows, (block + 1) * rows)
            total = a_ref[at, :].astype(F32) + b_ref[at, :].astype(F32)
            ref[i * rows : (i + 1) * rows, :] = total.astype(ref.dtype)


def sum_kernel(count, *refs):
    total = refs[0][...].astype(F32)
    for ref in refs[1:count]:
        total = total + ref[...].astype(F32)
    refs[-1][...] = total.astype(BF16)


def join_kernel(count, *refs):
    start = 0
    for ref in refs[:count]:
        refs[-1][start : start + ref.shape[0], :] = ref[...]
        start += ref.shape[0]


def enter_part(at, in_ref, own_ref, other_ref):
    x = jnp.concatenate([own_ref[...], other_ref[...]], axis=0)
    return dot_f32(in_ref[:, at], x, ((1,), (1,)))


def enter_kernel(at, in_ref, own_ref, other_ref, out_ref):
    out_ref[...] = enter_part(at, in_ref, own_ref, other_ref)


def hidden_kernel(at, slices, experts, in_ref, own_ref, other_ref, before_ref, member_ref, out_ref):
    total = before_ref[...] + enter_part(at, in_ref, own_ref, other_ref)
    t, hid = out_ref.shape
    gate, up, logits = total[0:hid], total[hid : 2 * hid], total[2 * hid : 2 * hid + experts]
    raised = jnp.where(member_ref[0:experts, :] > 0.5, jnp.exp(logits), 0.0)
    mine = iota2((experts, t), 0) == lax.axis_index("exp") // slices
    prob = jnp.sum(jnp.where(mine, raised, 0.0), axis=0, keepdims=True) / jnp.sum(raised, axis=0, keepdims=True)
    out_ref[...] = (gate / (1.0 + jnp.exp(-gate)) * up * prob).T.astype(BF16)


def result_kernel(count, *refs):
    out_ref = refs[-1]
    width = refs[0].shape[1]
    for i in range(len(refs) // count):
        total = refs[i * count][...].astype(F32)
        for ref in refs[i * count + 1 : (i + 1) * count]:
            total = total + ref[...].astype(F32)
        out_ref[:, i * width : (i + 1) * width] = total.astype(BF16)


def call(kernel, outs, args, scratch=(), far=0):
    whole = pl.BlockSpec(memory_space=pltpu.VMEM)
    if far:
        args = [pltpu.with_memory_space_constraint(a, pltpu.HBM) for a in args[:far]] + list(args[far:])
    return pl.pallas_call(
        kernel,
        out_shape=outs,
        in_specs=[pl.BlockSpec(memory_space=pl.ANY) if far else whole] * len(args),
        out_specs=[whole] * len(outs),
        scratch_shapes=list(scratch),
        compiler_params=pltpu.CompilerParams(vmem_limit_bytes=VMEM_LIMIT),
        cost_estimate=pl.CostEstimate(flops=0, bytes_accessed=0, transcendentals=0),
    )(*args)


def local(query, key_in, value, decay_log, norm_gain, w_out, router, routes, w_gate, w_up, w_down):
    t, d = query.shape
    width = w_out.shape[1]
    exp_count, seq_count = lax.axis_size("exp"), lax.axis_size("seq")
    n_pair = exp_count // 2
    rows = t // exp_count
    experts = router.shape[1]
    slices = exp_count // experts
    hid = w_gate.shape[2]
    out = jax.ShapeDtypeStruct
    dma = pltpu.SemaphoreType.DMA

    def shift(x, r):
        return lax.ppermute(x, "exp", [(e, (e + 2 * r) % exp_count) for e in range(exp_count)])

    def across(x):
        return lax.ppermute(x, "exp", [(e, e ^ 1) for e in range(exp_count)])

    size = width // 2
    ranges = [slice(0, size), slice(size, width)]

    def rows_of(count):
        return out((count * rows, size), BF16)

    def send(terms):
        return [[term[0]] + [shift(term[r], r) for r in range(1, n_pair)] for term in terms]

    decay_row = decay_log.T
    block = pltpu.VMEM((t, d), BF16)
    decay_block = pltpu.VMEM((1, t), F32)
    (state,) = call(
        state_kernel,
        [out((d + TILE_ROWS, d), BF16)],
        (key_in, value, decay_row),
        [block, block, decay_block, dma((3,))],
        far=3,
    )
    order = [2, 1] + list(range(3, seq_count))
    moves = [lambda i, k=k: i ^ k for k in order]
    states = [lax.ppermute(state, "seq", [(move(i), i) for i in range(seq_count)]) for move in moves]
    intra, grown, query_near, gain, w_out_near, w_in, member = call(
        functools.partial(within_kernel, n_pair),
        [
            out((t, d), F32),
            out((t, d), F32),
            out((t, d), BF16),
            out((8, d), F32),
            out(w_out.shape, BF16),
            out((2 * hid + TILE_ROWS, width), BF16),
            out((-(-experts // 8) * 8, t), F32),
        ],
        (query, key_in, value, decay_row, norm_gain[None, :], router.T, routes.T, w_out, w_gate[0].T, w_up[0].T, state),
        [
            block,
            block,
            decay_block,
            pltpu.VMEM((1, d), BF16),
            pltpu.VMEM((experts, width), BF16),
            pltpu.VMEM((routes.shape[1], t), jnp.int32),
            dma((10,)),
        ],
        far=10,
    )
    w_out_other = across(w_out)
    mine, theirs = call(
        functools.partial(normed_kernel, n_pair, moves),
        [out((t // 2, d), BF16)] * 2,
        (*states, intra, grown, query_near, gain),
    )
    other = across(theirs)
    terms = send(
        call(functools.partial(product_kernel, at), [rows_of(1)] * n_pair, (mine, other, w_out_near, w_out_other))
        for at in ranges
    )
    mixed = [call(functools.partial(sum_kernel, n_pair), [rows_of(1)], term)[0] for term in terms]
    gathered = [[shift(m, -r) if r else m for r in range(n_pair)] for m in mixed]
    own, after = [], ()
    for blocks in gathered:
        own += call(functools.partial(join_kernel, n_pair), [rows_of(n_pair)], (*blocks, *after))
        if not after:
            w_down_near, token = call(
                fetch_down_kernel, [out((hid, width), BF16), out((8, 128), F32)], (w_down[0], own[0]), [dma], far=1
            )
            after = (token,)
    left, right = ranges
    (total,) = call(functools.partial(enter_kernel, left), [out((w_in.shape[0], t), F32)], (w_in, own[0], across(own[0])))
    (hidden,) = call(
        functools.partial(hidden_kernel, right, slices, experts),
        [out((t, hid), BF16)],
        (w_in, own[1], across(own[1]), total, member),
    )
    products = [
        call(functools.partial(halves_kernel, at), [rows_of(n_pair)] * 2, (hidden, w_down_near)) for at in ranges
    ]
    others = [across(theirs) for _, theirs in products]
    sums = send(
        call(functools.partial(add_kernel, [[r] for r in range(n_pair)]), [rows_of(1)] * n_pair, (mine, other))
        for (mine, _), other in zip(products, others)
    )
    args = [x for some, m in zip(sums, mixed) for x in (*some, m)]
    return call(functools.partial(result_kernel, n_pair + 1), [out((rows, width), BF16)], args)[0]


def solution(mesh):
    placed = (
        P("seq", "exp"),
        P("seq", "exp"),
        P("seq", "exp"),
        P("seq", "exp"),
        P("exp"),
        P("exp", None),
        P(),
        P("seq", None),
        P("exp", None, None),
        P("exp", None, None),
        P("exp", None, None),
    )

    def pick(query, key_in, value, decay_log, *rest):
        rows = query.shape[0] // lax.axis_size("exp")
        exp_count = lax.axis_size("exp")
        tiled = rows % TILE_ROWS == 0 and decay_log.shape[1] == 1
        for count in (exp_count, lax.axis_size("seq")):
            tiled = tiled and count >= 4 and count & (count - 1) == 0
        plan = local if tiled else plain_plan
        return plan(query, key_in, value, decay_log, *rest)

    return jax.shard_map(
        pick, mesh=mesh, in_specs=placed, out_specs=P(("seq", "exp"), None), check_vma=False
    )
```

```python
import functools

import jax
import jax.numpy as jnp
from jax import lax
from jax.experimental import pallas as pl
from jax.experimental.pallas import tpu as pltpu
from jax.sharding import PartitionSpec as P

F32 = jnp.float32
BF16 = jnp.bfloat16
TILE_ROWS = 16
COLUMNS = 1024
VMEM_LIMIT = 16 * 1024 * 1024


def plain_plan(query, key_in, value, decay_log, norm_gain, w_out, router, routes, w_gate, w_up, w_down):
    tok_count = query.shape[0]
    head_count = decay_log.shape[1]
    head_size = query.shape[1] // head_count
    top_count = routes.shape[1]
    expert_count = router.shape[1]
    capacity = max(2, 3 * tok_count * top_count // (2 * expert_count))
    exp_count = lax.axis_size("exp")
    slice_count = exp_count // expert_count
    queries = query.reshape(tok_count, head_count, head_size)
    keys_local = key_in.reshape(tok_count, head_count, head_size)
    values_local = value.reshape(tok_count, head_count, head_size)
    cumulative = jnp.cumsum(decay_log, axis=0)
    scores = jnp.einsum("thd,shd->hts", queries, keys_local, preferred_element_type=jnp.float32)
    spread = cumulative.T[:, :, None] - cumulative.T[:, None, :]
    causal = jnp.arange(tok_count)[:, None] >= jnp.arange(tok_count)[None, :]
    weights = jnp.where(causal, jnp.exp(jnp.where(causal, spread, 0.0)), 0.0)
    attend = (scores * weights / head_size).astype(jnp.bfloat16)
    intra_part = jnp.einsum(
        "hts,she->the", attend, values_local, preferred_element_type=jnp.float32
    )
    totals = cumulative[-1]
    tail_decay = jnp.exp(totals[None, :] - cumulative)
    state_delta = jnp.einsum(
        "shd,she->hde",
        keys_local.astype(jnp.float32) * tail_decay[:, :, None],
        values_local.astype(jnp.float32),
        precision=lax.Precision.HIGHEST,
    )
    decay_rows = lax.all_gather(totals[None, :], "seq", axis=0, tiled=True)
    my_rank = lax.axis_index("seq")
    seq_ranks = jnp.arange(decay_rows.shape[0])
    state_piece = lax.all_gather(
        state_delta[None].astype(jnp.bfloat16), "seq", axis=0, tiled=True
    ).astype(jnp.float32)
    piece_rank = jnp.arange(state_piece.shape[0])
    between = (seq_ranks[None, :] > piece_rank[:, None]) & (seq_ranks[None, :] < my_rank)
    logsum = jnp.dot(between.astype(jnp.float32), decay_rows, precision=lax.Precision.HIGHEST)
    factor = jnp.where((piece_rank < my_rank)[:, None], jnp.exp(logsum), 0.0)
    incoming = jnp.zeros_like(state_delta) + jnp.einsum(
        "ih,ihde->hde", factor, state_piece, precision=lax.Precision.HIGHEST
    )
    inter_part = (
        jnp.exp(cumulative)[:, :, None]
        * jnp.einsum(
            "thd,hde->the", queries.astype(jnp.float32), incoming, precision=lax.Precision.HIGHEST
        )
        / head_size
    )
    attended = intra_part + inter_part
    inverse_rms = lax.rsqrt(jnp.mean(attended * attended, axis=-1, keepdims=True) + 1e-06)
    gain_f32 = norm_gain.astype(jnp.float32).reshape(head_count, head_size)
    normed = (
        (attended * inverse_rms * gain_f32)
        .astype(jnp.bfloat16)
        .reshape(tok_count, head_count * head_size)
    )
    own_mixed = lax.psum_scatter(
        jnp.dot(normed, w_out, preferred_element_type=jnp.float32),
        "exp",
        scatter_dimension=0,
        tiled=True,
    ).astype(jnp.bfloat16)
    mixed = lax.all_gather(own_mixed, "exp", axis=0, tiled=True)
    logits = jnp.dot(mixed, router, preferred_element_type=jnp.float32)
    member = routes[:, :, None] == jnp.arange(expert_count)[None, None, :]
    picked = jnp.sum(jnp.where(member, logits[:, None, :], 0.0), axis=-1)
    raised = jnp.exp(picked)
    gate_probs = raised / jnp.sum(raised, axis=-1, keepdims=True)
    my_expert = lax.axis_index("exp") // slice_count
    flat_hit = (routes.reshape(-1) == my_expert).astype(jnp.int32)
    slot_flat = jnp.cumsum(flat_hit) - flat_hit
    slot_match = (slot_flat[:, None] == jnp.arange(capacity)[None, :]) & (flat_hit[:, None] > 0)
    token_select = jnp.sum(
        slot_match.reshape(tok_count, top_count, capacity).astype(jnp.float32), axis=1
    )
    token_gate = jnp.sum(jnp.where(routes == my_expert, gate_probs, 0.0), axis=1)
    slot_rows = jnp.dot(
        token_select.astype(jnp.bfloat16).T, mixed, preferred_element_type=jnp.float32
    ).astype(jnp.bfloat16)
    gate_part = jnp.dot(slot_rows, w_gate[0], preferred_element_type=jnp.float32)
    up_part = jnp.dot(slot_rows, w_up[0], preferred_element_type=jnp.float32)
    hidden = (jax.nn.silu(gate_part) * up_part).astype(jnp.bfloat16)
    slice_out = jnp.dot(hidden, w_down[0], preferred_element_type=jnp.float32)
    spread_out = jnp.dot(token_select, slice_out, precision=lax.Precision.HIGHEST)
    summed = lax.psum_scatter(
        token_gate[:, None] * spread_out, "exp", scatter_dimension=0, tiled=True
    )
    return (own_mixed.astype(jnp.float32) + summed).astype(jnp.bfloat16)


def iota2(shape, axis):
    return lax.broadcasted_iota(jnp.int32, shape, axis)


def cumulate(decay_row):
    t = decay_row.shape[1]
    row, col = iota2((t, t), 0), iota2((t, t), 1)
    spread = jnp.broadcast_to(decay_row, (t, t))
    column = jnp.sum(jnp.where(col <= row, spread, 0.0), axis=1, keepdims=True)
    own = jnp.sum(jnp.where(col == row, spread, 0.0), axis=1, keepdims=True)
    line = jnp.sum(jnp.where(row <= col, own, 0.0), axis=0, keepdims=True)
    return column, line


def dot_f32(a, b, dims):
    return lax.dot_general(a, b, (dims, ((), ())), preferred_element_type=F32)


def split_dot(a_f32, b, dims):
    high = a_f32.astype(BF16)
    low = (a_f32 - high.astype(F32)).astype(BF16)
    return dot_f32(high, b, dims) + dot_f32(low, b, dims)


def dma_in(sems, pairs):
    copies = [pltpu.make_async_copy(a, b, sems.at[i]) for i, (a, b) in enumerate(pairs)]
    for copy in copies:
        copy.start()
    return copies


def put_state(out_ref, state, total):
    d = state.shape[1]
    out_ref[0:d, :] = state.astype(BF16)
    wide = jnp.broadcast_to(total, (TILE_ROWS, d))
    part0 = wide.astype(BF16).astype(F32)
    part1 = (wide - part0).astype(BF16).astype(F32)
    part2 = wide - part0 - part1
    row = iota2((TILE_ROWS, d), 0)
    parts = jnp.where(row == 0, part0, jnp.where(row == 1, part1, jnp.where(row == 2, part2, 0.0)))
    out_ref[d:, :] = parts.astype(BF16)


def get_state(ref):
    d = ref.shape[1]
    return ref[0:d, :].astype(F32), jnp.sum(ref[d:, :].astype(F32), axis=0, keepdims=True)


def state_kernel(key_hbm, value_hbm, decay_hbm, out_ref, key_ref, value_ref, decay_ref, sems):
    t, d = key_ref.shape
    copies = dma_in(sems, [(decay_hbm, decay_ref), (key_hbm, key_ref), (value_hbm, value_ref)])
    for copy in copies:
        copy.wait()
    column, _ = cumulate(decay_ref[...])
    total = column[t - 1 :, :]
    keyed = key_ref[...].astype(F32) * jnp.exp(total - column)
    put_state(out_ref, split_dot(keyed, value_ref[...], ((0,), (0,))), jnp.broadcast_to(total, (1, d)))


def within_kernel(
    n_pair, query_hbm, key_hbm, value_hbm, decay_hbm, gain_hbm, router_hbm, routes_hbm, w_out_hbm, gate_hbm, up_hbm, _,
    intra_ref, grown_ref, query_ref, gain_ref, w_out_ref, in_ref, member_ref,
    key_ref, value_ref, decay_ref, gain_in_ref, router_ref, routes_ref, sems,
):
    t, d = query_ref.shape
    hid = gate_hbm.shape[0]
    copies = dma_in(
        sems,
        [
            (decay_hbm, decay_ref),
            (query_hbm, query_ref),
            (key_hbm, key_ref),
            (value_hbm, value_ref),
            (gain_hbm, gain_in_ref),
            (router_hbm, router_ref),
            (routes_hbm, routes_ref),
            (w_out_hbm, w_out_ref),
            (gate_hbm, in_ref.at[0:hid]),
            (up_hbm, in_ref.at[hid : 2 * hid]),
        ],
    )
    for copy in copies[:7]:
        copy.wait()
    column, line = cumulate(decay_ref[...])
    query, key, value = query_ref[...], key_ref[...], value_ref[...]
    scores = dot_f32(query, key, ((1,), (1,)))
    causal = iota2((t, t), 0) >= iota2((t, t), 1)
    weights = jnp.where(causal, jnp.exp(jnp.where(causal, column - line, 0.0)), 0.0)
    attend = (scores * weights * (1.0 / d)).astype(BF16)
    intra_ref[...] = dot_f32(attend, value, ((1,), (0,)))
    grown_ref[...] = jnp.broadcast_to(jnp.exp(column) * (1.0 / d), (t, d))
    gain_ref[...] = jnp.broadcast_to(gain_in_ref[...].astype(F32), gain_ref.shape)
    experts = router_ref.shape[0]
    in_ref[2 * hid :, :] = jnp.zeros((TILE_ROWS, in_ref.shape[1]), BF16)
    in_ref[2 * hid : 2 * hid + experts, :] = router_ref[...]
    padded = member_ref.shape[0]
    hits = jnp.zeros((padded, t), F32)
    for k in range(routes_ref.shape[0]):
        hits = hits + jnp.where(routes_ref[k : k + 1, :] == iota2((padded, t), 0), 1.0, 0.0)
    exp_index = lax.axis_index("exp")
    place = place_matrix(t // (2 * n_pair), n_pair, exp_index // 2, exp_index % 2)
    member_ref[...] = dot_f32(hits.astype(BF16), place, ((1,), (1,)))
    for copy in copies[7:]:
        copy.wait()


def place_matrix(rows, n_pair, pair, core):
    size = 2 * n_pair * rows
    i, j = iota2((size, size), 0), iota2((size, size), 1)
    half, inner = i // (n_pair * rows), i % (n_pair * rows)
    who = (inner // rows + pair) % n_pair
    source = (2 * who + (core + half) % 2) * rows + inner % rows
    return jnp.where(source == j, 1.0, 0.0).astype(BF16)


def fetch_down_kernel(down_hbm, _, down_ref, token_ref, sem):
    copy = pltpu.make_async_copy(down_hbm, down_ref, sem)
    copy.start()
    token_ref[...] = jnp.zeros(token_ref.shape, F32)
    copy.wait()


def normed_kernel(n_pair, moves, *refs):
    states = refs[: len(moves)]
    intra_ref, grown_ref, query_ref, gain_ref, mine_ref, theirs_ref = refs[len(moves) :]
    t, d = query_ref.shape
    me = lax.axis_index("seq")
    ranks = [move(me) for move in moves]
    parts = [get_state(ref) for ref in states]
    incoming = jnp.zeros((d, d), F32)
    for rank, (state, _) in zip(ranks, parts):
        logsum = jnp.zeros((1, d), F32)
        for other, (_, total) in zip(ranks, parts):
            logsum = logsum + jnp.where(jnp.logical_and(rank < other, other < me), total, 0.0)
        incoming = incoming + jnp.where(rank < me, jnp.exp(logsum), 0.0) * state
    high = incoming.astype(BF16)
    low = (incoming - high.astype(F32)).astype(BF16)
    query = query_ref[...]
    read = dot_f32(query, high, ((1,), (0,))) + dot_f32(query, low, ((1,), (0,)))
    attended = intra_ref[...] + grown_ref[...] * read
    inverse = lax.rsqrt(jnp.mean(attended * attended, axis=1, keepdims=True) + 1e-06)
    normed = (attended * inverse * gain_ref[0:1, :]).astype(BF16)
    exp_index = lax.axis_index("exp")
    place = place_matrix(t // (2 * n_pair), n_pair, exp_index // 2, exp_index % 2)
    normed = dot_f32(place, normed, ((1,), (0,))).astype(BF16)
    mine_ref[...] = normed[: t // 2]
    theirs_ref[...] = normed[t // 2 :]


def product_kernel(at, a_ref, b_ref, wa_ref, wb_ref, *outs):
    rows = outs[0].shape[0]
    for i in range(at.start, at.stop, COLUMNS):
        some, there = slice(i, i + COLUMNS), slice(i - at.start, i - at.start + COLUMNS)
        part = dot_f32(a_ref[...], wa_ref[:, some], ((1,), (0,))) + dot_f32(b_ref[...], wb_ref[:, some], ((1,), (0,)))
        for r, ref in enumerate(outs):
            ref[:, there] = part[r * rows : (r + 1) * rows].astype(BF16)


def halves_kernel(at, x_ref, w_ref, mine_ref, theirs_ref):
    half = mine_ref.shape[0]
    for i in range(at.start, at.stop, COLUMNS):
        part = dot_f32(x_ref[...], w_ref[:, i : i + COLUMNS], ((1,), (0,))).astype(BF16)
        mine_ref[:, i - at.start : i - at.start + COLUMNS] = part[:half]
        theirs_ref[:, i - at.start : i - at.start + COLUMNS] = part[half:]


def add_kernel(groups, a_ref, b_ref, *refs):
    outs = refs[-len(groups) :]
    rows = outs[0].shape[0] // len(groups[0])
    for group, ref in zip(groups, outs):
        for i, block in enumerate(group):
            at = slice(block * rows, (block + 1) * rows)
            total = a_ref[at, :].astype(F32) + b_ref[at, :].astype(F32)
            ref[i * rows : (i + 1) * rows, :] = total.astype(ref.dtype)


def sum_kernel(count, *refs):
    total = refs[0][...].astype(F32)
    for ref in refs[1:count]:
        total = total + ref[...].astype(F32)
    refs[-1][...] = total.astype(BF16)


def join_kernel(count, *refs):
    start = 0
    for ref in refs[:count]:
        refs[-1][start : start + ref.shape[0], :] = ref[...]
        start += ref.shape[0]


def enter_part(at, in_ref, own_ref, other_ref):
    x = jnp.concatenate([own_ref[...], other_ref[...]], axis=0)
    return dot_f32(in_ref[:, at], x, ((1,), (1,)))


def enter_kernel(at, in_ref, own_ref, other_ref, out_ref):
    out_ref[...] = enter_part(at, in_ref, own_ref, other_ref)


def hidden_kernel(at, slices, experts, in_ref, own_ref, other_ref, before_ref, member_ref, out_ref):
    total = before_ref[...] + enter_part(at, in_ref, own_ref, other_ref)
    t, hid = out_ref.shape
    gate, up, logits = total[0:hid], total[hid : 2 * hid], total[2 * hid : 2 * hid + experts]
    raised = jnp.where(member_ref[0:experts, :] > 0.5, jnp.exp(logits), 0.0)
    mine = iota2((experts, t), 0) == lax.axis_index("exp") // slices
    prob = jnp.sum(jnp.where(mine, raised, 0.0), axis=0, keepdims=True) / jnp.sum(raised, axis=0, keepdims=True)
    out_ref[...] = (gate / (1.0 + jnp.exp(-gate)) * up * prob).T.astype(BF16)


def result_kernel(count, *refs):
    out_ref = refs[-1]
    width = refs[0].shape[1]
    for i in range(len(refs) // count):
        total = refs[i * count][...].astype(F32)
        for ref in refs[i * count + 1 : (i + 1) * count]:
            total = total + ref[...].astype(F32)
        out_ref[:, i * width : (i + 1) * width] = total.astype(BF16)


def call(kernel, outs, args, scratch=(), far=0):
    whole = pl.BlockSpec(memory_space=pltpu.VMEM)
    if far:
        args = [pltpu.with_memory_space_constraint(a, pltpu.HBM) for a in args[:far]] + list(args[far:])
    return pl.pallas_call(
        kernel,
        out_shape=outs,
        in_specs=[pl.BlockSpec(memory_space=pl.ANY) if far else whole] * len(args),
        out_specs=[whole] * len(outs),
        scratch_shapes=list(scratch),
        compiler_params=pltpu.CompilerParams(vmem_limit_bytes=VMEM_LIMIT),
        cost_estimate=pl.CostEstimate(flops=0, bytes_accessed=0, transcendentals=0),
    )(*args)


def local(query, key_in, value, decay_log, norm_gain, w_out, router, routes, w_gate, w_up, w_down):
    t, d = query.shape
    width = w_out.shape[1]
    exp_count, seq_count = lax.axis_size("exp"), lax.axis_size("seq")
    n_pair = exp_count // 2
    rows = t // exp_count
    experts = router.shape[1]
    slices = exp_count // experts
    hid = w_gate.shape[2]
    out = jax.ShapeDtypeStruct
    dma = pltpu.SemaphoreType.DMA

    def shift(x, r):
        return lax.ppermute(x, "exp", [(e, (e + 2 * r) % exp_count) for e in range(exp_count)])

    def across(x):
        return lax.ppermute(x, "exp", [(e, e ^ 1) for e in range(exp_count)])

    size = width // 2
    ranges = [slice(0, size), slice(size, width)]

    def rows_of(count):
        return out((count * rows, size), BF16)

    def send(terms):
        ways = [list(range(1, n_pair)), list(range(n_pair - 1, 0, -1))]
        return [[term[0]] + [shift(term[r], r) for r in ways[i % 2]] for i, term in enumerate(terms)]

    decay_row = decay_log.T
    block = pltpu.VMEM((t, d), BF16)
    decay_block = pltpu.VMEM((1, t), F32)
    (state,) = call(
        state_kernel,
        [out((d + TILE_ROWS, d), BF16)],
        (key_in, value, decay_row),
        [block, block, decay_block, dma((3,))],
        far=3,
    )
    moves = [lambda i, k=k: i ^ k for k in range(1, seq_count)]
    states = [lax.ppermute(state, "seq", [(move(i), i) for i in range(seq_count)]) for move in moves]
    intra, grown, query_near, gain, w_out_near, w_in, member = call(
        functools.partial(within_kernel, n_pair),
        [
            out((t, d), F32),
            out((t, d), F32),
            out((t, d), BF16),
            out((8, d), F32),
            out(w_out.shape, BF16),
            out((2 * hid + TILE_ROWS, width), BF16),
            out((-(-experts // 8) * 8, t), F32),
        ],
        (query, key_in, value, decay_row, norm_gain[None, :], router.T, routes.T, w_out, w_gate[0].T, w_up[0].T, state),
        [
            block,
            block,
            decay_block,
            pltpu.VMEM((1, d), BF16),
            pltpu.VMEM((experts, width), BF16),
            pltpu.VMEM((routes.shape[1], t), jnp.int32),
            dma((10,)),
        ],
        far=10,
    )
    w_out_other = across(w_out)
    mine, theirs = call(
        functools.partial(normed_kernel, n_pair, moves),
        [out((t // 2, d), BF16)] * 2,
        (*states, intra, grown, query_near, gain),
    )
    other = across(theirs)
    terms = send(
        call(functools.partial(product_kernel, at), [rows_of(1)] * n_pair, (mine, other, w_out_near, w_out_other))
        for at in ranges
    )
    mixed = [call(functools.partial(sum_kernel, n_pair), [rows_of(1)], term)[0] for term in terms]
    gathered = [[shift(m, -r) if r else m for r in range(n_pair)] for m in mixed]
    own, after = [], ()
    for blocks in gathered:
        own += call(functools.partial(join_kernel, n_pair), [rows_of(n_pair)], (*blocks, *after))
        if not after:
            w_down_near, token = call(
                fetch_down_kernel, [out((hid, width), BF16), out((8, 128), F32)], (w_down[0], own[0]), [dma], far=1
            )
            after = (token,)
    left, right = ranges
    (total,) = call(functools.partial(enter_kernel, left), [out((w_in.shape[0], t), F32)], (w_in, own[0], across(own[0])))
    (hidden,) = call(
        functools.partial(hidden_kernel, right, slices, experts),
        [out((t, hid), BF16)],
        (w_in, own[1], across(own[1]), total, member),
    )
    products = [
        call(functools.partial(halves_kernel, at), [rows_of(n_pair)] * 2, (hidden, w_down_near)) for at in ranges
    ]
    others = [across(theirs) for _, theirs in products]
    sums = send(
        call(functools.partial(add_kernel, [[r] for r in range(n_pair)]), [rows_of(1)] * n_pair, (mine, other))
        for (mine, _), other in zip(products, others)
    )
    args = [x for some, m in zip(sums, mixed) for x in (*some, m)]
    return call(functools.partial(result_kernel, n_pair + 1), [out((rows, width), BF16)], args)[0]


def solution(mesh):
    placed = (
        P("seq", "exp"),
        P("seq", "exp"),
        P("seq", "exp"),
        P("seq", "exp"),
        P("exp"),
        P("exp", None),
        P(),
        P("seq", None),
        P("exp", None, None),
        P("exp", None, None),
        P("exp", None, None),
    )

    def pick(query, key_in, value, decay_log, *rest):
        rows = query.shape[0] // lax.axis_size("exp")
        exp_count = lax.axis_size("exp")
        tiled = rows % TILE_ROWS == 0 and decay_log.shape[1] == 1
        for count in (exp_count, lax.axis_size("seq")):
            tiled = tiled and count >= 4 and count & (count - 1) == 0
        plan = local if tiled else plain_plan
        return plan(query, key_in, value, decay_log, *rest)

    return jax.shard_map(
        pick, mesh=mesh, in_specs=placed, out_specs=P(("seq", "exp"), None), check_vma=False
    )
```

```python
import functools

import jax
import jax.numpy as jnp
from jax import lax
from jax.experimental import pallas as pl
from jax.experimental.pallas import tpu as pltpu
from jax.sharding import PartitionSpec as P

F32 = jnp.float32
BF16 = jnp.bfloat16
TILE_ROWS = 16
COLUMNS = 2048
VMEM_LIMIT = 16 * 1024 * 1024


def plain_plan(query, key_in, value, decay_log, norm_gain, w_out, router, routes, w_gate, w_up, w_down):
    tok_count = query.shape[0]
    head_count = decay_log.shape[1]
    head_size = query.shape[1] // head_count
    top_count = routes.shape[1]
    expert_count = router.shape[1]
    capacity = max(2, 3 * tok_count * top_count // (2 * expert_count))
    exp_count = lax.axis_size("exp")
    slice_count = exp_count // expert_count
    queries = query.reshape(tok_count, head_count, head_size)
    keys_local = key_in.reshape(tok_count, head_count, head_size)
    values_local = value.reshape(tok_count, head_count, head_size)
    cumulative = jnp.cumsum(decay_log, axis=0)
    scores = jnp.einsum("thd,shd->hts", queries, keys_local, preferred_element_type=jnp.float32)
    spread = cumulative.T[:, :, None] - cumulative.T[:, None, :]
    causal = jnp.arange(tok_count)[:, None] >= jnp.arange(tok_count)[None, :]
    weights = jnp.where(causal, jnp.exp(jnp.where(causal, spread, 0.0)), 0.0)
    attend = (scores * weights / head_size).astype(jnp.bfloat16)
    intra_part = jnp.einsum(
        "hts,she->the", attend, values_local, preferred_element_type=jnp.float32
    )
    totals = cumulative[-1]
    tail_decay = jnp.exp(totals[None, :] - cumulative)
    state_delta = jnp.einsum(
        "shd,she->hde",
        keys_local.astype(jnp.float32) * tail_decay[:, :, None],
        values_local.astype(jnp.float32),
        precision=lax.Precision.HIGHEST,
    )
    decay_rows = lax.all_gather(totals[None, :], "seq", axis=0, tiled=True)
    my_rank = lax.axis_index("seq")
    seq_ranks = jnp.arange(decay_rows.shape[0])
    state_piece = lax.all_gather(
        state_delta[None].astype(jnp.bfloat16), "seq", axis=0, tiled=True
    ).astype(jnp.float32)
    piece_rank = jnp.arange(state_piece.shape[0])
    between = (seq_ranks[None, :] > piece_rank[:, None]) & (seq_ranks[None, :] < my_rank)
    logsum = jnp.dot(between.astype(jnp.float32), decay_rows, precision=lax.Precision.HIGHEST)
    factor = jnp.where((piece_rank < my_rank)[:, None], jnp.exp(logsum), 0.0)
    incoming = jnp.zeros_like(state_delta) + jnp.einsum(
        "ih,ihde->hde", factor, state_piece, precision=lax.Precision.HIGHEST
    )
    inter_part = (
        jnp.exp(cumulative)[:, :, None]
        * jnp.einsum(
            "thd,hde->the", queries.astype(jnp.float32), incoming, precision=lax.Precision.HIGHEST
        )
        / head_size
    )
    attended = intra_part + inter_part
    inverse_rms = lax.rsqrt(jnp.mean(attended * attended, axis=-1, keepdims=True) + 1e-06)
    gain_f32 = norm_gain.astype(jnp.float32).reshape(head_count, head_size)
    normed = (
        (attended * inverse_rms * gain_f32)
        .astype(jnp.bfloat16)
        .reshape(tok_count, head_count * head_size)
    )
    own_mixed = lax.psum_scatter(
        jnp.dot(normed, w_out, preferred_element_type=jnp.float32),
        "exp",
        scatter_dimension=0,
        tiled=True,
    ).astype(jnp.bfloat16)
    mixed = lax.all_gather(own_mixed, "exp", axis=0, tiled=True)
    logits = jnp.dot(mixed, router, preferred_element_type=jnp.float32)
    member = routes[:, :, None] == jnp.arange(expert_count)[None, None, :]
    picked = jnp.sum(jnp.where(member, logits[:, None, :], 0.0), axis=-1)
    raised = jnp.exp(picked)
    gate_probs = raised / jnp.sum(raised, axis=-1, keepdims=True)
    my_expert = lax.axis_index("exp") // slice_count
    flat_hit = (routes.reshape(-1) == my_expert).astype(jnp.int32)
    slot_flat = jnp.cumsum(flat_hit) - flat_hit
    slot_match = (slot_flat[:, None] == jnp.arange(capacity)[None, :]) & (flat_hit[:, None] > 0)
    token_select = jnp.sum(
        slot_match.reshape(tok_count, top_count, capacity).astype(jnp.float32), axis=1
    )
    token_gate = jnp.sum(jnp.where(routes == my_expert, gate_probs, 0.0), axis=1)
    slot_rows = jnp.dot(
        token_select.astype(jnp.bfloat16).T, mixed, preferred_element_type=jnp.float32
    ).astype(jnp.bfloat16)
    gate_part = jnp.dot(slot_rows, w_gate[0], preferred_element_type=jnp.float32)
    up_part = jnp.dot(slot_rows, w_up[0], preferred_element_type=jnp.float32)
    hidden = (jax.nn.silu(gate_part) * up_part).astype(jnp.bfloat16)
    slice_out = jnp.dot(hidden, w_down[0], preferred_element_type=jnp.float32)
    spread_out = jnp.dot(token_select, slice_out, precision=lax.Precision.HIGHEST)
    summed = lax.psum_scatter(
        token_gate[:, None] * spread_out, "exp", scatter_dimension=0, tiled=True
    )
    return (own_mixed.astype(jnp.float32) + summed).astype(jnp.bfloat16)


def iota2(shape, axis):
    return lax.broadcasted_iota(jnp.int32, shape, axis)


def cumulate(decay_row):
    t = decay_row.shape[1]
    row, col = iota2((t, t), 0), iota2((t, t), 1)
    spread = jnp.broadcast_to(decay_row, (t, t))
    column = jnp.sum(jnp.where(col <= row, spread, 0.0), axis=1, keepdims=True)
    own = jnp.sum(jnp.where(col == row, spread, 0.0), axis=1, keepdims=True)
    line = jnp.sum(jnp.where(row <= col, own, 0.0), axis=0, keepdims=True)
    return column, line


def dot_f32(a, b, dims):
    return lax.dot_general(a, b, (dims, ((), ())), preferred_element_type=F32)


def split_dot(a_f32, b, dims):
    high = a_f32.astype(BF16)
    low = (a_f32 - high.astype(F32)).astype(BF16)
    return dot_f32(high, b, dims) + dot_f32(low, b, dims)


def dma_in(sems, pairs):
    copies = [pltpu.make_async_copy(a, b, sems.at[i]) for i, (a, b) in enumerate(pairs)]
    for copy in copies:
        copy.start()
    return copies


def put_state(out_ref, state, total):
    d = state.shape[1]
    out_ref[0:d, :] = state.astype(BF16)
    wide = jnp.broadcast_to(total, (TILE_ROWS, d))
    part0 = wide.astype(BF16).astype(F32)
    part1 = (wide - part0).astype(BF16).astype(F32)
    part2 = wide - part0 - part1
    row = iota2((TILE_ROWS, d), 0)
    parts = jnp.where(row == 0, part0, jnp.where(row == 1, part1, jnp.where(row == 2, part2, 0.0)))
    out_ref[d:, :] = parts.astype(BF16)


def get_state(ref):
    d = ref.shape[1]
    return ref[0:d, :].astype(F32), jnp.sum(ref[d:, :].astype(F32), axis=0, keepdims=True)


def state_kernel(key_hbm, value_hbm, decay_hbm, out_ref, key_ref, value_ref, decay_ref, sems):
    t, d = key_ref.shape
    copies = dma_in(sems, [(decay_hbm, decay_ref), (key_hbm, key_ref), (value_hbm, value_ref)])
    for copy in copies:
        copy.wait()
    column, _ = cumulate(decay_ref[...])
    total = column[t - 1 :, :]
    keyed = key_ref[...].astype(F32) * jnp.exp(total - column)
    put_state(out_ref, split_dot(keyed, value_ref[...], ((0,), (0,))), jnp.broadcast_to(total, (1, d)))


def within_kernel(
    n_pair, query_hbm, key_hbm, value_hbm, decay_hbm, gain_hbm, router_hbm, routes_hbm, w_out_hbm, gate_hbm, up_hbm, _,
    intra_ref, grown_ref, query_ref, gain_ref, w_out_ref, in_ref, member_ref,
    key_ref, value_ref, decay_ref, gain_in_ref, router_ref, routes_ref, sems,
):
    t, d = query_ref.shape
    hid = gate_hbm.shape[0]
    copies = dma_in(
        sems,
        [
            (decay_hbm, decay_ref),
            (query_hbm, query_ref),
            (key_hbm, key_ref),
            (value_hbm, value_ref),
            (gain_hbm, gain_in_ref),
            (router_hbm, router_ref),
            (routes_hbm, routes_ref),
            (w_out_hbm, w_out_ref),
            (gate_hbm, in_ref.at[0:hid]),
            (up_hbm, in_ref.at[hid : 2 * hid]),
        ],
    )
    for copy in copies[:7]:
        copy.wait()
    column, line = cumulate(decay_ref[...])
    query, key, value = query_ref[...], key_ref[...], value_ref[...]
    scores = dot_f32(query, key, ((1,), (1,)))
    causal = iota2((t, t), 0) >= iota2((t, t), 1)
    weights = jnp.where(causal, jnp.exp(jnp.where(causal, column - line, 0.0)), 0.0)
    attend = (scores * weights * (1.0 / d)).astype(BF16)
    intra_ref[...] = dot_f32(attend, value, ((1,), (0,)))
    grown_ref[...] = jnp.broadcast_to(jnp.exp(column) * (1.0 / d), (t, d))
    gain_ref[...] = jnp.broadcast_to(gain_in_ref[...].astype(F32), gain_ref.shape)
    experts = router_ref.shape[0]
    in_ref[2 * hid :, :] = jnp.zeros((TILE_ROWS, in_ref.shape[1]), BF16)
    in_ref[2 * hid : 2 * hid + experts, :] = router_ref[...]
    padded = member_ref.shape[0]
    hits = jnp.zeros((padded, t), F32)
    for k in range(routes_ref.shape[0]):
        hits = hits + jnp.where(routes_ref[k : k + 1, :] == iota2((padded, t), 0), 1.0, 0.0)
    exp_index = lax.axis_index("exp")
    place = place_matrix(t // (2 * n_pair), n_pair, exp_index // 2, exp_index % 2)
    member_ref[...] = dot_f32(hits.astype(BF16), place, ((1,), (1,)))
    for copy in copies[7:]:
        copy.wait()


def place_matrix(rows, n_pair, pair, core):
    size = 2 * n_pair * rows
    i, j = iota2((size, size), 0), iota2((size, size), 1)
    half, inner = i // (n_pair * rows), i % (n_pair * rows)
    who = (inner // rows + pair) % n_pair
    source = (2 * who + (core + half) % 2) * rows + inner % rows
    return jnp.where(source == j, 1.0, 0.0).astype(BF16)


def fetch_down_kernel(down_hbm, _, down_ref, token_ref, sem):
    copy = pltpu.make_async_copy(down_hbm, down_ref, sem)
    copy.start()
    token_ref[...] = jnp.zeros(token_ref.shape, F32)
    copy.wait()


def normed_kernel(n_pair, moves, *refs):
    states = refs[: len(moves)]
    intra_ref, grown_ref, query_ref, gain_ref, mine_ref, theirs_ref = refs[len(moves) :]
    t, d = query_ref.shape
    me = lax.axis_index("seq")
    ranks = [move(me) for move in moves]
    parts = [get_state(ref) for ref in states]
    incoming = jnp.zeros((d, d), F32)
    for rank, (state, _) in zip(ranks, parts):
        logsum = jnp.zeros((1, d), F32)
        for other, (_, total) in zip(ranks, parts):
            logsum = logsum + jnp.where(jnp.logical_and(rank < other, other < me), total, 0.0)
        incoming = incoming + jnp.where(rank < me, jnp.exp(logsum), 0.0) * state
    high = incoming.astype(BF16)
    low = (incoming - high.astype(F32)).astype(BF16)
    query = query_ref[...]
    read = dot_f32(query, high, ((1,), (0,))) + dot_f32(query, low, ((1,), (0,)))
    attended = intra_ref[...] + grown_ref[...] * read
    inverse = lax.rsqrt(jnp.mean(attended * attended, axis=1, keepdims=True) + 1e-06)
    normed = (attended * inverse * gain_ref[0:1, :]).astype(BF16)
    exp_index = lax.axis_index("exp")
    place = place_matrix(t // (2 * n_pair), n_pair, exp_index // 2, exp_index % 2)
    normed = dot_f32(place, normed, ((1,), (0,))).astype(BF16)
    mine_ref[...] = normed[: t // 2]
    theirs_ref[...] = normed[t // 2 :]


def product_kernel(at, a_ref, b_ref, wa_ref, wb_ref, *outs):
    rows = outs[0].shape[0]
    for i in range(at.start, at.stop, COLUMNS):
        some, there = slice(i, i + COLUMNS), slice(i - at.start, i - at.start + COLUMNS)
        part = dot_f32(a_ref[...], wa_ref[:, some], ((1,), (0,))) + dot_f32(b_ref[...], wb_ref[:, some], ((1,), (0,)))
        for r, ref in enumerate(outs):
            ref[:, there] = part[r * rows : (r + 1) * rows].astype(BF16)


def halves_kernel(at, x_ref, w_ref, mine_ref, theirs_ref):
    half = mine_ref.shape[0]
    for i in range(at.start, at.stop, COLUMNS):
        part = dot_f32(x_ref[...], w_ref[:, i : i + COLUMNS], ((1,), (0,))).astype(BF16)
        mine_ref[:, i - at.start : i - at.start + COLUMNS] = part[:half]
        theirs_ref[:, i - at.start : i - at.start + COLUMNS] = part[half:]


def add_kernel(groups, a_ref, b_ref, *refs):
    outs = refs[-len(groups) :]
    rows = outs[0].shape[0] // len(groups[0])
    for group, ref in zip(groups, outs):
        for i, block in enumerate(group):
            at = slice(block * rows, (block + 1) * rows)
            total = a_ref[at, :].astype(F32) + b_ref[at, :].astype(F32)
            ref[i * rows : (i + 1) * rows, :] = total.astype(ref.dtype)


def sum_kernel(count, *refs):
    total = refs[0][...].astype(F32)
    for ref in refs[1:count]:
        total = total + ref[...].astype(F32)
    refs[-1][...] = total.astype(BF16)


def join_kernel(count, *refs):
    start = 0
    for ref in refs[:count]:
        refs[-1][start : start + ref.shape[0], :] = ref[...]
        start += ref.shape[0]


def enter_part(at, in_ref, own_ref, other_ref):
    x = jnp.concatenate([own_ref[...], other_ref[...]], axis=0)
    return dot_f32(in_ref[:, at], x, ((1,), (1,)))


def enter_kernel(at, in_ref, own_ref, other_ref, out_ref):
    out_ref[...] = enter_part(at, in_ref, own_ref, other_ref)


def hidden_kernel(at, slices, experts, in_ref, own_ref, other_ref, before_ref, member_ref, out_ref):
    total = before_ref[...] + enter_part(at, in_ref, own_ref, other_ref)
    t, hid = out_ref.shape
    gate, up, logits = total[0:hid], total[hid : 2 * hid], total[2 * hid : 2 * hid + experts]
    raised = jnp.where(member_ref[0:experts, :] > 0.5, jnp.exp(logits), 0.0)
    mine = iota2((experts, t), 0) == lax.axis_index("exp") // slices
    prob = jnp.sum(jnp.where(mine, raised, 0.0), axis=0, keepdims=True) / jnp.sum(raised, axis=0, keepdims=True)
    out_ref[...] = (gate / (1.0 + jnp.exp(-gate)) * up * prob).T.astype(BF16)


def result_kernel(count, *refs):
    out_ref = refs[-1]
    width = refs[0].shape[1]
    for i in range(len(refs) // count):
        total = refs[i * count][...].astype(F32)
        for ref in refs[i * count + 1 : (i + 1) * count]:
            total = total + ref[...].astype(F32)
        out_ref[:, i * width : (i + 1) * width] = total.astype(BF16)


def call(kernel, outs, args, scratch=(), far=0):
    whole = pl.BlockSpec(memory_space=pltpu.VMEM)
    if far:
        args = [pltpu.with_memory_space_constraint(a, pltpu.HBM) for a in args[:far]] + list(args[far:])
    return pl.pallas_call(
        kernel,
        out_shape=outs,
        in_specs=[pl.BlockSpec(memory_space=pl.ANY) if far else whole] * len(args),
        out_specs=[whole] * len(outs),
        scratch_shapes=list(scratch),
        compiler_params=pltpu.CompilerParams(vmem_limit_bytes=VMEM_LIMIT),
        cost_estimate=pl.CostEstimate(flops=0, bytes_accessed=0, transcendentals=0),
    )(*args)


def local(query, key_in, value, decay_log, norm_gain, w_out, router, routes, w_gate, w_up, w_down):
    t, d = query.shape
    width = w_out.shape[1]
    exp_count, seq_count = lax.axis_size("exp"), lax.axis_size("seq")
    n_pair = exp_count // 2
    rows = t // exp_count
    experts = router.shape[1]
    slices = exp_count // experts
    hid = w_gate.shape[2]
    out = jax.ShapeDtypeStruct
    dma = pltpu.SemaphoreType.DMA

    def shift(x, r):
        return lax.ppermute(x, "exp", [(e, (e + 2 * r) % exp_count) for e in range(exp_count)])

    def across(x):
        return lax.ppermute(x, "exp", [(e, e ^ 1) for e in range(exp_count)])

    size = width // 2
    ranges = [slice(0, size), slice(size, width)]

    def rows_of(count):
        return out((count * rows, size), BF16)

    def send(terms):
        return [[term[0]] + [shift(term[r], r) for r in range(1, n_pair)] for term in terms]

    decay_row = decay_log.T
    block = pltpu.VMEM((t, d), BF16)
    decay_block = pltpu.VMEM((1, t), F32)
    (state,) = call(
        state_kernel,
        [out((d + TILE_ROWS, d), BF16)],
        (key_in, value, decay_row),
        [block, block, decay_block, dma((3,))],
        far=3,
    )
    moves = [lambda i, k=k: i ^ k for k in range(1, seq_count)]
    states = [lax.ppermute(state, "seq", [(move(i), i) for i in range(seq_count)]) for move in moves]
    intra, grown, query_near, gain, w_out_near, w_in, member = call(
        functools.partial(within_kernel, n_pair),
        [
            out((t, d), F32),
            out((t, d), F32),
            out((t, d), BF16),
            out((8, d), F32),
            out(w_out.shape, BF16),
            out((2 * hid + TILE_ROWS, width), BF16),
            out((-(-experts // 8) * 8, t), F32),
        ],
        (query, key_in, value, decay_row, norm_gain[None, :], router.T, routes.T, w_out, w_gate[0].T, w_up[0].T, state),
        [
            block,
            block,
            decay_block,
            pltpu.VMEM((1, d), BF16),
            pltpu.VMEM((experts, width), BF16),
            pltpu.VMEM((routes.shape[1], t), jnp.int32),
            dma((10,)),
        ],
        far=10,
    )
    w_out_other = across(w_out)
    mine, theirs = call(
        functools.partial(normed_kernel, n_pair, moves),
        [out((t // 2, d), BF16)] * 2,
        (*states, intra, grown, query_near, gain),
    )
    other = across(theirs)
    terms = send(
        call(functools.partial(product_kernel, at), [rows_of(1)] * n_pair, (mine, other, w_out_near, w_out_other))
        for at in ranges
    )
    mixed = [call(functools.partial(sum_kernel, n_pair), [rows_of(1)], term)[0] for term in terms]
    gathered = [[shift(m, -r) if r else m for r in range(n_pair)] for m in mixed]
    own, after = [], ()
    for blocks in gathered:
        own += call(functools.partial(join_kernel, n_pair), [rows_of(n_pair)], (*blocks, *after))
        if not after:
            w_down_near, token = call(
                fetch_down_kernel, [out((hid, width), BF16), out((8, 128), F32)], (w_down[0], own[0]), [dma], far=1
            )
            after = (token,)
    left, right = ranges
    (total,) = call(functools.partial(enter_kernel, left), [out((w_in.shape[0], t), F32)], (w_in, own[0], across(own[0])))
    (hidden,) = call(
        functools.partial(hidden_kernel, right, slices, experts),
        [out((t, hid), BF16)],
        (w_in, own[1], across(own[1]), total, member),
    )
    products = [
        call(functools.partial(halves_kernel, at), [rows_of(n_pair)] * 2, (hidden, w_down_near)) for at in ranges
    ]
    others = [across(theirs) for _, theirs in products]
    sums = send(
        call(functools.partial(add_kernel, [[r] for r in range(n_pair)]), [rows_of(1)] * n_pair, (mine, other))
        for (mine, _), other in zip(products, others)
    )
    args = [x for some, m in zip(sums, mixed) for x in (*some, m)]
    return call(functools.partial(result_kernel, n_pair + 1), [out((rows, width), BF16)], args)[0]


def solution(mesh):
    placed = (
        P("seq", "exp"),
        P("seq", "exp"),
        P("seq", "exp"),
        P("seq", "exp"),
        P("exp"),
        P("exp", None),
        P(),
        P("seq", None),
        P("exp", None, None),
        P("exp", None, None),
        P("exp", None, None),
    )

    def pick(query, key_in, value, decay_log, *rest):
        rows = query.shape[0] // lax.axis_size("exp")
        exp_count = lax.axis_size("exp")
        tiled = rows % TILE_ROWS == 0 and decay_log.shape[1] == 1
        for count in (exp_count, lax.axis_size("seq")):
            tiled = tiled and count >= 4 and count & (count - 1) == 0
        plan = local if tiled else plain_plan
        return plan(query, key_in, value, decay_log, *rest)

    return jax.shard_map(
        pick, mesh=mesh, in_specs=placed, out_specs=P(("seq", "exp"), None), check_vma=False
    )
```
